32 devices in a mesh: section: 2 (over x), dp: 16 (over z, y, core).
Axes of the slice: x: 2, y: 2, z: 4, core: 2. Of those that a mesh axis runs over, the one named last changes fastest.
Arguments:
- patches: bfloat16 [32, 196, 768], P('dp'), may hold values from -6 to 6
- cotangent: bfloat16 [32, 98, 768], P('dp'), may hold values from -6 to 6
- ordering: int32 [32, 196], P('dp'), may hold values from 0 to 195, each once within a row
- lead_qkv: bfloat16 [2, 768, 2304], P('section', 'dp'), may hold values from -0.21875 to 0.21875
- lead_proj: bfloat16 [2, 768, 768], P('section', 'dp'), may hold values from -0.4375 to 0.4375
- lead_up: bfloat16 [2, 768, 3072], P('section', 'dp'), may hold values from -0.21875 to 0.21875
- lead_down: bfloat16 [2, 3072, 768], P('section', 'dp'), may hold values from -0.109375 to 0.109375
- lead_vectors: bfloat16 [2, 12, 768], P('section', None, 'dp'), may hold values from -3 to 3, as said below
- lead_bias: bfloat16 [2, 3072], P('section', 'dp'), may hold values from -1 to 1
- side_qkv: bfloat16 [2, 768, 2304], P('section', 'dp'), may hold values from -0.21875 to 0.21875
- side_proj: bfloat16 [2, 768, 768], P('section', 'dp'), may hold values from -0.4375 to 0.4375
- side_up: bfloat16 [2, 768, 3072], P('section', 'dp'), may hold values from -0.21875 to 0.21875
- side_down: bfloat16 [2, 3072, 768], P('section', 'dp'), may hold values from -0.109375 to 0.109375
- side_vectors: bfloat16 [2, 13, 768], P('section', None, 'dp'), may hold values from -3 to 3, as said below
- side_bias: bfloat16 [2, 3072], P('section', 'dp'), may hold values from -1 to 1
Outputs:
- section_rows: float32 [2, 32, 196, 768], P('section', 'dp')
- lead_qkv_grad: float32 [2, 768, 2304], P('section', 'dp')
- lead_proj_grad: float32 [2, 768, 768], P('section', 'dp')
- lead_up_grad: float32 [2, 768, 3072], P('section', 'dp')
- lead_down_grad: float32 [2, 3072, 768], P('section', 'dp')
- lead_vectors_grad: float32 [2, 12, 768], P('section', None, 'dp')
- lead_bias_grad: float32 [2, 3072], P('section', 'dp')
- decoder_qkv_grad: float32 [768, 2304], P(('section', 'dp'))
- decoder_proj_grad: float32 [768, 768], P(('section', 'dp'))
- decoder_up_grad: float32 [768, 3072], P(('section', 'dp'))
- decoder_down_grad: float32 [3072, 768], P(('section', 'dp'))
- decoder_vectors_grad: float32 [13, 768], P(None, ('section', 'dp'))
- decoder_bias_grad: float32 [3072], P(('section', 'dp'))
The draws below stay inside these ranges and needn't reach their ends.
Inputs may be any that keep to these rules, and one draw needn't show every extreme that they name: `ordering`: each row lists every patch of one crop once; its first 98 entries are the masked patches, the remaining ones the visible patches, in the order in which the blocks take them. `lead_vectors`: gains (rows 0, 2, 4) lie near 1, layer scales (rows 10, 11) between 0.5 and 1.5. `side_vectors`: gains (rows 0, 2, 4) lie near 1, layer scales (rows 10, 11) between 0.5 and 1.5.
All inputs are finite; a program needn't handle non-finite values.
Results may differ from the reference program's by a relative error of at most 0.014.
Values may be sent and summed in bfloat16 or wider, within the bound.
A program may use at most 320 MiB of HBM per device.

```python
import math
import jax
import jax.numpy as jnp
from jax import lax

D = 768
HEADS = 12
HEAD_DIM = 64
FF = 3072
GRID = 14
PATCHES = 196
MASKED = 98
CROPS_DEV = 2
CROPS = 32


def vector_table(key, row_count):
    keys = jax.random.split(key, 4)
    shape = (2, row_count, D)
    gains = 1.0 + 0.15 * jax.random.truncated_normal(keys[0], -3.0, 3.0, shape, jnp.float32)
    shifts = 0.2 * jax.random.truncated_normal(keys[1], -3.0, 3.0, shape, jnp.float32)
    scales = jnp.exp(jax.random.uniform(keys[2], shape, jnp.float32, math.log(0.5), math.log(1.5)))
    token = jax.random.truncated_normal(keys[3], -3.0, 3.0, shape, jnp.float32)
    row_ids = lax.broadcasted_iota(jnp.int32, shape, 1)
    gain_rows = (row_ids == 0) | (row_ids == 2) | (row_ids == 4)
    scale_rows = (row_ids == 10) | (row_ids == 11)
    return jnp.where(gain_rows, gains, jnp.where(scale_rows, scales, jnp.where(row_ids == 12, token, shifts)))


def draw_lead_vectors(key, part):
    key = jax.random.fold_in(key, 1)
    return vector_table(key, 12).astype(jnp.bfloat16)


def draw_side_vectors(key, part):
    key = jax.random.fold_in(key, 2)
    return vector_table(key, 13).astype(jnp.bfloat16)


def level_of(own_key, extent, shards, smallest, top_value):
    factor_of = 1.0
    for dim, parts in shards:
        draws = jax.random.uniform(jax.random.fold_in(jax.random.fold_in(own_key, 6), dim), (parts,), jnp.float32, smallest / len(shards), top_value / len(shards))
        factor_of = factor_of * jnp.repeat(jnp.exp(draws), extent[dim] // parts).reshape((-1,) + (1,) * (len(extent) - 1 - dim))
    return factor_of


def scatter_about(key, dims, scale, most, cuts=(), kind=jnp.bfloat16):
    drawn = jax.random.normal(key, dims, jnp.float32) * scale
    if len(cuts) > 0:
        drawn = level_of(key, dims, cuts, -0.22, 0.18) * drawn
    return jnp.clip(drawn, min=-most, max=most).astype(kind)


def setup_inputs(seed: int = 0) -> dict:
    seeds = jax.random.split(jax.random.key(seed), 16)
    return {
        "patches": scatter_about(seeds[0], (CROPS, PATCHES, D), 1.0, 6.0, ((0, 16),)),
        "cotangent": scatter_about(seeds[1], (CROPS, MASKED, D), 1.0, 6.0, ((0, 16),)),
        "ordering": jax.vmap(lambda own: jax.random.permutation(own, PATCHES))(jax.random.split(seeds[2], CROPS)).reshape((CROPS, PATCHES)).astype(jnp.int32),
        "lead_qkv": scatter_about(seeds[3], (2, D, 3 * D), D ** -0.5, 0.21875, ((0, 2), (1, 16))),
        "lead_proj": scatter_about(seeds[4], (2, D, D), (D // 4) ** -0.5, 0.4375, ((0, 2), (1, 16))),
        "lead_up": scatter_about(seeds[5], (2, D, FF), D ** -0.5, 0.21875, ((0, 2), (1, 16))),
        "lead_down": scatter_about(seeds[6], (2, FF, D), FF ** -0.5, 0.109375, ((0, 2), (1, 16))),
        "lead_vectors": draw_lead_vectors(jax.random.fold_in(seeds[15], 71), 0),
        "lead_bias": scatter_about(seeds[8], (2, FF), 0.2, 1.0, ((0, 2), (1, 16))),
        "side_qkv": scatter_about(seeds[9], (2, D, 3 * D), D ** -0.5, 0.21875, ((0, 2), (1, 16))),
        "side_proj": scatter_about(seeds[10], (2, D, D), (D // 4) ** -0.5, 0.4375, ((0, 2), (1, 16))),
        "side_up": scatter_about(seeds[11], (2, D, FF), D ** -0.5, 0.21875, ((0, 2), (1, 16))),
        "side_down": scatter_about(seeds[12], (2, FF, D), FF ** -0.5, 0.109375, ((0, 2), (1, 16))),
        "side_vectors": draw_side_vectors(jax.random.fold_in(seeds[15], 71), 0),
        "side_bias": scatter_about(seeds[14], (2, FF), 0.2, 1.0, ((0, 2), (1, 16))),
    }


@jax.custom_vjp
def low(v):
    return lax.optimization_barrier(v.astype(jnp.bfloat16)).astype(jnp.float32)

@jax.custom_vjp
def low_back(v):
    return v

def low_keep(v):
    return (low(v), None)

def low_pass(kept, grad):
    return (grad,)

def back_keep(v):
    return (v, None)

def back_low(kept, grad):
    return (low(grad),)
low.defvjp(low_keep, low_pass)
low_back.defvjp(back_keep, back_low)

def layer_norm(values, gain, shift):
    center = values - lax.optimization_barrier(jnp.mean(values, axis=-1, keepdims=True))
    spread = lax.optimization_barrier(jnp.mean(center * center, axis=-1, keepdims=True))
    return center * lax.rsqrt(spread + 1e-06) * gain + shift

def positions():
    patch_ids = jnp.arange(PATCHES)
    height = (patch_ids // GRID).astype(jnp.float32)
    across = (patch_ids % GRID).astype(jnp.float32)
    quarter = D // 4
    frequency = 1.0 / 10000.0 ** (jnp.arange(quarter).astype(jnp.float32) / quarter)
    angle_rows = height[:, None] * frequency[None, :]
    angle_cols = across[:, None] * frequency[None, :]
    return jnp.concatenate([jnp.sin(angle_cols), jnp.cos(angle_cols), jnp.sin(angle_rows), jnp.cos(angle_rows)], axis=1)

def dense(values, weight):
    return jnp.dot(values, weight, precision=lax.Precision.HIGHEST)

def attend(queries, key_rows, value_rows):
    groups, rows_q, _ = queries.shape
    rows_k = key_rows.shape[1]
    query_heads = queries.reshape(groups, rows_q, HEADS, HEAD_DIM)
    key_heads = key_rows.reshape(groups, rows_k, HEADS, HEAD_DIM)
    value_heads = value_rows.reshape(groups, rows_k, HEADS, HEAD_DIM)
    scores = jnp.einsum('gqhd,gkhd->ghqk', query_heads, key_heads, precision=lax.Precision.HIGHEST)
    scores = low_back(scores * HEAD_DIM ** (-0.5))
    probs = low(jax.nn.softmax(scores, axis=-1))
    mixed_rows = jnp.einsum('ghqk,gkhd->gqhd', probs, value_heads, precision=lax.Precision.HIGHEST)
    return mixed_rows.reshape(groups, rows_q, HEADS * HEAD_DIM)

def block(stream, context, weights):
    qkv_weight, proj_weight, up_weight, down_weight, vectors, up_bias = weights
    rows_q = stream.shape[1]
    source = stream if context is None else jnp.concatenate([context, stream], axis=1)
    normed = low(layer_norm(source, vectors[0], vectors[1]))
    queries = low(low_back(dense(normed[:, -rows_q:], qkv_weight[:, :D]) + vectors[6]))
    key_rows = low(low_back(dense(normed, qkv_weight[:, D:2 * D])))
    value_rows = low(low_back(dense(normed, qkv_weight[:, 2 * D:]) + vectors[7]))
    mixed_rows = low(low_back(attend(queries, key_rows, value_rows)))
    attn_out = low_back(dense(mixed_rows, proj_weight) + vectors[8])
    residual = stream + vectors[10] * attn_out
    second = low(layer_norm(residual, vectors[2], vectors[3]))
    pre_gelu = low_back(dense(second, up_weight) + up_bias)
    hidden = low(jax.nn.gelu(pre_gelu, approximate=False))
    branch = low_back(dense(hidden, down_weight) + vectors[9])
    return layer_norm(residual + vectors[11] * branch, vectors[4], vectors[5])

def reference(patches, cotangent, ordering, lead_qkv, lead_proj, lead_up, lead_down, lead_vectors, lead_bias, side_qkv, side_proj, side_up, side_down, side_vectors, side_bias):
    pos_table = positions()
    lead_arrays = (lead_qkv, lead_proj, lead_up, lead_down, lead_vectors, lead_bias)
    side_arrays = (side_qkv, side_proj, side_up, side_down, side_vectors, side_bias)
    encoder = tuple((member[0].astype(jnp.float32) for member in lead_arrays))
    regressor = tuple((member[1].astype(jnp.float32) for member in lead_arrays))
    teacher = tuple((member[0].astype(jnp.float32) for member in side_arrays))
    decoder = tuple((member[1].astype(jnp.float32) for member in side_arrays))
    groups = CROPS // CROPS_DEV
    patch_groups = patches.reshape(groups, CROPS_DEV, PATCHES, D)
    cot_groups = cotangent.reshape(groups, CROPS_DEV, MASKED, D)
    order_groups = ordering.reshape(groups, CROPS_DEV, PATCHES)

    def crop_step(totals, inputs):
        patch_group, cot_group, order_group = inputs
        patch_float = patch_group.astype(jnp.float32)
        masked_ids = order_group[:, :MASKED]
        visible_ids = order_group[:, MASKED:]
        masked_rows = jnp.take_along_axis(patch_float, masked_ids[:, :, None], axis=1)
        targets = low(block(masked_rows, None, teacher))
        pos_visible = pos_table[visible_ids]
        pos_masked = pos_table[masked_ids]

        def forward(patch_all, enc_weights, reg_weights, dec_weights):
            visible_rows = jnp.take_along_axis(patch_all, visible_ids[:, :, None], axis=1)
            latents = low(low_back(block(visible_rows, None, enc_weights)))
            mask_queries = dec_weights[4][12] + pos_masked
            regressed = block(mask_queries, latents + pos_visible, reg_weights)
            decoded = block(regressed + pos_masked, None, dec_weights)
            return (regressed, decoded)
        (regressed, decoded), pullback = jax.vjp(forward, patch_float, encoder, regressor, decoder)
        grad_in, enc_grad, reg_grad, dec_grad = pullback((regressed - targets, cot_group.astype(jnp.float32)))
        totals = jax.tree.map(jnp.add, totals, (enc_grad, reg_grad, dec_grad))
        return (totals, (grad_in, jnp.concatenate([regressed, decoded], axis=1)))
    zero_grads = jax.tree.map(jnp.zeros_like, (encoder, regressor, decoder))
    (enc_total, reg_total, dec_total), (grad_rows, latent_rows) = lax.scan(crop_step, zero_grads, (patch_groups, cot_groups, order_groups))
    section_rows = jnp.stack([grad_rows.reshape(CROPS, PATCHES, D), latent_rows.reshape(CROPS, PATCHES, D)])
    lead_grads = tuple((jnp.stack([enc_part, reg_part]) for enc_part, reg_part in zip(enc_total, reg_total)))
    return (section_rows, lead_grads[0], lead_grads[1], lead_grads[2], lead_grads[3], lead_grads[4], lead_grads[5], dec_total[0], dec_total[1], dec_total[2], dec_total[3], dec_total[4], dec_total[5])
```

```python
import functools

import jax
import jax.experimental.pallas as pl
import jax.experimental.pallas.tpu as pltpu
import jax.numpy as jnp
from jax import lax
from jax.sharding import PartitionSpec as P

D = 768
HEADS = 12
HEAD_DIM = 64
FF = 3072
GRID = 14
PATCHES = 196
MASKED = 98


def passed_along(array, axis, by):
    count = lax.axis_size(axis)
    pairs = [(i, i + by) for i in range(count) if 0 <= i + by < count]
    return lax.ppermute(array, axis, pairs)


def layer_norm(values, gain, shift):
    center = values - jnp.mean(values, axis=-1, keepdims=True)
    spread = jnp.mean(center * center, axis=-1, keepdims=True)
    return center * lax.rsqrt(spread + 1e-06) * gain + shift


def positions():
    patch_ids = jnp.arange(PATCHES)
    height = (patch_ids // GRID).astype(jnp.float32)
    across = (patch_ids % GRID).astype(jnp.float32)
    quarter = D // 4
    frequency = 1.0 / 10000.0 ** (jnp.arange(quarter).astype(jnp.float32) / quarter)
    angle_rows = height[:, None] * frequency[None, :]
    angle_cols = across[:, None] * frequency[None, :]
    return jnp.concatenate(
        [jnp.sin(angle_cols), jnp.cos(angle_cols), jnp.sin(angle_rows), jnp.cos(angle_rows)], axis=1
    )


def gelu_exact(values):
    return jax.nn.gelu(values, approximate=False)


def project(values, weight):
    return jnp.dot(values, weight, preferred_element_type=jnp.float32)


def contract_rows(left, right):
    return jnp.einsum("gli,glo->io", left, right, preferred_element_type=jnp.float32)


def back_project(grad_rows, weight):
    return jnp.einsum("glo,io->gli", grad_rows, weight, preferred_element_type=jnp.float32)


def row_total(values):
    return jnp.sum(values.astype(jnp.float32), axis=(0, 1))


def split_heads(values):
    return values.reshape(values.shape[0], values.shape[1], HEADS, HEAD_DIM)


def attend_forward(queries, key_rows, value_rows):
    scores = jnp.einsum(
        "gqhd,gkhd->ghqk",
        split_heads(queries),
        split_heads(key_rows),
        preferred_element_type=jnp.float32,
    )
    scores = scores * HEAD_DIM ** (-0.5)
    top_score = jnp.max(scores, axis=-1, keepdims=True)
    powers = jnp.exp(scores - top_score)
    total_mass = jnp.sum(powers, axis=-1, keepdims=True)
    probs = (powers / total_mass).astype(jnp.bfloat16)
    mixed_rows = jnp.einsum(
        "ghqk,gkhd->gqhd", probs, split_heads(value_rows), preferred_element_type=jnp.float32
    )
    return (
        mixed_rows.reshape(queries.shape[0], queries.shape[1], D),
        top_score + jnp.log(total_mass),
    )


def attend_backward(queries, key_rows, value_rows, log_total, grad_mixed):
    query_heads = split_heads(queries)
    key_heads = split_heads(key_rows)
    scores = jnp.einsum(
        "gqhd,gkhd->ghqk", query_heads, key_heads, preferred_element_type=jnp.float32
    )
    probs = jnp.exp(scores * HEAD_DIM ** (-0.5) - log_total)
    grad_heads = split_heads(grad_mixed)
    grad_values = jnp.einsum(
        "ghqk,gqhd->gkhd",
        probs.astype(jnp.bfloat16),
        grad_heads,
        preferred_element_type=jnp.float32,
    )
    grad_probs = jnp.einsum(
        "gqhd,gkhd->ghqk", grad_heads, split_heads(value_rows), preferred_element_type=jnp.float32
    )
    grad_scores = probs * (grad_probs - jnp.sum(grad_probs * probs, axis=-1, keepdims=True))
    grad_scores = grad_scores.astype(jnp.bfloat16)
    grad_queries = jnp.einsum(
        "ghqk,gkhd->gqhd", grad_scores, key_heads, preferred_element_type=jnp.float32
    ) * HEAD_DIM ** (-0.5)
    grad_keys = jnp.einsum(
        "ghqk,gqhd->gkhd", grad_scores, query_heads, preferred_element_type=jnp.float32
    ) * HEAD_DIM ** (-0.5)
    rows_q = queries.shape[1]
    rows_k = key_rows.shape[1]
    groups = queries.shape[0]
    return (
        grad_queries.reshape(groups, rows_q, D).astype(jnp.bfloat16),
        grad_keys.reshape(groups, rows_k, D).astype(jnp.bfloat16),
        grad_values.reshape(groups, rows_k, D).astype(jnp.bfloat16),
    )


def run_block(stream, context, weights):
    qkv_weight, proj_weight, up_weight, down_weight, vectors, up_bias = weights
    rows_q = stream.shape[1]
    source = stream if context is None else jnp.concatenate([context, stream], axis=1)
    normed, first_back = jax.vjp(layer_norm, source, vectors[0], vectors[1])
    normed_low = normed.astype(jnp.bfloat16)
    if context is None:
        combined = project(normed_low, qkv_weight)
        queries = combined[..., :D] + vectors[6]
        key_rows = combined[..., D : 2 * D]
        value_rows = combined[..., 2 * D :] + vectors[7]
    else:
        queries = project(normed_low[:, -rows_q:], qkv_weight[:, :D]) + vectors[6]
        pair_rows = project(normed_low, qkv_weight[:, D:])
        key_rows = pair_rows[..., :D]
        value_rows = pair_rows[..., D:] + vectors[7]
    queries = queries.astype(jnp.bfloat16)
    key_rows = key_rows.astype(jnp.bfloat16)
    value_rows = value_rows.astype(jnp.bfloat16)
    mixed_rows, log_total = attend_forward(queries, key_rows, value_rows)
    mixed_low = mixed_rows.astype(jnp.bfloat16)
    attn_out = project(mixed_low, proj_weight) + vectors[8]
    residual = stream + vectors[10] * attn_out
    second, second_back = jax.vjp(layer_norm, residual, vectors[2], vectors[3])
    second_low = second.astype(jnp.bfloat16)
    pre_gelu = project(second_low, up_weight) + up_bias
    hidden, gelu_back = jax.vjp(gelu_exact, pre_gelu)
    hidden_low = hidden.astype(jnp.bfloat16)
    branch = project(hidden_low, down_weight) + vectors[9]
    output, final_back = jax.vjp(
        layer_norm, residual + vectors[11] * branch, vectors[4], vectors[5]
    )

    def backward(grad_out):
        grad_final, grad_final_gain, grad_final_shift = final_back(grad_out)
        grad_scale_two = row_total(grad_final * branch)
        grad_branch = (vectors[11] * grad_final).astype(jnp.bfloat16)
        grad_hidden = back_project(grad_branch, down_weight)
        (grad_pre,) = gelu_back(grad_hidden)
        grad_pre = grad_pre.astype(jnp.bfloat16)
        grad_second = back_project(grad_pre, up_weight)
        grad_resid, grad_gain_two, grad_shift_two = second_back(grad_second)
        grad_resid = grad_resid + grad_final
        grad_scale_one = row_total(grad_resid * attn_out)
        grad_attn = (vectors[10] * grad_resid).astype(jnp.bfloat16)
        grad_mixed = back_project(grad_attn, proj_weight).astype(jnp.bfloat16)
        grad_queries, grad_keys, grad_values = attend_backward(
            queries, key_rows, value_rows, log_total, grad_mixed
        )
        tail_rows = ((mixed_low, grad_attn), (second_low, grad_pre), (hidden_low, grad_branch))
        if context is None:
            grad_joined = jnp.concatenate([grad_queries, grad_keys, grad_values], axis=-1)
            grad_normed = back_project(grad_joined, qkv_weight)
            pairs = ((normed_low, grad_joined),) + tail_rows
        else:
            grad_pair = jnp.concatenate([grad_keys, grad_values], axis=-1)
            grad_normed = back_project(grad_pair, qkv_weight[:, D:])
            grad_query_rows = back_project(grad_queries, qkv_weight[:, :D])
            grad_normed = jnp.concatenate(
                [grad_normed[:, :-rows_q], grad_normed[:, -rows_q:] + grad_query_rows], axis=1
            )
            pairs = ((normed_low[:, -rows_q:], grad_queries), (normed_low, grad_pair)) + tail_rows
        grad_source, grad_gain_one, grad_shift_one = first_back(grad_normed)
        grad_vectors = jnp.stack(
            [
                grad_gain_one,
                grad_shift_one,
                grad_gain_two,
                grad_shift_two,
                grad_final_gain,
                grad_final_shift,
                row_total(grad_queries),
                row_total(grad_values),
                row_total(grad_attn),
                row_total(grad_branch),
                grad_scale_one,
                grad_scale_two,
            ]
        )
        grad_bias = row_total(grad_pre)
        if context is None:
            grad_stream = grad_resid + grad_source
            grad_context = None
        else:
            grad_stream = grad_resid + grad_source[:, -rows_q:]
            grad_context = grad_source[:, :-rows_q]
        return (grad_stream, grad_context, pairs, (grad_vectors, grad_bias))

    return (output, backward)


def empty_pairs(count, rows_q, rows_k, cross):

    def blank(rows, width):
        return jnp.zeros((count, rows, width), jnp.bfloat16)

    if cross:
        first = ((blank(rows_q, D), blank(rows_q, D)), (blank(rows_k, D), blank(rows_k, 2 * D)))
    else:
        first = ((blank(rows_q, D), blank(rows_q, 3 * D)),)
    return first + (
        (blank(rows_q, D), blank(rows_q, D)),
        (blank(rows_q, D), blank(rows_q, FF)),
        (blank(rows_q, FF), blank(rows_q, D)),
    )


def empty_small(row_count):
    return (jnp.zeros((row_count, D), jnp.float32), jnp.zeros((FF,), jnp.float32))


def weight_grads(pairs, cross):
    if cross:
        grad_qkv = jnp.concatenate([contract_rows(*pairs[0]), contract_rows(*pairs[1])], axis=1)
        rest = pairs[2:]
    else:
        grad_qkv = contract_rows(*pairs[0])
        rest = pairs[1:]
    return (grad_qkv, contract_rows(*rest[0]), contract_rows(*rest[1]), contract_rows(*rest[2]))


def encode(patch_part, order_part, lead_set, side_set):
    visible = jnp.take_along_axis(patch_part, order_part[:, MASKED:, None], axis=1).astype(
        jnp.float32
    )
    masked = jnp.take_along_axis(patch_part, order_part[:, :MASKED, None], axis=1).astype(
        jnp.float32
    )
    latents, unused_back = run_block(visible, None, lead_set)
    targets, unused_teacher = run_block(masked, None, side_set)
    return jnp.stack([latents.astype(jnp.bfloat16), targets.astype(jnp.bfloat16)])


def encode_back(patch_part, order_part, grad_latents, lead_set):
    visible = jnp.take_along_axis(patch_part, order_part[:, MASKED:, None], axis=1).astype(
        jnp.float32
    )
    unused_out, backward = run_block(visible, None, lead_set)
    grad_rows, unused_context, pairs, small = backward(grad_latents.astype(jnp.float32))
    crop_ids = lax.broadcasted_iota(jnp.int32, (patch_part.shape[0], 1), 0)
    grad_in = (
        jnp.zeros(patch_part.shape, jnp.float32).at[crop_ids, order_part[:, MASKED:]].set(grad_rows)
    )
    return (pairs, small, grad_in)


def regress(latent_pack, order_part, cot_part, lead_set, side_set):
    pos_table = positions()
    pos_visible = jnp.take(pos_table, order_part[:, MASKED:], axis=0)
    pos_masked = jnp.take(pos_table, order_part[:, :MASKED], axis=0)
    mask_queries = side_set[4][12] + pos_masked
    latents = latent_pack[0].astype(jnp.float32)
    targets = latent_pack[1].astype(jnp.float32)
    regressed, regress_back = run_block(mask_queries, latents + pos_visible, lead_set)
    decoded, decode_back = run_block(regressed + pos_masked, None, side_set)
    grad_decode_in, unused_context, dec_pairs, dec_small = decode_back(cot_part.astype(jnp.float32))
    grad_queries, grad_latents, reg_pairs, reg_small = regress_back(
        grad_decode_in + regressed - targets
    )
    dec_small = (
        jnp.concatenate([dec_small[0], row_total(grad_queries)[None]], axis=0),
        dec_small[1],
    )
    return (
        grad_latents.astype(jnp.bfloat16),
        jnp.concatenate([regressed, decoded], axis=1),
        reg_pairs,
        reg_small,
        dec_pairs,
        dec_small,
    )


MESH_ID = pl.DeviceIdType.MESH


def each(count, body):
    if count <= 4:
        for k in range(count):
            body(k)
    else:
        lax.fori_loop(0, count, lambda k, carry: (body(k), carry)[1], 0)


def place():
    section = lax.axis_index("section")
    index = lax.axis_index("dp")
    return section, index, index // 4, (index // 2) % 2, index % 2


def slot(outer, mid, core):
    return outer * 4 + mid * 2 + core


def remote(src, dst, send_sem, recv_sem, device):
    return pltpu.make_async_remote_copy(
        src_ref=src,
        dst_ref=dst,
        send_sem=send_sem,
        recv_sem=recv_sem,
        device_id=device,
        device_id_type=MESH_ID,
    )


def greet(devices):
    barrier = pltpu.get_barrier_semaphore()
    for device in devices:
        pl.semaphore_signal(barrier, inc=1, device_id=device, device_id_type=MESH_ID)


def gather_kernel(count, groups, *refs):
    shards_in = refs[:count]
    wholes = refs[count : 2 * count]
    own_sem, z_send, z_recv, y_send, y_recv, c_send, c_recv = refs[2 * count :]
    section, index, outer, mid, core = place()
    mid_device = (section, slot(outer, 1 - mid, core))
    core_device = (section, slot(outer, mid, 1 - core))

    def outer_device(k):
        return (section, slot((outer + k) % groups, mid, core))

    barrier = pltpu.get_barrier_semaphore()
    greet([mid_device, core_device])
    each(
        groups - 1,
        lambda k: pl.semaphore_signal(
            barrier, inc=1, device_id=outer_device(k + 1), device_id_type=MESH_ID
        ),
    )
    pl.semaphore_wait(barrier, groups + 1)

    def own_copy(m):
        return pltpu.make_async_copy(shards_in[m], wholes[m].at[index], own_sem.at[m])

    def z_copy(m, k):
        return remote(
            shards_in[m], wholes[m].at[index], z_send.at[m, k], z_recv.at[m, k], outer_device(k)
        )

    def z_arrival(m, k):
        origin = slot((outer - k + groups) % groups, mid, core)
        return remote(
            shards_in[m], wholes[m].at[origin], z_send.at[m, k], z_recv.at[m, k], outer_device(k)
        )

    def y_copy(m, k, own):
        origin = slot((outer - k + groups) % groups, mid, core)
        src = shards_in[m] if own else wholes[m].at[origin]
        return remote(src, wholes[m].at[origin], y_send.at[m, k], y_recv.at[m, k], mid_device)

    def y_arrival(m, k):
        origin = slot((outer - k + groups) % groups, 1 - mid, core)
        piece = wholes[m].at[origin]
        return remote(piece, piece, y_send.at[m, k], y_recv.at[m, k], mid_device)

    def c_copy(m, k, far, own):
        origin = slot((outer - k + groups) % groups, 1 - mid if far else mid, core)
        src = shards_in[m] if own else wholes[m].at[origin]
        at = k * 2 + far
        return remote(src, wholes[m].at[origin], c_send.at[m, at], c_recv.at[m, at], core_device)

    def c_arrival(m, k, far):
        origin = slot((outer - k + groups) % groups, 1 - mid if far else mid, 1 - core)
        piece = wholes[m].at[origin]
        at = k * 2 + far
        return remote(piece, piece, c_send.at[m, at], c_recv.at[m, at], core_device)

    for m in range(count):
        each(groups - 1, lambda k: z_copy(m, k + 1).start())
        y_copy(m, 0, True).start()
    for m in range(count):
        own_copy(m).start()
        c_copy(m, 0, 0, True).start()
    for m in range(count):

        def pass_on(k):
            z_arrival(m, k + 1).wait_recv()
            y_copy(m, k + 1, False).start()
            c_copy(m, k + 1, 0, False).start()

        each(groups - 1, pass_on)
    for m in range(count):

        def hand_over(k):
            y_arrival(m, k).wait_recv()
            c_copy(m, k, 1, False).start()

        each(groups, hand_over)
    for m in range(count):
        own_copy(m).wait()
        each(groups - 1, lambda k: z_copy(m, k + 1).wait_send())

        def finish(k):
            y_arrival(m, k).wait_send()
            for far in range(2):
                c_arrival(m, k, far).wait_send()
                c_arrival(m, k, far).wait_recv()

        each(groups, finish)


def gather_all(pieces):
    devices = lax.axis_size("dp")
    groups = devices // 4
    count = len(pieces)
    sems = [pltpu.SemaphoreType.DMA((count,))]
    for width in (groups, groups, groups, groups, 2 * groups, 2 * groups):
        sems.append(pltpu.SemaphoreType.DMA((count, width)))
    return pl.pallas_call(
        functools.partial(gather_kernel, count, groups),
        out_shape=[jax.ShapeDtypeStruct((devices,) + p.shape, p.dtype) for p in pieces],
        in_specs=[pl.BlockSpec(memory_space=pl.ANY)] * count,
        out_specs=[pl.BlockSpec(memory_space=pl.ANY)] * count,
        scratch_shapes=sems,
        compiler_params=pltpu.CompilerParams(collective_id=1, has_side_effects=True),
        name="gather_weights",
    )(*pieces)


def add_rows(target, at, other, other_at):
    rows = target.shape[-2]
    step = 16 if target.dtype == jnp.bfloat16 else 8

    def body(r, carry):
        where = pl.ds(r * step, step)
        total = target[at, where, :].astype(jnp.float32) + other[other_at, where, :].astype(
            jnp.float32
        )
        target[at, where, :] = total.astype(target.dtype)
        return carry

    lax.fori_loop(0, rows // step, body, 0)


def reduce_kernel(lead_count, dec_count, groups, shapes, *refs):
    refs = list(refs)

    def grab(n):
        taken = refs[:n]
        del refs[:n]
        return taken

    lead_in, dec_in = grab(lead_count), grab(dec_count)
    lead_out, dec_out = grab(lead_count), grab(dec_count)
    lead_own, lead_c, lead_y, lead_z = (grab(lead_count) for _ in range(4))
    dec_own, dec_c, dec_y, dec_z = (grab(dec_count) for _ in range(4))
    load, c_send, c_recv, x_send, x_recv, y_send, y_recv, z_send, z_recv = refs
    section, index, outer, mid, core = place()
    x_device = (1 - section, index)
    mid_device = (section, slot(outer, 1 - mid, core))
    core_device = (section, slot(outer, mid, 1 - core))

    def outer_device(k):
        return (section, slot((outer + k) % groups, mid, core))

    barrier = pltpu.get_barrier_semaphore()
    greet([mid_device, core_device, x_device])
    each(
        groups - 1,
        lambda k: pl.semaphore_signal(
            barrier, inc=1, device_id=outer_device(k + 1), device_id_type=MESH_ID
        ),
    )
    pl.semaphore_wait(barrier, groups + 2)

    def lead_load(m, j):
        return pltpu.make_async_copy(
            lead_in[m].at[j * 2 + core], lead_own[m].at[j], load.at[m, j]
        )

    def lead_core(m, j):
        return remote(
            lead_in[m].at[j * 2 + 1 - core],
            lead_c[m].at[j],
            c_send.at[m, j],
            c_recv.at[m, j],
            core_device,
        )

    def dec_load(m, t, j):
        at = lead_count + 2 * m + t
        return pltpu.make_async_copy(
            dec_in[m].at[t, j * 2 + core], dec_own[m].at[t, j], load.at[at, j]
        )

    def dec_core(m, t, j):
        at = lead_count + 2 * m + t
        return remote(
            dec_in[m].at[t, j * 2 + 1 - core],
            dec_c[m].at[t, j],
            c_send.at[at, j],
            c_recv.at[at, j],
            core_device,
        )

    def x_copy(m, j):
        return remote(
            dec_own[m].at[0, j], dec_own[m].at[1, j], x_send.at[m, j], x_recv.at[m, j], x_device
        )

    own_of = [lead_own[m] for m in range(lead_count)] + [dec_own[m].at[1] for m in range(dec_count)]
    y_of, z_of, out_of = lead_y + dec_y, lead_z + dec_z, lead_out + dec_out

    def y_copy(n, g):
        return remote(
            own_of[n].at[g * 2 + 1 - mid],
            y_of[n].at[g],
            y_send.at[n, g],
            y_recv.at[n, g],
            mid_device,
        )

    def z_copy(n, k):
        other = (outer + k) % groups
        return remote(
            own_of[n].at[other * 2 + mid],
            z_of[n].at[k],
            z_send.at[n, k],
            z_recv.at[n, k],
            outer_device(k),
        )

    for m in range(lead_count):
        each(2 * groups, lambda j: lead_core(m, j).start())
        each(2 * groups, lambda j: lead_load(m, j).start())

    @pl.when(section == 1)
    def _():
        for m in range(dec_count):
            for t in range(2):
                each(2 * groups, lambda j: dec_core(m, t, j).start())
                each(2 * groups, lambda j: dec_load(m, t, j).start())

    def lead_pair(m, j):
        lead_load(m, j).wait()
        lead_core(m, j).wait_recv()
        add_rows(lead_own[m], j, lead_c[m], j)

    for m in range(lead_count):

        def far_pair(g):
            lead_pair(m, g * 2 + 1 - mid)
            y_copy(m, g).start()

        each(groups, far_pair)
        each(groups, lambda g: lead_pair(m, g * 2 + mid))

    @pl.when(section == 1)
    def _():
        for t in range(2):
            for m in range(dec_count):

                def dec_pair(j):
                    dec_load(m, t, j).wait()
                    dec_core(m, t, j).wait_recv()
                    add_rows(dec_own[m].at[t], j, dec_c[m].at[t], j)
                    if t == 0:
                        x_copy(m, j).start()

                each(2 * groups, dec_pair)

    def across(n):
        def other_rows(k):
            other = (outer + k) % groups
            y_copy(n, other).wait_recv()
            add_rows(own_of[n], other * 2 + mid, y_of[n], other)
            z_copy(n, k).start()

        each(groups - 1, lambda k: other_rows(k + 1))
        y_copy(n, outer).wait_recv()

    for m in range(lead_count):
        across(m)
    for m in range(dec_count):
        n = lead_count + m

        @pl.when(section == 0)
        def _():
            each(2 * groups, lambda j: x_copy(m, j).wait_recv())

        each(groups, lambda g: y_copy(n, g).start())
    for m in range(dec_count):
        across(lead_count + m)

    for n in range(lead_count + dec_count):
        each(groups - 1, lambda k: z_copy(n, k + 1).wait_recv())
        own, partner, others, out = own_of[n], y_of[n], z_of[n], out_of[n]
        rows, columns = own.shape[-2], own.shape[-1]
        stacked = out.shape[-1] != columns
        step = rows // 2 if stacked else (16 if own.dtype == jnp.bfloat16 else 8)
        for r in range(rows // step):
            where = pl.ds(r * step, step)

            def total_of(lanes):
                total = own[outer * 2 + mid, where, lanes].astype(jnp.float32)
                total = total + partner[outer, where, lanes].astype(jnp.float32)
                return lax.fori_loop(
                    1, groups, lambda k, acc: acc + others[k, where, lanes].astype(jnp.float32), total
                )

            if stacked:
                for q in range(columns // 128):
                    lanes = slice(q * 128, q * 128 + 128)
                    out[:, (2 * q + r) * 128 : (2 * q + r + 1) * 128] = total_of(lanes)
            else:
                out[where, :] = total_of(slice(None))

    for m in range(lead_count):
        each(2 * groups, lambda j: lead_core(m, j).wait_send())

    @pl.when(section == 1)
    def _():
        for m in range(dec_count):
            for t in range(2):
                each(2 * groups, lambda j: dec_core(m, t, j).wait_send())
            each(2 * groups, lambda j: x_copy(m, j).wait_send())

    for n in range(lead_count + dec_count):
        each(groups, lambda g: y_copy(n, g).wait_send())
        each(groups - 1, lambda k: z_copy(n, k + 1).wait_send())


def reduce_all(lead, dec, dec_outs):
    devices = lax.axis_size("dp")
    groups = devices // 4
    half = devices // 2
    nl, nd = len(lead), len(dec)
    scratch = []
    for lead_shape in (half, half, groups, groups):
        scratch += [pltpu.VMEM((lead_shape,) + a.shape[1:], a.dtype) for a in lead]
    scratch += [pltpu.VMEM((2, half) + a.shape[2:], a.dtype) for a in dec]
    scratch += [pltpu.VMEM((2, half) + a.shape[2:], a.dtype) for a in dec]
    for _ in range(2):
        scratch += [pltpu.VMEM((groups,) + a.shape[2:], a.dtype) for a in dec]
    sems = [(nl + 2 * nd, half)] * 3 + [(nd, half)] * 2 + [(nl + nd, groups)] * 4
    outs = pl.pallas_call(
        functools.partial(reduce_kernel, nl, nd, groups, None),
        out_shape=[jax.ShapeDtypeStruct(a.shape[1:], jnp.float32) for a in lead]
        + [jax.ShapeDtypeStruct(s, jnp.float32) for s in dec_outs],
        in_specs=[pl.BlockSpec(memory_space=pl.ANY)] * (nl + nd),
        out_specs=[pl.BlockSpec(memory_space=pltpu.VMEM)] * (nl + nd),
        scratch_shapes=scratch + [pltpu.SemaphoreType.DMA(s) for s in sems],
        compiler_params=pltpu.CompilerParams(
            collective_id=2, has_side_effects=True, vmem_limit_bytes=60 << 20
        ),
        name="reduce_grads",
    )(*lead, *dec)
    return list(outs[:nl]), list(outs[nl:])


def stack_halves(grad, devices):
    rows, columns = grad.shape
    r = rows // (2 * devices)
    if r % 16 == 0:
        return grad.reshape(2, devices, r, columns)
    view = grad.reshape(2, devices, r, columns // 256, 2, 128)
    return view.transpose(0, 1, 4, 2, 3, 5).reshape(2, devices, 2 * r, columns // 2)

def exchange(pieces):
    devices = lax.axis_size("dp")
    if devices % 4 == 0 and all(p.shape[0] % 16 == 0 for p in pieces):
        return gather_all(pieces)
    return [lax.all_gather(p, "dp", axis=0) for p in pieces]


def as_small(parts, rows_of):
    flat = jnp.concatenate([p.reshape(-1) for p in parts])
    block = rows_of * 128
    padded = -(-flat.shape[0] // block) * block
    return jnp.pad(flat, (0, padded - flat.shape[0])).reshape(-1, 128)


def take_flat(flat, shapes):
    taken, offset = [], 0
    for shape in shapes:
        size = 1
        for extent in shape:
            size *= extent
        taken.append(flat[:, offset : offset + size].reshape((-1,) + shape))
        offset += size
    return taken


def spread_columns(gathered):
    return gathered.transpose(1, 0, 2).reshape(gathered.shape[1], -1)


def small_chunks(vectors, bias, chunks):
    rows, columns = vectors.shape
    cut = vectors.reshape(rows, chunks, columns // chunks).transpose(1, 0, 2).reshape(chunks, -1)
    flat = jnp.concatenate([cut, bias.reshape(chunks, -1)], axis=1)
    padded = -(-flat.shape[1] // 1024) * 1024
    return jnp.pad(flat, ((0, 0), (0, padded - flat.shape[1]))).reshape(chunks, -1, 128)


def small_pieces(chunk, rows, chunks):
    flat = chunk.reshape(-1)
    vectors = rows * (D // chunks)
    bias = FF // chunks
    return flat[:vectors].reshape(rows, D // chunks), flat[vectors : vectors + bias]


def total_grads(lead_big, lead_small, dec_big, dec_small):
    devices = lax.axis_size("dp")
    on_encoder = lax.axis_index("section") == 0
    lead_chunks = [g.reshape(devices, -1, g.shape[1]) for g in lead_big]
    lead_chunks.append(small_chunks(*lead_small, devices))
    dec_chunk_small = small_chunks(*dec_small, 2 * devices)
    dec_shapes = [(g.shape[0] // (2 * devices), g.shape[1]) for g in dec_big]
    if devices % 4 == 0 and lead_chunks[0].shape[1] % 16 == 0:
        dec_chunks = [stack_halves(g, devices) for g in dec_big]
        dec_chunks.append(dec_chunk_small.reshape((2, devices) + dec_chunk_small.shape[1:]))
        lead_out, dec_out = reduce_all(
            lead_chunks, dec_chunks, dec_shapes + [dec_chunk_small.shape[1:]]
        )
    else:
        dec_chunks = [g.reshape(2, devices, -1, g.shape[1]) for g in dec_big]
        dec_chunks.append(dec_chunk_small.reshape((2, devices) + dec_chunk_small.shape[1:]))
        lead_out = [
            lax.psum_scatter(g.astype(jnp.float32), "dp", scatter_dimension=0) for g in lead_chunks
        ]
        dec_out = []
        for g in dec_chunks:
            mine = jnp.where(on_encoder, jnp.zeros_like(g), g).astype(jnp.float32)
            mine = lax.psum_scatter(mine, "dp", scatter_dimension=1)
            dec_out.append(lax.psum_scatter(mine, "section", scatter_dimension=0))
    lead_vectors, lead_bias = small_pieces(lead_out[4], 12, devices)
    dec_vectors, dec_bias = small_pieces(dec_out[4], 13, 2 * devices)
    return lead_out[:4] + [lead_vectors, lead_bias], dec_out[:4] + [dec_vectors, dec_bias]


def shards(
    patches,
    cotangent,
    ordering,
    lead_qkv,
    lead_proj,
    lead_up,
    lead_down,
    lead_vectors,
    lead_bias,
    side_qkv,
    side_proj,
    side_up,
    side_down,
    side_vectors,
    side_bias,
):
    section_id = lax.axis_index("section")
    on_encoder = section_id == 0
    small = as_small([lead_vectors[0], lead_bias[0], side_vectors[0], side_bias[0]], 16)
    pieces = [lead_qkv[0], lead_proj[0], lead_up[0], lead_down[0]]
    pieces += [side_qkv[0], side_proj[0], side_up[0], side_down[0], small]
    wholes = exchange(pieces)
    big = [w.reshape(-1, w.shape[2]) for w in wholes[:8]]
    flat = wholes[8].reshape(wholes[8].shape[0], -1).astype(jnp.float32)
    lv, lb, sv, sb = take_flat(
        flat,
        [lead_vectors.shape[1:], lead_bias.shape[1:], side_vectors.shape[1:], side_bias.shape[1:]],
    )
    lead_set = tuple(big[:4]) + (spread_columns(lv), lb.reshape(-1))
    side_set = tuple(big[4:]) + (spread_columns(sv), sb.reshape(-1))
    crops = patches.shape[0]
    visible_count = PATCHES - MASKED
    latent_pack = lax.cond(
        on_encoder,
        lambda: encode(patches, ordering, lead_set, side_set),
        lambda: jnp.zeros((2, crops, MASKED, D), jnp.bfloat16),
    )
    arrived = passed_along(latent_pack, "section", 1)
    grad_pack, latent_rows, reg_pairs, reg_small, dec_pairs, dec_small = lax.cond(
        on_encoder,
        lambda: (
            jnp.zeros((crops, visible_count, D), jnp.bfloat16),
            jnp.zeros((crops, PATCHES, D), jnp.float32),
            empty_pairs(crops, MASKED, PATCHES, True),
            empty_small(12),
            empty_pairs(crops, MASKED, MASKED, False),
            empty_small(13),
        ),
        lambda: regress(arrived, ordering, cotangent, lead_set, side_set),
    )
    returned = passed_along(grad_pack, "section", -1)
    enc_pairs, enc_small, grad_rows = lax.cond(
        on_encoder,
        lambda: encode_back(patches, ordering, returned, lead_set),
        lambda: (
            empty_pairs(crops, visible_count, visible_count, False),
            empty_small(12),
            latent_rows,
        ),
    )

    def low_all(grads):
        return tuple(g.astype(jnp.bfloat16) for g in grads)

    lead_big = lax.cond(
        on_encoder,
        lambda: low_all(weight_grads(enc_pairs, False)),
        lambda: low_all(weight_grads(reg_pairs, True)),
    )
    dec_big = lax.cond(
        on_encoder,
        lambda: tuple(jnp.zeros(member.shape, jnp.bfloat16) for member in side_set[:4]),
        lambda: low_all(weight_grads(dec_pairs, False)),
    )
    lead_small = jax.tree.map(lambda a, b: jnp.where(on_encoder, a, b), enc_small, reg_small)
    lead_out, dec_out = total_grads(lead_big, lead_small, dec_big, dec_small)
    return (grad_rows[None],) + tuple(o[None] for o in lead_out) + tuple(dec_out)


def solution(mesh):
    return jax.shard_map(
        shards,
        mesh=mesh,
        in_specs=(
            P("dp", None, None),
            P("dp", None, None),
            P("dp", None),
            P("section", "dp", None),
            P("section", "dp", None),
            P("section", "dp", None),
            P("section", "dp", None),
            P("section", None, "dp"),
            P("section", "dp"),
            P("section", "dp", None),
            P("section", "dp", None),
            P("section", "dp", None),
            P("section", "dp", None),
            P("section", None, "dp"),
            P("section", "dp"),
        ),
        out_specs=(
            P("section", "dp", None, None),
            P("section", "dp", None),
            P("section", "dp", None),
            P("section", "dp", None),
            P("section", "dp", None),
            P("section", None, "dp"),
            P("section", "dp"),
            P(("section", "dp"), None),
            P(("section", "dp"), None),
            P(("section", "dp"), None),
            P(("section", "dp"), None),
            P(None, ("section", "dp")),
            P(("section", "dp")),
        ),
        check_vma=False,
    )
```

```python
import functools

import jax
import jax.experimental.pallas as pl
import jax.experimental.pallas.tpu as pltpu
import jax.numpy as jnp
import numpy as np
from jax import lax
from jax.sharding import PartitionSpec as P

D = 768
HEADS = 12
HEAD_DIM = 64
FF = 3072
GRID = 14
PATCHES = 196
MASKED = 98


def passed_along(array, axis, by):
    count = lax.axis_size(axis)
    pairs = [(i, i + by) for i in range(count) if 0 <= i + by < count]
    return lax.ppermute(array, axis, pairs)


def positions():
    ids = np.arange(PATCHES)
    quarter = D // 4
    frequency = 10000.0 ** (-np.arange(quarter) / quarter)
    rows = (ids // GRID)[:, None] * frequency
    cols = (ids % GRID)[:, None] * frequency
    return np.concatenate([np.sin(cols), np.cos(cols), np.sin(rows), np.cos(rows)], axis=1)


def position_parts():
    rest = positions().astype(np.float32)
    parts = []
    for _ in range(3):
        part = rest.astype(jnp.bfloat16)
        rest = rest - part.astype(np.float32)
        parts.append(part)
    return jnp.asarray(np.stack(parts))


MESH_ID = pl.DeviceIdType.MESH


def each(count, body):
    if count <= 4:
        for k in range(count):
            body(k)
    else:
        lax.fori_loop(0, count, lambda k, carry: (body(k), carry)[1], 0)


def place():
    section = lax.axis_index("section")
    index = lax.axis_index("dp")
    return section, index, index // 4, (index // 2) % 2, index % 2


def slot(outer, mid, core):
    return outer * 4 + mid * 2 + core


def remote(src, dst, send_sem, recv_sem, device):
    return pltpu.make_async_remote_copy(
        src_ref=src,
        dst_ref=dst,
        send_sem=send_sem,
        recv_sem=recv_sem,
        device_id=device,
        device_id_type=MESH_ID,
    )


def greet(devices):
    barrier = pltpu.get_barrier_semaphore()
    for device in devices:
        pl.semaphore_signal(barrier, inc=1, device_id=device, device_id_type=MESH_ID)


def gather_kernel(count, groups, *refs):
    shards_in = refs[:count]
    wholes = refs[count : 2 * count]
    own_sem, z_send, z_recv, y_send, y_recv, c_send, c_recv = refs[2 * count :]
    section, index, outer, mid, core = place()
    mid_device = (section, slot(outer, 1 - mid, core))
    core_device = (section, slot(outer, mid, 1 - core))

    def outer_device(k):
        return (section, slot((outer + k) % groups, mid, core))

    barrier = pltpu.get_barrier_semaphore()
    greet([mid_device, core_device])
    each(
        groups - 1,
        lambda k: pl.semaphore_signal(
            barrier, inc=1, device_id=outer_device(k + 1), device_id_type=MESH_ID
        ),
    )
    pl.semaphore_wait(barrier, groups + 1)

    def own_copy(m):
        return pltpu.make_async_copy(shards_in[m], wholes[m].at[index], own_sem.at[m])

    def z_copy(m, k):
        return remote(
            shards_in[m], wholes[m].at[index], z_send.at[m, k], z_recv.at[m, k], outer_device(k)
        )

    def z_arrival(m, k):
        origin = slot((outer - k + groups) % groups, mid, core)
        return remote(
            shards_in[m], wholes[m].at[origin], z_send.at[m, k], z_recv.at[m, k], outer_device(k)
        )

    def y_copy(m, k, own):
        origin = slot((outer - k + groups) % groups, mid, core)
        src = shards_in[m] if own else wholes[m].at[origin]
        return remote(src, wholes[m].at[origin], y_send.at[m, k], y_recv.at[m, k], mid_device)

    def y_arrival(m, k):
        origin = slot((outer - k + groups) % groups, 1 - mid, core)
        piece = wholes[m].at[origin]
        return remote(piece, piece, y_send.at[m, k], y_recv.at[m, k], mid_device)

    def c_copy(m, k, far, own):
        origin = slot((outer - k + groups) % groups, 1 - mid if far else mid, core)
        src = shards_in[m] if own else wholes[m].at[origin]
        at = k * 2 + far
        return remote(src, wholes[m].at[origin], c_send.at[m, at], c_recv.at[m, at], core_device)

    def c_arrival(m, k, far):
        origin = slot((outer - k + groups) % groups, 1 - mid if far else mid, 1 - core)
        piece = wholes[m].at[origin]
        at = k * 2 + far
        return remote(piece, piece, c_send.at[m, at], c_recv.at[m, at], core_device)

    for m in range(count):
        each(groups - 1, lambda k: z_copy(m, k + 1).start())
        y_copy(m, 0, True).start()
    for m in range(count):
        own_copy(m).start()
        c_copy(m, 0, 0, True).start()
    for m in range(count):

        def pass_on(k):
            z_arrival(m, k + 1).wait_recv()
            y_copy(m, k + 1, False).start()
            c_copy(m, k + 1, 0, False).start()

        each(groups - 1, pass_on)
    for m in range(count):

        def hand_over(k):
            y_arrival(m, k).wait_recv()
            c_copy(m, k, 1, False).start()

        each(groups, hand_over)
    for m in range(count):
        own_copy(m).wait()
        each(groups - 1, lambda k: z_copy(m, k + 1).wait_send())

        def finish(k):
            y_arrival(m, k).wait_send()
            for far in range(2):
                c_arrival(m, k, far).wait_send()
                c_arrival(m, k, far).wait_recv()

        each(groups, finish)


def gather_all(pieces):
    devices = lax.axis_size("dp")
    groups = devices // 4
    count = len(pieces)
    sems = [pltpu.SemaphoreType.DMA((count,))]
    for width in (groups, groups, groups, groups, 2 * groups, 2 * groups):
        sems.append(pltpu.SemaphoreType.DMA((count, width)))
    return pl.pallas_call(
        functools.partial(gather_kernel, count, groups),
        out_shape=[jax.ShapeDtypeStruct((devices,) + p.shape, p.dtype) for p in pieces],
        in_specs=[pl.BlockSpec(memory_space=pl.ANY)] * count,
        out_specs=[pl.BlockSpec(memory_space=pl.ANY)] * count,
        scratch_shapes=sems,
        compiler_params=pltpu.CompilerParams(collective_id=1, has_side_effects=True),
        name="gather_weights",
    )(*pieces)


def add_rows(target, at, other, other_at):
    rows = target.shape[-2]
    step = 16 if target.dtype == jnp.bfloat16 else 8

    def body(r, carry):
        where = pl.ds(r * step, step)
        total = target[at, where, :].astype(jnp.float32) + other[other_at, where, :].astype(
            jnp.float32
        )
        target[at, where, :] = total.astype(target.dtype)
        return carry

    lax.fori_loop(0, rows // step, body, 0)


def reduce_kernel(lead_count, dec_count, groups, shapes, *refs):
    refs = list(refs)

    def grab(n):
        taken = refs[:n]
        del refs[:n]
        return taken

    lead_in, dec_in = grab(lead_count), grab(dec_count)
    lead_out, dec_out = grab(lead_count), grab(dec_count)
    lead_own, lead_c, lead_y, lead_z = (grab(lead_count) for _ in range(4))
    dec_own, dec_c, dec_y, dec_z = (grab(dec_count) for _ in range(4))
    load, c_send, c_recv, x_send, x_recv, y_send, y_recv, z_send, z_recv = refs
    section, index, outer, mid, core = place()
    x_device = (1 - section, index)
    mid_device = (section, slot(outer, 1 - mid, core))
    core_device = (section, slot(outer, mid, 1 - core))

    def outer_device(k):
        return (section, slot((outer + k) % groups, mid, core))

    barrier = pltpu.get_barrier_semaphore()
    greet([mid_device, core_device, x_device])
    each(
        groups - 1,
        lambda k: pl.semaphore_signal(
            barrier, inc=1, device_id=outer_device(k + 1), device_id_type=MESH_ID
        ),
    )
    pl.semaphore_wait(barrier, groups + 2)

    def lead_load(m, j):
        return pltpu.make_async_copy(
            lead_in[m].at[j * 2 + core], lead_own[m].at[j], load.at[m, j]
        )

    def lead_core(m, j):
        return remote(
            lead_in[m].at[j * 2 + 1 - core],
            lead_c[m].at[j],
            c_send.at[m, j],
            c_recv.at[m, j],
            core_device,
        )

    def dec_load(m, t, j):
        at = lead_count + 2 * m + t
        return pltpu.make_async_copy(
            dec_in[m].at[t, j * 2 + core], dec_own[m].at[t, j], load.at[at, j]
        )

    def dec_core(m, t, j):
        at = lead_count + 2 * m + t
        return remote(
            dec_in[m].at[t, j * 2 + 1 - core],
            dec_c[m].at[t, j],
            c_send.at[at, j],
            c_recv.at[at, j],
            core_device,
        )

    def x_copy(m, j):
        return remote(
            dec_own[m].at[0, j], dec_own[m].at[1, j], x_send.at[m, j], x_recv.at[m, j], x_device
        )

    own_of = [lead_own[m] for m in range(lead_count)] + [dec_own[m].at[1] for m in range(dec_count)]
    y_of, z_of, out_of = lead_y + dec_y, lead_z + dec_z, lead_out + dec_out

    def y_copy(n, g):
        return remote(
            own_of[n].at[g * 2 + 1 - mid],
            y_of[n].at[g],
            y_send.at[n, g],
            y_recv.at[n, g],
            mid_device,
        )

    def z_copy(n, k):
        other = (outer + k) % groups
        return remote(
            own_of[n].at[other * 2 + mid],
            z_of[n].at[k],
            z_send.at[n, k],
            z_recv.at[n, k],
            outer_device(k),
        )

    for m in range(lead_count):
        each(2 * groups, lambda j: lead_core(m, j).start())
        each(2 * groups, lambda j: lead_load(m, j).start())

    @pl.when(section == 1)
    def _():
        for m in range(dec_count):
            for t in range(2):
                each(2 * groups, lambda j: dec_core(m, t, j).start())
                each(2 * groups, lambda j: dec_load(m, t, j).start())

    def lead_pair(m, j):
        lead_load(m, j).wait()
        lead_core(m, j).wait_recv()
        add_rows(lead_own[m], j, lead_c[m], j)

    for m in range(lead_count):

        def far_pair(g):
            lead_pair(m, g * 2 + 1 - mid)
            y_copy(m, g).start()

        each(groups, far_pair)
        each(groups, lambda g: lead_pair(m, g * 2 + mid))

    @pl.when(section == 1)
    def _():
        for t in range(2):
            for m in range(dec_count):

                def dec_pair(j):
                    dec_load(m, t, j).wait()
                    dec_core(m, t, j).wait_recv()
                    add_rows(dec_own[m].at[t], j, dec_c[m].at[t], j)
                    if t == 0:
                        x_copy(m, j).start()

                each(2 * groups, dec_pair)

    def across(n):
        def other_rows(k):
            other = (outer + k) % groups
            y_copy(n, other).wait_recv()
            add_rows(own_of[n], other * 2 + mid, y_of[n], other)
            z_copy(n, k).start()

        each(groups - 1, lambda k: other_rows(k + 1))
        y_copy(n, outer).wait_recv()

    for m in range(lead_count):
        across(m)
    for m in range(dec_count):
        n = lead_count + m

        @pl.when(section == 0)
        def _():
            each(2 * groups, lambda j: x_copy(m, j).wait_recv())

        each(groups, lambda g: y_copy(n, g).start())
    for m in range(dec_count):
        across(lead_count + m)

    for n in range(lead_count + dec_count):
        each(groups - 1, lambda k: z_copy(n, k + 1).wait_recv())
        own, partner, others, out = own_of[n], y_of[n], z_of[n], out_of[n]
        rows, columns = own.shape[-2], own.shape[-1]
        stacked = out.shape[-1] != columns
        step = rows // 2 if stacked else (16 if own.dtype == jnp.bfloat16 else 8)
        for r in range(rows // step):
            where = pl.ds(r * step, step)

            def total_of(lanes):
                total = own[outer * 2 + mid, where, lanes].astype(jnp.float32)
                total = total + partner[outer, where, lanes].astype(jnp.float32)
                return lax.fori_loop(
                    1, groups, lambda k, acc: acc + others[k, where, lanes].astype(jnp.float32), total
                )

            if stacked:
                for q in range(columns // 128):
                    lanes = slice(q * 128, q * 128 + 128)
                    out[:, (2 * q + r) * 128 : (2 * q + r + 1) * 128] = total_of(lanes)
            else:
                out[where, :] = total_of(slice(None))

    for m in range(lead_count):
        each(2 * groups, lambda j: lead_core(m, j).wait_send())

    @pl.when(section == 1)
    def _():
        for m in range(dec_count):
            for t in range(2):
                each(2 * groups, lambda j: dec_core(m, t, j).wait_send())
            each(2 * groups, lambda j: x_copy(m, j).wait_send())

    for n in range(lead_count + dec_count):
        each(groups, lambda g: y_copy(n, g).wait_send())
        each(groups - 1, lambda k: z_copy(n, k + 1).wait_send())


def reduce_all(lead, dec, dec_outs):
    devices = lax.axis_size("dp")
    groups = devices // 4
    half = devices // 2
    nl, nd = len(lead), len(dec)
    scratch = []
    for lead_shape in (half, half, groups, groups):
        scratch += [pltpu.VMEM((lead_shape,) + a.shape[1:], a.dtype) for a in lead]
    scratch += [pltpu.VMEM((2, half) + a.shape[2:], a.dtype) for a in dec]
    scratch += [pltpu.VMEM((2, half) + a.shape[2:], a.dtype) for a in dec]
    for _ in range(2):
        scratch += [pltpu.VMEM((groups,) + a.shape[2:], a.dtype) for a in dec]
    sems = [(nl + 2 * nd, half)] * 3 + [(nd, half)] * 2 + [(nl + nd, groups)] * 4
    outs = pl.pallas_call(
        functools.partial(reduce_kernel, nl, nd, groups, None),
        out_shape=[jax.ShapeDtypeStruct(a.shape[1:], jnp.float32) for a in lead]
        + [jax.ShapeDtypeStruct(s, jnp.float32) for s in dec_outs],
        in_specs=[pl.BlockSpec(memory_space=pl.ANY)] * (nl + nd),
        out_specs=[pl.BlockSpec(memory_space=pltpu.VMEM)] * (nl + nd),
        scratch_shapes=scratch + [pltpu.SemaphoreType.DMA(s) for s in sems],
        compiler_params=pltpu.CompilerParams(
            collective_id=2, has_side_effects=True, vmem_limit_bytes=60 << 20
        ),
        name="reduce_grads",
    )(*lead, *dec)
    return list(outs[:nl]), list(outs[nl:])


ROWS = 112
LOW = jnp.bfloat16
HIGH = jnp.float32
VISIBLE = PATCHES - MASKED
CHUNK = 32
NAMES_SELF = ("normed", "qkv", "probs", "mixed", "attn", "x1", "r1", "x2", "r2", "second")
NAMES_SELF += ("slope", "hidden", "branch", "x3", "r3")
NAMES_CROSS = ("normed_c", "kv_c", "probs_c", "x1_c", "r1_c")
NAMES_GRAD = ("dqkv", "dattn", "dpre", "dbranch")


def save_shape(name, tokens):
    pairs = tokens // ROWS * (HEADS // 2)
    kinds = {
        "qkv": ((tokens, 3 * D), LOW),
        "kv_c": ((tokens, 2 * D), LOW),
        "dqkv": ((tokens, 3 * D), LOW),
        "dkv_c": ((tokens, 2 * D), LOW),
        "probs": ((pairs, 2 * ROWS, ROWS), HIGH),
        "probs_c": ((pairs, 2 * ROWS, ROWS), HIGH),
        "hidden": ((tokens, FF), LOW),
        "dpre": ((tokens, FF), LOW),
        "slope": ((tokens, FF), HIGH),
    }
    if name in kinds:
        return kinds[name]
    if name in ("r1", "r2", "r3", "r1_c"):
        return ((tokens, 1), HIGH)
    if name in ("attn", "x1", "x1_c", "x2", "x3", "branch"):
        return ((tokens, D), HIGH)
    return ((tokens, D), LOW)


def dot(left, right):
    return jnp.dot(left, right, preferred_element_type=HIGH)


def dot_nt(left, right):
    return lax.dot_general(left, right, (((1,), (1,)), ((), ())), preferred_element_type=HIGH)


def dot_tn(left, right):
    return lax.dot_general(left, right, (((0,), (0,)), ((), ())), preferred_element_type=HIGH)


def by_rows(tokens, body, init=()):
    def step(i, carry):
        return body(pl.ds(pl.multiple_of(i * CHUNK, CHUNK), CHUNK), carry)

    return lax.fori_loop(0, tokens // CHUNK, step, init)


def tiles(width, body, size=256, unroll=1):
    def step(i, carry):
        body(pl.ds(pl.multiple_of(i * size, size), size))
        return carry

    lax.fori_loop(0, width // size, step, 0, unroll=unroll)


def fold(values):
    return jnp.sum(values.reshape(-1, 8, values.shape[-1]), axis=0)


def norm_forward(source, gain, shift, kept, spread, low, out=None):
    def body(where, carry):
        values = source[where, :]
        center = values - jnp.mean(values, axis=-1, keepdims=True)
        scale = lax.rsqrt(jnp.mean(center * center, axis=-1, keepdims=True) + 1e-06)
        center = center * scale
        if kept is not None:
            kept[where, :] = center
            spread[where, :] = scale
        result = center * gain + shift
        if low is not None:
            low[where, :] = result.astype(LOW)
        if out is not None:
            out[where, :] = result
        return carry

    by_rows(source.shape[0], body)


def norm_grad(grad, gain, center, scale):
    weighted = grad * gain
    first = jnp.mean(weighted, axis=-1, keepdims=True)
    second = jnp.mean(weighted * center, axis=-1, keepdims=True)
    return scale * (weighted - first - center * second)


def pair_masks(rows):
    lane = lax.broadcasted_iota(jnp.int32, (rows, 2 * HEAD_DIM), 1)
    return lane < HEAD_DIM


def two_heads(values):
    low_lanes = pair_masks(values.shape[0])
    zero = jnp.zeros_like(values)
    return jnp.concatenate(
        [jnp.where(low_lanes, values, zero), jnp.where(low_lanes, zero, values)], axis=0
    )


def one_pair(stacked):
    half = stacked.shape[0] // 2
    return jnp.where(pair_masks(half), stacked[:half], stacked[half:])


def head_loop(tokens, body):
    def step(p, carry):
        for crop in range(tokens // ROWS):
            rows = pl.ds(crop * ROWS, ROWS)
            body(crop * (HEADS // 2) + p, rows, p)
        return carry

    lax.fori_loop(0, HEADS // 2, step, 0)


def lanes_of(p, base):
    return pl.ds(pl.multiple_of(base + p * 128, 128), 128)


def attention(s, cross):
    tokens = s["normed"].shape[0]
    valid = lax.broadcasted_iota(jnp.int32, (2 * ROWS, ROWS), 1) < MASKED

    def body(at, rows, p):
        q2 = two_heads(s["qkv"][rows, lanes_of(p, 0)])
        sources = [(s["qkv"][rows, lanes_of(p, D)], s["qkv"][rows, lanes_of(p, 2 * D)], "probs")]
        if cross:
            sources.append(
                (s["kv_c"][rows, lanes_of(p, 0)], s["kv_c"][rows, lanes_of(p, D)], "probs_c")
            )
        scores = [
            jnp.where(valid, dot_nt(q2, k) * HEAD_DIM ** (-0.5), -1e30) for k, _, _ in sources
        ]
        top = jnp.max(scores[0], axis=-1, keepdims=True)
        if cross:
            top = jnp.maximum(top, jnp.max(scores[1], axis=-1, keepdims=True))
        powers = [jnp.exp(x - top) for x in scores]
        mass = jnp.sum(powers[0], axis=-1, keepdims=True)
        if cross:
            mass = mass + jnp.sum(powers[1], axis=-1, keepdims=True)
        mixed = None
        inverse = 1.0 / mass
        for power, (_, v, name) in zip(powers, sources):
            probs = power * inverse
            if name in s:
                s[name][at] = probs
            part = dot(probs.astype(LOW), v)
            mixed = part if mixed is None else mixed + part
        s["mixed"][rows, lanes_of(p, 0)] = one_pair(mixed).astype(LOW)

    head_loop(tokens, body)


def block_forward(s, stream, context, resid, weights, vectors, bias, out):
    def row(r, where=slice(None)):
        return vectors[r : r + 1, where]

    norm_forward(stream, row(0), row(1), s.get("x1"), s.get("r1"), s["normed"])
    if context is not None:
        norm_forward(context, row(0), row(1), s["x1_c"], s["r1_c"], s["normed_c"])
    w = weights.open(0)

    def qkv_tile(j):
        where = slice(j * 256, j * 256 + 256)
        kind, local = divmod(j, 3)
        extra = None if kind == 1 else row(6 if kind == 0 else 7, slice(local * 256, local * 256 + 256))
        values = dot(s["normed"][...], w[:, where])
        s["qkv"][:, where] = (values if extra is None else values + extra).astype(LOW)
        if context is not None and kind > 0:
            values = dot(s["normed_c"][...], w[:, where])
            here = slice(j * 256 - D, j * 256 - D + 256)
            s["kv_c"][:, here] = (values if extra is None else values + extra).astype(LOW)

    for j in range(9):
        qkv_tile(j)
    weights.close(0)
    attention(s, context is not None)
    w = weights.open(1)
    for j in range(3):
        where = slice(j * 256, j * 256 + 256)
        attn = dot(s["mixed"][...], w[:, where]) + row(8, where)
        if "attn" in s:
            s["attn"][:, where] = attn
        resid[:, where] = stream[:, where] + row(10, where) * attn
    weights.close(1)
    norm_forward(resid, row(2), row(3), s.get("x2"), s.get("r2"), s["second"])
    w = weights.open(2)

    def up_tile(where):
        pre = dot(s["second"][...], w[:, where]) + bias[0:1, where]
        phi = 0.5 + 0.5 * lax.erf(pre * 0.5**0.5)
        s["hidden"][:, where] = (pre * phi).astype(LOW)
        if "slope" in s:
            s["slope"][:, where] = phi + pre * jnp.exp(-0.5 * pre * pre) * 0.3989422804014327

    tiles(FF, up_tile)
    weights.close(2)
    w = weights.open(3)
    for j in range(3):
        where = slice(j * 256, j * 256 + 256)
        branch = dot(s["hidden"][...], w[:, where]) + row(9, where)
        if "branch" in s:
            s["branch"][:, where] = branch
        resid[:, where] = resid[:, where] + row(11, where) * branch
    weights.close(3)
    norm_forward(resid, row(4), row(5), s.get("x3"), s.get("r3"), None, out)


def attention_backward(s, grad_mixed, cross):
    tokens = s["normed"].shape[0]
    scale = HEAD_DIM ** (-0.5)

    def body(at, rows, p):
        q2 = two_heads(s["qkv"][rows, lanes_of(p, 0)])
        g2 = two_heads(grad_mixed[rows, lanes_of(p, 0)])
        sources = [("qkv", D, "dqkv", "probs")]
        if cross:
            sources.append(("kv_c", 0, "dkv_c", "probs_c"))
        parts = []
        inner = None
        for name, base, grad_name, probs_name in sources:
            v = s[name][rows, lanes_of(p, base + D)]
            probs = s[probs_name][at]
            s[grad_name][rows, lanes_of(p, base + D)] = dot_tn(probs.astype(LOW), g2).astype(LOW)
            dprobs = dot_nt(g2, v)
            parts.append((probs, dprobs))
            total = jnp.sum(dprobs * probs, axis=-1, keepdims=True)
            inner = total if inner is None else inner + total
        dq = None
        for (probs, dprobs), (name, base, grad_name, _) in zip(parts, sources):
            dscores = (probs * (dprobs - inner)).astype(LOW)
            part = dot(dscores, s[name][rows, lanes_of(p, base)])
            dq = part if dq is None else dq + part
            s[grad_name][rows, lanes_of(p, base)] = (dot_tn(dscores, q2) * scale).astype(LOW)
        s["dqkv"][rows, lanes_of(p, 0)] = (one_pair(dq) * scale).astype(LOW)

    head_loop(tokens, body)


def block_backward(s, grad, temp, low_temp, weights, vectors, vec_grad, bias_grad, cross, context_grad):
    tokens = grad.shape[0]
    zero = jnp.zeros((8, D), HIGH)

    def row(r):
        return vectors[r : r + 1, :]

    def put(r, total):
        vec_grad[r : r + 1, :] = jnp.sum(total, axis=0, keepdims=True)

    def final_rows(where, sums):
        gain, shift, scale, offset = sums
        g = grad[where, :]
        center = s["x3"][where, :]
        gf = norm_grad(g, row(4), center, s["r3"][where, :])
        grad[where, :] = gf
        low = (row(11) * gf).astype(LOW)
        s["dbranch"][where, :] = low
        return (
            gain + fold(g * center),
            shift + fold(g),
            scale + fold(gf * s["branch"][where, :]),
            offset + fold(low.astype(HIGH)),
        )

    sums = by_rows(tokens, final_rows, (zero,) * 4)
    for r, total in zip((4, 5, 11, 9), sums):
        put(r, total)
    w = weights.open(3)

    def down_tile(where):
        low = (dot_nt(s["dbranch"][...], w[where, :]) * s["slope"][:, where]).astype(LOW)
        s["dpre"][:, where] = low
        bias_grad[0:1, where] = jnp.sum(low.astype(HIGH), axis=0, keepdims=True)

    tiles(FF, down_tile)
    weights.close(3)
    w = weights.open(2)
    for j in range(3):
        where = slice(j * 256, j * 256 + 256)
        temp[:, where] = dot_nt(s["dpre"][...], w[where, :])
    weights.close(2)

    def second_rows(where, sums):
        gain, shift, scale, offset = sums
        g = temp[where, :]
        center = s["x2"][where, :]
        gr = norm_grad(g, row(2), center, s["r2"][where, :]) + grad[where, :]
        grad[where, :] = gr
        low = (row(10) * gr).astype(LOW)
        s["dattn"][where, :] = low
        return (
            gain + fold(g * center),
            shift + fold(g),
            scale + fold(gr * s["attn"][where, :]),
            offset + fold(low.astype(HIGH)),
        )

    sums = by_rows(tokens, second_rows, (zero,) * 4)
    for r, total in zip((2, 3, 10, 8), sums):
        put(r, total)
    w = weights.open(1)
    for j in range(3):
        where = slice(j * 256, j * 256 + 256)
        low_temp[:, where] = dot_nt(s["dattn"][...], w[where, :]).astype(LOW)
    weights.close(1)
    attention_backward(s, low_temp, cross)
    w = weights.open(0)
    for j in range(3):
        where = slice(j * 256, j * 256 + 256)
        temp[:, where] = dot_nt(s["dqkv"][...], w[where, :])
        if cross:
            context_grad[:, where] = dot_nt(s["dkv_c"][...], w[where, D:])
    weights.close(0)

    def first_rows(where, sums):
        gain, shift, dq, dv = sums
        g = temp[where, :]
        center = s["x1"][where, :]
        grad[where, :] = grad[where, :] + norm_grad(g, row(0), center, s["r1"][where, :])
        gain, shift = gain + fold(g * center), shift + fold(g)
        dq = dq + fold(s["dqkv"][where, 0:D].astype(HIGH))
        dv = dv + fold(s["dqkv"][where, 2 * D :].astype(HIGH))
        if cross:
            g = context_grad[where, :]
            center = s["x1_c"][where, :]
            context_grad[where, :] = norm_grad(g, row(0), center, s["r1_c"][where, :])
            gain, shift = gain + fold(g * center), shift + fold(g)
            dv = dv + fold(s["dkv_c"][where, D:].astype(HIGH))
        return gain, shift, dq, dv

    sums = by_rows(tokens, first_rows, (zero,) * 4)
    for r, total in zip((0, 1, 6, 7), sums):
        put(r, total)


class Slots:
    def __init__(self, places, sems):
        self.places, self.sems = places, sems
        self.queue = [[] for _ in places]
        self.ready = [False] * len(places)

    def copy(self, m, source):
        return pltpu.make_async_copy(source, self.places[m], self.sems.at[m])

    def plan(self, m, source):
        self.queue[m].append(source)
        if len(self.queue[m]) == 1:
            self.copy(m, source).start()

    def open(self, m):
        if not self.ready[m]:
            self.copy(m, self.queue[m][0]).wait()
            self.ready[m] = True
        return self.places[m]

    def close(self, m):
        self.queue[m].pop(0)
        self.ready[m] = False
        if self.queue[m]:
            self.copy(m, self.queue[m][0]).start()


class Held:
    def __init__(self, slots):
        self.slots = slots

    def open(self, m):
        return self.slots.open(m)

    def close(self, m):
        pass


def transposed(place, source):
    width = source.shape[1]
    for j in range(width // 256):
        where = slice(j * 256, j * 256 + 256)
        place[where, :] = source[:, where].T


def weight_grad(out, left, right, place, stacked=0, extra=None, base=0):
    rows, columns = left.shape[1], right.shape[1]
    transposed(place, left)
    if extra is not None:
        transposed(extra[2], extra[0])

    def column_tile(j, with_extra):
        where = pl.ds(pl.multiple_of(j * 256, 256), 256)
        for i in range(rows // 384):
            down = slice(i * 384, i * 384 + 384)
            total = dot(place[down, :], right[:, where])
            if with_extra:
                there = pl.ds(pl.multiple_of(j * 256 - base, 256), 256)
                total = total + dot(extra[2][down, :], extra[1][:, there])
            if stacked:
                count = 384 // stacked
                cut = total.reshape(count, stacked, 256)
                both = jnp.concatenate([cut[:, :, :128], cut[:, :, 128:]], axis=1)
                here = pl.ds(pl.multiple_of(j * 128, 128), 128)
                out[i * count : (i + 1) * count, :, here] = both.astype(LOW)
            else:
                out[down, where] = total.astype(LOW)

    def plain(j, carry):
        column_tile(j, False)
        return carry

    def joined(j, carry):
        column_tile(j, True)
        return carry

    first = base // 256 if extra is not None else columns // 256
    lax.fori_loop(0, first, plain, 0)
    if extra is not None:
        lax.fori_loop(first, columns // 256, joined, 0)


def crop_rows(c):
    return slice(c * ROWS, c * ROWS + ROWS)


def one_hot(orders, kind, crop):
    ids = orders[kind, crop_rows(crop), :]
    return (ids == lax.broadcasted_iota(jnp.int32, (ROWS, PATCHES), 1)).astype(LOW)


def encode_kernel(crops, *refs):
    refs = list(refs)
    patches, orders, pos = refs[:3]
    lead_w, side_w = refs[3:7], refs[7:11]
    lead_vec, lead_bias, side_vec, side_bias = refs[11:15]
    pack, pos_visible, pos_masked = refs[15:18]
    refs = refs[18:]
    saved = dict(zip(NAMES_SELF, refs))
    refs = refs[len(NAMES_SELF) :]
    places, (sems, stream, resid, latent) = refs[:4], refs[4:8]
    brief = dict(zip(("normed", "qkv", "mixed", "second", "hidden"), refs[8:13]))
    section = lax.axis_index("section")

    @pl.when(section == 0)
    def _():
        slots = Slots(places, sems)
        for source in (lead_w, side_w):
            for m in range(4):
                slots.plan(m, source[m])
        for kind in range(2):
            for c in range(crops):
                rows = dot(one_hot(orders, kind, c), patches[c])
                stream[crop_rows(c), :] = rows
            if kind == 0:
                block_forward(saved, stream, None, resid, slots, lead_vec, lead_bias, latent)
            else:
                block_forward(brief, stream, None, resid, slots, side_vec, side_bias, latent)
            pack[kind] = latent[...].astype(LOW)

    @pl.when(section == 1)
    def _():
        for kind, place_of in enumerate((pos_visible, pos_masked)):
            for c in range(crops):
                pick = one_hot(orders, kind, c)
                place_of[crop_rows(c), :] = sum(dot(pick, pos[t]) for t in (2, 1, 0))


def regress_kernel(crops, *refs):
    refs = list(refs)
    pack, pos_visible, pos_masked, cotangent = refs[:4]
    lead_w, side_w = refs[4:8], refs[8:12]
    lead_vec, lead_bias, side_vec, side_bias = refs[12:16]
    refs = refs[16:]

    def grab(names):
        taken = dict(zip(names, refs))
        del refs[: len(names)]
        return taken

    grad_latents, rows_out, reg_vec, reg_bias, dec_vec, dec_bias = refs[:6]
    del refs[:6]
    reg, dec = grab(OUT_REG), grab(OUT_DEC)
    reg.update(grab(KEEP_REG))
    dec.update(grab(KEEP_DEC))
    places = refs[:4]
    sems, stream, context, resid, regressed, grad, temp, low_temp = refs[4:]
    tokens = crops * ROWS

    @pl.when(lax.axis_index("section") == 1)
    def _():
        slots = Slots(places, sems)
        for source in (lead_w, side_w, lead_w):
            for m in range(4):
                slots.plan(m, source[m])
        stream[...] = side_vec[12:13, :] + pos_masked[...]
        context[...] = pack[0].astype(HIGH) + pos_visible[...]
        block_forward(reg, stream, context, resid, slots, lead_vec, lead_bias, regressed)
        stream[...] = regressed[...] + pos_masked[...]
        block_forward(dec, stream, None, resid, Held(slots), side_vec, side_bias, temp)
        for c in range(crops):
            first = c * ROWS
            rows_out[c, 0:MASKED, :] = regressed[first : first + MASKED, :]
            rows_out[c, MASKED : 2 * MASKED, :] = temp[first : first + MASKED, :]
            grad[first : first + ROWS, :] = jnp.zeros((ROWS, D), HIGH)
            grad[first : first + MASKED, :] = cotangent[c].astype(HIGH)
        block_backward(
            dec, grad, temp, low_temp, slots, side_vec, dec_vec, dec_bias, False, None
        )
        inside = lax.broadcasted_iota(jnp.int32, (ROWS, D), 0) < MASKED
        for c in range(crops):
            here = crop_rows(c)
            apart = regressed[here, :] - pack[1, here, :].astype(HIGH)
            grad[here, :] = grad[here, :] + jnp.where(inside, apart, 0.0)
        block_backward(
            reg, grad, temp, low_temp, slots, lead_vec, reg_vec, reg_bias, True, context
        )
        dec_vec[12:13, :] = jnp.sum(grad[...], axis=0, keepdims=True)
        grad_latents[...] = context[...].astype(LOW)


PAIRS = (("normed", "dqkv"), ("mixed", "dattn"), ("second", "dpre"), ("hidden", "dbranch"))
OUT_DEC = tuple(n for pair in PAIRS for n in pair)
OUT_REG = OUT_DEC + ("normed_c", "dkv_c")
KEEP_DEC = tuple(n for n in NAMES_SELF if n not in OUT_DEC)
KEEP_REG = KEEP_DEC + tuple(n for n in NAMES_CROSS if n not in OUT_REG)


def ship(m, scratch, outs, sems):
    return pltpu.make_async_copy(scratch[m], outs[m], sems.at[m])


def decoder_weights_kernel(stacks, *refs):
    pairs, outs = dict(zip(OUT_DEC, refs[:8])), refs[8:12]
    scratch, (place, sems) = refs[12:16], refs[16:]

    @pl.when(lax.axis_index("section") == 1)
    def _():
        for m in (3, 2, 1, 0):
            left, right = PAIRS[m]
            rows = pairs[left].shape[1]
            weight_grad(
                scratch[m], pairs[left], pairs[right], place.at[0:rows, :], stacks[m]
            )
            ship(m, scratch, outs, sems).start()
        for m in range(4):
            ship(m, scratch, outs, sems).wait()


def finish_kernel(crops, *refs):
    refs = list(refs)
    returned, orders = refs[:2]
    lead_w, lead_vec, lead_bias = refs[2:6], refs[6], refs[7]
    del refs[:8]

    def grab(names):
        taken = dict(zip(names, refs))
        del refs[: len(names)]
        return taken

    enc, reg = grab(NAMES_SELF), grab(OUT_REG)
    outs, (rows_out, enc_vec, enc_bias) = refs[:4], refs[4:7]
    del refs[:7]
    enc.update(grab(NAMES_GRAD))
    places = refs[:4]
    scratch = refs[4:8]
    sems, out_sems, place, place_c, grad, temp, low_temp = refs[8:]
    section = lax.axis_index("section")

    def weights_of(pairs, joined):
        for m in (3, 2, 1, 0):
            left, right = PAIRS[m]
            rows = pairs[left].shape[1]
            extra = (pairs["normed_c"], pairs["dkv_c"], place_c) if joined and m == 0 else None
            weight_grad(
                scratch[m], pairs[left], pairs[right], place.at[0:rows, :], 0, extra, D
            )
            ship(m, scratch, outs, out_sems).start()
        for m in range(4):
            ship(m, scratch, outs, out_sems).wait()

    @pl.when(section == 0)
    def _():
        slots = Slots(places, sems)
        for m in (3, 2, 1, 0):
            slots.plan(m, lead_w[m])
        grad[...] = returned[...].astype(HIGH)
        block_backward(enc, grad, temp, low_temp, slots, lead_vec, enc_vec, enc_bias, False, None)
        for c in range(crops):
            rest = grad[crop_rows(c), :]
            pick = one_hot(orders, 0, c)
            total = jnp.zeros((PATCHES, D), HIGH)
            for _ in range(3):
                part = rest.astype(LOW)
                rest = rest - part.astype(HIGH)
                total = total + dot_tn(pick, part)
            rows_out[c] = total
        weights_of(enc, False)

    @pl.when(section == 1)
    def _():
        weights_of(reg, True)


ANYWHERE = pl.BlockSpec(memory_space=pl.ANY)
INSIDE = pl.BlockSpec(memory_space=pltpu.VMEM)


def specs(shapes):
    return [jax.ShapeDtypeStruct(s, d) for s, d in shapes]


def places_for(shapes):
    return [pltpu.VMEM(s, d) for s, d in shapes]


def params():
    return pltpu.CompilerParams(vmem_limit_bytes=60 << 20)


WEIGHT_SHAPES = [((D, 3 * D), LOW), ((D, D), LOW), ((D, FF), LOW), ((FF, D), LOW)]
SMALL_SHAPES = [((16, D), HIGH), ((1, FF), HIGH)]


def encode(crops, patches, orders, pos, lead_w, side_w, smalls):
    tokens = crops * ROWS
    shapes = [((2, tokens, D), LOW), ((tokens, D), HIGH), ((tokens, D), HIGH)]
    shapes += [save_shape(n, tokens) for n in NAMES_SELF]
    scratch = places_for(WEIGHT_SHAPES) + [pltpu.SemaphoreType.DMA((4,))]
    scratch += places_for([((tokens, D), HIGH)] * 3)
    scratch += places_for(
        [save_shape(n, tokens) for n in ("normed", "qkv", "mixed", "second", "hidden")]
    )
    return pl.pallas_call(
        functools.partial(encode_kernel, crops),
        out_shape=specs(shapes),
        in_specs=[INSIDE] * 3 + [ANYWHERE] * 8 + [INSIDE] * 4,
        out_specs=[INSIDE] * len(shapes),
        scratch_shapes=scratch,
        compiler_params=params(),
        name="encode",
    )(patches, orders, pos, *lead_w, *side_w, *smalls)


def regress(crops, pack, pos_visible, pos_masked, cotangent, lead_w, side_w, smalls):
    tokens = crops * ROWS
    shapes = [((tokens, D), LOW), ((crops, PATCHES, D), HIGH)] + SMALL_SHAPES * 2
    shapes += [save_shape(n, tokens) for n in OUT_REG + OUT_DEC]
    scratch = places_for([save_shape(n, tokens) for n in KEEP_REG + KEEP_DEC])
    scratch += places_for(WEIGHT_SHAPES) + [pltpu.SemaphoreType.DMA((4,))]
    scratch += places_for([((tokens, D), HIGH)] * 6 + [((tokens, D), LOW)])
    return pl.pallas_call(
        functools.partial(regress_kernel, crops),
        out_shape=specs(shapes),
        in_specs=[INSIDE] * 4 + [ANYWHERE] * 8 + [INSIDE] * 4,
        out_specs=[INSIDE] * len(shapes),
        scratch_shapes=scratch,
        compiler_params=params(),
        name="regress",
    )(pack, pos_visible, pos_masked, cotangent, *lead_w, *side_w, *smalls)


def dec_grad_shapes(devices, own_path):
    shapes, stacks = [], []
    for (rows, columns), kind in WEIGHT_SHAPES:
        r = rows // (2 * devices)
        stack = r if own_path and r % 16 else 0
        stacks.append(stack)
        shapes.append(
            ((2 * devices, 2 * r, columns // 2), kind) if stack else ((rows, columns), kind)
        )
    return shapes, tuple(stacks)


def decoder_weights(crops, pairs, devices, own_path):
    shapes, stacks = dec_grad_shapes(devices, own_path)
    return pl.pallas_call(
        functools.partial(decoder_weights_kernel, stacks),
        out_shape=specs(shapes),
        in_specs=[INSIDE] * 8,
        out_specs=[ANYWHERE] * 4,
        scratch_shapes=places_for(shapes)
        + places_for([((FF, crops * ROWS), LOW)])
        + [pltpu.SemaphoreType.DMA((4,))],
        compiler_params=params(),
        name="decoder_weights",
    )(*pairs)


def finish(crops, returned, orders, lead_w, lead_small, enc_saved, reg_pairs):
    tokens = crops * ROWS
    shapes = WEIGHT_SHAPES + [((crops, PATCHES, D), HIGH)] + SMALL_SHAPES
    scratch = places_for([save_shape(n, tokens) for n in NAMES_GRAD])
    scratch += places_for(WEIGHT_SHAPES * 2) + [pltpu.SemaphoreType.DMA((4,))] * 2
    scratch += places_for([((FF, tokens), LOW), ((D, tokens), LOW)])
    scratch += places_for([((tokens, D), HIGH)] * 2 + [((tokens, D), LOW)])
    count = len(enc_saved) + len(reg_pairs)
    return pl.pallas_call(
        functools.partial(finish_kernel, crops),
        out_shape=specs(shapes),
        in_specs=[INSIDE] * 2 + [ANYWHERE] * 4 + [INSIDE] * (2 + count),
        out_specs=[ANYWHERE] * 4 + [INSIDE] * 3,
        scratch_shapes=scratch,
        compiler_params=params(),
        name="finish",
    )(returned, orders, *lead_w, *lead_small, *enc_saved, *reg_pairs)


def exchange(pieces, own_path):
    if own_path:
        return gather_all(pieces)
    return [lax.all_gather(p, "dp", axis=0) for p in pieces]


def as_small(parts, rows_of):
    flat = jnp.concatenate([p.reshape(-1) for p in parts])
    block = rows_of * 128
    padded = -(-flat.shape[0] // block) * block
    return jnp.pad(flat, (0, padded - flat.shape[0])).reshape(-1, 128)


def take_flat(flat, shapes):
    taken, offset = [], 0
    for shape in shapes:
        size = 1
        for extent in shape:
            size *= extent
        taken.append(flat[:, offset : offset + size].reshape((-1,) + shape))
        offset += size
    return taken


def spread_columns(gathered):
    return gathered.transpose(1, 0, 2).reshape(gathered.shape[1], -1)


def small_chunks(vectors, bias, chunks):
    rows, columns = vectors.shape
    cut = vectors.reshape(rows, chunks, columns // chunks).transpose(1, 0, 2).reshape(chunks, -1)
    flat = jnp.concatenate([cut, bias.reshape(chunks, -1)], axis=1)
    padded = -(-flat.shape[1] // 1024) * 1024
    return jnp.pad(flat, ((0, 0), (0, padded - flat.shape[1]))).reshape(chunks, -1, 128)


def small_pieces(chunk, rows, chunks):
    flat = chunk.reshape(-1)
    vectors = rows * (D // chunks)
    bias = FF // chunks
    return flat[:vectors].reshape(rows, D // chunks), flat[vectors : vectors + bias]


def total_grads(lead_big, lead_small, dec_big, dec_small, own_path):
    devices = lax.axis_size("dp")
    on_encoder = lax.axis_index("section") == 0
    dec_shapes = [(rows // (2 * devices), columns) for (rows, columns), _ in WEIGHT_SHAPES]
    lead_chunks = [g.reshape(devices, -1, g.shape[1]) for g in lead_big]
    lead_chunks.append(small_chunks(*lead_small, devices))
    dec_chunk_small = small_chunks(*dec_small, 2 * devices)
    if own_path:
        dec_chunks = [
            g.reshape(2, devices, *g.shape[1:])
            if g.ndim == 3
            else g.reshape(2, devices, -1, g.shape[1])
            for g in dec_big
        ]
        dec_chunks.append(dec_chunk_small.reshape((2, devices) + dec_chunk_small.shape[1:]))
        lead_out, dec_out = reduce_all(
            lead_chunks, dec_chunks, dec_shapes + [dec_chunk_small.shape[1:]]
        )
    else:
        dec_chunks = [g.reshape(2, devices, -1, g.shape[1]) for g in dec_big]
        dec_chunks.append(dec_chunk_small.reshape((2, devices) + dec_chunk_small.shape[1:]))
        lead_out = [
            lax.psum_scatter(g.astype(jnp.float32), "dp", scatter_dimension=0) for g in lead_chunks
        ]
        dec_out = []
        for g in dec_chunks:
            mine = jnp.where(on_encoder, jnp.zeros_like(g), g).astype(jnp.float32)
            mine = lax.psum_scatter(mine, "dp", scatter_dimension=1)
            dec_out.append(lax.psum_scatter(mine, "section", scatter_dimension=0))
    lead_vectors, lead_bias = small_pieces(lead_out[4], 12, devices)
    dec_vectors, dec_bias = small_pieces(dec_out[4], 13, 2 * devices)
    return lead_out[:4] + [lead_vectors, lead_bias], dec_out[:4] + [dec_vectors, dec_bias]


def padded_orders(ordering, part):
    cut = ordering[:, MASKED:] if part == 0 else ordering[:, :MASKED]
    cut = jnp.pad(cut, ((0, 0), (0, ROWS - MASKED)), constant_values=-1)
    return cut.reshape(-1, 1)


def shards(
    patches,
    cotangent,
    ordering,
    lead_qkv,
    lead_proj,
    lead_up,
    lead_down,
    lead_vectors,
    lead_bias,
    side_qkv,
    side_proj,
    side_up,
    side_down,
    side_vectors,
    side_bias,
):
    on_encoder = lax.axis_index("section") == 0
    devices = lax.axis_size("dp")
    own_path = devices % 4 == 0 and lead_qkv.shape[1] % 16 == 0
    crops = patches.shape[0]
    small = as_small([lead_vectors[0], lead_bias[0], side_vectors[0], side_bias[0]], 16)
    pieces = [lead_qkv[0], lead_proj[0], lead_up[0], lead_down[0]]
    pieces += [side_qkv[0], side_proj[0], side_up[0], side_down[0], small]
    wholes = exchange(pieces, own_path)
    big = [w.reshape(-1, w.shape[2]) for w in wholes[:8]]
    flat = wholes[8].reshape(devices, -1).astype(jnp.float32)
    lv, lb, sv, sb = take_flat(
        flat,
        [lead_vectors.shape[1:], lead_bias.shape[1:], side_vectors.shape[1:], side_bias.shape[1:]],
    )

    def sixteen(vectors):
        rows = spread_columns(vectors)
        return jnp.pad(rows, ((0, 16 - rows.shape[0]), (0, 0)))

    lead_w, side_w = big[:4], big[4:]
    lead_small = [sixteen(lv), lb.reshape(1, -1)]
    smalls = lead_small + [sixteen(sv), sb.reshape(1, -1)]
    orders = jnp.stack([padded_orders(ordering, 0), padded_orders(ordering, 1)])
    pack, pos_visible, pos_masked, *enc_saved = encode(
        crops, patches, orders, position_parts(), lead_w, side_w, smalls
    )
    arrived = passed_along(pack, "section", 1)
    grad_latents, latent_rows, reg_vec, reg_bias, dec_vec, dec_bias, *pairs = regress(
        crops, arrived, pos_visible, pos_masked, cotangent, lead_w, side_w, smalls
    )
    reg_pairs, dec_pairs = pairs[: len(OUT_REG)], pairs[len(OUT_REG) :]
    returned = passed_along(grad_latents, "section", -1)
    dec_big = decoder_weights(crops, dec_pairs, devices, own_path)
    *lead_big, grad_rows, enc_vec, enc_bias = finish(
        crops, returned, orders, lead_w, lead_small, enc_saved, reg_pairs
    )
    vec = jnp.where(on_encoder, enc_vec, reg_vec)[:12]
    bias = jnp.where(on_encoder, enc_bias, reg_bias)
    lead_out, dec_out = total_grads(
        lead_big, (vec, bias[0]), dec_big, (dec_vec[:13], dec_bias[0]), own_path
    )
    rows = jnp.where(on_encoder, grad_rows, latent_rows)
    return (rows[None],) + tuple(o[None] for o in lead_out) + tuple(dec_out)


def solution(mesh):
    return jax.shard_map(
        shards,
        mesh=mesh,
        in_specs=(
            P("dp", None, None),
            P("dp", None, None),
            P("dp", None),
            P("section", "dp", None),
            P("section", "dp", None),
            P("section", "dp", None),
            P("section", "dp", None),
            P("section", None, "dp"),
            P("section", "dp"),
            P("section", "dp", None),
            P("section", "dp", None),
            P("section", "dp", None),
            P("section", "dp", None),
            P("section", None, "dp"),
            P("section", "dp"),
        ),
        out_specs=(
            P("section", "dp", None, None),
            P("section", "dp", None),
            P("section", "dp", None),
            P("section", "dp", None),
            P("section", "dp", None),
            P("section", None, "dp"),
            P("section", "dp"),
            P(("section", "dp"), None),
            P(("section", "dp"), None),
            P(("section", "dp"), None),
            P(("section", "dp"), None),
            P(None, ("section", "dp")),
            P(("section", "dp")),
        ),
        check_vma=False,
    )
```

```python
import copy
import functools

import jax
import jax.experimental.pallas as pl
import jax.experimental.pallas.tpu as pltpu
import jax.numpy as jnp
import numpy as np
from jax import lax
from jax.sharding import PartitionSpec as P

D = 768
HEADS = 12
HEAD_DIM = 64
FF = 3072
GRID = 14
PATCHES = 196
MASKED = 98


def passed_along(array, axis, by):
    count = lax.axis_size(axis)
    pairs = [(i, i + by) for i in range(count) if 0 <= i + by < count]
    return lax.ppermute(array, axis, pairs)


def positions():
    ids = np.arange(PATCHES)
    quarter = D // 4
    frequency = 10000.0 ** (-np.arange(quarter) / quarter)
    rows = (ids // GRID)[:, None] * frequency
    cols = (ids % GRID)[:, None] * frequency
    return np.concatenate([np.sin(cols), np.cos(cols), np.sin(rows), np.cos(rows)], axis=1)


def position_parts():
    rest = positions().astype(np.float32)
    parts = []
    for _ in range(3):
        part = rest.astype(jnp.bfloat16)
        rest = rest - part.astype(np.float32)
        parts.append(part)
    return jnp.asarray(np.stack(parts))


MESH_ID = pl.DeviceIdType.MESH


def each(count, body):
    if count <= 4:
        for k in range(count):
            body(k)
    else:
        lax.fori_loop(0, count, lambda k, carry: (body(k), carry)[1], 0)


def place():
    section = lax.axis_index("section")
    index = lax.axis_index("dp")
    return section, index, index // 4, (index // 2) % 2, index % 2


def slot(outer, mid, core):
    return outer * 4 + mid * 2 + core


def remote(src, dst, send_sem, recv_sem, device):
    return pltpu.make_async_remote_copy(
        src_ref=src,
        dst_ref=dst,
        send_sem=send_sem,
        recv_sem=recv_sem,
        device_id=device,
        device_id_type=MESH_ID,
    )


def greet(devices):
    barrier = pltpu.get_barrier_semaphore()
    for device in devices:
        pl.semaphore_signal(barrier, inc=1, device_id=device, device_id_type=MESH_ID)


def add_rows(target, at, other, other_at):
    rows = target.shape[-2]
    step = 16 if target.dtype == jnp.bfloat16 else 8

    def body(r, carry):
        where = pl.ds(r * step, step)
        total = target[at, where, :].astype(jnp.float32) + other[other_at, where, :].astype(
            jnp.float32
        )
        target[at, where, :] = total.astype(target.dtype)
        return carry

    lax.fori_loop(0, rows // step, body, 0)


def reduce_kernel(lead_count, dec_count, groups, shapes, *refs):
    refs = list(refs)

    def grab(n):
        taken = refs[:n]
        del refs[:n]
        return taken

    lead_in, dec_in = grab(lead_count), grab(dec_count)
    lead_out, dec_out = grab(lead_count), grab(dec_count)
    lead_own, lead_c, lead_y, lead_z = (grab(lead_count) for _ in range(4))
    dec_own, dec_c, dec_y, dec_z = (grab(dec_count) for _ in range(4))
    load, c_send, c_recv, x_send, x_recv, y_send, y_recv, z_send, z_recv = refs
    section, index, outer, mid, core = place()
    x_device = (1 - section, index)
    mid_device = (section, slot(outer, 1 - mid, core))
    core_device = (section, slot(outer, mid, 1 - core))

    def outer_device(k):
        return (section, slot((outer + k) % groups, mid, core))

    barrier = pltpu.get_barrier_semaphore()
    greet([mid_device, core_device, x_device])
    each(
        groups - 1,
        lambda k: pl.semaphore_signal(
            barrier, inc=1, device_id=outer_device(k + 1), device_id_type=MESH_ID
        ),
    )
    pl.semaphore_wait(barrier, groups + 2)

    def lead_load(m, j):
        return pltpu.make_async_copy(
            lead_in[m].at[j * 2 + core], lead_own[m].at[j], load.at[m, j]
        )

    def lead_core(m, j):
        return remote(
            lead_in[m].at[j * 2 + 1 - core],
            lead_c[m].at[j],
            c_send.at[m, j],
            c_recv.at[m, j],
            core_device,
        )

    def dec_load(m, t, j):
        at = lead_count + 2 * m + t
        return pltpu.make_async_copy(
            dec_in[m].at[t, j * 2 + core], dec_own[m].at[t, j], load.at[at, j]
        )

    def dec_core(m, t, j):
        at = lead_count + 2 * m + t
        return remote(
            dec_in[m].at[t, j * 2 + 1 - core],
            dec_c[m].at[t, j],
            c_send.at[at, j],
            c_recv.at[at, j],
            core_device,
        )

    def x_copy(m, j):
        return remote(
            dec_own[m].at[0, j], dec_own[m].at[1, j], x_send.at[m, j], x_recv.at[m, j], x_device
        )

    own_of = [lead_own[m] for m in range(lead_count)] + [dec_own[m].at[1] for m in range(dec_count)]
    y_of, z_of, out_of = lead_y + dec_y, lead_z + dec_z, lead_out + dec_out

    def y_copy(n, g):
        return remote(
            own_of[n].at[g * 2 + 1 - mid],
            y_of[n].at[g],
            y_send.at[n, g],
            y_recv.at[n, g],
            mid_device,
        )

    def z_copy(n, k):
        other = (outer + k) % groups
        return remote(
            own_of[n].at[other * 2 + mid],
            z_of[n].at[k],
            z_send.at[n, k],
            z_recv.at[n, k],
            outer_device(k),
        )

    for m in range(lead_count):
        each(2 * groups, lambda j: lead_core(m, j).start())
        each(2 * groups, lambda j: lead_load(m, j).start())

    @pl.when(section == 1)
    def _():
        for m in range(dec_count):
            for t in range(2):
                each(2 * groups, lambda j: dec_core(m, t, j).start())
                each(2 * groups, lambda j: dec_load(m, t, j).start())

    def lead_pair(m, j):
        lead_load(m, j).wait()
        lead_core(m, j).wait_recv()
        add_rows(lead_own[m], j, lead_c[m], j)

    for m in range(lead_count):

        def far_pair(g):
            lead_pair(m, g * 2 + 1 - mid)
            y_copy(m, g).start()

        each(groups, far_pair)
        each(groups, lambda g: lead_pair(m, g * 2 + mid))

    @pl.when(section == 1)
    def _():
        for t in range(2):
            for m in range(dec_count):

                def dec_pair(j):
                    dec_load(m, t, j).wait()
                    dec_core(m, t, j).wait_recv()
                    add_rows(dec_own[m].at[t], j, dec_c[m].at[t], j)
                    if t == 0:
                        x_copy(m, j).start()

                each(2 * groups, dec_pair)

    def across(n):
        def other_rows(k):
            other = (outer + k) % groups
            y_copy(n, other).wait_recv()
            add_rows(own_of[n], other * 2 + mid, y_of[n], other)
            z_copy(n, k).start()

        each(groups - 1, lambda k: other_rows(k + 1))
        y_copy(n, outer).wait_recv()

    for m in range(lead_count):
        across(m)
    for m in range(dec_count):
        n = lead_count + m

        @pl.when(section == 0)
        def _():
            each(2 * groups, lambda j: x_copy(m, j).wait_recv())

        each(groups, lambda g: y_copy(n, g).start())
    for m in range(dec_count):
        across(lead_count + m)

    for n in range(lead_count + dec_count):
        each(groups - 1, lambda k: z_copy(n, k + 1).wait_recv())
        own, partner, others, out = own_of[n], y_of[n], z_of[n], out_of[n]
        rows, columns = own.shape[-2], own.shape[-1]
        stacked = out.shape[-1] != columns
        step = rows // 2 if stacked else (16 if own.dtype == jnp.bfloat16 else 8)
        for r in range(rows // step):
            where = pl.ds(r * step, step)

            def total_of(lanes):
                total = own[outer * 2 + mid, where, lanes].astype(jnp.float32)
                total = total + partner[outer, where, lanes].astype(jnp.float32)
                return lax.fori_loop(
                    1, groups, lambda k, acc: acc + others[k, where, lanes].astype(jnp.float32), total
                )

            if stacked:
                for q in range(columns // 128):
                    lanes = slice(q * 128, q * 128 + 128)
                    out[:, (2 * q + r) * 128 : (2 * q + r + 1) * 128] = total_of(lanes)
            else:
                out[where, :] = total_of(slice(None))

    for m in range(lead_count):
        each(2 * groups, lambda j: lead_core(m, j).wait_send())

    @pl.when(section == 1)
    def _():
        for m in range(dec_count):
            for t in range(2):
                each(2 * groups, lambda j: dec_core(m, t, j).wait_send())
            each(2 * groups, lambda j: x_copy(m, j).wait_send())

    for n in range(lead_count + dec_count):
        each(groups, lambda g: y_copy(n, g).wait_send())
        each(groups - 1, lambda k: z_copy(n, k + 1).wait_send())


def reduce_all(lead, dec, dec_outs):
    devices = lax.axis_size("dp")
    groups = devices // 4
    half = devices // 2
    nl, nd = len(lead), len(dec)
    scratch = []
    for lead_shape in (half, half, groups, groups):
        scratch += [pltpu.VMEM((lead_shape,) + a.shape[1:], a.dtype) for a in lead]
    scratch += [pltpu.VMEM((2, half) + a.shape[2:], a.dtype) for a in dec]
    scratch += [pltpu.VMEM((2, half) + a.shape[2:], a.dtype) for a in dec]
    for _ in range(2):
        scratch += [pltpu.VMEM((groups,) + a.shape[2:], a.dtype) for a in dec]
    sems = [(nl + 2 * nd, half)] * 3 + [(nd, half)] * 2 + [(nl + nd, groups)] * 4
    outs = pl.pallas_call(
        functools.partial(reduce_kernel, nl, nd, groups, None),
        out_shape=[jax.ShapeDtypeStruct(a.shape[1:], jnp.float32) for a in lead]
        + [jax.ShapeDtypeStruct(s, jnp.float32) for s in dec_outs],
        in_specs=[pl.BlockSpec(memory_space=pl.ANY)] * (nl + nd),
        out_specs=[pl.BlockSpec(memory_space=pltpu.VMEM)] * (nl + nd),
        scratch_shapes=scratch + [pltpu.SemaphoreType.DMA(s) for s in sems],
        compiler_params=pltpu.CompilerParams(
            collective_id=2, has_side_effects=True, vmem_limit_bytes=60 << 20
        ),
        name="reduce_grads",
    )(*lead, *dec)
    return list(outs[:nl]), list(outs[nl:])


ROWS = 112
LOW = jnp.bfloat16
HIGH = jnp.float32
VISIBLE = PATCHES - MASKED
CHUNK = 32
NAMES_SELF = ("normed", "qkv", "probs", "mixed", "attn", "x1", "r1", "x2", "r2", "second")
NAMES_SELF += ("slope", "hidden", "branch", "x3", "r3")
NAMES_CROSS = ("normed_c", "kv_c", "probs_c", "x1_c", "r1_c")
NAMES_GRAD = ("dqkv", "dattn", "dpre", "dbranch")


def save_shape(name, tokens):
    pairs = tokens // ROWS * (HEADS // 2)
    kinds = {
        "qkv": ((tokens, 3 * D), LOW),
        "kv_c": ((tokens, 2 * D), LOW),
        "dqkv": ((tokens, 3 * D), LOW),
        "dkv_c": ((tokens, 2 * D), LOW),
        "probs": ((pairs, 2 * ROWS, ROWS), HIGH),
        "probs_c": ((pairs, 2 * ROWS, ROWS), HIGH),
        "hidden": ((tokens, FF), LOW),
        "dpre": ((tokens, FF), LOW),
        "slope": ((tokens, FF), HIGH),
    }
    if name in kinds:
        return kinds[name]
    if name in ("r1", "r2", "r3", "r1_c"):
        return ((tokens, 1), HIGH)
    if name in ("attn", "x1", "x1_c", "x2", "x3", "branch"):
        return ((tokens, D), HIGH)
    return ((tokens, D), LOW)


def dot(left, right):
    return jnp.dot(left, right, preferred_element_type=HIGH)


def dot_nt(left, right):
    return lax.dot_general(left, right, (((1,), (1,)), ((), ())), preferred_element_type=HIGH)


def dot_tn(left, right):
    return lax.dot_general(left, right, (((0,), (0,)), ((), ())), preferred_element_type=HIGH)


def by_rows(tokens, body, init=()):
    def step(i, carry):
        return body(pl.ds(pl.multiple_of(i * CHUNK, CHUNK), CHUNK), carry)

    return lax.fori_loop(0, tokens // CHUNK, step, init)


def tiles(width, body, size=256, unroll=1):
    def step(i, carry):
        body(pl.ds(pl.multiple_of(i * size, size), size))
        return carry

    lax.fori_loop(0, width // size, step, 0, unroll=unroll)


def fold(values):
    return jnp.sum(values.reshape(-1, 8, values.shape[-1]), axis=0)


def norm_forward(source, gain, shift, kept, spread, low, out=None):
    def body(where, carry):
        values = source[where, :]
        center = values - jnp.mean(values, axis=-1, keepdims=True)
        scale = lax.rsqrt(jnp.mean(center * center, axis=-1, keepdims=True) + 1e-06)
        center = center * scale
        if kept is not None:
            kept[where, :] = center
            spread[where, :] = scale
        result = center * gain + shift
        if low is not None:
            low[where, :] = result.astype(LOW)
        if out is not None:
            out[where, :] = result
        return carry

    by_rows(source.shape[0], body)


def norm_grad(grad, gain, center, scale):
    weighted = grad * gain
    first = jnp.mean(weighted, axis=-1, keepdims=True)
    second = jnp.mean(weighted * center, axis=-1, keepdims=True)
    return scale * (weighted - first - center * second)


def pair_masks(rows):
    lane = lax.broadcasted_iota(jnp.int32, (rows, 2 * HEAD_DIM), 1)
    return lane < HEAD_DIM


def two_heads(values):
    low_lanes = pair_masks(values.shape[0])
    zero = jnp.zeros_like(values)
    return jnp.concatenate(
        [jnp.where(low_lanes, values, zero), jnp.where(low_lanes, zero, values)], axis=0
    )


def one_pair(stacked):
    half = stacked.shape[0] // 2
    return jnp.where(pair_masks(half), stacked[:half], stacked[half:])


def head_loop(tokens, body):
    def step(p, carry):
        for crop in range(tokens // ROWS):
            rows = pl.ds(crop * ROWS, ROWS)
            body(crop * (HEADS // 2) + p, rows, p)
        return carry

    lax.fori_loop(0, HEADS // 2, step, 0)


def lanes_of(p, base):
    return pl.ds(pl.multiple_of(base + p * 128, 128), 128)


def attention(s, cross):
    tokens = s["normed"].shape[0]
    valid = lax.broadcasted_iota(jnp.int32, (2 * ROWS, ROWS), 1) < MASKED

    def body(at, rows, p):
        q2 = two_heads(s["qkv"][rows, lanes_of(p, 0)])
        sources = [(s["qkv"][rows, lanes_of(p, D)], s["qkv"][rows, lanes_of(p, 2 * D)], "probs")]
        if cross:
            sources.append(
                (s["kv_c"][rows, lanes_of(p, 0)], s["kv_c"][rows, lanes_of(p, D)], "probs_c")
            )
        scores = [
            jnp.where(valid, dot_nt(q2, k) * HEAD_DIM ** (-0.5), -1e30) for k, _, _ in sources
        ]
        top = jnp.max(scores[0], axis=-1, keepdims=True)
        if cross:
            top = jnp.maximum(top, jnp.max(scores[1], axis=-1, keepdims=True))
        powers = [jnp.exp(x - top) for x in scores]
        mass = jnp.sum(powers[0], axis=-1, keepdims=True)
        if cross:
            mass = mass + jnp.sum(powers[1], axis=-1, keepdims=True)
        mixed = None
        inverse = 1.0 / mass
        for power, (_, v, name) in zip(powers, sources):
            probs = power * inverse
            if name in s:
                s[name][at] = probs
            part = dot(probs.astype(LOW), v)
            mixed = part if mixed is None else mixed + part
        s["mixed"][rows, lanes_of(p, 0)] = one_pair(mixed).astype(LOW)

    head_loop(tokens, body)


def block_forward(s, stream, context, resid, weights, vectors, bias, out):
    def row(r, where=slice(None)):
        return vectors[r : r + 1, where]

    norm_forward(stream, row(0), row(1), s.get("x1"), s.get("r1"), s["normed"])
    if context is not None:
        norm_forward(context, row(0), row(1), s["x1_c"], s["r1_c"], s["normed_c"])
    w = weights.open(0)

    def qkv_tile(j):
        where = slice(j * 256, j * 256 + 256)
        kind, local = divmod(j, 3)
        extra = None if kind == 1 else row(6 if kind == 0 else 7, slice(local * 256, local * 256 + 256))
        values = dot(s["normed"][...], w[:, where])
        s["qkv"][:, where] = (values if extra is None else values + extra).astype(LOW)
        if context is not None and kind > 0:
            values = dot(s["normed_c"][...], w[:, where])
            here = slice(j * 256 - D, j * 256 - D + 256)
            s["kv_c"][:, here] = (values if extra is None else values + extra).astype(LOW)

    for j in range(9):
        qkv_tile(j)
    weights.close(0)
    attention(s, context is not None)
    w = weights.open(1)
    for j in range(3):
        where = slice(j * 256, j * 256 + 256)
        attn = dot(s["mixed"][...], w[:, where]) + row(8, where)
        if "attn" in s:
            s["attn"][:, where] = attn
        resid[:, where] = stream[:, where] + row(10, where) * attn
    weights.close(1)
    norm_forward(resid, row(2), row(3), s.get("x2"), s.get("r2"), s["second"])
    w = weights.open(2)

    def up_tile(where):
        pre = dot(s["second"][...], w[:, where]) + bias[0:1, where]
        phi = 0.5 + 0.5 * lax.erf(pre * 0.5**0.5)
        s["hidden"][:, where] = (pre * phi).astype(LOW)
        if "slope" in s:
            s["slope"][:, where] = phi + pre * jnp.exp(-0.5 * pre * pre) * 0.3989422804014327

    tiles(FF, up_tile)
    weights.close(2)
    w = weights.open(3)
    for j in range(3):
        where = slice(j * 256, j * 256 + 256)
        branch = dot(s["hidden"][...], w[:, where]) + row(9, where)
        if "branch" in s:
            s["branch"][:, where] = branch
        resid[:, where] = resid[:, where] + row(11, where) * branch
    weights.close(3)
    norm_forward(resid, row(4), row(5), s.get("x3"), s.get("r3"), None, out)


def attention_backward(s, grad_mixed, cross):
    tokens = s["normed"].shape[0]
    scale = HEAD_DIM ** (-0.5)

    def body(at, rows, p):
        q2 = two_heads(s["qkv"][rows, lanes_of(p, 0)])
        g2 = two_heads(grad_mixed[rows, lanes_of(p, 0)])
        sources = [("qkv", D, "dqkv", "probs")]
        if cross:
            sources.append(("kv_c", 0, "dkv_c", "probs_c"))
        parts = []
        inner = None
        for name, base, grad_name, probs_name in sources:
            v = s[name][rows, lanes_of(p, base + D)]
            probs = s[probs_name][at]
            s[grad_name][rows, lanes_of(p, base + D)] = dot_tn(probs.astype(LOW), g2).astype(LOW)
            dprobs = dot_nt(g2, v)
            parts.append((probs, dprobs))
            total = jnp.sum(dprobs * probs, axis=-1, keepdims=True)
            inner = total if inner is None else inner + total
        dq = None
        for (probs, dprobs), (name, base, grad_name, _) in zip(parts, sources):
            dscores = (probs * (dprobs - inner)).astype(LOW)
            part = dot(dscores, s[name][rows, lanes_of(p, base)])
            dq = part if dq is None else dq + part
            s[grad_name][rows, lanes_of(p, base)] = (dot_tn(dscores, q2) * scale).astype(LOW)
        s["dqkv"][rows, lanes_of(p, 0)] = (one_pair(dq) * scale).astype(LOW)

    head_loop(tokens, body)


def block_backward(s, grad, temp, low_temp, weights, vectors, vec_grad, bias_grad, cross, context_grad):
    tokens = grad.shape[0]
    zero = jnp.zeros((8, D), HIGH)

    def row(r):
        return vectors[r : r + 1, :]

    def put(r, total):
        vec_grad[r : r + 1, :] = jnp.sum(total, axis=0, keepdims=True)

    def final_rows(where, sums):
        gain, shift, scale, offset = sums
        g = grad[where, :]
        center = s["x3"][where, :]
        gf = norm_grad(g, row(4), center, s["r3"][where, :])
        grad[where, :] = gf
        low = (row(11) * gf).astype(LOW)
        s["dbranch"][where, :] = low
        return (
            gain + fold(g * center),
            shift + fold(g),
            scale + fold(gf * s["branch"][where, :]),
            offset + fold(low.astype(HIGH)),
        )

    sums = by_rows(tokens, final_rows, (zero,) * 4)
    for r, total in zip((4, 5, 11, 9), sums):
        put(r, total)
    w = weights.open(3)

    def down_tile(where):
        low = (dot_nt(s["dbranch"][...], w[where, :]) * s["slope"][:, where]).astype(LOW)
        s["dpre"][:, where] = low
        bias_grad[0:1, where] = jnp.sum(low.astype(HIGH), axis=0, keepdims=True)

    tiles(FF, down_tile)
    weights.close(3)
    w = weights.open(2)
    for j in range(3):
        where = slice(j * 256, j * 256 + 256)
        temp[:, where] = dot_nt(s["dpre"][...], w[where, :])
    weights.close(2)

    def second_rows(where, sums):
        gain, shift, scale, offset = sums
        g = temp[where, :]
        center = s["x2"][where, :]
        gr = norm_grad(g, row(2), center, s["r2"][where, :]) + grad[where, :]
        grad[where, :] = gr
        low = (row(10) * gr).astype(LOW)
        s["dattn"][where, :] = low
        return (
            gain + fold(g * center),
            shift + fold(g),
            scale + fold(gr * s["attn"][where, :]),
            offset + fold(low.astype(HIGH)),
        )

    sums = by_rows(tokens, second_rows, (zero,) * 4)
    for r, total in zip((2, 3, 10, 8), sums):
        put(r, total)
    w = weights.open(1)
    for j in range(3):
        where = slice(j * 256, j * 256 + 256)
        low_temp[:, where] = dot_nt(s["dattn"][...], w[where, :]).astype(LOW)
    weights.close(1)
    attention_backward(s, low_temp, cross)
    w = weights.open(0)
    for j in range(3):
        where = slice(j * 256, j * 256 + 256)
        temp[:, where] = dot_nt(s["dqkv"][...], w[where, :])
        if cross:
            context_grad[:, where] = dot_nt(s["dkv_c"][...], w[where, D:])
    weights.close(0)

    def first_rows(where, sums):
        gain, shift, dq, dv = sums
        g = temp[where, :]
        center = s["x1"][where, :]
        grad[where, :] = grad[where, :] + norm_grad(g, row(0), center, s["r1"][where, :])
        gain, shift = gain + fold(g * center), shift + fold(g)
        dq = dq + fold(s["dqkv"][where, 0:D].astype(HIGH))
        dv = dv + fold(s["dqkv"][where, 2 * D :].astype(HIGH))
        if cross:
            g = context_grad[where, :]
            center = s["x1_c"][where, :]
            context_grad[where, :] = norm_grad(g, row(0), center, s["r1_c"][where, :])
            gain, shift = gain + fold(g * center), shift + fold(g)
            dv = dv + fold(s["dkv_c"][where, D:].astype(HIGH))
        return gain, shift, dq, dv

    sums = by_rows(tokens, first_rows, (zero,) * 4)
    for r, total in zip((0, 1, 6, 7), sums):
        put(r, total)


class Slots:
    def __init__(self, places, sems):
        self.places, self.sems = places, sems
        self.queue = [[] for _ in places]
        self.ready = [False] * len(places)

    def copy(self, m, source):
        return pltpu.make_async_copy(source, self.places[m], self.sems.at[m])

    def plan(self, m, source):
        self.queue[m].append(source)
        if len(self.queue[m]) == 1:
            self.copy(m, source).start()

    def open(self, m):
        if not self.ready[m]:
            self.copy(m, self.queue[m][0]).wait()
            self.ready[m] = True
        return self.places[m]

    def close(self, m):
        self.queue[m].pop(0)
        self.ready[m] = False
        if self.queue[m]:
            self.copy(m, self.queue[m][0]).start()


class Held:
    def __init__(self, slots):
        self.slots = slots

    def open(self, m):
        return self.slots.open(m)

    def close(self, m):
        pass


def transposed(place, source):
    width = source.shape[1]
    for j in range(width // 256):
        where = slice(j * 256, j * 256 + 256)
        place[where, :] = source[:, where].T


def weight_grad(out, left, right, place, stacked=0, extra=None, base=0):
    rows, columns = left.shape[1], right.shape[1]
    transposed(place, left)
    if extra is not None:
        transposed(extra[2], extra[0])

    def column_tile(j, with_extra):
        where = pl.ds(pl.multiple_of(j * 256, 256), 256)
        for i in range(rows // 384):
            down = slice(i * 384, i * 384 + 384)
            total = dot(place[down, :], right[:, where])
            if with_extra:
                there = pl.ds(pl.multiple_of(j * 256 - base, 256), 256)
                total = total + dot(extra[2][down, :], extra[1][:, there])
            if stacked:
                count = 384 // stacked
                cut = total.reshape(count, stacked, 256)
                both = jnp.concatenate([cut[:, :, :128], cut[:, :, 128:]], axis=1)
                here = pl.ds(pl.multiple_of(j * 128, 128), 128)
                out[i * count : (i + 1) * count, :, here] = both.astype(LOW)
            else:
                out[down, where] = total.astype(LOW)

    def plain(j, carry):
        column_tile(j, False)
        return carry

    def joined(j, carry):
        column_tile(j, True)
        return carry

    first = base // 256 if extra is not None else columns // 256
    lax.fori_loop(0, first, plain, 0)
    if extra is not None:
        lax.fori_loop(first, columns // 256, joined, 0)


def crop_rows(c):
    return slice(c * ROWS, c * ROWS + ROWS)


def one_hot(orders, kind, crop):
    ids = orders[kind, crop_rows(crop), :]
    return (ids == lax.broadcasted_iota(jnp.int32, (ROWS, PATCHES), 1)).astype(LOW)


def encode_kernel(crops, *refs):
    refs = list(refs)
    patches, orders, pos = refs[:3]
    lead_w, side_w = refs[3:7], refs[7:11]
    lead_vec, lead_bias, side_vec, side_bias = refs[11:15]
    pack, pos_visible, pos_masked = refs[15:18]
    refs = refs[18:]
    saved = dict(zip(NAMES_SELF, refs))
    refs = refs[len(NAMES_SELF) :]
    places, (sems, stream, resid, latent) = refs[:4], refs[4:8]
    brief = dict(zip(("normed", "qkv", "mixed", "second", "hidden"), refs[8:13]))
    section = lax.axis_index("section")

    @pl.when(section == 0)
    def _():
        slots = Slots(places, sems)
        for source in (lead_w, side_w):
            for m in range(4):
                slots.plan(m, source[m])
        for kind in range(2):
            for c in range(crops):
                rows = dot(one_hot(orders, kind, c), patches[c])
                stream[crop_rows(c), :] = rows
            if kind == 0:
                block_forward(saved, stream, None, resid, slots, lead_vec, lead_bias, latent)
            else:
                block_forward(brief, stream, None, resid, slots, side_vec, side_bias, latent)
            pack[kind] = latent[...].astype(LOW)

    @pl.when(section == 1)
    def _():
        for kind, place_of in enumerate((pos_visible, pos_masked)):
            for c in range(crops):
                pick = one_hot(orders, kind, c)
                place_of[crop_rows(c), :] = sum(dot(pick, pos[t]) for t in (2, 1, 0))


def regress_kernel(crops, *refs):
    refs = list(refs)
    pack, pos_visible, pos_masked, cotangent = refs[:4]
    lead_w, side_w = refs[4:8], refs[8:12]
    lead_vec, lead_bias, side_vec, side_bias = refs[12:16]
    refs = refs[16:]

    def grab(names):
        taken = dict(zip(names, refs))
        del refs[: len(names)]
        return taken

    grad_latents, rows_out, reg_vec, reg_bias, dec_vec, dec_bias = refs[:6]
    del refs[:6]
    reg, dec = grab(OUT_REG), grab(OUT_DEC)
    reg.update(grab(KEEP_REG))
    dec.update(grab(KEEP_DEC))
    places = refs[:4]
    sems, stream, context, resid, regressed, grad, temp, low_temp = refs[4:]
    tokens = crops * ROWS

    @pl.when(lax.axis_index("section") == 1)
    def _():
        slots = Slots(places, sems)
        for source in (lead_w, side_w, lead_w):
            for m in range(4):
                slots.plan(m, source[m])
        stream[...] = side_vec[12:13, :] + pos_masked[...]
        context[...] = pack[0].astype(HIGH) + pos_visible[...]
        block_forward(reg, stream, context, resid, slots, lead_vec, lead_bias, regressed)
        stream[...] = regressed[...] + pos_masked[...]
        block_forward(dec, stream, None, resid, Held(slots), side_vec, side_bias, temp)
        for c in range(crops):
            first = c * ROWS
            rows_out[c, 0:MASKED, :] = regressed[first : first + MASKED, :]
            rows_out[c, MASKED : 2 * MASKED, :] = temp[first : first + MASKED, :]
            grad[first : first + ROWS, :] = jnp.zeros((ROWS, D), HIGH)
            grad[first : first + MASKED, :] = cotangent[c].astype(HIGH)
        block_backward(
            dec, grad, temp, low_temp, slots, side_vec, dec_vec, dec_bias, False, None
        )
        inside = lax.broadcasted_iota(jnp.int32, (ROWS, D), 0) < MASKED
        for c in range(crops):
            here = crop_rows(c)
            apart = regressed[here, :] - pack[1, here, :].astype(HIGH)
            grad[here, :] = grad[here, :] + jnp.where(inside, apart, 0.0)
        block_backward(
            reg, grad, temp, low_temp, slots, lead_vec, reg_vec, reg_bias, True, context
        )
        dec_vec[12:13, :] = jnp.sum(grad[...], axis=0, keepdims=True)
        grad_latents[...] = context[...].astype(LOW)


PAIRS = (("normed", "dqkv"), ("mixed", "dattn"), ("second", "dpre"), ("hidden", "dbranch"))
OUT_DEC = tuple(n for pair in PAIRS for n in pair)
OUT_REG = OUT_DEC + ("normed_c", "dkv_c")
KEEP_DEC = tuple(n for n in NAMES_SELF if n not in OUT_DEC)
KEEP_REG = KEEP_DEC + tuple(n for n in NAMES_CROSS if n not in OUT_REG)


def ship(m, scratch, outs, sems):
    return pltpu.make_async_copy(scratch[m], outs[m], sems.at[m])


def decoder_weights_kernel(stacks, *refs):
    pairs, outs = dict(zip(OUT_DEC, refs[:8])), refs[8:12]
    scratch, (place, sems) = refs[12:16], refs[16:]

    @pl.when(lax.axis_index("section") == 1)
    def _():
        for m in (3, 2, 1, 0):
            left, right = PAIRS[m]
            rows = pairs[left].shape[1]
            weight_grad(
                scratch[m], pairs[left], pairs[right], place.at[0:rows, :], stacks[m]
            )
            ship(m, scratch, outs, sems).start()
        for m in range(4):
            ship(m, scratch, outs, sems).wait()


def finish_kernel(crops, *refs):
    refs = list(refs)
    returned, orders = refs[:2]
    lead_w, lead_vec, lead_bias = refs[2:6], refs[6], refs[7]
    del refs[:8]

    def grab(names):
        taken = dict(zip(names, refs))
        del refs[: len(names)]
        return taken

    enc, reg = grab(NAMES_SELF), grab(OUT_REG)
    outs, (rows_out, enc_vec, enc_bias) = refs[:4], refs[4:7]
    del refs[:7]
    enc.update(grab(NAMES_GRAD))
    places = refs[:4]
    scratch = refs[4:8]
    sems, out_sems, place, place_c, grad, temp, low_temp = refs[8:]
    section = lax.axis_index("section")

    def weights_of(pairs, joined):
        for m in (3, 2, 1, 0):
            left, right = PAIRS[m]
            rows = pairs[left].shape[1]
            extra = (pairs["normed_c"], pairs["dkv_c"], place_c) if joined and m == 0 else None
            weight_grad(
                scratch[m], pairs[left], pairs[right], place.at[0:rows, :], 0, extra, D
            )
            ship(m, scratch, outs, out_sems).start()
        for m in range(4):
            ship(m, scratch, outs, out_sems).wait()

    @pl.when(section == 0)
    def _():
        slots = Slots(places, sems)
        for m in (3, 2, 1, 0):
            slots.plan(m, lead_w[m])
        grad[...] = returned[...].astype(HIGH)
        block_backward(enc, grad, temp, low_temp, slots, lead_vec, enc_vec, enc_bias, False, None)
        for c in range(crops):
            rest = grad[crop_rows(c), :]
            pick = one_hot(orders, 0, c)
            total = jnp.zeros((PATCHES, D), HIGH)
            for _ in range(3):
                part = rest.astype(LOW)
                rest = rest - part.astype(HIGH)
                total = total + dot_tn(pick, part)
            rows_out[c] = total
        weights_of(enc, False)

    @pl.when(section == 1)
    def _():
        weights_of(reg, True)


ANYWHERE = pl.BlockSpec(memory_space=pl.ANY)
INSIDE = pl.BlockSpec(memory_space=pltpu.VMEM)


def specs(shapes):
    return [jax.ShapeDtypeStruct(s, d) for s, d in shapes]


def places_for(shapes):
    return [pltpu.VMEM(s, d) for s, d in shapes]


def params():
    return pltpu.CompilerParams(vmem_limit_bytes=60 << 20)


WEIGHT_SHAPES = [((D, 3 * D), LOW), ((D, D), LOW), ((D, FF), LOW), ((FF, D), LOW)]
SMALL_SHAPES = [((16, D), HIGH), ((1, FF), HIGH)]


def encode(crops, patches, orders, pos, lead_w, side_w, smalls):
    tokens = crops * ROWS
    shapes = [((2, tokens, D), LOW), ((tokens, D), HIGH), ((tokens, D), HIGH)]
    shapes += [save_shape(n, tokens) for n in NAMES_SELF]
    scratch = places_for(WEIGHT_SHAPES) + [pltpu.SemaphoreType.DMA((4,))]
    scratch += places_for([((tokens, D), HIGH)] * 3)
    scratch += places_for(
        [save_shape(n, tokens) for n in ("normed", "qkv", "mixed", "second", "hidden")]
    )
    return pl.pallas_call(
        functools.partial(encode_kernel, crops),
        out_shape=specs(shapes),
        in_specs=[INSIDE] * 3 + [ANYWHERE] * 8 + [INSIDE] * 4,
        out_specs=[INSIDE] * len(shapes),
        scratch_shapes=scratch,
        compiler_params=params(),
        name="encode",
    )(patches, orders, pos, *lead_w, *side_w, *smalls)


def regress(crops, pack, pos_visible, pos_masked, cotangent, lead_w, side_w, smalls):
    tokens = crops * ROWS
    shapes = [((tokens, D), LOW), ((crops, PATCHES, D), HIGH)] + SMALL_SHAPES * 2
    shapes += [save_shape(n, tokens) for n in OUT_REG + OUT_DEC]
    scratch = places_for([save_shape(n, tokens) for n in KEEP_REG + KEEP_DEC])
    scratch += places_for(WEIGHT_SHAPES) + [pltpu.SemaphoreType.DMA((4,))]
    scratch += places_for([((tokens, D), HIGH)] * 6 + [((tokens, D), LOW)])
    return pl.pallas_call(
        functools.partial(regress_kernel, crops),
        out_shape=specs(shapes),
        in_specs=[INSIDE] * 4 + [ANYWHERE] * 8 + [INSIDE] * 4,
        out_specs=[INSIDE] * len(shapes),
        scratch_shapes=scratch,
        compiler_params=params(),
        name="regress",
    )(pack, pos_visible, pos_masked, cotangent, *lead_w, *side_w, *smalls)


def dec_grad_shapes(devices, own_path):
    shapes, stacks = [], []
    for (rows, columns), kind in WEIGHT_SHAPES:
        r = rows // (2 * devices)
        stack = r if own_path and r % 16 else 0
        stacks.append(stack)
        shapes.append(
            ((2 * devices, 2 * r, columns // 2), kind) if stack else ((rows, columns), kind)
        )
    return shapes, tuple(stacks)


def decoder_weights(crops, pairs, devices, own_path):
    shapes, stacks = dec_grad_shapes(devices, own_path)
    return pl.pallas_call(
        functools.partial(decoder_weights_kernel, stacks),
        out_shape=specs(shapes),
        in_specs=[INSIDE] * 8,
        out_specs=[ANYWHERE] * 4,
        scratch_shapes=places_for(shapes)
        + places_for([((FF, crops * ROWS), LOW)])
        + [pltpu.SemaphoreType.DMA((4,))],
        compiler_params=params(),
        name="decoder_weights",
    )(*pairs)


def finish(crops, returned, orders, lead_w, lead_small, enc_saved, reg_pairs):
    tokens = crops * ROWS
    shapes = WEIGHT_SHAPES + [((crops, PATCHES, D), HIGH)] + SMALL_SHAPES
    scratch = places_for([save_shape(n, tokens) for n in NAMES_GRAD])
    scratch += places_for(WEIGHT_SHAPES * 2) + [pltpu.SemaphoreType.DMA((4,))] * 2
    scratch += places_for([((FF, tokens), LOW), ((D, tokens), LOW)])
    scratch += places_for([((tokens, D), HIGH)] * 2 + [((tokens, D), LOW)])
    count = len(enc_saved) + len(reg_pairs)
    return pl.pallas_call(
        functools.partial(finish_kernel, crops),
        out_shape=specs(shapes),
        in_specs=[INSIDE] * 2 + [ANYWHERE] * 4 + [INSIDE] * (2 + count),
        out_specs=[ANYWHERE] * 4 + [INSIDE] * 3,
        scratch_shapes=scratch,
        compiler_params=params(),
        name="finish",
    )(returned, orders, *lead_w, *lead_small, *enc_saved, *reg_pairs)


SMALL_ROWS = 48


class Feed:
    WINDOW = 3

    def __init__(self, groups, shards_in, wholes, sems):
        self.groups, self.shards, self.wholes = groups, shards_in, wholes
        self.own, self.zs, self.zr, self.ys, self.yr, self.cs, self.cr = sems
        self.count = len(shards_in)
        self.section, self.index, self.outer, self.mid, self.core = place()
        self.begun = self.at = 0
        self.done = set()
        self.steps = [("z", 0), ("y", 0), ("z", 1)]
        for m in range(2, self.count):
            self.steps += [("z", m), ("y", m - 1)]
        self.steps.append(("y", self.count - 1))

    def branch(self):
        other = copy.copy(self)
        other.done = set(self.done)
        return other

    def devices(self):
        mid = (self.section, slot(self.outer, 1 - self.mid, self.core))
        core = (self.section, slot(self.outer, self.mid, 1 - self.core))
        return mid, core

    def outer_device(self, k):
        return (self.section, slot((self.outer + k) % self.groups, self.mid, self.core))

    def origin(self, k, far=0, other_core=False):
        outer = (self.outer - k + self.groups) % self.groups
        mid = 1 - self.mid if far else self.mid
        return slot(outer, mid, 1 - self.core if other_core else self.core)

    def own_copy(self, m):
        return pltpu.make_async_copy(
            self.shards[m], self.wholes[m].at[self.index], self.own.at[m]
        )

    def z_copy(self, m, k, arrival=False):
        at = self.origin(k) if arrival else self.index
        return remote(
            self.shards[m],
            self.wholes[m].at[at],
            self.zs.at[m, k],
            self.zr.at[m, k],
            self.outer_device(k),
        )

    def y_copy(self, m, k, own=False, arrival=False):
        piece = self.wholes[m].at[self.origin(k, far=1 if arrival else 0)]
        src = self.shards[m] if own else piece
        return remote(src, piece, self.ys.at[m, k], self.yr.at[m, k], self.devices()[0])

    def c_copy(self, m, k, far, own=False, arrival=False):
        piece = self.wholes[m].at[self.origin(k, far, arrival)]
        src = self.shards[m] if own else piece
        at = k * 2 + far
        return remote(src, piece, self.cs.at[m, at], self.cr.at[m, at], self.devices()[1])

    def begin(self, upto):
        while self.begun < min(upto, self.count):
            m = self.begun
            each(self.groups - 1, lambda k: self.z_copy(m, k + 1).start())
            self.y_copy(m, 0, own=True).start()
            self.c_copy(m, 0, 0, own=True).start()
            self.own_copy(m).start()
            self.begun += 1

    def step(self):
        kind, m = self.steps[self.at]
        self.at += 1
        if kind == "z":

            def pass_on(k):
                self.z_copy(m, k + 1, arrival=True).wait_recv()
                self.y_copy(m, k + 1).start()
                self.c_copy(m, k + 1, 0).start()

            each(self.groups - 1, pass_on)
            self.begin(m + 1 + self.WINDOW)
        else:

            def hand_over(k):
                self.y_copy(m, k, arrival=True).wait_recv()
                self.c_copy(m, k, 1).start()

            each(self.groups, hand_over)

    def pump(self, kind, m):
        while (kind, m) in self.steps[self.at :]:
            self.step()

    def need(self, m):
        self.pump("y", m)
        if m in self.done:
            return
        self.done.add(m)

        def last(k):
            for far in range(2):
                self.c_copy(m, k, far, arrival=True).wait_recv()

        each(self.groups, last)
        self.own_copy(m).wait()

    def drain(self):
        for m in range(self.count):
            self.need(m)
            each(self.groups - 1, lambda k: self.z_copy(m, k + 1).wait_send())

            def finish_sends(k):
                self.y_copy(m, k).wait_send()
                for far in range(2):
                    self.c_copy(m, k, far).wait_send()

            each(self.groups, finish_sends)


class FedSlots(Slots):
    def __init__(self, places, sems, feed):
        super().__init__(places, sems)
        self.feed = feed
        self.started = [False] * len(places)

    def plan(self, m, piece):
        self.queue[m].append(piece)

    def fetch(self, m):
        if not self.started[m] and self.queue[m]:
            piece = self.queue[m][0]
            self.feed.need(piece)
            self.copy(m, self.feed.flat[piece]).start()
            self.started[m] = True

    def open(self, m):
        self.fetch(m)
        if not self.ready[m]:
            self.copy(m, self.feed.flat[self.queue[m][0]]).wait()
            self.ready[m] = True
        return self.places[m]

    def close(self, m):
        self.queue[m].pop(0)
        self.ready[m] = self.started[m] = False
        if self.queue[m] and self.queue[m][0] in self.feed.done:
            self.fetch(m)


def unpack_small(small, devices, lead_vec, lead_bias, side_vec, side_bias):
    width = D // devices
    per = FF // devices // width
    for d in range(devices):
        lanes = slice(d * width, d * width + width)
        block = small[d].astype(HIGH)
        lead_vec[0:16, lanes] = block[0:16, 0:width]
        side_vec[0:16, lanes] = block[16:32, 0:width]
        for i in range(per):
            first = (d * per + i) * width
            lead_bias[0:1, first : first + width] = block[32 + i : 33 + i, 0:width]
            side_bias[0:1, first : first + width] = block[40 + i : 41 + i, 0:width]


def pack_small(lead_vectors, lead_bias, side_vectors, side_bias):
    width = lead_vectors.shape[1]

    def block(rows, height):
        rows = rows.reshape(-1, width)
        return jnp.pad(rows, ((0, height - rows.shape[0]), (0, 128 - width)))

    return jnp.concatenate(
        [block(lead_vectors, 16), block(side_vectors, 16), block(lead_bias, 8), block(side_bias, 8)]
    )


def layer_kernel(crops, devices, *refs):
    refs = list(refs)

    def grab(n):
        taken = refs[:n]
        del refs[:n]
        return taken

    def named(names):
        return dict(zip(names, grab(len(names))))

    shards_in = grab(9)
    patches, orders, pos, cotangent = grab(4)
    wholes = grab(9)
    rows_out, lead_vec_grad, lead_bias_grad, dec_vec_grad, dec_bias_grad = grab(5)
    own, reg = named(OUT_DEC), named(OUT_REG)
    own.update(named(KEEP_DEC))
    reg.update(named(KEEP_REG))
    places = grab(4)
    lead_vec, lead_bias, side_vec, side_bias, small = grab(5)
    stream, context, resid, regressed, grad, temp, pos_visible, pos_masked = grab(8)
    low_temp, first_pack, second_pack = grab(3)
    sems, small_sem, x_send, x_recv = grab(4)
    groups = devices // 4
    feed = Feed(groups, shards_in, wholes, refs)
    feed.flat = [None] + [
        w.reshape(devices * w.shape[1], w.shape[2]) for w in wholes[1:]
    ]
    section = feed.section
    tokens = crops * ROWS
    x_device = (1 - section, feed.index)
    greet([*feed.devices(), x_device])
    barrier = pltpu.get_barrier_semaphore()
    each(
        groups - 1,
        lambda k: pl.semaphore_signal(
            barrier, inc=1, device_id=feed.outer_device(k + 1), device_id_type=MESH_ID
        ),
    )
    pl.semaphore_wait(barrier, groups + 2)
    feed.begin(Feed.WINDOW)

    def x_copy(n):
        piece = (first_pack.at[0], first_pack.at[1], second_pack)[n]
        return remote(piece, piece, x_send.at[n], x_recv.at[n], x_device)

    def vectors_in(feed):
        feed.need(0)
        fetched = pltpu.make_async_copy(wholes[0], small, small_sem)
        fetched.start()
        fetched.wait()
        unpack_small(small, devices, lead_vec, lead_bias, side_vec, side_bias)

    def slots_of(feed):
        slots = FedSlots(places, sems, feed)
        for base in (1, 5, 1):
            for m in range(4):
                slots.plan(m, base + m)
        return slots

    start = feed

    @pl.when(section == 0)
    def _():
        feed = start.branch()
        slots = slots_of(feed)
        for kind, vec, bias, keep in ((0, lead_vec, lead_bias, own), (1, side_vec, side_bias, reg)):
            for c in range(crops):
                stream[crop_rows(c), :] = dot(one_hot(orders, kind, c), patches[c])
            if kind == 0:
                vectors_in(feed)
            else:
                names = ("normed", "qkv", "mixed", "second", "hidden")
                keep = {n: reg[n] for n in names}
            block_forward(keep, stream, None, resid, slots, vec, bias, regressed)
            first_pack[kind] = regressed[...].astype(LOW)
            x_copy(kind).start()
        x_copy(2).wait_recv()
        grad[...] = second_pack[...].astype(HIGH)
        block_backward(
            own, grad, temp, low_temp, slots, lead_vec, lead_vec_grad, lead_bias_grad, False, None
        )
        for c in range(crops):
            rest = grad[crop_rows(c), :]
            pick = one_hot(orders, 0, c)
            total = jnp.zeros((PATCHES, D), HIGH)
            for _ in range(3):
                part = rest.astype(LOW)
                rest = rest - part.astype(HIGH)
                total = total + dot_tn(pick, part)
            rows_out[c] = total
        for n in range(2):
            x_copy(n).wait_send()
        feed.drain()

    @pl.when(section == 1)
    def _():
        feed = start.branch()
        slots = slots_of(feed)
        for kind, place_of in enumerate((pos_visible, pos_masked)):
            for c in range(crops):
                pick = one_hot(orders, kind, c)
                place_of[crop_rows(c), :] = sum(dot(pick, pos[t]) for t in (2, 1, 0))
        vectors_in(feed)
        stream[...] = side_vec[12:13, :] + pos_masked[...]
        for m in range(4):
            slots.fetch(m)
        feed.pump("z", 5)
        x_copy(0).wait_recv()
        context[...] = first_pack[0].astype(HIGH) + pos_visible[...]
        block_forward(reg, stream, context, resid, slots, lead_vec, lead_bias, regressed)
        stream[...] = regressed[...] + pos_masked[...]
        block_forward(own, stream, None, resid, Held(slots), side_vec, side_bias, temp)
        for c in range(crops):
            first = c * ROWS
            rows_out[c, 0:MASKED, :] = regressed[first : first + MASKED, :]
            rows_out[c, MASKED : 2 * MASKED, :] = temp[first : first + MASKED, :]
            grad[first : first + ROWS, :] = jnp.zeros((ROWS, D), HIGH)
            grad[first : first + MASKED, :] = cotangent[c].astype(HIGH)
        block_backward(
            own, grad, temp, low_temp, slots, side_vec, dec_vec_grad, dec_bias_grad, False, None
        )
        x_copy(1).wait_recv()
        inside = lax.broadcasted_iota(jnp.int32, (ROWS, D), 0) < MASKED
        for c in range(crops):
            here = crop_rows(c)
            apart = regressed[here, :] - first_pack[1, here, :].astype(HIGH)
            grad[here, :] = grad[here, :] + jnp.where(inside, apart, 0.0)
        block_backward(
            reg, grad, temp, low_temp, slots, lead_vec, lead_vec_grad, lead_bias_grad, True, context
        )
        second_pack[...] = context[...].astype(LOW)
        x_copy(2).start()
        dec_vec_grad[12:13, :] = jnp.sum(grad[...], axis=0, keepdims=True)
        feed.drain()
        x_copy(2).wait_send()


def layer(crops, devices, pieces, patches, orders, pos, cotangent):
    tokens = crops * ROWS
    groups = devices // 4
    inside = [((crops, PATCHES, D), HIGH)] + SMALL_SHAPES * 2
    inside += [save_shape(n, tokens) for n in OUT_DEC + OUT_REG]
    scratch = places_for([save_shape(n, tokens) for n in KEEP_DEC + KEEP_REG])
    scratch += places_for(WEIGHT_SHAPES + SMALL_SHAPES * 2)
    scratch += places_for([((devices, SMALL_ROWS, 128), LOW)])
    scratch += places_for([((tokens, D), HIGH)] * 8)
    scratch += places_for([((tokens, D), LOW), ((2, tokens, D), LOW), ((tokens, D), LOW)])
    scratch += [pltpu.SemaphoreType.DMA(s) for s in ((4,), (), (3,), (3,))]
    scratch += [pltpu.SemaphoreType.DMA((9,))]
    for width in (groups, groups, groups, groups, 2 * groups, 2 * groups):
        scratch.append(pltpu.SemaphoreType.DMA((9, width)))
    wholes = [((devices,) + p.shape, p.dtype) for p in pieces]
    return pl.pallas_call(
        functools.partial(layer_kernel, crops, devices),
        out_shape=specs(wholes + inside),
        in_specs=[ANYWHERE] * 9 + [INSIDE] * 4,
        out_specs=[ANYWHERE] * 9 + [INSIDE] * len(inside),
        scratch_shapes=scratch,
        compiler_params=pltpu.CompilerParams(
            collective_id=1, has_side_effects=True, vmem_limit_bytes=60 << 20
        ),
        name="layer",
    )(*pieces, patches, orders, pos, cotangent)


def lead_weights_kernel(*refs):
    refs = list(refs)
    own, reg = dict(zip(OUT_DEC, refs[:8])), dict(zip(OUT_REG, refs[8:18]))
    outs, scratch, (place_a, place_c, sems) = refs[18:22], refs[22:26], refs[26:]

    def weights_of(pairs, joined):
        for m in (3, 2, 1, 0):
            left, right = PAIRS[m]
            rows = pairs[left].shape[1]
            extra = (pairs["normed_c"], pairs["dkv_c"], place_c) if joined and m == 0 else None
            weight_grad(
                scratch[m], pairs[left], pairs[right], place_a.at[0:rows, :], 0, extra, D
            )
            ship(m, scratch, outs, sems).start()
        for m in range(4):
            ship(m, scratch, outs, sems).wait()

    @pl.when(lax.axis_index("section") == 0)
    def _():
        weights_of(own, False)

    @pl.when(lax.axis_index("section") == 1)
    def _():
        weights_of(reg, True)


def lead_weights(crops, own_pairs, reg_pairs):
    tokens = crops * ROWS
    return pl.pallas_call(
        lead_weights_kernel,
        out_shape=specs(WEIGHT_SHAPES),
        in_specs=[INSIDE] * 18,
        out_specs=[ANYWHERE] * 4,
        scratch_shapes=places_for(WEIGHT_SHAPES + [((FF, tokens), LOW), ((D, tokens), LOW)])
        + [pltpu.SemaphoreType.DMA((4,))],
        compiler_params=params(),
        name="lead_weights",
    )(*own_pairs, *reg_pairs)


def exchange(pieces):
    return [lax.all_gather(p, "dp", axis=0) for p in pieces]


def as_small(parts, rows_of):
    flat = jnp.concatenate([p.reshape(-1) for p in parts])
    block = rows_of * 128
    padded = -(-flat.shape[0] // block) * block
    return jnp.pad(flat, (0, padded - flat.shape[0])).reshape(-1, 128)


def take_flat(flat, shapes):
    taken, offset = [], 0
    for shape in shapes:
        size = 1
        for extent in shape:
            size *= extent
        taken.append(flat[:, offset : offset + size].reshape((-1,) + shape))
        offset += size
    return taken


def spread_columns(gathered):
    return gathered.transpose(1, 0, 2).reshape(gathered.shape[1], -1)


def small_chunks(vectors, bias, chunks):
    rows, columns = vectors.shape
    cut = vectors.reshape(rows, chunks, columns // chunks).transpose(1, 0, 2).reshape(chunks, -1)
    flat = jnp.concatenate([cut, bias.reshape(chunks, -1)], axis=1)
    padded = -(-flat.shape[1] // 1024) * 1024
    return jnp.pad(flat, ((0, 0), (0, padded - flat.shape[1]))).reshape(chunks, -1, 128)


def small_pieces(chunk, rows, chunks):
    flat = chunk.reshape(-1)
    vectors = rows * (D // chunks)
    bias = FF // chunks
    return flat[:vectors].reshape(rows, D // chunks), flat[vectors : vectors + bias]


def total_grads(lead_big, lead_small, dec_big, dec_small, own_path):
    devices = lax.axis_size("dp")
    on_encoder = lax.axis_index("section") == 0
    dec_shapes = [(rows // (2 * devices), columns) for (rows, columns), _ in WEIGHT_SHAPES]
    lead_chunks = [g.reshape(devices, -1, g.shape[1]) for g in lead_big]
    lead_chunks.append(small_chunks(*lead_small, devices))
    dec_chunk_small = small_chunks(*dec_small, 2 * devices)
    if own_path:
        dec_chunks = [
            g.reshape(2, devices, *g.shape[1:])
            if g.ndim == 3
            else g.reshape(2, devices, -1, g.shape[1])
            for g in dec_big
        ]
        dec_chunks.append(dec_chunk_small.reshape((2, devices) + dec_chunk_small.shape[1:]))
        lead_out, dec_out = reduce_all(
            lead_chunks, dec_chunks, dec_shapes + [dec_chunk_small.shape[1:]]
        )
    else:
        dec_chunks = [g.reshape(2, devices, -1, g.shape[1]) for g in dec_big]
        dec_chunks.append(dec_chunk_small.reshape((2, devices) + dec_chunk_small.shape[1:]))
        lead_out = [
            lax.psum_scatter(g.astype(jnp.float32), "dp", scatter_dimension=0) for g in lead_chunks
        ]
        dec_out = []
        for g in dec_chunks:
            mine = jnp.where(on_encoder, jnp.zeros_like(g), g).astype(jnp.float32)
            mine = lax.psum_scatter(mine, "dp", scatter_dimension=1)
            dec_out.append(lax.psum_scatter(mine, "section", scatter_dimension=0))
    lead_vectors, lead_bias = small_pieces(lead_out[4], 12, devices)
    dec_vectors, dec_bias = small_pieces(dec_out[4], 13, 2 * devices)
    return lead_out[:4] + [lead_vectors, lead_bias], dec_out[:4] + [dec_vectors, dec_bias]


def run_fused(crops, devices, patches, cotangent, orders, lead, side, smalls):
    pieces = [pack_small(*smalls)] + lead + side
    outs = layer(crops, devices, pieces, patches, orders, position_parts(), cotangent)
    rows, vec, bias, dec_vec, dec_bias, *pairs = outs[9:]
    own_pairs, reg_pairs = pairs[: len(OUT_DEC)], pairs[len(OUT_DEC) :]
    dec_big = decoder_weights(crops, own_pairs, devices, True)
    lead_big = lead_weights(crops, own_pairs, reg_pairs)
    return rows, lead_big, (vec[:12], bias[0]), dec_big, (dec_vec[:13], dec_bias[0])


def run_apart(crops, devices, patches, cotangent, orders, lead, side, smalls):
    on_encoder = lax.axis_index("section") == 0
    wholes = exchange(lead + side + [as_small(smalls, 16)])
    big = [w.reshape(-1, w.shape[2]) for w in wholes[:8]]
    flat = wholes[8].reshape(devices, -1).astype(jnp.float32)
    lv, lb, sv, sb = take_flat(flat, [p.shape for p in smalls])

    def sixteen(vectors):
        rows = spread_columns(vectors)
        return jnp.pad(rows, ((0, 16 - rows.shape[0]), (0, 0)))

    lead_w, side_w = big[:4], big[4:]
    lead_small = [sixteen(lv), lb.reshape(1, -1)]
    all_small = lead_small + [sixteen(sv), sb.reshape(1, -1)]
    pack, pos_visible, pos_masked, *enc_saved = encode(
        crops, patches, orders, position_parts(), lead_w, side_w, all_small
    )
    arrived = passed_along(pack, "section", 1)
    grad_latents, latent_rows, reg_vec, reg_bias, dec_vec, dec_bias, *pairs = regress(
        crops, arrived, pos_visible, pos_masked, cotangent, lead_w, side_w, all_small
    )
    reg_pairs, dec_pairs = pairs[: len(OUT_REG)], pairs[len(OUT_REG) :]
    returned = passed_along(grad_latents, "section", -1)
    dec_big = decoder_weights(crops, dec_pairs, devices, False)
    *lead_big, grad_rows, enc_vec, enc_bias = finish(
        crops, returned, orders, lead_w, lead_small, enc_saved, reg_pairs
    )
    vec = jnp.where(on_encoder, enc_vec, reg_vec)[:12]
    bias = jnp.where(on_encoder, enc_bias, reg_bias)
    rows = jnp.where(on_encoder, grad_rows, latent_rows)
    return rows, lead_big, (vec, bias[0]), dec_big, (dec_vec[:13], dec_bias[0])


def padded_orders(ordering, part):
    cut = ordering[:, MASKED:] if part == 0 else ordering[:, :MASKED]
    cut = jnp.pad(cut, ((0, 0), (0, ROWS - MASKED)), constant_values=-1)
    return cut.reshape(-1, 1)


def shards(
    patches,
    cotangent,
    ordering,
    lead_qkv,
    lead_proj,
    lead_up,
    lead_down,
    lead_vectors,
    lead_bias,
    side_qkv,
    side_proj,
    side_up,
    side_down,
    side_vectors,
    side_bias,
):
    devices = lax.axis_size("dp")
    crops = patches.shape[0]
    orders = jnp.stack([padded_orders(ordering, 0), padded_orders(ordering, 1)])
    lead = [lead_qkv[0], lead_proj[0], lead_up[0], lead_down[0]]
    side = [side_qkv[0], side_proj[0], side_up[0], side_down[0]]
    smalls = [lead_vectors[0], lead_bias[0], side_vectors[0], side_bias[0]]
    own_path = devices % 4 == 0 and lead[0].shape[0] % 16 == 0
    run = run_fused if own_path else run_apart
    rows, lead_big, lead_small, dec_big, dec_small = run(
        crops, devices, patches, cotangent, orders, lead, side, smalls
    )
    lead_out, dec_out = total_grads(lead_big, lead_small, dec_big, dec_small, own_path)
    return (rows[None],) + tuple(o[None] for o in lead_out) + tuple(dec_out)


def solution(mesh):
    return jax.shard_map(
        shards,
        mesh=mesh,
        in_specs=(
            P("dp", None, None),
            P("dp", None, None),
            P("dp", None),
            P("section", "dp", None),
            P("section", "dp", None),
            P("section", "dp", None),
            P("section", "dp", None),
            P("section", None, "dp"),
            P("section", "dp"),
            P("section", "dp", None),
            P("section", "dp", None),
            P("section", "dp", None),
            P("section", "dp", None),
            P("section", None, "dp"),
            P("section", "dp"),
        ),
        out_specs=(
            P("section", "dp", None, None),
            P("section", "dp", None),
            P("section", "dp", None),
            P("section", "dp", None),
            P("section", "dp", None),
            P("section", None, "dp"),
            P("section", "dp"),
            P(("section", "dp"), None),
            P(("section", "dp"), None),
            P(("section", "dp"), None),
            P(("section", "dp"), None),
            P(None, ("section", "dp")),
            P(("section", "dp")),
        ),
        check_vma=False,
    )
```

```python
import copy
import functools

import jax
import jax.experimental.pallas as pl
import jax.experimental.pallas.tpu as pltpu
import jax.numpy as jnp
import numpy as np
from jax import lax
from jax.sharding import PartitionSpec as P

D = 768
HEADS = 12
HEAD_DIM = 64
FF = 3072
GRID = 14
PATCHES = 196
MASKED = 98


def passed_along(array, axis, by):
    count = lax.axis_size(axis)
    pairs = [(i, i + by) for i in range(count) if 0 <= i + by < count]
    return lax.ppermute(array, axis, pairs)


def positions():
    ids = np.arange(PATCHES)
    quarter = D // 4
    frequency = 10000.0 ** (-np.arange(quarter) / quarter)
    rows = (ids // GRID)[:, None] * frequency
    cols = (ids % GRID)[:, None] * frequency
    return np.concatenate([np.sin(cols), np.cos(cols), np.sin(rows), np.cos(rows)], axis=1)


def position_parts():
    rest = positions().astype(np.float32)
    parts = []
    for _ in range(3):
        part = rest.astype(jnp.bfloat16)
        rest = rest - part.astype(np.float32)
        parts.append(part)
    return jnp.asarray(np.stack(parts))


MESH_ID = pl.DeviceIdType.MESH


def each(count, body):
    if count <= 4:
        for k in range(count):
            body(k)
    else:
        lax.fori_loop(0, count, lambda k, carry: (body(k), carry)[1], 0)


def place():
    section = lax.axis_index("section")
    index = lax.axis_index("dp")
    return section, index, index // 4, (index // 2) % 2, index % 2


def slot(outer, mid, core):
    return outer * 4 + mid * 2 + core


def remote(src, dst, send_sem, recv_sem, device):
    return pltpu.make_async_remote_copy(
        src_ref=src,
        dst_ref=dst,
        send_sem=send_sem,
        recv_sem=recv_sem,
        device_id=device,
        device_id_type=MESH_ID,
    )


def greet(devices):
    barrier = pltpu.get_barrier_semaphore()
    for device in devices:
        pl.semaphore_signal(barrier, inc=1, device_id=device, device_id_type=MESH_ID)


def add_rows(target, at, other, other_at):
    rows = target.shape[-2]
    step = 16 if target.dtype == jnp.bfloat16 else 8

    def body(r, carry):
        where = pl.ds(r * step, step)
        total = target[at, where, :].astype(jnp.float32) + other[other_at, where, :].astype(
            jnp.float32
        )
        target[at, where, :] = total.astype(target.dtype)
        return carry

    lax.fori_loop(0, rows // step, body, 0, unroll=True)


ROWS = 112
LOW = jnp.bfloat16
HIGH = jnp.float32
VISIBLE = PATCHES - MASKED
CHUNK = 32
NAMES_SELF = ("normed", "qkv", "probs", "mixed", "attn", "x1", "r1", "x2", "r2", "second")
NAMES_SELF += ("slope", "hidden", "branch", "x3", "r3")
NAMES_CROSS = ("normed_c", "kv_c", "probs_c", "x1_c", "r1_c")
NAMES_GRAD = ("dqkv", "dattn", "dpre", "dbranch")


def save_shape(name, tokens):
    pairs = tokens // ROWS * (HEADS // 2)
    kinds = {
        "qkv": ((tokens, 3 * D), LOW),
        "kv_c": ((tokens, 2 * D), LOW),
        "dqkv": ((tokens, 3 * D), LOW),
        "dkv_c": ((tokens, 2 * D), LOW),
        "probs": ((pairs, 2 * ROWS, ROWS), HIGH),
        "probs_c": ((pairs, 2 * ROWS, ROWS), HIGH),
        "hidden": ((tokens, FF), LOW),
        "dpre": ((tokens, FF), LOW),
        "slope": ((tokens, FF), HIGH),
    }
    if name in kinds:
        return kinds[name]
    if name in ("r1", "r2", "r3", "r1_c"):
        return ((tokens, 1), HIGH)
    if name in ("attn", "x1", "x1_c", "x2", "x3", "branch"):
        return ((tokens, D), HIGH)
    return ((tokens, D), LOW)


def dot(left, right):
    return jnp.dot(left, right, preferred_element_type=HIGH)


def dot_nt(left, right):
    return lax.dot_general(left, right, (((1,), (1,)), ((), ())), preferred_element_type=HIGH)


def dot_tn(left, right):
    return lax.dot_general(left, right, (((0,), (0,)), ((), ())), preferred_element_type=HIGH)


def by_rows(tokens, body, init=()):
    def step(i, carry):
        return body(pl.ds(pl.multiple_of(i * CHUNK, CHUNK), CHUNK), carry)

    return lax.fori_loop(0, tokens // CHUNK, step, init, unroll=True)


def tiles(width, body, size=256, unroll=True):
    def step(i, carry):
        body(pl.ds(pl.multiple_of(i * size, size), size))
        return carry

    lax.fori_loop(0, width // size, step, 0, unroll=unroll)


def fold(values):
    return jnp.sum(values.reshape(-1, 8, values.shape[-1]), axis=0)


def norm_forward(source, gain, shift, kept, spread, low, out=None):
    def body(where, carry):
        values = source[where, :]
        center = values - jnp.mean(values, axis=-1, keepdims=True)
        scale = lax.rsqrt(jnp.mean(center * center, axis=-1, keepdims=True) + 1e-06)
        center = center * scale
        if kept is not None:
            kept[where, :] = center
            spread[where, :] = scale
        result = center * gain + shift
        if low is not None:
            low[where, :] = result.astype(LOW)
        if out is not None:
            out[where, :] = result
        return carry

    by_rows(source.shape[0], body)


def norm_grad(grad, gain, center, scale):
    weighted = grad * gain
    first = jnp.mean(weighted, axis=-1, keepdims=True)
    second = jnp.mean(weighted * center, axis=-1, keepdims=True)
    return scale * (weighted - first - center * second)


def pair_masks(rows):
    lane = lax.broadcasted_iota(jnp.int32, (rows, 2 * HEAD_DIM), 1)
    return lane < HEAD_DIM


def two_heads(values):
    low_lanes = pair_masks(values.shape[0])
    zero = jnp.zeros_like(values)
    return jnp.concatenate(
        [jnp.where(low_lanes, values, zero), jnp.where(low_lanes, zero, values)], axis=0
    )


def one_pair(stacked):
    half = stacked.shape[0] // 2
    return jnp.where(pair_masks(half), stacked[:half], stacked[half:])


def head_loop(tokens, body):
    def step(p, carry):
        for crop in range(tokens // ROWS):
            rows = pl.ds(crop * ROWS, ROWS)
            body(crop * (HEADS // 2) + p, rows, p)
        return carry

    lax.fori_loop(0, HEADS // 2, step, 0, unroll=True)


def lanes_of(p, base):
    return pl.ds(pl.multiple_of(base + p * 128, 128), 128)


def attention(s, cross):
    tokens = s["normed"].shape[0]
    valid = lax.broadcasted_iota(jnp.int32, (2 * ROWS, ROWS), 1) < MASKED

    def body(at, rows, p):
        q2 = two_heads(s["qkv"][rows, lanes_of(p, 0)])
        sources = [(s["qkv"][rows, lanes_of(p, D)], s["qkv"][rows, lanes_of(p, 2 * D)], "probs")]
        if cross:
            sources.append(
                (s["kv_c"][rows, lanes_of(p, 0)], s["kv_c"][rows, lanes_of(p, D)], "probs_c")
            )
        scores = [
            jnp.where(valid, dot_nt(q2, k) * HEAD_DIM ** (-0.5), -1e30) for k, _, _ in sources
        ]
        top = jnp.max(scores[0], axis=-1, keepdims=True)
        if cross:
            top = jnp.maximum(top, jnp.max(scores[1], axis=-1, keepdims=True))
        powers = [jnp.exp(x - top) for x in scores]
        mass = jnp.sum(powers[0], axis=-1, keepdims=True)
        if cross:
            mass = mass + jnp.sum(powers[1], axis=-1, keepdims=True)
        mixed = None
        inverse = 1.0 / mass
        for power, (_, v, name) in zip(powers, sources):
            probs = power * inverse
            if name in s:
                s[name][at] = probs
            part = dot(probs.astype(LOW), v)
            mixed = part if mixed is None else mixed + part
        s["mixed"][rows, lanes_of(p, 0)] = one_pair(mixed).astype(LOW)

    head_loop(tokens, body)


def block_forward(s, stream, context, resid, weights, vectors, bias, out):
    def row(r, where=slice(None)):
        return vectors[r : r + 1, where]

    norm_forward(stream, row(0), row(1), s.get("x1"), s.get("r1"), s["normed"])
    if context is not None:
        norm_forward(context, row(0), row(1), s["x1_c"], s["r1_c"], s["normed_c"])
    w = weights.open(0)

    def qkv_tile(j):
        where = slice(j * 256, j * 256 + 256)
        kind, local = divmod(j, 3)
        extra = None if kind == 1 else row(6 if kind == 0 else 7, slice(local * 256, local * 256 + 256))
        values = dot(s["normed"][...], w[:, where])
        s["qkv"][:, where] = (values if extra is None else values + extra).astype(LOW)
        if context is not None and kind > 0:
            values = dot(s["normed_c"][...], w[:, where])
            here = slice(j * 256 - D, j * 256 - D + 256)
            s["kv_c"][:, here] = (values if extra is None else values + extra).astype(LOW)

    for j in range(9):
        qkv_tile(j)
    weights.close(0)
    attention(s, context is not None)
    w = weights.open(1)
    for j in range(3):
        where = slice(j * 256, j * 256 + 256)
        attn = dot(s["mixed"][...], w[:, where]) + row(8, where)
        if "attn" in s:
            s["attn"][:, where] = attn
        resid[:, where] = stream[:, where] + row(10, where) * attn
    weights.close(1)
    norm_forward(resid, row(2), row(3), s.get("x2"), s.get("r2"), s["second"])
    w = weights.open(2)

    def up_tile(where):
        pre = dot(s["second"][...], w[:, where]) + bias[0:1, where]
        phi = 0.5 + 0.5 * lax.erf(pre * 0.5**0.5)
        s["hidden"][:, where] = (pre * phi).astype(LOW)
        if "slope" in s:
            s["slope"][:, where] = phi + pre * jnp.exp(-0.5 * pre * pre) * 0.3989422804014327

    tiles(FF, up_tile)
    weights.close(2)
    w = weights.open(3)
    for j in range(3):
        where = slice(j * 256, j * 256 + 256)
        branch = dot(s["hidden"][...], w[:, where]) + row(9, where)
        if "branch" in s:
            s["branch"][:, where] = branch
        resid[:, where] = resid[:, where] + row(11, where) * branch
    weights.close(3)
    norm_forward(resid, row(4), row(5), s.get("x3"), s.get("r3"), None, out)


def attention_backward(s, grad_mixed, cross):
    tokens = s["normed"].shape[0]
    scale = HEAD_DIM ** (-0.5)

    def body(at, rows, p):
        q2 = two_heads(s["qkv"][rows, lanes_of(p, 0)])
        g2 = two_heads(grad_mixed[rows, lanes_of(p, 0)])
        sources = [("qkv", D, "dqkv", "probs")]
        if cross:
            sources.append(("kv_c", 0, "dkv_c", "probs_c"))
        parts = []
        inner = None
        for name, base, grad_name, probs_name in sources:
            v = s[name][rows, lanes_of(p, base + D)]
            probs = s[probs_name][at]
            s[grad_name][rows, lanes_of(p, base + D)] = dot_tn(probs.astype(LOW), g2).astype(LOW)
            dprobs = dot_nt(g2, v)
            parts.append((probs, dprobs))
            total = jnp.sum(dprobs * probs, axis=-1, keepdims=True)
            inner = total if inner is None else inner + total
        dq = None
        for (probs, dprobs), (name, base, grad_name, _) in zip(parts, sources):
            dscores = (probs * (dprobs - inner)).astype(LOW)
            part = dot(dscores, s[name][rows, lanes_of(p, base)])
            dq = part if dq is None else dq + part
            s[grad_name][rows, lanes_of(p, base)] = (dot_tn(dscores, q2) * scale).astype(LOW)
        s["dqkv"][rows, lanes_of(p, 0)] = (one_pair(dq) * scale).astype(LOW)

    head_loop(tokens, body)


def block_backward(s, grad, temp, low_temp, weights, vectors, vec_grad, bias_grad, cross, context_grad):
    tokens = grad.shape[0]
    zero = jnp.zeros((8, D), HIGH)

    def row(r):
        return vectors[r : r + 1, :]

    def put(r, total):
        vec_grad[r : r + 1, :] = jnp.sum(total, axis=0, keepdims=True)

    def final_rows(where, sums):
        gain, shift, scale, offset = sums
        g = grad[where, :]
        center = s["x3"][where, :]
        gf = norm_grad(g, row(4), center, s["r3"][where, :])
        grad[where, :] = gf
        low = (row(11) * gf).astype(LOW)
        s["dbranch"][where, :] = low
        return (
            gain + fold(g * center),
            shift + fold(g),
            scale + fold(gf * s["branch"][where, :]),
            offset + fold(low.astype(HIGH)),
        )

    sums = by_rows(tokens, final_rows, (zero,) * 4)
    for r, total in zip((4, 5, 11, 9), sums):
        put(r, total)
    w = weights.open(3)

    def down_tile(where):
        low = (dot_nt(s["dbranch"][...], w[where, :]) * s["slope"][:, where]).astype(LOW)
        s["dpre"][:, where] = low
        bias_grad[0:1, where] = jnp.sum(low.astype(HIGH), axis=0, keepdims=True)

    tiles(FF, down_tile)
    weights.close(3)
    w = weights.open(2)
    for j in range(3):
        where = slice(j * 256, j * 256 + 256)
        temp[:, where] = dot_nt(s["dpre"][...], w[where, :])
    weights.close(2)

    def second_rows(where, sums):
        gain, shift, scale, offset = sums
        g = temp[where, :]
        center = s["x2"][where, :]
        gr = norm_grad(g, row(2), center, s["r2"][where, :]) + grad[where, :]
        grad[where, :] = gr
        low = (row(10) * gr).astype(LOW)
        s["dattn"][where, :] = low
        return (
            gain + fold(g * center),
            shift + fold(g),
            scale + fold(gr * s["attn"][where, :]),
            offset + fold(low.astype(HIGH)),
        )

    sums = by_rows(tokens, second_rows, (zero,) * 4)
    for r, total in zip((2, 3, 10, 8), sums):
        put(r, total)
    w = weights.open(1)
    for j in range(3):
        where = slice(j * 256, j * 256 + 256)
        low_temp[:, where] = dot_nt(s["dattn"][...], w[where, :]).astype(LOW)
    weights.close(1)
    attention_backward(s, low_temp, cross)
    w = weights.open(0)
    for j in range(3):
        where = slice(j * 256, j * 256 + 256)
        temp[:, where] = dot_nt(s["dqkv"][...], w[where, :])
        if cross:
            context_grad[:, where] = dot_nt(s["dkv_c"][...], w[where, D:])
    weights.close(0)

    def first_rows(where, sums):
        gain, shift, dq, dv = sums
        g = temp[where, :]
        center = s["x1"][where, :]
        grad[where, :] = grad[where, :] + norm_grad(g, row(0), center, s["r1"][where, :])
        gain, shift = gain + fold(g * center), shift + fold(g)
        dq = dq + fold(s["dqkv"][where, 0:D].astype(HIGH))
        dv = dv + fold(s["dqkv"][where, 2 * D :].astype(HIGH))
        if cross:
            g = context_grad[where, :]
            center = s["x1_c"][where, :]
            context_grad[where, :] = norm_grad(g, row(0), center, s["r1_c"][where, :])
            gain, shift = gain + fold(g * center), shift + fold(g)
            dv = dv + fold(s["dkv_c"][where, D:].astype(HIGH))
        return gain, shift, dq, dv

    sums = by_rows(tokens, first_rows, (zero,) * 4)
    for r, total in zip((0, 1, 6, 7), sums):
        put(r, total)


class Slots:
    def __init__(self, places, sems):
        self.places, self.sems = places, sems
        self.queue = [[] for _ in places]
        self.ready = [False] * len(places)

    def copy(self, m, source):
        return pltpu.make_async_copy(source, self.places[m], self.sems.at[m])

    def plan(self, m, source):
        self.queue[m].append(source)
        if len(self.queue[m]) == 1:
            self.copy(m, source).start()

    def open(self, m):
        if not self.ready[m]:
            self.copy(m, self.queue[m][0]).wait()
            self.ready[m] = True
        return self.places[m]

    def close(self, m):
        self.queue[m].pop(0)
        self.ready[m] = False
        if self.queue[m]:
            self.copy(m, self.queue[m][0]).start()


class Held:
    def __init__(self, slots):
        self.slots = slots

    def open(self, m):
        return self.slots.open(m)

    def close(self, m):
        pass


def transposed(place, source):
    width = source.shape[1]
    for j in range(width // 256):
        where = slice(j * 256, j * 256 + 256)
        place[where, :] = source[:, where].T


def weight_grad(out, left, right, place, stacked=0, extra=None, base=0):
    rows, columns = left.shape[1], right.shape[1]
    transposed(place, left)
    if extra is not None:
        transposed(extra[2], extra[0])

    def column_tile(j, with_extra):
        where = pl.ds(pl.multiple_of(j * 256, 256), 256)
        for i in range(rows // 384):
            down = slice(i * 384, i * 384 + 384)
            total = dot(place[down, :], right[:, where])
            if with_extra:
                there = pl.ds(pl.multiple_of(j * 256 - base, 256), 256)
                total = total + dot(extra[2][down, :], extra[1][:, there])
            if stacked:
                count = 384 // stacked
                cut = total.reshape(count, stacked, 256)
                both = jnp.concatenate([cut[:, :, :128], cut[:, :, 128:]], axis=1)
                here = pl.ds(pl.multiple_of(j * 128, 128), 128)
                out[i * count : (i + 1) * count, :, here] = both.astype(LOW)
            else:
                out[down, where] = total.astype(LOW)

    def plain(j, carry):
        column_tile(j, False)
        return carry

    def joined(j, carry):
        column_tile(j, True)
        return carry

    first = base // 256 if extra is not None else columns // 256
    lax.fori_loop(0, first, plain, 0, unroll=True)
    if extra is not None:
        lax.fori_loop(first, columns // 256, joined, 0, unroll=True)


def crop_rows(c):
    return slice(c * ROWS, c * ROWS + ROWS)


def one_hot(orders, kind, crop):
    ids = orders[kind, crop_rows(crop), :]
    return (ids == lax.broadcasted_iota(jnp.int32, (ROWS, PATCHES), 1)).astype(LOW)


def encode_kernel(crops, *refs):
    refs = list(refs)
    patches, orders, pos = refs[:3]
    lead_w, side_w = refs[3:7], refs[7:11]
    lead_vec, lead_bias, side_vec, side_bias = refs[11:15]
    pack, pos_visible, pos_masked = refs[15:18]
    refs = refs[18:]
    saved = dict(zip(NAMES_SELF, refs))
    refs = refs[len(NAMES_SELF) :]
    places, (sems, stream, resid, latent) = refs[:4], refs[4:8]
    brief = dict(zip(("normed", "qkv", "mixed", "second", "hidden"), refs[8:13]))
    section = lax.axis_index("section")

    @pl.when(section == 0)
    def _():
        slots = Slots(places, sems)
        for source in (lead_w, side_w):
            for m in range(4):
                slots.plan(m, source[m])
        for kind in range(2):
            for c in range(crops):
                rows = dot(one_hot(orders, kind, c), patches[c])
                stream[crop_rows(c), :] = rows
            if kind == 0:
                block_forward(saved, stream, None, resid, slots, lead_vec, lead_bias, latent)
            else:
                block_forward(brief, stream, None, resid, slots, side_vec, side_bias, latent)
            pack[kind] = latent[...].astype(LOW)

    @pl.when(section == 1)
    def _():
        for kind, place_of in enumerate((pos_visible, pos_masked)):
            for c in range(crops):
                pick = one_hot(orders, kind, c)
                place_of[crop_rows(c), :] = sum(dot(pick, pos[t]) for t in (2, 1, 0))


def regress_kernel(crops, *refs):
    refs = list(refs)
    pack, pos_visible, pos_masked, cotangent = refs[:4]
    lead_w, side_w = refs[4:8], refs[8:12]
    lead_vec, lead_bias, side_vec, side_bias = refs[12:16]
    refs = refs[16:]

    def grab(names):
        taken = dict(zip(names, refs))
        del refs[: len(names)]
        return taken

    grad_latents, rows_out, reg_vec, reg_bias, dec_vec, dec_bias = refs[:6]
    del refs[:6]
    reg, dec = grab(OUT_REG), grab(OUT_DEC)
    reg.update(grab(KEEP_REG))
    dec.update(grab(KEEP_DEC))
    places = refs[:4]
    sems, stream, context, resid, regressed, grad, temp, low_temp = refs[4:]
    tokens = crops * ROWS

    @pl.when(lax.axis_index("section") == 1)
    def _():
        slots = Slots(places, sems)
        for source in (lead_w, side_w, lead_w):
            for m in range(4):
                slots.plan(m, source[m])
        stream[...] = side_vec[12:13, :] + pos_masked[...]
        context[...] = pack[0].astype(HIGH) + pos_visible[...]
        block_forward(reg, stream, context, resid, slots, lead_vec, lead_bias, regressed)
        stream[...] = regressed[...] + pos_masked[...]
        block_forward(dec, stream, None, resid, Held(slots), side_vec, side_bias, temp)
        for c in range(crops):
            first = c * ROWS
            rows_out[c, 0:MASKED, :] = regressed[first : first + MASKED, :]
            rows_out[c, MASKED : 2 * MASKED, :] = temp[first : first + MASKED, :]
            grad[first : first + ROWS, :] = jnp.zeros((ROWS, D), HIGH)
            grad[first : first + MASKED, :] = cotangent[c].astype(HIGH)
        block_backward(
            dec, grad, temp, low_temp, slots, side_vec, dec_vec, dec_bias, False, None
        )
        inside = lax.broadcasted_iota(jnp.int32, (ROWS, D), 0) < MASKED
        for c in range(crops):
            here = crop_rows(c)
            apart = regressed[here, :] - pack[1, here, :].astype(HIGH)
            grad[here, :] = grad[here, :] + jnp.where(inside, apart, 0.0)
        block_backward(
            reg, grad, temp, low_temp, slots, lead_vec, reg_vec, reg_bias, True, context
        )
        dec_vec[12:13, :] = jnp.sum(grad[...], axis=0, keepdims=True)
        grad_latents[...] = context[...].astype(LOW)


PAIRS = (("normed", "dqkv"), ("mixed", "dattn"), ("second", "dpre"), ("hidden", "dbranch"))
OUT_DEC = tuple(n for pair in PAIRS for n in pair)
OUT_REG = OUT_DEC + ("normed_c", "dkv_c")
KEEP_DEC = tuple(n for n in NAMES_SELF if n not in OUT_DEC)
KEEP_REG = KEEP_DEC + tuple(n for n in NAMES_CROSS if n not in OUT_REG)


def ship(m, scratch, outs, sems):
    return pltpu.make_async_copy(scratch[m], outs[m], sems.at[m])


def decoder_weights_kernel(stacks, *refs):
    pairs, outs = dict(zip(OUT_DEC, refs[:8])), refs[8:12]
    scratch, (place, sems) = refs[12:16], refs[16:]

    @pl.when(lax.axis_index("section") == 1)
    def _():
        for m in (3, 2, 1, 0):
            left, right = PAIRS[m]
            rows = pairs[left].shape[1]
            weight_grad(
                scratch[m], pairs[left], pairs[right], place.at[0:rows, :], stacks[m]
            )
            ship(m, scratch, outs, sems).start()
        for m in range(4):
            ship(m, scratch, outs, sems).wait()


def finish_kernel(crops, *refs):
    refs = list(refs)
    returned, orders = refs[:2]
    lead_w, lead_vec, lead_bias = refs[2:6], refs[6], refs[7]
    del refs[:8]

    def grab(names):
        taken = dict(zip(names, refs))
        del refs[: len(names)]
        return taken

    enc, reg = grab(NAMES_SELF), grab(OUT_REG)
    outs, (rows_out, enc_vec, enc_bias) = refs[:4], refs[4:7]
    del refs[:7]
    enc.update(grab(NAMES_GRAD))
    places = refs[:4]
    scratch = refs[4:8]
    sems, out_sems, place, place_c, grad, temp, low_temp = refs[8:]
    section = lax.axis_index("section")

    def weights_of(pairs, joined):
        for m in (3, 2, 1, 0):
            left, right = PAIRS[m]
            rows = pairs[left].shape[1]
            extra = (pairs["normed_c"], pairs["dkv_c"], place_c) if joined and m == 0 else None
            weight_grad(
                scratch[m], pairs[left], pairs[right], place.at[0:rows, :], 0, extra, D
            )
            ship(m, scratch, outs, out_sems).start()
        for m in range(4):
            ship(m, scratch, outs, out_sems).wait()

    @pl.when(section == 0)
    def _():
        slots = Slots(places, sems)
        for m in (3, 2, 1, 0):
            slots.plan(m, lead_w[m])
        grad[...] = returned[...].astype(HIGH)
        block_backward(enc, grad, temp, low_temp, slots, lead_vec, enc_vec, enc_bias, False, None)
        for c in range(crops):
            rest = grad[crop_rows(c), :]
            pick = one_hot(orders, 0, c)
            total = jnp.zeros((PATCHES, D), HIGH)
            for _ in range(3):
                part = rest.astype(LOW)
                rest = rest - part.astype(HIGH)
                total = total + dot_tn(pick, part)
            rows_out[c] = total
        weights_of(enc, False)

    @pl.when(section == 1)
    def _():
        weights_of(reg, True)


ANYWHERE = pl.BlockSpec(memory_space=pl.ANY)
INSIDE = pl.BlockSpec(memory_space=pltpu.VMEM)


def specs(shapes):
    return [jax.ShapeDtypeStruct(s, d) for s, d in shapes]


def places_for(shapes):
    return [pltpu.VMEM(s, d) for s, d in shapes]


def params():
    return pltpu.CompilerParams(vmem_limit_bytes=60 << 20)


WEIGHT_SHAPES = [((D, 3 * D), LOW), ((D, D), LOW), ((D, FF), LOW), ((FF, D), LOW)]
SMALL_SHAPES = [((16, D), HIGH), ((1, FF), HIGH)]


def encode(crops, patches, orders, pos, lead_w, side_w, smalls):
    tokens = crops * ROWS
    shapes = [((2, tokens, D), LOW), ((tokens, D), HIGH), ((tokens, D), HIGH)]
    shapes += [save_shape(n, tokens) for n in NAMES_SELF]
    scratch = places_for(WEIGHT_SHAPES) + [pltpu.SemaphoreType.DMA((4,))]
    scratch += places_for([((tokens, D), HIGH)] * 3)
    scratch += places_for(
        [save_shape(n, tokens) for n in ("normed", "qkv", "mixed", "second", "hidden")]
    )
    return pl.pallas_call(
        functools.partial(encode_kernel, crops),
        out_shape=specs(shapes),
        in_specs=[INSIDE] * 3 + [ANYWHERE] * 8 + [INSIDE] * 4,
        out_specs=[INSIDE] * len(shapes),
        scratch_shapes=scratch,
        compiler_params=params(),
        name="encode",
    )(patches, orders, pos, *lead_w, *side_w, *smalls)


def regress(crops, pack, pos_visible, pos_masked, cotangent, lead_w, side_w, smalls):
    tokens = crops * ROWS
    shapes = [((tokens, D), LOW), ((crops, PATCHES, D), HIGH)] + SMALL_SHAPES * 2
    shapes += [save_shape(n, tokens) for n in OUT_REG + OUT_DEC]
    scratch = places_for([save_shape(n, tokens) for n in KEEP_REG + KEEP_DEC])
    scratch += places_for(WEIGHT_SHAPES) + [pltpu.SemaphoreType.DMA((4,))]
    scratch += places_for([((tokens, D), HIGH)] * 6 + [((tokens, D), LOW)])
    return pl.pallas_call(
        functools.partial(regress_kernel, crops),
        out_shape=specs(shapes),
        in_specs=[INSIDE] * 4 + [ANYWHERE] * 8 + [INSIDE] * 4,
        out_specs=[INSIDE] * len(shapes),
        scratch_shapes=scratch,
        compiler_params=params(),
        name="regress",
    )(pack, pos_visible, pos_masked, cotangent, *lead_w, *side_w, *smalls)


def dec_grad_shapes(devices, own_path):
    shapes, stacks = [], []
    for (rows, columns), kind in WEIGHT_SHAPES:
        r = rows // (2 * devices)
        stack = r if own_path and r % 16 else 0
        stacks.append(stack)
        shapes.append(
            ((2 * devices, 2 * r, columns // 2), kind) if stack else ((rows, columns), kind)
        )
    return shapes, tuple(stacks)


def decoder_weights(crops, pairs, devices, own_path):
    shapes, stacks = dec_grad_shapes(devices, own_path)
    return pl.pallas_call(
        functools.partial(decoder_weights_kernel, stacks),
        out_shape=specs(shapes),
        in_specs=[INSIDE] * 8,
        out_specs=[ANYWHERE] * 4,
        scratch_shapes=places_for(shapes)
        + places_for([((FF, crops * ROWS), LOW)])
        + [pltpu.SemaphoreType.DMA((4,))],
        compiler_params=params(),
        name="decoder_weights",
    )(*pairs)


def finish(crops, returned, orders, lead_w, lead_small, enc_saved, reg_pairs):
    tokens = crops * ROWS
    shapes = WEIGHT_SHAPES + [((crops, PATCHES, D), HIGH)] + SMALL_SHAPES
    scratch = places_for([save_shape(n, tokens) for n in NAMES_GRAD])
    scratch += places_for(WEIGHT_SHAPES * 2) + [pltpu.SemaphoreType.DMA((4,))] * 2
    scratch += places_for([((FF, tokens), LOW), ((D, tokens), LOW)])
    scratch += places_for([((tokens, D), HIGH)] * 2 + [((tokens, D), LOW)])
    count = len(enc_saved) + len(reg_pairs)
    return pl.pallas_call(
        functools.partial(finish_kernel, crops),
        out_shape=specs(shapes),
        in_specs=[INSIDE] * 2 + [ANYWHERE] * 4 + [INSIDE] * (2 + count),
        out_specs=[ANYWHERE] * 4 + [INSIDE] * 3,
        scratch_shapes=scratch,
        compiler_params=params(),
        name="finish",
    )(returned, orders, *lead_w, *lead_small, *enc_saved, *reg_pairs)


SMALL_ROWS = 48


class Feed:
    WINDOW = 3

    def __init__(self, groups, shards_in, wholes, sems):
        self.groups, self.shards, self.wholes = groups, shards_in, wholes
        self.own, self.us, self.ur, self.ds, self.dr, self.ys, self.yr, self.cs, self.cr = sems
        self.count = len(shards_in)
        self.section, self.index, self.outer, self.mid, self.core = place()
        self.begun = self.at = 0
        self.done = set()
        self.steps = [("z", 0), ("y", 0), ("z", 1)]
        for m in range(2, self.count):
            self.steps += [("z", m), ("y", m - 1)]
        self.steps.append(("y", self.count - 1))

    def branch(self):
        other = copy.copy(self)
        other.done = set(self.done)
        return other

    def devices(self):
        mid = (self.section, slot(self.outer, 1 - self.mid, self.core))
        core = (self.section, slot(self.outer, self.mid, 1 - self.core))
        return mid, core

    def outer_device(self, k):
        return (self.section, slot((self.outer + k) % self.groups, self.mid, self.core))

    def origin(self, k, far=0, other_core=False):
        outer = (self.outer - k + self.groups) % self.groups
        mid = 1 - self.mid if far else self.mid
        return slot(outer, mid, 1 - self.core if other_core else self.core)

    def own_copy(self, m):
        return pltpu.make_async_copy(
            self.shards[m], self.wholes[m].at[self.index], self.own.at[m]
        )

    def up_copy(self, m, k):
        piece = self.wholes[m].at[self.origin(k)]
        src = self.shards[m] if isinstance(k, int) and k == 0 else piece
        return remote(src, piece, self.us.at[m, k], self.ur.at[m, k], self.outer_device(1))

    def down_copy(self, m, k):
        piece = self.wholes[m].at[self.origin(k)]
        src = self.shards[m] if isinstance(k, int) and k == 0 else piece
        below = self.outer_device(self.groups - 1)
        return remote(src, piece, self.ds.at[m, k], self.dr.at[m, k], below)

    def up_arrival(self, m, k):
        piece = self.wholes[m].at[self.origin(k)]
        return remote(
            piece, piece, self.us.at[m, k - 1], self.ur.at[m, k - 1], self.outer_device(1)
        )

    def down_arrival(self, m, distance):
        k = (self.groups - distance) % self.groups
        piece = self.wholes[m].at[self.origin(k)]
        at = (self.groups - distance + 1) % self.groups
        return remote(piece, piece, self.ds.at[m, at], self.dr.at[m, at], self.outer_device(1))

    def y_copy(self, m, k, own=False, arrival=False):
        piece = self.wholes[m].at[self.origin(k, far=1 if arrival else 0)]
        src = self.shards[m] if own else piece
        return remote(src, piece, self.ys.at[m, k], self.yr.at[m, k], self.devices()[0])

    def c_copy(self, m, k, far, own=False, arrival=False):
        piece = self.wholes[m].at[self.origin(k, far, arrival)]
        src = self.shards[m] if own else piece
        at = k * 2 + far
        return remote(src, piece, self.cs.at[m, at], self.cr.at[m, at], self.devices()[1])

    def begin(self, upto):
        while self.begun < min(upto, self.count):
            m = self.begun

            @pl.when(self.outer < self.groups - 1)
            def _():
                self.up_copy(m, 0).start()

            @pl.when(self.outer > 0)
            def _():
                self.down_copy(m, 0).start()

            self.y_copy(m, 0, own=True).start()
            self.c_copy(m, 0, 0, own=True).start()
            self.own_copy(m).start()
            self.begun += 1

    def step(self):
        kind, m = self.steps[self.at]
        self.at += 1
        if kind == "z":

            top = self.groups - 1

            def spread(k):
                self.y_copy(m, k).start()
                self.c_copy(m, k, 0).start()

            def pass_on(before):
                distance = before + 1

                @pl.when(self.outer >= distance)
                def _():
                    self.up_arrival(m, distance).wait_recv()

                    @pl.when(self.outer < top)
                    def _():
                        self.up_copy(m, distance).start()

                    spread(distance)

                @pl.when(self.outer + distance <= top)
                def _():
                    self.down_arrival(m, distance).wait_recv()

                    @pl.when(self.outer > 0)
                    def _():
                        self.down_copy(m, self.groups - distance).start()

                    spread(self.groups - distance)

            each(top, pass_on)
            self.begin(m + 1 + self.WINDOW)
        else:

            def hand_over(k):
                self.y_copy(m, k, arrival=True).wait_recv()
                self.c_copy(m, k, 1).start()

            each(self.groups, hand_over)

    def pump(self, kind, m):
        while (kind, m) in self.steps[self.at :]:
            self.step()

    def need(self, m):
        self.pump("y", m)
        if m in self.done:
            return
        self.done.add(m)

        def last(k):
            for far in range(2):
                self.c_copy(m, k, far, arrival=True).wait_recv()

        each(self.groups, last)
        self.own_copy(m).wait()

    def drain(self):
        for m in range(self.count):
            self.need(m)
            top = self.groups - 1

            def line_sends(k):
                @pl.when((self.outer < top) & (self.outer >= k))
                def _():
                    self.up_copy(m, k).wait_send()

                @pl.when((self.outer > 0) & (self.outer + k <= top))
                def _():
                    self.down_copy(m, (self.groups - k) % self.groups).wait_send()

            each(self.groups, line_sends)

            def finish_sends(k):
                self.y_copy(m, k).wait_send()
                for far in range(2):
                    self.c_copy(m, k, far).wait_send()

            each(self.groups, finish_sends)


class FedSlots(Slots):
    def __init__(self, places, sems, feed):
        super().__init__(places, sems)
        self.feed = feed
        self.started = [False] * len(places)

    def plan(self, m, piece):
        self.queue[m].append(piece)

    def fetch(self, m):
        if not self.started[m] and self.queue[m]:
            piece = self.queue[m][0]
            self.feed.need(piece)
            self.copy(m, self.feed.flat[piece]).start()
            self.started[m] = True

    def open(self, m):
        self.fetch(m)
        if not self.ready[m]:
            self.copy(m, self.feed.flat[self.queue[m][0]]).wait()
            self.ready[m] = True
        return self.places[m]

    def close(self, m):
        self.queue[m].pop(0)
        self.ready[m] = self.started[m] = False
        if self.queue[m] and self.queue[m][0] in self.feed.done:
            self.fetch(m)


def unpack_small(small, devices, lead_vec, lead_bias, side_vec, side_bias):
    width = D // devices
    per = FF // devices // width
    for d in range(devices):
        lanes = slice(d * width, d * width + width)
        block = small[d].astype(HIGH)
        lead_vec[0:16, lanes] = block[0:16, 0:width]
        side_vec[0:16, lanes] = block[16:32, 0:width]
        for i in range(per):
            first = (d * per + i) * width
            lead_bias[0:1, first : first + width] = block[32 + i : 33 + i, 0:width]
            side_bias[0:1, first : first + width] = block[40 + i : 41 + i, 0:width]


def pack_small(lead_vectors, lead_bias, side_vectors, side_bias):
    width = lead_vectors.shape[1]

    def block(rows, height):
        rows = rows.reshape(-1, width)
        return jnp.pad(rows, ((0, height - rows.shape[0]), (0, 128 - width)))

    return jnp.concatenate(
        [block(lead_vectors, 16), block(side_vectors, 16), block(lead_bias, 8), block(side_bias, 8)]
    )


def layer_kernel(crops, devices, *refs):
    refs = list(refs)

    def grab(n):
        taken = refs[:n]
        del refs[:n]
        return taken

    def named(names):
        return dict(zip(names, grab(len(names))))

    shards_in = grab(9)
    patches, orders, pos, cotangent = grab(4)
    wholes = grab(9)
    rows_out, lead_small_out, dec_small_out = grab(3)
    own, reg = named(OUT_DEC), named(OUT_REG)
    own.update(named(KEEP_DEC))
    reg.update(named(KEEP_REG))
    places = grab(4)
    lead_vec_grad, lead_bias_grad, dec_vec_grad, dec_bias_grad = grab(4)
    lead_vec, lead_bias, side_vec, side_bias, small = grab(5)
    stream, context, resid, regressed, grad, temp, pos_visible, pos_masked = grab(8)
    low_temp, first_pack, second_pack = grab(3)
    sems, small_sem, x_send, x_recv = grab(4)
    groups = devices // 4
    feed = Feed(groups, shards_in, wholes, refs)
    feed.flat = [None] + [
        w.reshape(devices * w.shape[1], w.shape[2]) for w in wholes[1:]
    ]
    section = feed.section
    tokens = crops * ROWS
    x_device = (1 - section, feed.index)
    greet([*feed.devices(), x_device])
    barrier = pltpu.get_barrier_semaphore()
    each(
        groups - 1,
        lambda k: pl.semaphore_signal(
            barrier, inc=1, device_id=feed.outer_device(k + 1), device_id_type=MESH_ID
        ),
    )
    pl.semaphore_wait(barrier, groups + 2)
    feed.begin(Feed.WINDOW)

    def x_copy(n):
        piece = (first_pack.at[0], first_pack.at[1], second_pack)[n]
        return remote(piece, piece, x_send.at[n], x_recv.at[n], x_device)

    def vectors_in(feed):
        feed.need(0)
        fetched = pltpu.make_async_copy(wholes[0], small, small_sem)
        fetched.start()
        fetched.wait()
        unpack_small(small, devices, lead_vec, lead_bias, side_vec, side_bias)

    def slots_of(feed):
        slots = FedSlots(places, sems, feed)
        for base in (1, 5, 1):
            for m in range(4):
                slots.plan(m, base + m)
        return slots

    start = feed

    @pl.when(section == 0)
    def _():
        feed = start.branch()
        slots = slots_of(feed)
        for kind, vec, bias, keep in ((0, lead_vec, lead_bias, own), (1, side_vec, side_bias, reg)):
            for c in range(crops):
                stream[crop_rows(c), :] = dot(one_hot(orders, kind, c), patches[c])
            if kind == 0:
                vectors_in(feed)
            else:
                names = ("normed", "qkv", "mixed", "second", "hidden")
                keep = {n: reg[n] for n in names}
            block_forward(keep, stream, None, resid, slots, vec, bias, regressed)
            first_pack[kind] = regressed[...].astype(LOW)
            x_copy(kind).start()
        x_copy(2).wait_recv()
        grad[...] = second_pack[...].astype(HIGH)
        block_backward(
            own, grad, temp, low_temp, slots, lead_vec, lead_vec_grad, lead_bias_grad, False, None
        )
        for c in range(crops):
            rest = grad[crop_rows(c), :]
            pick = one_hot(orders, 0, c)
            total = jnp.zeros((PATCHES, D), HIGH)
            for _ in range(3):
                part = rest.astype(LOW)
                rest = rest - part.astype(HIGH)
                total = total + dot_tn(pick, part)
            rows_out[c] = total
        pack_small_grads(lead_small_out, lead_vec_grad, lead_bias_grad, 12, devices)
        for n in range(2):
            x_copy(n).wait_send()
        feed.drain()

    @pl.when(section == 1)
    def _():
        feed = start.branch()
        slots = slots_of(feed)
        for kind, place_of in enumerate((pos_visible, pos_masked)):
            for c in range(crops):
                pick = one_hot(orders, kind, c)
                place_of[crop_rows(c), :] = sum(dot(pick, pos[t]) for t in (2, 1, 0))
        vectors_in(feed)
        stream[...] = side_vec[12:13, :] + pos_masked[...]
        for m in range(4):
            slots.fetch(m)
        feed.pump("z", 5)
        x_copy(0).wait_recv()
        context[...] = first_pack[0].astype(HIGH) + pos_visible[...]
        block_forward(reg, stream, context, resid, slots, lead_vec, lead_bias, regressed)
        stream[...] = regressed[...] + pos_masked[...]
        block_forward(own, stream, None, resid, Held(slots), side_vec, side_bias, temp)
        for c in range(crops):
            first = c * ROWS
            rows_out[c, 0:MASKED, :] = regressed[first : first + MASKED, :]
            rows_out[c, MASKED : 2 * MASKED, :] = temp[first : first + MASKED, :]
            grad[first : first + ROWS, :] = jnp.zeros((ROWS, D), HIGH)
            grad[first : first + MASKED, :] = cotangent[c].astype(HIGH)
        block_backward(
            own, grad, temp, low_temp, slots, side_vec, dec_vec_grad, dec_bias_grad, False, None
        )
        x_copy(1).wait_recv()
        inside = lax.broadcasted_iota(jnp.int32, (ROWS, D), 0) < MASKED
        for c in range(crops):
            here = crop_rows(c)
            apart = regressed[here, :] - first_pack[1, here, :].astype(HIGH)
            grad[here, :] = grad[here, :] + jnp.where(inside, apart, 0.0)
        block_backward(
            reg, grad, temp, low_temp, slots, lead_vec, lead_vec_grad, lead_bias_grad, True, context
        )
        second_pack[...] = context[...].astype(LOW)
        x_copy(2).start()
        dec_vec_grad[12:13, :] = jnp.sum(grad[...], axis=0, keepdims=True)
        pack_small_grads(lead_small_out, lead_vec_grad, lead_bias_grad, 12, devices)
        for t in range(2):
            pack_small_grads(
                dec_small_out.at[t],
                dec_vec_grad.at[:, t * (D // 2) : (t + 1) * (D // 2)],
                dec_bias_grad.at[:, t * (FF // 2) : (t + 1) * (FF // 2)],
                13,
                devices,
                2,
            )
        feed.drain()
        x_copy(2).wait_send()


def layer(crops, devices, pieces, patches, orders, pos, cotangent):
    tokens = crops * ROWS
    groups = devices // 4
    inside = [((crops, PATCHES, D), HIGH), ((devices, LEAD_SMALL, 128), HIGH)]
    inside.append(((2, devices, DEC_SMALL, 128), HIGH))
    inside += [save_shape(n, tokens) for n in OUT_DEC + OUT_REG]
    scratch = places_for([save_shape(n, tokens) for n in KEEP_DEC + KEEP_REG])
    scratch += places_for(WEIGHT_SHAPES + SMALL_SHAPES * 4)
    scratch += places_for([((devices, SMALL_ROWS, 128), LOW)])
    scratch += places_for([((tokens, D), HIGH)] * 8)
    scratch += places_for([((tokens, D), LOW), ((2, tokens, D), LOW), ((tokens, D), LOW)])
    scratch += [pltpu.SemaphoreType.DMA(s) for s in ((4,), (), (3,), (3,))]
    scratch += [pltpu.SemaphoreType.DMA((9,))]
    for width in (groups,) * 6 + (2 * groups,) * 2:
        scratch.append(pltpu.SemaphoreType.DMA((9, width)))
    wholes = [((devices,) + p.shape, p.dtype) for p in pieces]
    return pl.pallas_call(
        functools.partial(layer_kernel, crops, devices),
        out_shape=specs(wholes + inside),
        in_specs=[ANYWHERE] * 9 + [INSIDE] * 4,
        out_specs=[ANYWHERE] * 9 + [INSIDE] * len(inside),
        scratch_shapes=scratch,
        compiler_params=pltpu.CompilerParams(
            collective_id=1, has_side_effects=True, vmem_limit_bytes=60 << 20
        ),
        name="layer",
    )(*pieces, patches, orders, pos, cotangent)


LEAD_SMALL = 16
DEC_SMALL = 24


def pack_small_grads(out, vectors, bias, rows, chunks, parts=1):
    width = D // (chunks * parts)
    for d in range(chunks):
        lanes = slice(d * width, d * width + width)
        out[d, 0:rows, 0:width] = vectors[0:rows, lanes]
        for i in range(FF // D):
            first = (d * (FF // D) + i) * width
            out[d, rows + i : rows + i + 1, 0:width] = bias[0:1, first : first + width]


def sums_kernel(devices, *refs):
    refs = list(refs)
    groups, half = devices // 4, devices // 2

    def grab(n):
        taken = refs[:n]
        del refs[:n]
        return taken

    own, reg = dict(zip(OUT_DEC, grab(8))), dict(zip(OUT_REG, grab(10)))
    (lead_small_in, dec_small_in) = grab(2)
    lead_out, dec_out = grab(4), grab(4)
    vec_out, bias_out, dec_vec_out, dec_bias_out = grab(4)
    dec_far = grab(5)
    lead_own, lead_c, lead_y, lead_z = (grab(5) for _ in range(4))
    dec_own, dec_near, dec_y, dec_z = (grab(5) for _ in range(4))
    left_buf, right_buf, far_left, far_right, place_of, place_far, lead_total, dec_total = grab(8)
    pair_sem, far_sem, near_sem, load = grab(4)
    c_send, c_recv, x_send, x_recv, y_send, y_recv, u_send, u_recv, d_send, d_recv = refs
    section, index, outer, mid, core = place()
    x_device = (1 - section, index)
    mid_device = (section, slot(outer, 1 - mid, core))
    core_device = (section, slot(outer, mid, 1 - core))

    def outer_device(k):
        return (section, slot((outer + k) % groups, mid, core))

    barrier = pltpu.get_barrier_semaphore()
    greet([mid_device, core_device, x_device])
    each(
        groups - 1,
        lambda k: pl.semaphore_signal(
            barrier, inc=1, device_id=outer_device(k + 1), device_id_type=MESH_ID
        ),
    )

    own_of = lead_own + [r.at[1] for r in dec_own]
    y_of, z_of = lead_y + dec_y, lead_z + dec_z

    def mine(j):
        return j * 2 + core

    def lead_core(m, j):
        return remote(
            lead_own[m].at[j * 2 + 1 - core],
            lead_c[m].at[j],
            c_send.at[m, j],
            c_recv.at[m, j],
            core_device,
        )

    def dec_core(m, t, j):
        at = 5 + 2 * m + t
        return remote(
            dec_own[m].at[t, j * 2 + 1 - core],
            dec_far[m].at[t, j],
            c_send.at[at, j],
            c_recv.at[at, j],
            core_device,
        )

    def dec_load(m, t, j):
        return pltpu.make_async_copy(
            dec_far[m].at[t, j], dec_near[m].at[t, j % 2], near_sem.at[m, t, j % 2]
        )

    def x_copy(m, j):
        return remote(
            dec_own[m].at[0, mine(j)],
            dec_own[m].at[1, mine(j)],
            x_send.at[m, j],
            x_recv.at[m, j],
            x_device,
        )

    def y_copy(n, g):
        return remote(
            own_of[n].at[mine(g * 2 + 1 - mid)],
            y_of[n].at[g],
            y_send.at[n, g],
            y_recv.at[n, g],
            mid_device,
        )

    top = groups - 1

    def up_copy(n, d):
        return remote(
            own_of[n].at[mine(d * 2 + mid)],
            z_of[n].at[d + 1],
            u_send.at[n, d],
            u_recv.at[n, d],
            outer_device(1),
        )

    def down_copy(n, d):
        return remote(
            own_of[n].at[mine(d * 2 + mid)],
            z_of[n].at[d],
            d_send.at[n, d],
            d_recv.at[n, d],
            outer_device(groups - 1),
        )

    small_loads = (
        pltpu.make_async_copy(lead_small_in, lead_own[4], load.at[0]),
        pltpu.make_async_copy(dec_small_in, dec_own[4], load.at[1]),
    )

    def lead_begin(m):
        each(half, lambda j: lead_core(m, j).start())

    def lead_sum(m):
        def far_pair(g):
            j = g * 2 + 1 - mid
            lead_core(m, j).wait_recv()
            add_rows(lead_own[m], mine(j), lead_c[m], j)
            y_copy(m, g).start()

        def near_pair(g):
            j = g * 2 + mid
            lead_core(m, j).wait_recv()
            add_rows(lead_own[m], mine(j), lead_c[m], j)

        each(groups, far_pair)
        each(groups, near_pair)

    def dec_begin(m):
        for t in range(2):
            each(half, lambda j: dec_core(m, t, j).start())

    def dec_sum(m):
        for t in range(2):
            dec_core(m, t, 0).wait_recv()
            dec_load(m, t, 0).start()
            for j in range(half):
                if j + 1 < half:
                    dec_core(m, t, j + 1).wait_recv()
                    dec_load(m, t, j + 1).start()
                dec_load(m, t, j).wait()
                add_rows(dec_own[m].at[t], mine(j), dec_near[m].at[t], j % 2)
                if t == 0:
                    x_copy(m, j).start()

    def across(n):
        def from_mid(d):
            y_copy(n, d).wait_recv()
            add_rows(own_of[n], mine(d * 2 + mid), y_of[n], d)

        def up(before):
            d = top - before

            @pl.when(d > outer)
            def _():
                from_mid(d)

                @pl.when(outer > 0)
                def _():
                    up_copy(n, d).wait_recv()
                    add_rows(own_of[n], mine(d * 2 + mid), z_of[n], d + 1)

                up_copy(n, d).start()

        def down(d):
            @pl.when(d < outer)
            def _():
                from_mid(d)

                @pl.when(outer < top)
                def _():
                    down_copy(n, d).wait_recv()
                    add_rows(own_of[n], mine(d * 2 + mid), z_of[n], d)

                down_copy(n, d).start()

        each(top, up)
        each(top, down)
        y_copy(n, outer).wait_recv()

        @pl.when(outer == 0)
        def _():
            blank(z_of[n], 1)

        @pl.when(outer == top)
        def _():
            blank(z_of[n], top)

    def blank(buffer, at):
        buffer[at] = jnp.zeros(buffer.shape[1:], buffer.dtype)

    class Pairs:
        def __init__(self, tasks):
            self.tasks, self.at = tasks, 0
            self.begin(0)

        def copies(self, i):
            pairs, m, joined = self.tasks[i]
            moved = []
            for side, (name, buf) in enumerate(zip(PAIRS[m], (left_buf, right_buf))):
                width = pairs[name].shape[1]
                moved.append((pairs[name], buf.at[i % 2, :, 0:width], pair_sem.at[i % 2, side]))
            if joined:
                moved.append((pairs["normed_c"], far_left, far_sem.at[0]))
                moved.append((pairs["dkv_c"], far_right, far_sem.at[1]))
            return [pltpu.make_async_copy(*a) for a in moved]

        def begin(self, i):
            if i < len(self.tasks):
                for moved in self.copies(i):
                    moved.start()

        def take(self, out, stacked):
            i = self.at
            self.begin(i + 1)
            for moved in self.copies(i):
                moved.wait()
            pairs, m, joined = self.tasks[i]
            left, right = PAIRS[m]
            rows, columns = pairs[left].shape[1], pairs[right].shape[1]
            extra = (far_left, far_right, place_far) if joined else None
            weight_grad(
                out,
                left_buf.at[i % 2, :, 0:rows],
                right_buf.at[i % 2, :, 0:columns],
                place_of.at[0:rows, :],
                stacked,
                extra,
                D,
            )
            self.at += 1

    def lead_view(m):
        rows = lead_own[m].shape[1]
        return lead_own[m].reshape(devices * rows, lead_own[m].shape[2])

    def dec_view(m):
        (rows, columns), _ = WEIGHT_SHAPES[m]
        piece = dec_own[m].shape[2:]
        if piece[1] == columns:
            return dec_own[m].reshape(rows, columns), 0
        return dec_own[m].reshape(2 * devices, *piece), piece[0] // 2

    small_loads[0].start()
    order = (1, 3, 2, 0)

    @pl.when(section == 0)
    def _():
        pairs = Pairs([(own, m, False) for m in order])
        pairs.take(lead_view(order[0]), 0)
        pl.semaphore_wait(barrier, groups + 2)
        small_loads[0].wait()
        lead_begin(order[0])
        lead_begin(4)
        for i in range(1, 4):
            pairs.take(lead_view(order[i]), 0)
            lead_begin(order[i])
            lead_sum(order[i - 1])
        lead_sum(order[3])
        lead_sum(4)

    @pl.when(section == 1)
    def _():
        dec_order = (3, 2, 0, 1)
        small_loads[1].start()
        tasks = []
        for i in range(4):
            tasks.append((reg, order[i], order[i] == 0))
            tasks.append((own, dec_order[i], False))
        pairs = Pairs(tasks)
        for i in range(4):
            pairs.take(lead_view(order[i]), 0)
            if i == 0:
                pl.semaphore_wait(barrier, groups + 2)
                for moved in small_loads:
                    moved.wait()
                lead_begin(4)
                dec_begin(4)
            lead_begin(order[i])
            pairs.take(*dec_view(dec_order[i]))
            dec_begin(dec_order[i])
            lead_sum(order[i])
            if i:
                dec_sum(dec_order[i - 1])
        dec_sum(dec_order[3])
        dec_sum(4)
        lead_sum(4)

    order = order + (4,)
    dec_order = (3, 2, 0, 1, 4)
    for m in order:
        across(m)
    for m in dec_order:

        @pl.when(section == 0)
        def _():
            each(half, lambda j: x_copy(m, j).wait_recv())

        each(groups, lambda g: y_copy(5 + m, g).start())
    for m in dec_order:
        across(5 + m)

    def total_of(n, where, lanes):
        total = own_of[n][mine(outer * 2 + mid), where, lanes].astype(HIGH)
        total = total + y_of[n][outer, where, lanes].astype(HIGH)
        for k in (outer + 1, outer):
            total = total + z_of[n][k, where, lanes].astype(HIGH)
        return total

    for n in tuple(order) + tuple(5 + m for m in dec_order):

        @pl.when(outer > 0)
        def _():
            up_copy(n, outer).wait_recv()

        @pl.when(outer < top)
        def _():
            down_copy(n, outer).wait_recv()

        is_dec, m = divmod(n, 5)
        rows, columns = own_of[n].shape[-2:]
        if m == 4:
            total = dec_total if is_dec else lead_total
            total[...] = total_of(n, slice(None), slice(None))
            vec, bias = (dec_vec_out, dec_bias_out) if is_dec else (vec_out, bias_out)
            count, width = vec.shape
            vec[...] = total[0:count, 0:width]
            for i in range(FF // D):
                bias[0:1, i * width : i * width + width] = total[count + i : count + i + 1, 0:width]
            continue
        out = dec_out[m] if is_dec else lead_out[m]
        stacked = out.shape[-1] != columns
        step = rows // 2 if stacked else 16
        for r in range(rows // step):
            where = pl.ds(r * step, step)
            if stacked:
                for q in range(columns // 128):
                    lanes = slice(q * 128, q * 128 + 128)
                    out[:, (2 * q + r) * 128 : (2 * q + r + 1) * 128] = total_of(n, where, lanes)
            else:
                out[where, :] = total_of(n, where, slice(None))

    for m in range(5):
        each(half, lambda j: lead_core(m, j).wait_send())

    @pl.when(section == 1)
    def _():
        for m in range(5):
            for t in range(2):
                each(half, lambda j: dec_core(m, t, j).wait_send())
            each(half, lambda j: x_copy(m, j).wait_send())

    for n in range(10):
        each(groups, lambda g: y_copy(n, g).wait_send())


        def line_sends(d):
            @pl.when(d > outer)
            def _():
                up_copy(n, d).wait_send()

            @pl.when(d < outer)
            def _():
                down_copy(n, d).wait_send()

        each(groups, line_sends)


def sums(crops, devices, own_pairs, reg_pairs, lead_small, dec_small):
    tokens = crops * ROWS
    groups, half = devices // 4, devices // 2
    dec_kinds, _ = dec_grad_shapes(devices, True)
    lead_pieces, dec_pieces, lead_outs, dec_outs = [], [], [], []
    for (shape, kind), (dec_shape, _) in zip(WEIGHT_SHAPES, dec_kinds):
        rows, columns = shape
        lead_pieces.append(((rows // devices, columns), kind))
        lead_outs.append(((rows // devices, columns), HIGH))
        dec_outs.append(((rows // (2 * devices), columns), HIGH))
        piece = dec_shape[1:] if len(dec_shape) == 3 else (rows // (2 * devices), columns)
        dec_pieces.append((piece, kind))
    lead_pieces.append(((LEAD_SMALL, 128), HIGH))
    dec_pieces.append(((DEC_SMALL, 128), HIGH))
    small_outs = []
    for rows, chunks in ((12, devices), (13, 2 * devices)):
        small_outs += [((rows, D // chunks), HIGH), ((1, FF // chunks), HIGH)]
    far = [((2, half) + s, k) for s, k in dec_pieces]
    scratch = []
    for lead in ((devices,), (half,), (groups,), (groups + 1,)):
        scratch += places_for([(lead + s, k) for s, k in lead_pieces])
    for lead in ((2, devices), (2, 2), (groups,), (groups + 1,)):
        scratch += places_for([(lead + s, k) for s, k in dec_pieces])
    scratch += places_for(
        [((2, tokens, FF), LOW)] * 2
        + [((tokens, D), LOW), ((tokens, 2 * D), LOW), ((FF, tokens), LOW), ((D, tokens), LOW)]
        + [((LEAD_SMALL, 128), HIGH), ((DEC_SMALL, 128), HIGH)]
    )
    sems = [(2, 2), (2,), (5, 2, 2), (2,)]
    sems += [(15, half)] * 2 + [(5, half)] * 2 + [(10, groups)] * 6
    scratch += [pltpu.SemaphoreType.DMA(s) for s in sems]
    outs = pl.pallas_call(
        functools.partial(sums_kernel, devices),
        out_shape=specs(lead_outs + dec_outs + small_outs + far),
        in_specs=[ANYWHERE] * 20,
        out_specs=[INSIDE] * 12 + [ANYWHERE] * 5,
        scratch_shapes=scratch,
        compiler_params=pltpu.CompilerParams(
            collective_id=2, has_side_effects=True, vmem_limit_bytes=61 << 20
        ),
        name="sums",
    )(*own_pairs, *reg_pairs, lead_small, dec_small)
    lead, dec = list(outs[:4]), list(outs[4:8])
    lead += [outs[8], outs[9].reshape(-1)]
    dec += [outs[10], outs[11].reshape(-1)]
    return lead, dec


def exchange(pieces):
    return [lax.all_gather(p, "dp", axis=0) for p in pieces]


def as_small(parts, rows_of):
    flat = jnp.concatenate([p.reshape(-1) for p in parts])
    block = rows_of * 128
    padded = -(-flat.shape[0] // block) * block
    return jnp.pad(flat, (0, padded - flat.shape[0])).reshape(-1, 128)


def take_flat(flat, shapes):
    taken, offset = [], 0
    for shape in shapes:
        size = 1
        for extent in shape:
            size *= extent
        taken.append(flat[:, offset : offset + size].reshape((-1,) + shape))
        offset += size
    return taken


def spread_columns(gathered):
    return gathered.transpose(1, 0, 2).reshape(gathered.shape[1], -1)


def small_chunks(vectors, bias, chunks):
    rows, columns = vectors.shape
    cut = vectors.reshape(rows, chunks, columns // chunks).transpose(1, 0, 2).reshape(chunks, -1)
    flat = jnp.concatenate([cut, bias.reshape(chunks, -1)], axis=1)
    padded = -(-flat.shape[1] // 1024) * 1024
    return jnp.pad(flat, ((0, 0), (0, padded - flat.shape[1]))).reshape(chunks, -1, 128)


def small_pieces(chunk, rows, chunks):
    flat = chunk.reshape(-1)
    vectors = rows * (D // chunks)
    bias = FF // chunks
    return flat[:vectors].reshape(rows, D // chunks), flat[vectors : vectors + bias]


def total_grads(lead_big, lead_small, dec_big, dec_small):
    devices = lax.axis_size("dp")
    on_encoder = lax.axis_index("section") == 0
    lead_chunks = [g.reshape(devices, -1, g.shape[1]) for g in lead_big]
    lead_chunks.append(small_chunks(*lead_small, devices))
    dec_chunks = [g.reshape(2, devices, -1, g.shape[1]) for g in dec_big]
    dec_chunk_small = small_chunks(*dec_small, 2 * devices)
    dec_chunks.append(dec_chunk_small.reshape((2, devices) + dec_chunk_small.shape[1:]))
    lead_out = [
        lax.psum_scatter(g.astype(jnp.float32), "dp", scatter_dimension=0) for g in lead_chunks
    ]
    dec_out = []
    for g in dec_chunks:
        mine = jnp.where(on_encoder, jnp.zeros_like(g), g).astype(jnp.float32)
        mine = lax.psum_scatter(mine, "dp", scatter_dimension=1)
        dec_out.append(lax.psum_scatter(mine, "section", scatter_dimension=0))
    lead_vectors, lead_bias = small_pieces(lead_out[4], 12, devices)
    dec_vectors, dec_bias = small_pieces(dec_out[4], 13, 2 * devices)
    return lead_out[:4] + [lead_vectors, lead_bias], dec_out[:4] + [dec_vectors, dec_bias]


def run_fused(crops, devices, patches, cotangent, orders, lead, side, smalls):
    pieces = [pack_small(*smalls)] + lead + side
    outs = layer(crops, devices, pieces, patches, orders, position_parts(), cotangent)
    rows, lead_small, dec_small, *pairs = outs[9:]
    own_pairs, reg_pairs = pairs[: len(OUT_DEC)], pairs[len(OUT_DEC) :]
    return (rows, *sums(crops, devices, own_pairs, reg_pairs, lead_small, dec_small))


def run_apart(crops, devices, patches, cotangent, orders, lead, side, smalls):
    on_encoder = lax.axis_index("section") == 0
    wholes = exchange(lead + side + [as_small(smalls, 16)])
    big = [w.reshape(-1, w.shape[2]) for w in wholes[:8]]
    flat = wholes[8].reshape(devices, -1).astype(jnp.float32)
    lv, lb, sv, sb = take_flat(flat, [p.shape for p in smalls])

    def sixteen(vectors):
        rows = spread_columns(vectors)
        return jnp.pad(rows, ((0, 16 - rows.shape[0]), (0, 0)))

    lead_w, side_w = big[:4], big[4:]
    lead_small = [sixteen(lv), lb.reshape(1, -1)]
    all_small = lead_small + [sixteen(sv), sb.reshape(1, -1)]
    pack, pos_visible, pos_masked, *enc_saved = encode(
        crops, patches, orders, position_parts(), lead_w, side_w, all_small
    )
    arrived = passed_along(pack, "section", 1)
    grad_latents, latent_rows, reg_vec, reg_bias, dec_vec, dec_bias, *pairs = regress(
        crops, arrived, pos_visible, pos_masked, cotangent, lead_w, side_w, all_small
    )
    reg_pairs, dec_pairs = pairs[: len(OUT_REG)], pairs[len(OUT_REG) :]
    returned = passed_along(grad_latents, "section", -1)
    dec_big = decoder_weights(crops, dec_pairs, devices, False)
    *lead_big, grad_rows, enc_vec, enc_bias = finish(
        crops, returned, orders, lead_w, lead_small, enc_saved, reg_pairs
    )
    vec = jnp.where(on_encoder, enc_vec, reg_vec)[:12]
    bias = jnp.where(on_encoder, enc_bias, reg_bias)
    rows = jnp.where(on_encoder, grad_rows, latent_rows)
    lead_small, dec_small = (vec, bias[0]), (dec_vec[:13], dec_bias[0])
    return (rows, *total_grads(lead_big, lead_small, dec_big, dec_small))


def padded_orders(ordering, part):
    cut = ordering[:, MASKED:] if part == 0 else ordering[:, :MASKED]
    cut = jnp.pad(cut, ((0, 0), (0, ROWS - MASKED)), constant_values=-1)
    return cut.reshape(-1, 1)


def shards(
    patches,
    cotangent,
    ordering,
    lead_qkv,
    lead_proj,
    lead_up,
    lead_down,
    lead_vectors,
    lead_bias,
    side_qkv,
    side_proj,
    side_up,
    side_down,
    side_vectors,
    side_bias,
):
    devices = lax.axis_size("dp")
    crops = patches.shape[0]
    orders = jnp.stack([padded_orders(ordering, 0), padded_orders(ordering, 1)])
    lead = [lead_qkv[0], lead_proj[0], lead_up[0], lead_down[0]]
    side = [side_qkv[0], side_proj[0], side_up[0], side_down[0]]
    smalls = [lead_vectors[0], lead_bias[0], side_vectors[0], side_bias[0]]
    own_path = devices % 4 == 0 and lead[0].shape[0] % 16 == 0
    run = run_fused if own_path else run_apart
    rows, lead_out, dec_out = run(
        crops, devices, patches, cotangent, orders, lead, side, smalls
    )
    return (rows[None],) + tuple(o[None] for o in lead_out) + tuple(dec_out)


def solution(mesh):
    return jax.shard_map(
        shards,
        mesh=mesh,
        in_specs=(
            P("dp", None, None),
            P("dp", None, None),
            P("dp", None),
            P("section", "dp", None),
            P("section", "dp", None),
            P("section", "dp", None),
            P("section", "dp", None),
            P("section", None, "dp"),
            P("section", "dp"),
            P("section", "dp", None),
            P("section", "dp", None),
            P("section", "dp", None),
            P("section", "dp", None),
            P("section", None, "dp"),
            P("section", "dp"),
        ),
        out_specs=(
            P("section", "dp", None, None),
            P("section", "dp", None),
            P("section", "dp", None),
            P("section", "dp", None),
            P("section", "dp", None),
            P("section", None, "dp"),
            P("section", "dp"),
            P(("section", "dp"), None),
            P(("section", "dp"), None),
            P(("section", "dp"), None),
            P(("section", "dp"), None),
            P(None, ("section", "dp")),
            P(("section", "dp")),
        ),
        check_vma=False,
    )
```

```python
import copy
import functools

import jax
import jax.experimental.pallas as pl
import jax.experimental.pallas.tpu as pltpu
import jax.numpy as jnp
import numpy as np
from jax import lax
from jax.sharding import PartitionSpec as P

D = 768
HEADS = 12
HEAD_DIM = 64
FF = 3072
GRID = 14
PATCHES = 196
MASKED = 98


def passed_along(array, axis, by):
    count = lax.axis_size(axis)
    pairs = [(i, i + by) for i in range(count) if 0 <= i + by < count]
    return lax.ppermute(array, axis, pairs)


def positions():
    ids = np.arange(PATCHES)
    quarter = D // 4
    frequency = 10000.0 ** (-np.arange(quarter) / quarter)
    rows = (ids // GRID)[:, None] * frequency
    cols = (ids % GRID)[:, None] * frequency
    return np.concatenate([np.sin(cols), np.cos(cols), np.sin(rows), np.cos(rows)], axis=1)


def position_parts():
    rest = positions().astype(np.float32)
    parts = []
    for _ in range(3):
        part = rest.astype(jnp.bfloat16)
        rest = rest - part.astype(np.float32)
        parts.append(part)
    return jnp.asarray(np.stack(parts))


MESH_ID = pl.DeviceIdType.MESH


def each(count, body):
    if count <= 4:
        for k in range(count):
            body(k)
    else:
        lax.fori_loop(0, count, lambda k, carry: (body(k), carry)[1], 0)


def place():
    section = lax.axis_index("section")
    index = lax.axis_index("dp")
    return section, index, index // 4, (index // 2) % 2, index % 2


def slot(outer, mid, core):
    return outer * 4 + mid * 2 + core


def remote(src, dst, send_sem, recv_sem, device):
    return pltpu.make_async_remote_copy(
        src_ref=src,
        dst_ref=dst,
        send_sem=send_sem,
        recv_sem=recv_sem,
        device_id=device,
        device_id_type=MESH_ID,
    )


def greet(devices):
    barrier = pltpu.get_barrier_semaphore()
    for device in devices:
        pl.semaphore_signal(barrier, inc=1, device_id=device, device_id_type=MESH_ID)


def add_rows(target, at, other, other_at):
    rows = target.shape[-2]
    step = 16 if target.dtype == jnp.bfloat16 else 8

    def body(r, carry):
        where = pl.ds(r * step, step)
        total = target[at, where, :].astype(jnp.float32) + other[other_at, where, :].astype(
            jnp.float32
        )
        target[at, where, :] = total.astype(target.dtype)
        return carry

    lax.fori_loop(0, rows // step, body, 0, unroll=True)


ROWS = 112
LOW = jnp.bfloat16
HIGH = jnp.float32
VISIBLE = PATCHES - MASKED
CHUNK = 32
NAMES_SELF = ("normed", "qkv", "probs", "mixed", "attn", "x1", "r1", "x2", "r2", "second")
NAMES_SELF += ("slope", "hidden", "branch", "x3", "r3")
NAMES_CROSS = ("normed_c", "kv_c", "probs_c", "x1_c", "r1_c")
NAMES_GRAD = ("dqkv", "dattn", "dpre", "dbranch")


def save_shape(name, tokens):
    pairs = tokens // ROWS * (HEADS // 2)
    kinds = {
        "qkv": ((tokens, 3 * D), LOW),
        "kv_c": ((tokens, 2 * D), LOW),
        "dqkv": ((tokens, 3 * D), LOW),
        "dkv_c": ((tokens, 2 * D), LOW),
        "probs": ((pairs, 2 * ROWS, ROWS), HIGH),
        "probs_c": ((pairs, 2 * ROWS, ROWS), HIGH),
        "hidden": ((tokens, FF), LOW),
        "dpre": ((tokens, FF), LOW),
        "slope": ((tokens, FF), HIGH),
    }
    if name in kinds:
        return kinds[name]
    if name in ("r1", "r2", "r3", "r1_c"):
        return ((tokens, 1), HIGH)
    if name in ("attn", "x1", "x1_c", "x2", "x3", "branch"):
        return ((tokens, D), HIGH)
    return ((tokens, D), LOW)


def dot(left, right):
    return jnp.dot(left, right, preferred_element_type=HIGH)


def dot_nt(left, right):
    return lax.dot_general(left, right, (((1,), (1,)), ((), ())), preferred_element_type=HIGH)


def dot_tn(left, right):
    return lax.dot_general(left, right, (((0,), (0,)), ((), ())), preferred_element_type=HIGH)


def by_rows(tokens, body, init=()):
    def step(i, carry):
        return body(pl.ds(pl.multiple_of(i * CHUNK, CHUNK), CHUNK), carry)

    return lax.fori_loop(0, tokens // CHUNK, step, init, unroll=True)


def tiles(width, body, size=256, unroll=True):
    def step(i, carry):
        body(pl.ds(pl.multiple_of(i * size, size), size))
        return carry

    lax.fori_loop(0, width // size, step, 0, unroll=unroll)


def fold(values):
    return jnp.sum(values.reshape(-1, 8, values.shape[-1]), axis=0)


def norm_forward(source, gain, shift, kept, spread, low, out=None):
    def body(where, carry):
        values = source[where, :]
        center = values - jnp.mean(values, axis=-1, keepdims=True)
        scale = lax.rsqrt(jnp.mean(center * center, axis=-1, keepdims=True) + 1e-06)
        center = center * scale
        if kept is not None:
            kept[where, :] = center
            spread[where, :] = scale
        result = center * gain + shift
        if low is not None:
            low[where, :] = result.astype(LOW)
        if out is not None:
            out[where, :] = result
        return carry

    by_rows(source.shape[0], body)


def norm_grad(grad, gain, center, scale):
    weighted = grad * gain
    first = jnp.mean(weighted, axis=-1, keepdims=True)
    second = jnp.mean(weighted * center, axis=-1, keepdims=True)
    return scale * (weighted - first - center * second)


def pair_masks(rows):
    lane = lax.broadcasted_iota(jnp.int32, (rows, 2 * HEAD_DIM), 1)
    return lane < HEAD_DIM


def two_heads(values):
    low_lanes = pair_masks(values.shape[0])
    zero = jnp.zeros_like(values)
    return jnp.concatenate(
        [jnp.where(low_lanes, values, zero), jnp.where(low_lanes, zero, values)], axis=0
    )


def one_pair(stacked):
    half = stacked.shape[0] // 2
    return jnp.where(pair_masks(half), stacked[:half], stacked[half:])


def head_loop(tokens, body):
    def step(p, carry):
        for crop in range(tokens // ROWS):
            rows = pl.ds(crop * ROWS, ROWS)
            body(crop * (HEADS // 2) + p, rows, p)
        return carry

    lax.fori_loop(0, HEADS // 2, step, 0, unroll=True)


def lanes_of(p, base):
    return pl.ds(pl.multiple_of(base + p * 128, 128), 128)


def attention(s, cross):
    tokens = s["normed"].shape[0]
    valid = lax.broadcasted_iota(jnp.int32, (2 * ROWS, ROWS), 1) < MASKED

    def body(at, rows, p):
        q2 = two_heads(s["qkv"][rows, lanes_of(p, 0)])
        sources = [(s["qkv"][rows, lanes_of(p, D)], s["qkv"][rows, lanes_of(p, 2 * D)], "probs")]
        if cross:
            sources.append(
                (s["kv_c"][rows, lanes_of(p, 0)], s["kv_c"][rows, lanes_of(p, D)], "probs_c")
            )
        scores = [
            jnp.where(valid, dot_nt(q2, k) * HEAD_DIM ** (-0.5), -1e30) for k, _, _ in sources
        ]
        top = jnp.max(scores[0], axis=-1, keepdims=True)
        if cross:
            top = jnp.maximum(top, jnp.max(scores[1], axis=-1, keepdims=True))
        powers = [jnp.exp(x - top) for x in scores]
        mass = jnp.sum(powers[0], axis=-1, keepdims=True)
        if cross:
            mass = mass + jnp.sum(powers[1], axis=-1, keepdims=True)
        mixed = None
        inverse = 1.0 / mass
        for power, (_, v, name) in zip(powers, sources):
            probs = power * inverse
            if name in s:
                s[name][at] = probs
            part = dot(probs.astype(LOW), v)
            mixed = part if mixed is None else mixed + part
        s["mixed"][rows, lanes_of(p, 0)] = one_pair(mixed).astype(LOW)

    head_loop(tokens, body)


def block_forward(s, stream, context, resid, weights, vectors, bias, out):
    def row(r, where=slice(None)):
        return vectors[r : r + 1, where]

    norm_forward(stream, row(0), row(1), s.get("x1"), s.get("r1"), s["normed"])
    if context is not None:
        norm_forward(context, row(0), row(1), s["x1_c"], s["r1_c"], s["normed_c"])
    w = weights.open(0)

    def qkv_tile(j):
        where = slice(j * 256, j * 256 + 256)
        kind, local = divmod(j, 3)
        extra = None if kind == 1 else row(6 if kind == 0 else 7, slice(local * 256, local * 256 + 256))
        values = dot(s["normed"][...], w[:, where])
        s["qkv"][:, where] = (values if extra is None else values + extra).astype(LOW)
        if context is not None and kind > 0:
            values = dot(s["normed_c"][...], w[:, where])
            here = slice(j * 256 - D, j * 256 - D + 256)
            s["kv_c"][:, here] = (values if extra is None else values + extra).astype(LOW)

    for j in range(9):
        qkv_tile(j)
    weights.close(0)
    attention(s, context is not None)
    w = weights.open(1)
    for j in range(3):
        where = slice(j * 256, j * 256 + 256)
        attn = dot(s["mixed"][...], w[:, where]) + row(8, where)
        if "attn" in s:
            s["attn"][:, where] = attn
        resid[:, where] = stream[:, where] + row(10, where) * attn
    weights.close(1)
    norm_forward(resid, row(2), row(3), s.get("x2"), s.get("r2"), s["second"])
    w = weights.open(2)

    def up_tile(where):
        pre = dot(s["second"][...], w[:, where]) + bias[0:1, where]
        phi = 0.5 + 0.5 * lax.erf(pre * 0.5**0.5)
        s["hidden"][:, where] = (pre * phi).astype(LOW)
        if "slope" in s:
            s["slope"][:, where] = phi + pre * jnp.exp(-0.5 * pre * pre) * 0.3989422804014327

    tiles(FF, up_tile)
    weights.close(2)
    w = weights.open(3)
    for j in range(3):
        where = slice(j * 256, j * 256 + 256)
        branch = dot(s["hidden"][...], w[:, where]) + row(9, where)
        if "branch" in s:
            s["branch"][:, where] = branch
        resid[:, where] = resid[:, where] + row(11, where) * branch
    weights.close(3)
    norm_forward(resid, row(4), row(5), s.get("x3"), s.get("r3"), None, out)


def attention_backward(s, grad_mixed, cross):
    tokens = s["normed"].shape[0]
    scale = HEAD_DIM ** (-0.5)

    def body(at, rows, p):
        q2 = two_heads(s["qkv"][rows, lanes_of(p, 0)])
        g2 = two_heads(grad_mixed[rows, lanes_of(p, 0)])
        sources = [("qkv", D, "dqkv", "probs")]
        if cross:
            sources.append(("kv_c", 0, "dkv_c", "probs_c"))
        parts = []
        inner = None
        for name, base, grad_name, probs_name in sources:
            v = s[name][rows, lanes_of(p, base + D)]
            probs = s[probs_name][at]
            s[grad_name][rows, lanes_of(p, base + D)] = dot_tn(probs.astype(LOW), g2).astype(LOW)
            dprobs = dot_nt(g2, v)
            parts.append((probs, dprobs))
            total = jnp.sum(dprobs * probs, axis=-1, keepdims=True)
            inner = total if inner is None else inner + total
        dq = None
        for (probs, dprobs), (name, base, grad_name, _) in zip(parts, sources):
            dscores = (probs * (dprobs - inner)).astype(LOW)
            part = dot(dscores, s[name][rows, lanes_of(p, base)])
            dq = part if dq is None else dq + part
            s[grad_name][rows, lanes_of(p, base)] = (dot_tn(dscores, q2) * scale).astype(LOW)
        s["dqkv"][rows, lanes_of(p, 0)] = (one_pair(dq) * scale).astype(LOW)

    head_loop(tokens, body)


def block_backward(s, grad, temp, low_temp, weights, vectors, vec_grad, bias_grad, cross, context_grad):
    tokens = grad.shape[0]
    zero = jnp.zeros((8, D), HIGH)

    def row(r):
        return vectors[r : r + 1, :]

    def put(r, total):
        vec_grad[r : r + 1, :] = jnp.sum(total, axis=0, keepdims=True)

    def final_rows(where, sums):
        gain, shift, scale, offset = sums
        g = grad[where, :]
        center = s["x3"][where, :]
        gf = norm_grad(g, row(4), center, s["r3"][where, :])
        grad[where, :] = gf
        low = (row(11) * gf).astype(LOW)
        s["dbranch"][where, :] = low
        return (
            gain + fold(g * center),
            shift + fold(g),
            scale + fold(gf * s["branch"][where, :]),
            offset + fold(low.astype(HIGH)),
        )

    sums = by_rows(tokens, final_rows, (zero,) * 4)
    for r, total in zip((4, 5, 11, 9), sums):
        put(r, total)
    w = weights.open(3)

    def down_tile(where):
        low = (dot_nt(s["dbranch"][...], w[where, :]) * s["slope"][:, where]).astype(LOW)
        s["dpre"][:, where] = low
        bias_grad[0:1, where] = jnp.sum(low.astype(HIGH), axis=0, keepdims=True)

    tiles(FF, down_tile)
    weights.close(3)
    w = weights.open(2)
    for j in range(3):
        where = slice(j * 256, j * 256 + 256)
        temp[:, where] = dot_nt(s["dpre"][...], w[where, :])
    weights.close(2)

    def second_rows(where, sums):
        gain, shift, scale, offset = sums
        g = temp[where, :]
        center = s["x2"][where, :]
        gr = norm_grad(g, row(2), center, s["r2"][where, :]) + grad[where, :]
        grad[where, :] = gr
        low = (row(10) * gr).astype(LOW)
        s["dattn"][where, :] = low
        return (
            gain + fold(g * center),
            shift + fold(g),
            scale + fold(gr * s["attn"][where, :]),
            offset + fold(low.astype(HIGH)),
        )

    sums = by_rows(tokens, second_rows, (zero,) * 4)
    for r, total in zip((2, 3, 10, 8), sums):
        put(r, total)
    w = weights.open(1)
    for j in range(3):
        where = slice(j * 256, j * 256 + 256)
        low_temp[:, where] = dot_nt(s["dattn"][...], w[where, :]).astype(LOW)
    weights.close(1)
    attention_backward(s, low_temp, cross)
    w = weights.open(0)
    for j in range(3):
        where = slice(j * 256, j * 256 + 256)
        temp[:, where] = dot_nt(s["dqkv"][...], w[where, :])
        if cross:
            context_grad[:, where] = dot_nt(s["dkv_c"][...], w[where, D:])
    weights.close(0)

    def first_rows(where, sums):
        gain, shift, dq, dv = sums
        g = temp[where, :]
        center = s["x1"][where, :]
        grad[where, :] = grad[where, :] + norm_grad(g, row(0), center, s["r1"][where, :])
        gain, shift = gain + fold(g * center), shift + fold(g)
        dq = dq + fold(s["dqkv"][where, 0:D].astype(HIGH))
        dv = dv + fold(s["dqkv"][where, 2 * D :].astype(HIGH))
        if cross:
            g = context_grad[where, :]
            center = s["x1_c"][where, :]
            context_grad[where, :] = norm_grad(g, row(0), center, s["r1_c"][where, :])
            gain, shift = gain + fold(g * center), shift + fold(g)
            dv = dv + fold(s["dkv_c"][where, D:].astype(HIGH))
        return gain, shift, dq, dv

    sums = by_rows(tokens, first_rows, (zero,) * 4)
    for r, total in zip((0, 1, 6, 7), sums):
        put(r, total)


class Slots:
    def __init__(self, places, sems):
        self.places, self.sems = places, sems
        self.queue = [[] for _ in places]
        self.ready = [False] * len(places)

    def copy(self, m, source):
        return pltpu.make_async_copy(source, self.places[m], self.sems.at[m])

    def plan(self, m, source):
        self.queue[m].append(source)
        if len(self.queue[m]) == 1:
            self.copy(m, source).start()

    def open(self, m):
        if not self.ready[m]:
            self.copy(m, self.queue[m][0]).wait()
            self.ready[m] = True
        return self.places[m]

    def close(self, m):
        self.queue[m].pop(0)
        self.ready[m] = False
        if self.queue[m]:
            self.copy(m, self.queue[m][0]).start()


class Held:
    def __init__(self, slots):
        self.slots = slots

    def open(self, m):
        return self.slots.open(m)

    def close(self, m):
        pass


def transposed(place, source):
    width = source.shape[1]
    for j in range(width // 256):
        where = slice(j * 256, j * 256 + 256)
        place[where, :] = source[:, where].T


def weight_grad(out, left, right, place, stacked=0, extra=None, base=0):
    rows, columns = left.shape[1], right.shape[1]
    transposed(place, left)
    if extra is not None:
        transposed(extra[2], extra[0])

    def column_tile(j, with_extra):
        where = pl.ds(pl.multiple_of(j * 256, 256), 256)
        for i in range(rows // 384):
            down = slice(i * 384, i * 384 + 384)
            total = dot(place[down, :], right[:, where])
            if with_extra:
                there = pl.ds(pl.multiple_of(j * 256 - base, 256), 256)
                total = total + dot(extra[2][down, :], extra[1][:, there])
            if stacked:
                count = 384 // stacked
                cut = total.reshape(count, stacked, 256)
                both = jnp.concatenate([cut[:, :, :128], cut[:, :, 128:]], axis=1)
                here = pl.ds(pl.multiple_of(j * 128, 128), 128)
                out[i * count : (i + 1) * count, :, here] = both.astype(LOW)
            else:
                out[down, where] = total.astype(LOW)

    def plain(j, carry):
        column_tile(j, False)
        return carry

    def joined(j, carry):
        column_tile(j, True)
        return carry

    first = base // 256 if extra is not None else columns // 256
    lax.fori_loop(0, first, plain, 0, unroll=True)
    if extra is not None:
        lax.fori_loop(first, columns // 256, joined, 0, unroll=True)


def crop_rows(c):
    return slice(c * ROWS, c * ROWS + ROWS)


def one_hot(orders, kind, crop):
    ids = orders[kind, crop_rows(crop), :]
    return (ids == lax.broadcasted_iota(jnp.int32, (ROWS, PATCHES), 1)).astype(LOW)


def encode_kernel(crops, *refs):
    refs = list(refs)
    patches, orders, pos = refs[:3]
    lead_w, side_w = refs[3:7], refs[7:11]
    lead_vec, lead_bias, side_vec, side_bias = refs[11:15]
    pack, pos_visible, pos_masked = refs[15:18]
    refs = refs[18:]
    saved = dict(zip(NAMES_SELF, refs))
    refs = refs[len(NAMES_SELF) :]
    places, (sems, stream, resid, latent) = refs[:4], refs[4:8]
    brief = dict(zip(("normed", "qkv", "mixed", "second", "hidden"), refs[8:13]))
    section = lax.axis_index("section")

    @pl.when(section == 0)
    def _():
        slots = Slots(places, sems)
        for source in (lead_w, side_w):
            for m in range(4):
                slots.plan(m, source[m])
        for kind in range(2):
            for c in range(crops):
                rows = dot(one_hot(orders, kind, c), patches[c])
                stream[crop_rows(c), :] = rows
            if kind == 0:
                block_forward(saved, stream, None, resid, slots, lead_vec, lead_bias, latent)
            else:
                block_forward(brief, stream, None, resid, slots, side_vec, side_bias, latent)
            pack[kind] = latent[...].astype(LOW)

    @pl.when(section == 1)
    def _():
        for kind, place_of in enumerate((pos_visible, pos_masked)):
            for c in range(crops):
                pick = one_hot(orders, kind, c)
                place_of[crop_rows(c), :] = sum(dot(pick, pos[t]) for t in (2, 1, 0))


def regress_kernel(crops, *refs):
    refs = list(refs)
    pack, pos_visible, pos_masked, cotangent = refs[:4]
    lead_w, side_w = refs[4:8], refs[8:12]
    lead_vec, lead_bias, side_vec, side_bias = refs[12:16]
    refs = refs[16:]

    def grab(names):
        taken = dict(zip(names, refs))
        del refs[: len(names)]
        return taken

    grad_latents, rows_out, reg_vec, reg_bias, dec_vec, dec_bias = refs[:6]
    del refs[:6]
    reg, dec = grab(OUT_REG), grab(OUT_DEC)
    reg.update(grab(KEEP_REG))
    dec.update(grab(KEEP_DEC))
    places = refs[:4]
    sems, stream, context, resid, regressed, grad, temp, low_temp = refs[4:]
    tokens = crops * ROWS

    @pl.when(lax.axis_index("section") == 1)
    def _():
        slots = Slots(places, sems)
        for source in (lead_w, side_w, lead_w):
            for m in range(4):
                slots.plan(m, source[m])
        stream[...] = side_vec[12:13, :] + pos_masked[...]
        context[...] = pack[0].astype(HIGH) + pos_visible[...]
        block_forward(reg, stream, context, resid, slots, lead_vec, lead_bias, regressed)
        stream[...] = regressed[...] + pos_masked[...]
        block_forward(dec, stream, None, resid, Held(slots), side_vec, side_bias, temp)
        for c in range(crops):
            first = c * ROWS
            rows_out[c, 0:MASKED, :] = regressed[first : first + MASKED, :]
            rows_out[c, MASKED : 2 * MASKED, :] = temp[first : first + MASKED, :]
            grad[first : first + ROWS, :] = jnp.zeros((ROWS, D), HIGH)
            grad[first : first + MASKED, :] = cotangent[c].astype(HIGH)
        block_backward(
            dec, grad, temp, low_temp, slots, side_vec, dec_vec, dec_bias, False, None
        )
        inside = lax.broadcasted_iota(jnp.int32, (ROWS, D), 0) < MASKED
        for c in range(crops):
            here = crop_rows(c)
            apart = regressed[here, :] - pack[1, here, :].astype(HIGH)
            grad[here, :] = grad[here, :] + jnp.where(inside, apart, 0.0)
        block_backward(
            reg, grad, temp, low_temp, slots, lead_vec, reg_vec, reg_bias, True, context
        )
        dec_vec[12:13, :] = jnp.sum(grad[...], axis=0, keepdims=True)
        grad_latents[...] = context[...].astype(LOW)


PAIRS = (("normed", "dqkv"), ("mixed", "dattn"), ("second", "dpre"), ("hidden", "dbranch"))
OUT_DEC = tuple(n for pair in PAIRS for n in pair)
OUT_REG = OUT_DEC + ("normed_c", "dkv_c")
KEEP_DEC = tuple(n for n in NAMES_SELF if n not in OUT_DEC)
KEEP_REG = KEEP_DEC + tuple(n for n in NAMES_CROSS if n not in OUT_REG)


def ship(m, scratch, outs, sems):
    return pltpu.make_async_copy(scratch[m], outs[m], sems.at[m])


def decoder_weights_kernel(stacks, *refs):
    pairs, outs = dict(zip(OUT_DEC, refs[:8])), refs[8:12]
    scratch, (place, sems) = refs[12:16], refs[16:]

    @pl.when(lax.axis_index("section") == 1)
    def _():
        for m in (3, 2, 1, 0):
            left, right = PAIRS[m]
            rows = pairs[left].shape[1]
            weight_grad(
                scratch[m], pairs[left], pairs[right], place.at[0:rows, :], stacks[m]
            )
            ship(m, scratch, outs, sems).start()
        for m in range(4):
            ship(m, scratch, outs, sems).wait()


def finish_kernel(crops, *refs):
    refs = list(refs)
    returned, orders = refs[:2]
    lead_w, lead_vec, lead_bias = refs[2:6], refs[6], refs[7]
    del refs[:8]

    def grab(names):
        taken = dict(zip(names, refs))
        del refs[: len(names)]
        return taken

    enc, reg = grab(NAMES_SELF), grab(OUT_REG)
    outs, (rows_out, enc_vec, enc_bias) = refs[:4], refs[4:7]
    del refs[:7]
    enc.update(grab(NAMES_GRAD))
    places = refs[:4]
    scratch = refs[4:8]
    sems, out_sems, place, place_c, grad, temp, low_temp = refs[8:]
    section = lax.axis_index("section")

    def weights_of(pairs, joined):
        for m in (3, 2, 1, 0):
            left, right = PAIRS[m]
            rows = pairs[left].shape[1]
            extra = (pairs["normed_c"], pairs["dkv_c"], place_c) if joined and m == 0 else None
            weight_grad(
                scratch[m], pairs[left], pairs[right], place.at[0:rows, :], 0, extra, D
            )
            ship(m, scratch, outs, out_sems).start()
        for m in range(4):
            ship(m, scratch, outs, out_sems).wait()

    @pl.when(section == 0)
    def _():
        slots = Slots(places, sems)
        for m in (3, 2, 1, 0):
            slots.plan(m, lead_w[m])
        grad[...] = returned[...].astype(HIGH)
        block_backward(enc, grad, temp, low_temp, slots, lead_vec, enc_vec, enc_bias, False, None)
        for c in range(crops):
            rest = grad[crop_rows(c), :]
            pick = one_hot(orders, 0, c)
            total = jnp.zeros((PATCHES, D), HIGH)
            for _ in range(3):
                part = rest.astype(LOW)
                rest = rest - part.astype(HIGH)
                total = total + dot_tn(pick, part)
            rows_out[c] = total
        weights_of(enc, False)

    @pl.when(section == 1)
    def _():
        weights_of(reg, True)


ANYWHERE = pl.BlockSpec(memory_space=pl.ANY)
INSIDE = pl.BlockSpec(memory_space=pltpu.VMEM)


def specs(shapes):
    return [jax.ShapeDtypeStruct(s, d) for s, d in shapes]


def places_for(shapes):
    return [pltpu.VMEM(s, d) for s, d in shapes]


def params():
    return pltpu.CompilerParams(vmem_limit_bytes=60 << 20)


WEIGHT_SHAPES = [((D, 3 * D), LOW), ((D, D), LOW), ((D, FF), LOW), ((FF, D), LOW)]
SMALL_SHAPES = [((16, D), HIGH), ((1, FF), HIGH)]


def encode(crops, patches, orders, pos, lead_w, side_w, smalls):
    tokens = crops * ROWS
    shapes = [((2, tokens, D), LOW), ((tokens, D), HIGH), ((tokens, D), HIGH)]
    shapes += [save_shape(n, tokens) for n in NAMES_SELF]
    scratch = places_for(WEIGHT_SHAPES) + [pltpu.SemaphoreType.DMA((4,))]
    scratch += places_for([((tokens, D), HIGH)] * 3)
    scratch += places_for(
        [save_shape(n, tokens) for n in ("normed", "qkv", "mixed", "second", "hidden")]
    )
    return pl.pallas_call(
        functools.partial(encode_kernel, crops),
        out_shape=specs(shapes),
        in_specs=[INSIDE] * 3 + [ANYWHERE] * 8 + [INSIDE] * 4,
        out_specs=[INSIDE] * len(shapes),
        scratch_shapes=scratch,
        compiler_params=params(),
        name="encode",
    )(patches, orders, pos, *lead_w, *side_w, *smalls)


def regress(crops, pack, pos_visible, pos_masked, cotangent, lead_w, side_w, smalls):
    tokens = crops * ROWS
    shapes = [((tokens, D), LOW), ((crops, PATCHES, D), HIGH)] + SMALL_SHAPES * 2
    shapes += [save_shape(n, tokens) for n in OUT_REG + OUT_DEC]
    scratch = places_for([save_shape(n, tokens) for n in KEEP_REG + KEEP_DEC])
    scratch += places_for(WEIGHT_SHAPES) + [pltpu.SemaphoreType.DMA((4,))]
    scratch += places_for([((tokens, D), HIGH)] * 6 + [((tokens, D), LOW)])
    return pl.pallas_call(
        functools.partial(regress_kernel, crops),
        out_shape=specs(shapes),
        in_specs=[INSIDE] * 4 + [ANYWHERE] * 8 + [INSIDE] * 4,
        out_specs=[INSIDE] * len(shapes),
        scratch_shapes=scratch,
        compiler_params=params(),
        name="regress",
    )(pack, pos_visible, pos_masked, cotangent, *lead_w, *side_w, *smalls)


def dec_grad_shapes(devices, own_path):
    shapes, stacks = [], []
    for (rows, columns), kind in WEIGHT_SHAPES:
        r = rows // (2 * devices)
        stack = r if own_path and r % 16 else 0
        stacks.append(stack)
        shapes.append(
            ((2 * devices, 2 * r, columns // 2), kind) if stack else ((rows, columns), kind)
        )
    return shapes, tuple(stacks)


def decoder_weights(crops, pairs, devices, own_path):
    shapes, stacks = dec_grad_shapes(devices, own_path)
    return pl.pallas_call(
        functools.partial(decoder_weights_kernel, stacks),
        out_shape=specs(shapes),
        in_specs=[INSIDE] * 8,
        out_specs=[ANYWHERE] * 4,
        scratch_shapes=places_for(shapes)
        + places_for([((FF, crops * ROWS), LOW)])
        + [pltpu.SemaphoreType.DMA((4,))],
        compiler_params=params(),
        name="decoder_weights",
    )(*pairs)


def finish(crops, returned, orders, lead_w, lead_small, enc_saved, reg_pairs):
    tokens = crops * ROWS
    shapes = WEIGHT_SHAPES + [((crops, PATCHES, D), HIGH)] + SMALL_SHAPES
    scratch = places_for([save_shape(n, tokens) for n in NAMES_GRAD])
    scratch += places_for(WEIGHT_SHAPES * 2) + [pltpu.SemaphoreType.DMA((4,))] * 2
    scratch += places_for([((FF, tokens), LOW), ((D, tokens), LOW)])
    scratch += places_for([((tokens, D), HIGH)] * 2 + [((tokens, D), LOW)])
    count = len(enc_saved) + len(reg_pairs)
    return pl.pallas_call(
        functools.partial(finish_kernel, crops),
        out_shape=specs(shapes),
        in_specs=[INSIDE] * 2 + [ANYWHERE] * 4 + [INSIDE] * (2 + count),
        out_specs=[ANYWHERE] * 4 + [INSIDE] * 3,
        scratch_shapes=scratch,
        compiler_params=params(),
        name="finish",
    )(returned, orders, *lead_w, *lead_small, *enc_saved, *reg_pairs)


SMALL_ROWS = 48


class Feed:
    WINDOW = 3

    def __init__(self, groups, shards_in, wholes, sems):
        self.groups, self.shards, self.wholes = groups, shards_in, wholes
        self.own, self.us, self.ur, self.ds, self.dr, self.ys, self.yr, self.cs, self.cr = sems
        self.count = len(shards_in)
        self.section, self.index, self.outer, self.mid, self.core = place()
        self.begun = self.at = 0
        self.done = set()
        self.steps = [("z", 0), ("y", 0), ("z", 1)]
        for m in range(2, self.count):
            self.steps += [("z", m), ("y", m - 1)]
        self.steps.append(("y", self.count - 1))

    def branch(self):
        other = copy.copy(self)
        other.done = set(self.done)
        return other

    def devices(self):
        mid = (self.section, slot(self.outer, 1 - self.mid, self.core))
        core = (self.section, slot(self.outer, self.mid, 1 - self.core))
        return mid, core

    def outer_device(self, k):
        return (self.section, slot((self.outer + k) % self.groups, self.mid, self.core))

    def origin(self, k, far=0, other_core=False):
        outer = (self.outer - k + self.groups) % self.groups
        mid = 1 - self.mid if far else self.mid
        return slot(outer, mid, 1 - self.core if other_core else self.core)

    def own_copy(self, m):
        return pltpu.make_async_copy(
            self.shards[m], self.wholes[m].at[self.index], self.own.at[m]
        )

    def up_copy(self, m, k):
        piece = self.wholes[m].at[self.origin(k)]
        src = self.shards[m] if isinstance(k, int) and k == 0 else piece
        return remote(src, piece, self.us.at[m, k], self.ur.at[m, k], self.outer_device(1))

    def down_copy(self, m, k):
        piece = self.wholes[m].at[self.origin(k)]
        src = self.shards[m] if isinstance(k, int) and k == 0 else piece
        below = self.outer_device(self.groups - 1)
        return remote(src, piece, self.ds.at[m, k], self.dr.at[m, k], below)

    def up_arrival(self, m, k):
        piece = self.wholes[m].at[self.origin(k)]
        return remote(
            piece, piece, self.us.at[m, k - 1], self.ur.at[m, k - 1], self.outer_device(1)
        )

    def down_arrival(self, m, distance):
        k = (self.groups - distance) % self.groups
        piece = self.wholes[m].at[self.origin(k)]
        at = (self.groups - distance + 1) % self.groups
        return remote(piece, piece, self.ds.at[m, at], self.dr.at[m, at], self.outer_device(1))

    def y_copy(self, m, k, own=False, arrival=False):
        piece = self.wholes[m].at[self.origin(k, far=1 if arrival else 0)]
        src = self.shards[m] if own else piece
        return remote(src, piece, self.ys.at[m, k], self.yr.at[m, k], self.devices()[0])

    def c_copy(self, m, k, far, own=False, arrival=False):
        piece = self.wholes[m].at[self.origin(k, far, arrival)]
        src = self.shards[m] if own else piece
        at = k * 2 + far
        return remote(src, piece, self.cs.at[m, at], self.cr.at[m, at], self.devices()[1])

    def begin(self, upto):
        while self.begun < min(upto, self.count):
            m = self.begun

            @pl.when(self.outer < self.groups - 1)
            def _():
                self.up_copy(m, 0).start()

            @pl.when(self.outer > 0)
            def _():
                self.down_copy(m, 0).start()

            self.y_copy(m, 0, own=True).start()
            self.c_copy(m, 0, 0, own=True).start()
            self.own_copy(m).start()
            self.begun += 1

    def step(self):
        kind, m = self.steps[self.at]
        self.at += 1
        if kind == "z":

            top = self.groups - 1

            def spread(k):
                self.y_copy(m, k).start()
                self.c_copy(m, k, 0).start()

            def pass_on(before):
                distance = before + 1

                @pl.when(self.outer >= distance)
                def _():
                    self.up_arrival(m, distance).wait_recv()

                    @pl.when(self.outer < top)
                    def _():
                        self.up_copy(m, distance).start()

                    spread(distance)

                @pl.when(self.outer + distance <= top)
                def _():
                    self.down_arrival(m, distance).wait_recv()

                    @pl.when(self.outer > 0)
                    def _():
                        self.down_copy(m, self.groups - distance).start()

                    spread(self.groups - distance)

            each(top, pass_on)
            self.begin(m + 1 + self.WINDOW)
        else:

            def hand_over(k):
                self.y_copy(m, k, arrival=True).wait_recv()
                self.c_copy(m, k, 1).start()

            each(self.groups, hand_over)

    def pump(self, kind, m):
        while (kind, m) in self.steps[self.at :]:
            self.step()

    def need(self, m):
        self.pump("y", m)
        if m in self.done:
            return
        self.done.add(m)

        def last(k):
            for far in range(2):
                self.c_copy(m, k, far, arrival=True).wait_recv()

        each(self.groups, last)
        self.own_copy(m).wait()

    def drain(self):
        for m in range(self.count):
            self.need(m)
            top = self.groups - 1

            def line_sends(k):
                @pl.when((self.outer < top) & (self.outer >= k))
                def _():
                    self.up_copy(m, k).wait_send()

                @pl.when((self.outer > 0) & (self.outer + k <= top))
                def _():
                    self.down_copy(m, (self.groups - k) % self.groups).wait_send()

            each(self.groups, line_sends)

            def finish_sends(k):
                self.y_copy(m, k).wait_send()
                for far in range(2):
                    self.c_copy(m, k, far).wait_send()

            each(self.groups, finish_sends)


class FedSlots(Slots):
    def __init__(self, places, sems, feed):
        super().__init__(places, sems)
        self.feed = feed
        self.started = [False] * len(places)

    def plan(self, m, piece):
        self.queue[m].append(piece)

    def fetch(self, m):
        if not self.started[m] and self.queue[m]:
            piece = self.queue[m][0]
            self.feed.need(piece)
            self.copy(m, self.feed.flat[piece]).start()
            self.started[m] = True

    def open(self, m):
        self.fetch(m)
        if not self.ready[m]:
            self.copy(m, self.feed.flat[self.queue[m][0]]).wait()
            self.ready[m] = True
        return self.places[m]

    def close(self, m):
        self.queue[m].pop(0)
        self.ready[m] = self.started[m] = False
        if self.queue[m] and self.queue[m][0] in self.feed.done:
            self.fetch(m)


def unpack_small(small, devices, lead_vec, lead_bias, side_vec, side_bias):
    width = D // devices
    per = FF // devices // width
    for d in range(devices):
        lanes = slice(d * width, d * width + width)
        block = small[d].astype(HIGH)
        lead_vec[0:16, lanes] = block[0:16, 0:width]
        side_vec[0:16, lanes] = block[16:32, 0:width]
        for i in range(per):
            first = (d * per + i) * width
            lead_bias[0:1, first : first + width] = block[32 + i : 33 + i, 0:width]
            side_bias[0:1, first : first + width] = block[40 + i : 41 + i, 0:width]


def pack_small(lead_vectors, lead_bias, side_vectors, side_bias):
    width = lead_vectors.shape[1]

    def block(rows, height):
        rows = rows.reshape(-1, width)
        return jnp.pad(rows, ((0, height - rows.shape[0]), (0, 128 - width)))

    return jnp.concatenate(
        [block(lead_vectors, 16), block(side_vectors, 16), block(lead_bias, 8), block(side_bias, 8)]
    )


def layer_kernel(crops, devices, *refs):
    refs = list(refs)

    def grab(n):
        taken = refs[:n]
        del refs[:n]
        return taken

    def named(names):
        return dict(zip(names, grab(len(names))))

    shards_in = grab(9)
    patches, orders, pos, cotangent = grab(4)
    wholes = grab(9)
    rows_out, lead_small_out, dec_small_out = grab(3)
    own, reg = named(OUT_DEC), named(OUT_REG)
    own.update(named(KEEP_DEC))
    reg.update(named(KEEP_REG))
    places = grab(4)
    lead_vec_grad, lead_bias_grad, dec_vec_grad, dec_bias_grad = grab(4)
    lead_vec, lead_bias, side_vec, side_bias, small = grab(5)
    stream, context, resid, regressed, grad, temp, pos_visible, pos_masked = grab(8)
    low_temp, first_pack, second_pack = grab(3)
    sems, small_sem, x_send, x_recv = grab(4)
    groups = devices // 4
    feed = Feed(groups, shards_in, wholes, refs)
    feed.flat = [None] + [
        w.reshape(devices * w.shape[1], w.shape[2]) for w in wholes[1:]
    ]
    section = feed.section
    tokens = crops * ROWS
    x_device = (1 - section, feed.index)
    greet([*feed.devices(), x_device])
    barrier = pltpu.get_barrier_semaphore()
    each(
        groups - 1,
        lambda k: pl.semaphore_signal(
            barrier, inc=1, device_id=feed.outer_device(k + 1), device_id_type=MESH_ID
        ),
    )
    pl.semaphore_wait(barrier, groups + 2)
    feed.begin(Feed.WINDOW)

    def x_copy(n):
        piece = (first_pack.at[0], first_pack.at[1], second_pack)[n]
        return remote(piece, piece, x_send.at[n], x_recv.at[n], x_device)

    def vectors_in(feed):
        feed.need(0)
        fetched = pltpu.make_async_copy(wholes[0], small, small_sem)
        fetched.start()
        fetched.wait()
        unpack_small(small, devices, lead_vec, lead_bias, side_vec, side_bias)

    def slots_of(feed):
        slots = FedSlots(places, sems, feed)
        for base in (1, 5, 1):
            for m in range(4):
                slots.plan(m, base + m)
        return slots

    start = feed

    @pl.when(section == 0)
    def _():
        feed = start.branch()
        slots = slots_of(feed)
        for kind, vec, bias, keep in ((0, lead_vec, lead_bias, own), (1, side_vec, side_bias, reg)):
            for c in range(crops):
                stream[crop_rows(c), :] = dot(one_hot(orders, kind, c), patches[c])
            if kind == 0:
                vectors_in(feed)
            else:
                names = ("normed", "qkv", "mixed", "second", "hidden")
                keep = {n: reg[n] for n in names}
            block_forward(keep, stream, None, resid, slots, vec, bias, regressed)
            first_pack[kind] = regressed[...].astype(LOW)
            x_copy(kind).start()
        x_copy(2).wait_recv()
        grad[...] = second_pack[...].astype(HIGH)
        block_backward(
            own, grad, temp, low_temp, slots, lead_vec, lead_vec_grad, lead_bias_grad, False, None
        )
        for c in range(crops):
            rest = grad[crop_rows(c), :]
            pick = one_hot(orders, 0, c)
            total = jnp.zeros((PATCHES, D), HIGH)
            for _ in range(3):
                part = rest.astype(LOW)
                rest = rest - part.astype(HIGH)
                total = total + dot_tn(pick, part)
            rows_out[c] = total
        pack_small_grads(lead_small_out, lead_vec_grad, lead_bias_grad, 12, devices)
        for n in range(2):
            x_copy(n).wait_send()
        feed.drain()

    @pl.when(section == 1)
    def _():
        feed = start.branch()
        slots = slots_of(feed)
        for kind, place_of in enumerate((pos_visible, pos_masked)):
            for c in range(crops):
                pick = one_hot(orders, kind, c)
                place_of[crop_rows(c), :] = sum(dot(pick, pos[t]) for t in (2, 1, 0))
        vectors_in(feed)
        stream[...] = side_vec[12:13, :] + pos_masked[...]
        for m in range(4):
            slots.fetch(m)
        feed.pump("z", 5)
        x_copy(0).wait_recv()
        context[...] = first_pack[0].astype(HIGH) + pos_visible[...]
        block_forward(reg, stream, context, resid, slots, lead_vec, lead_bias, regressed)
        stream[...] = regressed[...] + pos_masked[...]
        block_forward(own, stream, None, resid, Held(slots), side_vec, side_bias, temp)
        for c in range(crops):
            first = c * ROWS
            rows_out[c, 0:MASKED, :] = regressed[first : first + MASKED, :]
            rows_out[c, MASKED : 2 * MASKED, :] = temp[first : first + MASKED, :]
            grad[first : first + ROWS, :] = jnp.zeros((ROWS, D), HIGH)
            grad[first : first + MASKED, :] = cotangent[c].astype(HIGH)
        block_backward(
            own, grad, temp, low_temp, slots, side_vec, dec_vec_grad, dec_bias_grad, False, None
        )
        x_copy(1).wait_recv()
        inside = lax.broadcasted_iota(jnp.int32, (ROWS, D), 0) < MASKED
        for c in range(crops):
            here = crop_rows(c)
            apart = regressed[here, :] - first_pack[1, here, :].astype(HIGH)
            grad[here, :] = grad[here, :] + jnp.where(inside, apart, 0.0)
        block_backward(
            reg, grad, temp, low_temp, slots, lead_vec, lead_vec_grad, lead_bias_grad, True, context
        )
        second_pack[...] = context[...].astype(LOW)
        x_copy(2).start()
        dec_vec_grad[12:13, :] = jnp.sum(grad[...], axis=0, keepdims=True)
        pack_small_grads(lead_small_out, lead_vec_grad, lead_bias_grad, 12, devices)
        for t in range(2):
            pack_small_grads(
                dec_small_out.at[t],
                dec_vec_grad.at[:, t * (D // 2) : (t + 1) * (D // 2)],
                dec_bias_grad.at[:, t * (FF // 2) : (t + 1) * (FF // 2)],
                13,
                devices,
                2,
            )
        feed.drain()
        x_copy(2).wait_send()


def layer(crops, devices, pieces, patches, orders, pos, cotangent):
    tokens = crops * ROWS
    groups = devices // 4
    inside = [((crops, PATCHES, D), HIGH), ((devices, LEAD_SMALL, 128), HIGH)]
    inside.append(((2, devices, DEC_SMALL, 128), HIGH))
    inside += [save_shape(n, tokens) for n in OUT_DEC + OUT_REG]
    scratch = places_for([save_shape(n, tokens) for n in KEEP_DEC + KEEP_REG])
    scratch += places_for(WEIGHT_SHAPES + SMALL_SHAPES * 4)
    scratch += places_for([((devices, SMALL_ROWS, 128), LOW)])
    scratch += places_for([((tokens, D), HIGH)] * 8)
    scratch += places_for([((tokens, D), LOW), ((2, tokens, D), LOW), ((tokens, D), LOW)])
    scratch += [pltpu.SemaphoreType.DMA(s) for s in ((4,), (), (3,), (3,))]
    scratch += [pltpu.SemaphoreType.DMA((9,))]
    for width in (groups,) * 6 + (2 * groups,) * 2:
        scratch.append(pltpu.SemaphoreType.DMA((9, width)))
    wholes = [((devices,) + p.shape, p.dtype) for p in pieces]
    return pl.pallas_call(
        functools.partial(layer_kernel, crops, devices),
        out_shape=specs(wholes + inside),
        in_specs=[ANYWHERE] * 9 + [INSIDE] * 4,
        out_specs=[ANYWHERE] * 9 + [INSIDE] * len(inside),
        scratch_shapes=scratch,
        compiler_params=pltpu.CompilerParams(
            collective_id=1, has_side_effects=True, vmem_limit_bytes=60 << 20
        ),
        name="layer",
    )(*pieces, patches, orders, pos, cotangent)


LEAD_SMALL = 16
DEC_SMALL = 24
LATE = (2, 0)
AHEAD = 2
SENDS = 2


def pack_small_grads(out, vectors, bias, rows, chunks, parts=1):
    width = D // (chunks * parts)
    for d in range(chunks):
        lanes = slice(d * width, d * width + width)
        out[d, 0:rows, 0:width] = vectors[0:rows, lanes]
        for i in range(FF // D):
            first = (d * (FF // D) + i) * width
            out[d, rows + i : rows + i + 1, 0:width] = bias[0:1, first : first + width]


def sums_kernel(devices, *refs):
    refs = list(refs)
    groups, half = devices // 4, devices // 2

    def grab(n):
        taken = refs[:n]
        del refs[:n]
        return taken

    own, reg = dict(zip(OUT_DEC, grab(8))), dict(zip(OUT_REG, grab(10)))
    (lead_small_in, dec_small_in) = grab(2)
    lead_out, dec_out = grab(4), grab(4)
    vec_out, bias_out, dec_vec_out, dec_bias_out = grab(4)
    dec_far = grab(5)
    lead_own, lead_c, lead_y, lead_z = (grab(5) for _ in range(4))
    dec_own, dec_near = grab(5), grab(5)
    dec_y, dec_z = grab(5 + len(LATE)), grab(5 + len(LATE))
    late_out, late_in = grab(len(LATE)), grab(len(LATE))
    pair_buf, far_left, far_right, place_of, place_far, lead_total, dec_total = grab(7)
    pair_sem, far_sem, near_sem, load, ready, l_send, l_recv = grab(7)
    c_send, c_recv, x_send, x_recv, y_send, y_recv, u_send, u_recv, d_send, d_recv = refs
    section, index, outer, mid, core = place()
    x_device = (1 - section, index)
    mid_device = (section, slot(outer, 1 - mid, core))
    core_device = (section, slot(outer, mid, 1 - core))

    def outer_device(k):
        return (section, slot((outer + k) % groups, mid, core))

    barrier = pltpu.get_barrier_semaphore()
    greet([mid_device, core_device])

    @pl.when(section == 1)
    def _():
        greet([x_device])

    each(
        groups - 1,
        lambda k: pl.semaphore_signal(
            barrier, inc=1, device_id=outer_device(k + 1), device_id_type=MESH_ID
        ),
    )

    own_of = lead_own + [r.at[1] for r in dec_own] + [dec_own[m].at[0] for m in LATE]
    y_of, z_of = lead_y + dec_y, lead_z + dec_z

    def mine(j):
        return j * 2 + core

    def lead_core(m, j):
        return remote(
            lead_own[m].at[j * 2 + 1 - core],
            lead_c[m].at[j],
            c_send.at[m, j],
            c_recv.at[m, j],
            core_device,
        )

    def dec_core(m, t, j):
        at = 5 + 2 * m + t
        return remote(
            dec_own[m].at[t, j * 2 + 1 - core],
            dec_far[m].at[t, j],
            c_send.at[at, j],
            c_recv.at[at, j],
            core_device,
        )

    def dec_load(m, t, j):
        return pltpu.make_async_copy(
            dec_far[m].at[t, j], dec_near[m].at[j % 2], near_sem.at[m, j % 2]
        )

    def x_copy(m, j):
        return remote(
            dec_own[m].at[0, mine(j)],
            dec_own[m].at[1, mine(j)],
            x_send.at[m, j],
            x_recv.at[m, j],
            x_device,
        )

    def y_copy(n, g):
        return remote(
            own_of[n].at[mine(g * 2 + 1 - mid)],
            y_of[n].at[g],
            y_send.at[n, g],
            y_recv.at[n, g],
            mid_device,
        )

    top = groups - 1

    def up_copy(n, d):
        return remote(
            own_of[n].at[mine(d * 2 + mid)],
            z_of[n].at[d + 1],
            u_send.at[n, d],
            u_recv.at[n, d],
            outer_device(1),
        )

    def down_copy(n, d):
        return remote(
            own_of[n].at[mine(d * 2 + mid)],
            z_of[n].at[d],
            d_send.at[n, d],
            d_recv.at[n, d],
            outer_device(groups - 1),
        )

    small_loads = (
        pltpu.make_async_copy(lead_small_in, lead_own[4], load.at[0]),
        pltpu.make_async_copy(dec_small_in, dec_own[4], load.at[1]),
    )

    def lead_begin(m):
        each(half, lambda j: lead_core(m, j).start())

    def y_begin(n):
        each(groups, lambda g: y_copy(n, g).start())

    def lead_sum(m, send=False):
        def far_pair(g):
            j = g * 2 + 1 - mid
            lead_core(m, j).wait_recv()
            add_rows(lead_own[m], mine(j), lead_c[m], j)
            if send:
                y_copy(m, g).start()

        def near_pair(g):
            j = g * 2 + mid
            lead_core(m, j).wait_recv()
            add_rows(lead_own[m], mine(j), lead_c[m], j)

        each(groups, far_pair)
        each(groups, near_pair)

    def dec_begin(m):
        for t in range(2):
            each(half, lambda j: dec_core(m, t, j).start())

    def dec_sum(m):
        for t in range(2):
            dec_core(m, t, 0).wait_recv()
            dec_load(m, t, 0).start()
            for j in range(half):
                if j + 1 < half:
                    dec_core(m, t, j + 1).wait_recv()
                    dec_load(m, t, j + 1).start()
                dec_load(m, t, j).wait()
                add_rows(dec_own[m].at[t], mine(j), dec_near[m], j % 2)

    def from_mid(n):
        def add_one(d):
            y_copy(n, d).wait_recv()
            add_rows(own_of[n], mine(d * 2 + mid), y_of[n], d)

        def up_first(before):
            d = top - before

            @pl.when(d > outer)
            def _():
                add_one(d)

                @pl.when(outer == 0)
                def _():
                    up_copy(n, d).start()

        def down_first(d):
            @pl.when(d < outer)
            def _():
                add_one(d)

                @pl.when(outer == top)
                def _():
                    down_copy(n, d).start()

        each(top, up_first)
        each(top, down_first)
        y_copy(n, outer).wait_recv()

        @pl.when(outer == 0)
        def _():
            blank(z_of[n], 1)

        @pl.when(outer == top)
        def _():
            blank(z_of[n], top)

    def going_up(n):
        def hop(before):
            d = top - before

            @pl.when(d > outer)
            def _():
                up_copy(n, d).wait_recv()
                add_rows(own_of[n], mine(d * 2 + mid), z_of[n], d + 1)
                up_copy(n, d).start()

        each(top, hop)

    def going_down(n):
        def hop(d):
            @pl.when(d < outer)
            def _():
                down_copy(n, d).wait_recv()
                add_rows(own_of[n], mine(d * 2 + mid), z_of[n], d)
                down_copy(n, d).start()

        each(top, hop)

    def near_half(n):
        @pl.when((outer > 0) & (outer < groups // 2))
        def _():
            going_up(n)

        @pl.when((outer < top) & (outer >= groups // 2))
        def _():
            going_down(n)

    def far_half(n):
        @pl.when((outer > 0) & (outer < groups // 2))
        def _():
            going_down(n)

        @pl.when((outer < top) & (outer >= groups // 2))
        def _():
            going_up(n)

    def across(queue, hooks=()):
        hooks = dict(hooks)
        for i in range(len(queue) + 2):
            if i < len(queue):
                if i >= SENDS:
                    line_sent(queue[i - SENDS], True)
                from_mid(queue[i])
            if i + AHEAD < len(queue):
                y_begin(queue[i + AHEAD])
            if 1 <= i <= len(queue):
                near_half(queue[i - 1])
            if i >= 2:
                far_half(queue[i - 2])
            if i in hooks:
                hooks[i]()

    def blank(buffer, at):
        buffer[at] = jnp.zeros(buffer.shape[1:], buffer.dtype)

    class Pairs:
        def __init__(self, tasks):
            self.tasks, self.at = tasks, 0
            self.begin(0)

        def parts(self, i):
            pairs, m, _ = self.tasks[i]
            first, second = (pairs[name].shape[1] for name in PAIRS[m])
            buf = pair_buf.at[i % 2]
            return buf.at[:, 0:first], buf.at[:, first : first + second]

        def copies(self, i):
            pairs, m, joined = self.tasks[i]
            moved = []
            for side, (name, part) in enumerate(zip(PAIRS[m], self.parts(i))):
                moved.append((pairs[name], part, pair_sem.at[i % 2, side]))
            if joined:
                moved.append((pairs["normed_c"], far_left, far_sem.at[0]))
                moved.append((pairs["dkv_c"], far_right, far_sem.at[1]))
            return [pltpu.make_async_copy(*a) for a in moved]

        def begin(self, i):
            if i < len(self.tasks):
                for moved in self.copies(i):
                    moved.start()

        def take(self, out, stacked):
            i = self.at
            self.begin(i + 1)
            for moved in self.copies(i):
                moved.wait()
            pairs, m, joined = self.tasks[i]
            left, right = self.parts(i)
            extra = (far_left, far_right, place_far) if joined else None
            weight_grad(
                out,
                left,
                right,
                place_of.at[0 : left.shape[1], :],
                stacked,
                extra,
                D,
            )
            self.at += 1

    def lead_view(m):
        rows = lead_own[m].shape[1]
        return lead_own[m].reshape(devices * rows, lead_own[m].shape[2])

    def dec_view(m):
        (rows, columns), _ = WEIGHT_SHAPES[m]
        piece = dec_own[m].shape[2:]
        if piece[1] == columns:
            return dec_own[m].reshape(rows, columns), 0
        return dec_own[m].reshape(2 * devices, *piece), piece[0] // 2

    small_loads[0].start()

    def late_copy(i):
        return remote(late_out[i], late_in[i], l_send.at[i], l_recv.at[i], x_device)

    def total_of(n, where, lanes):
        total = own_of[n][mine(outer * 2 + mid), where, lanes].astype(HIGH)
        total = total + y_of[n][outer, where, lanes].astype(HIGH)
        for k in (outer + 1, outer):
            total = total + z_of[n][k, where, lanes].astype(HIGH)
        return total

    def arrive(n):
        @pl.when(outer > 0)
        def _():
            up_copy(n, outer).wait_recv()

        @pl.when(outer < top)
        def _():
            down_copy(n, outer).wait_recv()

    def emit(out, rows, columns, value):
        stacked = out.shape[-1] != columns
        step = rows // 2 if stacked else 16
        for r in range(rows // step):
            where = pl.ds(r * step, step)
            if stacked:
                for q in range(columns // 128):
                    lanes = slice(q * 128, q * 128 + 128)
                    out[:, (2 * q + r) * 128 : (2 * q + r + 1) * 128] = value(where, lanes)
            else:
                out[where, :] = value(where, slice(None))

    def finish_sum(n):
        arrive(n)
        is_dec, m = divmod(n, 5)
        if m == 4:
            total = dec_total if is_dec else lead_total
            total[...] = total_of(n, slice(None), slice(None))
            vec, bias = (dec_vec_out, dec_bias_out) if is_dec else (vec_out, bias_out)
            count, width = vec.shape
            vec[...] = total[0:count, 0:width]
            for i in range(FF // D):
                bias[0:1, i * width : i * width + width] = total[count + i : count + i + 1, 0:width]
            return
        rows, columns = own_of[n].shape[-2:]
        out = dec_out[m] if is_dec else lead_out[m]
        emit(out, rows, columns, functools.partial(total_of, n))

    def line_sent(n, ends):
        def one(d):
            @pl.when((d > outer) & ((outer == 0) if ends else (outer > 0)))
            def _():
                up_copy(n, d).wait_send()

            @pl.when((d < outer) & ((outer == top) if ends else (outer < top)))
            def _():
                down_copy(n, d).wait_send()

        each(groups, one)

    def sent(queue):
        for n in queue:
            each(groups, lambda g: y_copy(n, g).wait_send())
            line_sent(n, False)
        for n in queue[-SENDS:]:
            line_sent(n, True)

    order = (1, 3, 2, 0, 4)
    early = tuple(m for m in (3, 2, 0, 1, 4) if m not in LATE)

    @pl.when(section == 0)
    def _():
        pairs = Pairs([(own, m, False) for m in order[:4]])
        pairs.take(lead_view(order[0]), 0)
        pl.semaphore_wait(barrier, groups + 2)
        pl.semaphore_signal(ready, inc=1, device_id=x_device, device_id_type=MESH_ID)
        small_loads[0].wait()
        lead_begin(order[0])
        lead_begin(4)
        for i in range(1, 4):
            pairs.take(lead_view(order[i]), 0)
            lead_begin(order[i])
            lead_sum(order[i - 1], i <= AHEAD)
        lead_sum(order[3], 3 < AHEAD)
        lead_sum(4)

        def early_in():
            for e in early:
                each(half, lambda j: x_copy(e, j).wait_recv())

        across(order + tuple(5 + m for m in early), {4 - AHEAD: early_in})
        for m in order:
            finish_sum(m)
        for m in early:
            finish_sum(5 + m)
        for i, m in enumerate(LATE):
            late_copy(i).wait_recv()
            rows, columns = late_in[i].shape
            emit(dec_out[m], rows, columns, lambda *at: late_in[i][at].astype(HIGH))
        for m in range(5):
            each(half, lambda j: lead_core(m, j).wait_send())
        sent(order + tuple(5 + m for m in early))

    @pl.when(section == 1)
    def _():
        dec_order = (3, 2, 0, 1)
        small_loads[1].start()
        tasks = []
        for i in range(4):
            tasks.append((reg, order[i], order[i] == 0))
            tasks.append((own, dec_order[i], False))
        pairs = Pairs(tasks)
        for i in range(4):
            pairs.take(lead_view(order[i]), 0)
            if i == 0:
                pl.semaphore_wait(barrier, groups + 1)
                for moved in small_loads:
                    moved.wait()
                lead_begin(4)
                dec_begin(4)
            lead_begin(order[i])
            pairs.take(*dec_view(dec_order[i]))
            dec_begin(dec_order[i])
            lead_sum(order[i], i < AHEAD)
        lead_sum(4)
        late = tuple(10 + i for i in range(len(LATE)))
        rest = late + tuple(5 + m for m in dec_order) + (9,)

        def early_out():
            dec_sum(1)
            dec_sum(4)
            pl.semaphore_wait(ready, 1)
            for e in early:
                each(half, lambda j: x_copy(e, j).start())

        hooks = {i: functools.partial(dec_sum, m) for i, m in ((0, 3), (2, 2), (3, 0))}
        across(order + rest, hooks | {1: early_out})
        for i, n in enumerate(late):
            arrive(n)
            rows, columns = late_out[i].shape
            for r in range(rows // 16):
                where = pl.ds(r * 16, 16)
                late_out[i][where, :] = total_of(n, where, slice(None)).astype(LOW)
            late_copy(i).start()
        for m in order:
            finish_sum(m)
        for n in rest[len(LATE) :]:
            finish_sum(n)
        for m in range(5):
            each(half, lambda j: lead_core(m, j).wait_send())
            for t in range(2):
                each(half, lambda j: dec_core(m, t, j).wait_send())
        for m in early:
            each(half, lambda j: x_copy(m, j).wait_send())
        for i in range(len(LATE)):
            late_copy(i).wait_send()
        sent(order + rest)


def sums(crops, devices, own_pairs, reg_pairs, lead_small, dec_small):
    tokens = crops * ROWS
    groups, half = devices // 4, devices // 2
    dec_kinds, _ = dec_grad_shapes(devices, True)
    lead_pieces, dec_pieces, lead_outs, dec_outs = [], [], [], []
    for (shape, kind), (dec_shape, _) in zip(WEIGHT_SHAPES, dec_kinds):
        rows, columns = shape
        lead_pieces.append(((rows // devices, columns), kind))
        lead_outs.append(((rows // devices, columns), HIGH))
        dec_outs.append(((rows // (2 * devices), columns), HIGH))
        piece = dec_shape[1:] if len(dec_shape) == 3 else (rows // (2 * devices), columns)
        dec_pieces.append((piece, kind))
    lead_pieces.append(((LEAD_SMALL, 128), HIGH))
    dec_pieces.append(((DEC_SMALL, 128), HIGH))
    small_outs = []
    for rows, chunks in ((12, devices), (13, 2 * devices)):
        small_outs += [((rows, D // chunks), HIGH), ((1, FF // chunks), HIGH)]
    far = [((2, half) + s, k) for s, k in dec_pieces]
    scratch = []
    for lead in ((devices,), (half,), (groups,), (groups + 1,)):
        scratch += places_for([(lead + s, k) for s, k in lead_pieces])
    for lead in ((2, devices), (2,)):
        scratch += places_for([(lead + s, k) for s, k in dec_pieces])
    late_pieces = [dec_pieces[m] for m in LATE]
    for lead in (groups, groups + 1):
        scratch += places_for([((lead,) + s, k) for s, k in dec_pieces + late_pieces])
    scratch += places_for(late_pieces * 2)
    scratch += places_for(
        [((2, tokens, FF + D), LOW)]
        + [((tokens, D), LOW), ((tokens, 2 * D), LOW), ((FF, tokens), LOW), ((D, tokens), LOW)]
        + [((LEAD_SMALL, 128), HIGH), ((DEC_SMALL, 128), HIGH)]
    )
    scratch += [pltpu.SemaphoreType.DMA(s) for s in ((2, 2), (2,), (5, 2), (2,))]
    scratch.append(pltpu.SemaphoreType.REGULAR)
    sems = [(len(LATE),)] * 2 + [(15, half)] * 2 + [(5, half)] * 2
    sems += [(10 + len(LATE), groups)] * 6
    scratch += [pltpu.SemaphoreType.DMA(s) for s in sems]
    outs = pl.pallas_call(
        functools.partial(sums_kernel, devices),
        out_shape=specs(lead_outs + dec_outs + small_outs + far),
        in_specs=[ANYWHERE] * 20,
        out_specs=[INSIDE] * 12 + [ANYWHERE] * 5,
        scratch_shapes=scratch,
        compiler_params=pltpu.CompilerParams(
            collective_id=2, has_side_effects=True, vmem_limit_bytes=61 << 20
        ),
        name="sums",
    )(*own_pairs, *reg_pairs, lead_small, dec_small)
    lead, dec = list(outs[:4]), list(outs[4:8])
    lead += [outs[8], outs[9].reshape(-1)]
    dec += [outs[10], outs[11].reshape(-1)]
    return lead, dec


def exchange(pieces):
    return [lax.all_gather(p, "dp", axis=0) for p in pieces]


def as_small(parts, rows_of):
    flat = jnp.concatenate([p.reshape(-1) for p in parts])
    block = rows_of * 128
    padded = -(-flat.shape[0] // block) * block
    return jnp.pad(flat, (0, padded - flat.shape[0])).reshape(-1, 128)


def take_flat(flat, shapes):
    taken, offset = [], 0
    for shape in shapes:
        size = 1
        for extent in shape:
            size *= extent
        taken.append(flat[:, offset : offset + size].reshape((-1,) + shape))
        offset += size
    return taken


def spread_columns(gathered):
    return gathered.transpose(1, 0, 2).reshape(gathered.shape[1], -1)


def small_chunks(vectors, bias, chunks):
    rows, columns = vectors.shape
    cut = vectors.reshape(rows, chunks, columns // chunks).transpose(1, 0, 2).reshape(chunks, -1)
    flat = jnp.concatenate([cut, bias.reshape(chunks, -1)], axis=1)
    padded = -(-flat.shape[1] // 1024) * 1024
    return jnp.pad(flat, ((0, 0), (0, padded - flat.shape[1]))).reshape(chunks, -1, 128)


def small_pieces(chunk, rows, chunks):
    flat = chunk.reshape(-1)
    vectors = rows * (D // chunks)
    bias = FF // chunks
    return flat[:vectors].reshape(rows, D // chunks), flat[vectors : vectors + bias]


def total_grads(lead_big, lead_small, dec_big, dec_small):
    devices = lax.axis_size("dp")
    on_encoder = lax.axis_index("section") == 0
    lead_chunks = [g.reshape(devices, -1, g.shape[1]) for g in lead_big]
    lead_chunks.append(small_chunks(*lead_small, devices))
    dec_chunks = [g.reshape(2, devices, -1, g.shape[1]) for g in dec_big]
    dec_chunk_small = small_chunks(*dec_small, 2 * devices)
    dec_chunks.append(dec_chunk_small.reshape((2, devices) + dec_chunk_small.shape[1:]))
    lead_out = [
        lax.psum_scatter(g.astype(jnp.float32), "dp", scatter_dimension=0) for g in lead_chunks
    ]
    dec_out = []
    for g in dec_chunks:
        mine = jnp.where(on_encoder, jnp.zeros_like(g), g).astype(jnp.float32)
        mine = lax.psum_scatter(mine, "dp", scatter_dimension=1)
        dec_out.append(lax.psum_scatter(mine, "section", scatter_dimension=0))
    lead_vectors, lead_bias = small_pieces(lead_out[4], 12, devices)
    dec_vectors, dec_bias = small_pieces(dec_out[4], 13, 2 * devices)
    return lead_out[:4] + [lead_vectors, lead_bias], dec_out[:4] + [dec_vectors, dec_bias]


def run_fused(crops, devices, patches, cotangent, orders, lead, side, smalls):
    pieces = [pack_small(*smalls)] + lead + side
    outs = layer(crops, devices, pieces, patches, orders, position_parts(), cotangent)
    rows, lead_small, dec_small, *pairs = outs[9:]
    own_pairs, reg_pairs = pairs[: len(OUT_DEC)], pairs[len(OUT_DEC) :]
    return (rows, *sums(crops, devices, own_pairs, reg_pairs, lead_small, dec_small))


def run_apart(crops, devices, patches, cotangent, orders, lead, side, smalls):
    on_encoder = lax.axis_index("section") == 0
    wholes = exchange(lead + side + [as_small(smalls, 16)])
    big = [w.reshape(-1, w.shape[2]) for w in wholes[:8]]
    flat = wholes[8].reshape(devices, -1).astype(jnp.float32)
    lv, lb, sv, sb = take_flat(flat, [p.shape for p in smalls])

    def sixteen(vectors):
        rows = spread_columns(vectors)
        return jnp.pad(rows, ((0, 16 - rows.shape[0]), (0, 0)))

    lead_w, side_w = big[:4], big[4:]
    lead_small = [sixteen(lv), lb.reshape(1, -1)]
    all_small = lead_small + [sixteen(sv), sb.reshape(1, -1)]
    pack, pos_visible, pos_masked, *enc_saved = encode(
        crops, patches, orders, position_parts(), lead_w, side_w, all_small
    )
    arrived = passed_along(pack, "section", 1)
    grad_latents, latent_rows, reg_vec, reg_bias, dec_vec, dec_bias, *pairs = regress(
        crops, arrived, pos_visible, pos_masked, cotangent, lead_w, side_w, all_small
    )
    reg_pairs, dec_pairs = pairs[: len(OUT_REG)], pairs[len(OUT_REG) :]
    returned = passed_along(grad_latents, "section", -1)
    dec_big = decoder_weights(crops, dec_pairs, devices, False)
    *lead_big, grad_rows, enc_vec, enc_bias = finish(
        crops, returned, orders, lead_w, lead_small, enc_saved, reg_pairs
    )
    vec = jnp.where(on_encoder, enc_vec, reg_vec)[:12]
    bias = jnp.where(on_encoder, enc_bias, reg_bias)
    rows = jnp.where(on_encoder, grad_rows, latent_rows)
    lead_small, dec_small = (vec, bias[0]), (dec_vec[:13], dec_bias[0])
    return (rows, *total_grads(lead_big, lead_small, dec_big, dec_small))


def padded_orders(ordering, part):
    cut = ordering[:, MASKED:] if part == 0 else ordering[:, :MASKED]
    cut = jnp.pad(cut, ((0, 0), (0, ROWS - MASKED)), constant_values=-1)
    return cut.reshape(-1, 1)


def shards(
    patches,
    cotangent,
    ordering,
    lead_qkv,
    lead_proj,
    lead_up,
    lead_down,
    lead_vectors,
    lead_bias,
    side_qkv,
    side_proj,
    side_up,
    side_down,
    side_vectors,
    side_bias,
):
    devices = lax.axis_size("dp")
    crops = patches.shape[0]
    orders = jnp.stack([padded_orders(ordering, 0), padded_orders(ordering, 1)])
    lead = [lead_qkv[0], lead_proj[0], lead_up[0], lead_down[0]]
    side = [side_qkv[0], side_proj[0], side_up[0], side_down[0]]
    smalls = [lead_vectors[0], lead_bias[0], side_vectors[0], side_bias[0]]
    own_path = devices % 4 == 0 and lead[0].shape[0] % 16 == 0
    run = run_fused if own_path else run_apart
    rows, lead_out, dec_out = run(
        crops, devices, patches, cotangent, orders, lead, side, smalls
    )
    return (rows[None],) + tuple(o[None] for o in lead_out) + tuple(dec_out)


def solution(mesh):
    return jax.shard_map(
        shards,
        mesh=mesh,
        in_specs=(
            P("dp", None, None),
            P("dp", None, None),
            P("dp", None),
            P("section", "dp", None),
            P("section", "dp", None),
            P("section", "dp", None),
            P("section", "dp", None),
            P("section", None, "dp"),
            P("section", "dp"),
            P("section", "dp", None),
            P("section", "dp", None),
            P("section", "dp", None),
            P("section", "dp", None),
            P("section", None, "dp"),
            P("section", "dp"),
        ),
        out_specs=(
            P("section", "dp", None, None),
            P("section", "dp", None),
            P("section", "dp", None),
            P("section", "dp", None),
            P("section", "dp", None),
            P("section", None, "dp"),
            P("section", "dp"),
            P(("section", "dp"), None),
            P(("section", "dp"), None),
            P(("section", "dp"), None),
            P(("section", "dp"), None),
            P(None, ("section", "dp")),
            P(("section", "dp")),
        ),
        check_vma=False,
    )
```

```python
import copy
import functools

import jax
import jax.experimental.pallas as pl
import jax.experimental.pallas.tpu as pltpu
import jax.numpy as jnp
import numpy as np
from jax import lax
from jax.sharding import PartitionSpec as P

D = 768
HEADS = 12
HEAD_DIM = 64
FF = 3072
GRID = 14
PATCHES = 196
MASKED = 98


def passed_along(array, axis, by):
    count = lax.axis_size(axis)
    pairs = [(i, i + by) for i in range(count) if 0 <= i + by < count]
    return lax.ppermute(array, axis, pairs)


def positions():
    ids = np.arange(PATCHES)
    quarter = D // 4
    frequency = 10000.0 ** (-np.arange(quarter) / quarter)
    rows = (ids // GRID)[:, None] * frequency
    cols = (ids % GRID)[:, None] * frequency
    return np.concatenate([np.sin(cols), np.cos(cols), np.sin(rows), np.cos(rows)], axis=1)


def position_parts():
    rest = positions().astype(np.float32)
    parts = []
    for _ in range(3):
        part = rest.astype(jnp.bfloat16)
        rest = rest - part.astype(np.float32)
        parts.append(part)
    return jnp.asarray(np.stack(parts))


MESH_ID = pl.DeviceIdType.MESH


def each(count, body):
    if count <= 4:
        for k in range(count):
            body(k)
    else:
        lax.fori_loop(0, count, lambda k, carry: (body(k), carry)[1], 0)


def place():
    section = lax.axis_index("section")
    index = lax.axis_index("dp")
    return section, index, index // 4, (index // 2) % 2, index % 2


def slot(outer, mid, core):
    return outer * 4 + mid * 2 + core


def remote(src, dst, send_sem, recv_sem, device):
    return pltpu.make_async_remote_copy(
        src_ref=src,
        dst_ref=dst,
        send_sem=send_sem,
        recv_sem=recv_sem,
        device_id=device,
        device_id_type=MESH_ID,
    )


def greet(devices):
    barrier = pltpu.get_barrier_semaphore()
    for device in devices:
        pl.semaphore_signal(barrier, inc=1, device_id=device, device_id_type=MESH_ID)


def add_rows(target, at, other, other_at):
    rows = target.shape[-2]
    step = 16 if target.dtype == jnp.bfloat16 else 8

    def body(r, carry):
        where = pl.ds(r * step, step)
        total = target[at, where, :].astype(jnp.float32) + other[other_at, where, :].astype(
            jnp.float32
        )
        target[at, where, :] = total.astype(target.dtype)
        return carry

    lax.fori_loop(0, rows // step, body, 0, unroll=True)


ROWS = 112
LOW = jnp.bfloat16
HIGH = jnp.float32
VISIBLE = PATCHES - MASKED
CHUNK = 32
NAMES_SELF = ("normed", "qkv", "probs", "mixed", "attn", "x1", "r1", "x2", "r2", "second")
NAMES_SELF += ("slope", "hidden", "branch", "x3", "r3")
NAMES_CROSS = ("normed_c", "kv_c", "probs_c", "x1_c", "r1_c")
NAMES_GRAD = ("dqkv", "dattn", "dpre", "dbranch")


def save_shape(name, tokens):
    pairs = tokens // ROWS * (HEADS // 2)
    kinds = {
        "qkv": ((tokens, 3 * D), LOW),
        "kv_c": ((tokens, 2 * D), LOW),
        "dqkv": ((tokens, 3 * D), LOW),
        "dkv_c": ((tokens, 2 * D), LOW),
        "probs": ((pairs, 2 * ROWS, ROWS), HIGH),
        "probs_c": ((pairs, 2 * ROWS, ROWS), HIGH),
        "hidden": ((tokens, FF), LOW),
        "dpre": ((tokens, FF), LOW),
        "slope": ((tokens, FF), HIGH),
    }
    if name in kinds:
        return kinds[name]
    if name in ("r1", "r2", "r3", "r1_c"):
        return ((tokens, 1), HIGH)
    if name in ("attn", "x1", "x1_c", "x2", "x3", "branch"):
        return ((tokens, D), HIGH)
    return ((tokens, D), LOW)


def dot(left, right):
    return jnp.dot(left, right, preferred_element_type=HIGH)


def dot_nt(left, right):
    return lax.dot_general(left, right, (((1,), (1,)), ((), ())), preferred_element_type=HIGH)


def dot_tn(left, right):
    return lax.dot_general(left, right, (((0,), (0,)), ((), ())), preferred_element_type=HIGH)


def by_rows(tokens, body, init=()):
    def step(i, carry):
        return body(pl.ds(pl.multiple_of(i * CHUNK, CHUNK), CHUNK), carry)

    return lax.fori_loop(0, tokens // CHUNK, step, init, unroll=True)


def tiles(width, body, size=256, unroll=True):
    def step(i, carry):
        body(pl.ds(pl.multiple_of(i * size, size), size))
        return carry

    lax.fori_loop(0, width // size, step, 0, unroll=unroll)


def fold(values):
    return jnp.sum(values.reshape(-1, 8, values.shape[-1]), axis=0)


def norm_forward(source, gain, shift, kept, spread, low, out=None):
    def body(where, carry):
        values = source[where, :]
        center = values - jnp.mean(values, axis=-1, keepdims=True)
        scale = lax.rsqrt(jnp.mean(center * center, axis=-1, keepdims=True) + 1e-06)
        center = center * scale
        if kept is not None:
            kept[where, :] = center
            spread[where, :] = scale
        result = center * gain + shift
        if low is not None:
            low[where, :] = result.astype(LOW)
        if out is not None:
            out[where, :] = result
        return carry

    by_rows(source.shape[0], body)


def norm_grad(grad, gain, center, scale):
    weighted = grad * gain
    first = jnp.mean(weighted, axis=-1, keepdims=True)
    second = jnp.mean(weighted * center, axis=-1, keepdims=True)
    return scale * (weighted - first - center * second)


def pair_masks(rows):
    lane = lax.broadcasted_iota(jnp.int32, (rows, 2 * HEAD_DIM), 1)
    return lane < HEAD_DIM


def two_heads(values):
    low_lanes = pair_masks(values.shape[0])
    zero = jnp.zeros_like(values)
    return jnp.concatenate(
        [jnp.where(low_lanes, values, zero), jnp.where(low_lanes, zero, values)], axis=0
    )


def one_pair(stacked):
    half = stacked.shape[0] // 2
    return jnp.where(pair_masks(half), stacked[:half], stacked[half:])


def head_loop(tokens, body):
    def step(p, carry):
        for crop in range(tokens // ROWS):
            rows = pl.ds(crop * ROWS, ROWS)
            body(crop * (HEADS // 2) + p, rows, p)
        return carry

    lax.fori_loop(0, HEADS // 2, step, 0, unroll=True)


def lanes_of(p, base):
    return pl.ds(pl.multiple_of(base + p * 128, 128), 128)


def attention(s, cross):
    tokens = s["normed"].shape[0]
    valid = lax.broadcasted_iota(jnp.int32, (2 * ROWS, ROWS), 1) < MASKED

    def body(at, rows, p):
        q2 = two_heads(s["qkv"][rows, lanes_of(p, 0)])
        sources = [(s["qkv"][rows, lanes_of(p, D)], s["qkv"][rows, lanes_of(p, 2 * D)], "probs")]
        if cross:
            sources.append(
                (s["kv_c"][rows, lanes_of(p, 0)], s["kv_c"][rows, lanes_of(p, D)], "probs_c")
            )
        scores = [
            jnp.where(valid, dot_nt(q2, k) * HEAD_DIM ** (-0.5), -1e30) for k, _, _ in sources
        ]
        top = jnp.max(scores[0], axis=-1, keepdims=True)
        if cross:
            top = jnp.maximum(top, jnp.max(scores[1], axis=-1, keepdims=True))
        powers = [jnp.exp(x - top) for x in scores]
        mass = jnp.sum(powers[0], axis=-1, keepdims=True)
        if cross:
            mass = mass + jnp.sum(powers[1], axis=-1, keepdims=True)
        mixed = None
        inverse = 1.0 / mass
        for power, (_, v, name) in zip(powers, sources):
            probs = power * inverse
            if name in s:
                s[name][at] = probs
            part = dot(probs.astype(LOW), v)
            mixed = part if mixed is None else mixed + part
        s["mixed"][rows, lanes_of(p, 0)] = one_pair(mixed).astype(LOW)

    head_loop(tokens, body)


def block_forward(s, stream, context, resid, weights, vectors, bias, out):
    def row(r, where=slice(None)):
        return vectors[r : r + 1, where]

    norm_forward(stream, row(0), row(1), s.get("x1"), s.get("r1"), s["normed"])
    if context is not None:
        norm_forward(context, row(0), row(1), s["x1_c"], s["r1_c"], s["normed_c"])
    w = weights.open(0)

    def qkv_tile(j):
        where = slice(j * 256, j * 256 + 256)
        kind, local = divmod(j, 3)
        extra = None if kind == 1 else row(6 if kind == 0 else 7, slice(local * 256, local * 256 + 256))
        values = dot(s["normed"][...], w[:, where])
        s["qkv"][:, where] = (values if extra is None else values + extra).astype(LOW)
        if context is not None and kind > 0:
            values = dot(s["normed_c"][...], w[:, where])
            here = slice(j * 256 - D, j * 256 - D + 256)
            s["kv_c"][:, here] = (values if extra is None else values + extra).astype(LOW)

    for j in range(9):
        qkv_tile(j)
    weights.close(0)
    attention(s, context is not None)
    w = weights.open(1)
    for j in range(3):
        where = slice(j * 256, j * 256 + 256)
        attn = dot(s["mixed"][...], w[:, where]) + row(8, where)
        if "attn" in s:
            s["attn"][:, where] = attn
        resid[:, where] = stream[:, where] + row(10, where) * attn
    weights.close(1)
    norm_forward(resid, row(2), row(3), s.get("x2"), s.get("r2"), s["second"])
    w = weights.open(2)

    def up_tile(where):
        pre = dot(s["second"][...], w[:, where]) + bias[0:1, where]
        phi = 0.5 + 0.5 * lax.erf(pre * 0.5**0.5)
        s["hidden"][:, where] = (pre * phi).astype(LOW)
        if "slope" in s:
            s["slope"][:, where] = phi + pre * jnp.exp(-0.5 * pre * pre) * 0.3989422804014327

    tiles(FF, up_tile)
    weights.close(2)
    w = weights.open(3)
    for j in range(3):
        where = slice(j * 256, j * 256 + 256)
        branch = dot(s["hidden"][...], w[:, where]) + row(9, where)
        if "branch" in s:
            s["branch"][:, where] = branch
        resid[:, where] = resid[:, where] + row(11, where) * branch
    weights.close(3)
    norm_forward(resid, row(4), row(5), s.get("x3"), s.get("r3"), None, out)


def attention_backward(s, grad_mixed, cross):
    tokens = s["normed"].shape[0]
    scale = HEAD_DIM ** (-0.5)

    def body(at, rows, p):
        q2 = two_heads(s["qkv"][rows, lanes_of(p, 0)])
        g2 = two_heads(grad_mixed[rows, lanes_of(p, 0)])
        sources = [("qkv", D, "dqkv", "probs")]
        if cross:
            sources.append(("kv_c", 0, "dkv_c", "probs_c"))
        parts = []
        inner = None
        for name, base, grad_name, probs_name in sources:
            v = s[name][rows, lanes_of(p, base + D)]
            probs = s[probs_name][at]
            s[grad_name][rows, lanes_of(p, base + D)] = dot_tn(probs.astype(LOW), g2).astype(LOW)
            dprobs = dot_nt(g2, v)
            parts.append((probs, dprobs))
            total = jnp.sum(dprobs * probs, axis=-1, keepdims=True)
            inner = total if inner is None else inner + total
        dq = None
        for (probs, dprobs), (name, base, grad_name, _) in zip(parts, sources):
            dscores = (probs * (dprobs - inner)).astype(LOW)
            part = dot(dscores, s[name][rows, lanes_of(p, base)])
            dq = part if dq is None else dq + part
            s[grad_name][rows, lanes_of(p, base)] = (dot_tn(dscores, q2) * scale).astype(LOW)
        s["dqkv"][rows, lanes_of(p, 0)] = (one_pair(dq) * scale).astype(LOW)

    head_loop(tokens, body)


def block_backward(s, grad, temp, low_temp, weights, vectors, vec_grad, bias_grad, cross, context_grad):
    tokens = grad.shape[0]
    zero = jnp.zeros((8, D), HIGH)

    def row(r):
        return vectors[r : r + 1, :]

    def put(r, total):
        vec_grad[r : r + 1, :] = jnp.sum(total, axis=0, keepdims=True)

    def final_rows(where, sums):
        gain, shift, scale, offset = sums
        g = grad[where, :]
        center = s["x3"][where, :]
        gf = norm_grad(g, row(4), center, s["r3"][where, :])
        grad[where, :] = gf
        low = (row(11) * gf).astype(LOW)
        s["dbranch"][where, :] = low
        return (
            gain + fold(g * center),
            shift + fold(g),
            scale + fold(gf * s["branch"][where, :]),
            offset + fold(low.astype(HIGH)),
        )

    sums = by_rows(tokens, final_rows, (zero,) * 4)
    for r, total in zip((4, 5, 11, 9), sums):
        put(r, total)
    w = weights.open(3)

    def down_tile(where):
        low = (dot_nt(s["dbranch"][...], w[where, :]) * s["slope"][:, where]).astype(LOW)
        s["dpre"][:, where] = low
        bias_grad[0:1, where] = jnp.sum(low.astype(HIGH), axis=0, keepdims=True)

    tiles(FF, down_tile)
    weights.close(3)
    w = weights.open(2)
    for j in range(3):
        where = slice(j * 256, j * 256 + 256)
        temp[:, where] = dot_nt(s["dpre"][...], w[where, :])
    weights.close(2)

    def second_rows(where, sums):
        gain, shift, scale, offset = sums
        g = temp[where, :]
        center = s["x2"][where, :]
        gr = norm_grad(g, row(2), center, s["r2"][where, :]) + grad[where, :]
        grad[where, :] = gr
        low = (row(10) * gr).astype(LOW)
        s["dattn"][where, :] = low
        return (
            gain + fold(g * center),
            shift + fold(g),
            scale + fold(gr * s["attn"][where, :]),
            offset + fold(low.astype(HIGH)),
        )

    sums = by_rows(tokens, second_rows, (zero,) * 4)
    for r, total in zip((2, 3, 10, 8), sums):
        put(r, total)
    w = weights.open(1)
    for j in range(3):
        where = slice(j * 256, j * 256 + 256)
        low_temp[:, where] = dot_nt(s["dattn"][...], w[where, :]).astype(LOW)
    weights.close(1)
    attention_backward(s, low_temp, cross)
    w = weights.open(0)
    for j in range(3):
        where = slice(j * 256, j * 256 + 256)
        temp[:, where] = dot_nt(s["dqkv"][...], w[where, :])
        if cross:
            context_grad[:, where] = dot_nt(s["dkv_c"][...], w[where, D:])
    weights.close(0)

    def first_rows(where, sums):
        gain, shift, dq, dv = sums
        g = temp[where, :]
        center = s["x1"][where, :]
        grad[where, :] = grad[where, :] + norm_grad(g, row(0), center, s["r1"][where, :])
        gain, shift = gain + fold(g * center), shift + fold(g)
        dq = dq + fold(s["dqkv"][where, 0:D].astype(HIGH))
        dv = dv + fold(s["dqkv"][where, 2 * D :].astype(HIGH))
        if cross:
            g = context_grad[where, :]
            center = s["x1_c"][where, :]
            context_grad[where, :] = norm_grad(g, row(0), center, s["r1_c"][where, :])
            gain, shift = gain + fold(g * center), shift + fold(g)
            dv = dv + fold(s["dkv_c"][where, D:].astype(HIGH))
        return gain, shift, dq, dv

    sums = by_rows(tokens, first_rows, (zero,) * 4)
    for r, total in zip((0, 1, 6, 7), sums):
        put(r, total)


class Slots:
    def __init__(self, places, sems):
        self.places, self.sems = places, sems
        self.queue = [[] for _ in places]
        self.ready = [False] * len(places)

    def copy(self, m, source):
        return pltpu.make_async_copy(source, self.places[m], self.sems.at[m])

    def plan(self, m, source):
        self.queue[m].append(source)
        if len(self.queue[m]) == 1:
            self.copy(m, source).start()

    def open(self, m):
        if not self.ready[m]:
            self.copy(m, self.queue[m][0]).wait()
            self.ready[m] = True
        return self.places[m]

    def close(self, m):
        self.queue[m].pop(0)
        self.ready[m] = False
        if self.queue[m]:
            self.copy(m, self.queue[m][0]).start()


class Held:
    def __init__(self, slots):
        self.slots = slots

    def open(self, m):
        return self.slots.open(m)

    def close(self, m):
        pass


def transposed(place, source):
    width = source.shape[1]
    for j in range(width // 256):
        where = slice(j * 256, j * 256 + 256)
        place[where, :] = source[:, where].T


def weight_grad(out, left, right, place, stacked=0, extra=None, base=0):
    rows, columns = left.shape[1], right.shape[1]
    transposed(place, left)
    if extra is not None:
        transposed(extra[2], extra[0])

    def column_tile(j, with_extra):
        where = pl.ds(pl.multiple_of(j * 256, 256), 256)
        for i in range(rows // 384):
            down = slice(i * 384, i * 384 + 384)
            total = dot(place[down, :], right[:, where])
            if with_extra:
                there = pl.ds(pl.multiple_of(j * 256 - base, 256), 256)
                total = total + dot(extra[2][down, :], extra[1][:, there])
            if stacked:
                count = 384 // stacked
                cut = total.reshape(count, stacked, 256)
                both = jnp.concatenate([cut[:, :, :128], cut[:, :, 128:]], axis=1)
                here = pl.ds(pl.multiple_of(j * 128, 128), 128)
                out[i * count : (i + 1) * count, :, here] = both.astype(LOW)
            else:
                out[down, where] = total.astype(LOW)

    def plain(j, carry):
        column_tile(j, False)
        return carry

    def joined(j, carry):
        column_tile(j, True)
        return carry

    first = base // 256 if extra is not None else columns // 256
    lax.fori_loop(0, first, plain, 0, unroll=True)
    if extra is not None:
        lax.fori_loop(first, columns // 256, joined, 0, unroll=True)


def crop_rows(c):
    return slice(c * ROWS, c * ROWS + ROWS)


def one_hot(orders, kind, crop):
    ids = orders[kind, crop_rows(crop), :]
    return (ids == lax.broadcasted_iota(jnp.int32, (ROWS, PATCHES), 1)).astype(LOW)


def encode_kernel(crops, *refs):
    refs = list(refs)
    patches, orders, pos = refs[:3]
    lead_w, side_w = refs[3:7], refs[7:11]
    lead_vec, lead_bias, side_vec, side_bias = refs[11:15]
    pack, pos_visible, pos_masked = refs[15:18]
    refs = refs[18:]
    saved = dict(zip(NAMES_SELF, refs))
    refs = refs[len(NAMES_SELF) :]
    places, (sems, stream, resid, latent) = refs[:4], refs[4:8]
    brief = dict(zip(("normed", "qkv", "mixed", "second", "hidden"), refs[8:13]))
    section = lax.axis_index("section")

    @pl.when(section == 0)
    def _():
        slots = Slots(places, sems)
        for source in (lead_w, side_w):
            for m in range(4):
                slots.plan(m, source[m])
        for kind in range(2):
            for c in range(crops):
                rows = dot(one_hot(orders, kind, c), patches[c])
                stream[crop_rows(c), :] = rows
            if kind == 0:
                block_forward(saved, stream, None, resid, slots, lead_vec, lead_bias, latent)
            else:
                block_forward(brief, stream, None, resid, slots, side_vec, side_bias, latent)
            pack[kind] = latent[...].astype(LOW)

    @pl.when(section == 1)
    def _():
        for kind, place_of in enumerate((pos_visible, pos_masked)):
            for c in range(crops):
                pick = one_hot(orders, kind, c)
                place_of[crop_rows(c), :] = sum(dot(pick, pos[t]) for t in (2, 1, 0))


def regress_kernel(crops, *refs):
    refs = list(refs)
    pack, pos_visible, pos_masked, cotangent = refs[:4]
    lead_w, side_w = refs[4:8], refs[8:12]
    lead_vec, lead_bias, side_vec, side_bias = refs[12:16]
    refs = refs[16:]

    def grab(names):
        taken = dict(zip(names, refs))
        del refs[: len(names)]
        return taken

    grad_latents, rows_out, reg_vec, reg_bias, dec_vec, dec_bias = refs[:6]
    del refs[:6]
    reg, dec = grab(OUT_REG), grab(OUT_DEC)
    reg.update(grab(KEEP_REG))
    dec.update(grab(KEEP_DEC))
    places = refs[:4]
    sems, stream, context, resid, regressed, grad, temp, low_temp = refs[4:]
    tokens = crops * ROWS

    @pl.when(lax.axis_index("section") == 1)
    def _():
        slots = Slots(places, sems)
        for source in (lead_w, side_w, lead_w):
            for m in range(4):
                slots.plan(m, source[m])
        stream[...] = side_vec[12:13, :] + pos_masked[...]
        context[...] = pack[0].astype(HIGH) + pos_visible[...]
        block_forward(reg, stream, context, resid, slots, lead_vec, lead_bias, regressed)
        stream[...] = regressed[...] + pos_masked[...]
        block_forward(dec, stream, None, resid, Held(slots), side_vec, side_bias, temp)
        for c in range(crops):
            first = c * ROWS
            rows_out[c, 0:MASKED, :] = regressed[first : first + MASKED, :]
            rows_out[c, MASKED : 2 * MASKED, :] = temp[first : first + MASKED, :]
            grad[first : first + ROWS, :] = jnp.zeros((ROWS, D), HIGH)
            grad[first : first + MASKED, :] = cotangent[c].astype(HIGH)
        block_backward(
            dec, grad, temp, low_temp, slots, side_vec, dec_vec, dec_bias, False, None
        )
        inside = lax.broadcasted_iota(jnp.int32, (ROWS, D), 0) < MASKED
        for c in range(crops):
            here = crop_rows(c)
            apart = regressed[here, :] - pack[1, here, :].astype(HIGH)
            grad[here, :] = grad[here, :] + jnp.where(inside, apart, 0.0)
        block_backward(
            reg, grad, temp, low_temp, slots, lead_vec, reg_vec, reg_bias, True, context
        )
        dec_vec[12:13, :] = jnp.sum(grad[...], axis=0, keepdims=True)
        grad_latents[...] = context[...].astype(LOW)


PAIRS = (("normed", "dqkv"), ("mixed", "dattn"), ("second", "dpre"), ("hidden", "dbranch"))
OUT_DEC = tuple(n for pair in PAIRS for n in pair)
OUT_REG = OUT_DEC + ("normed_c", "dkv_c")
KEEP_DEC = tuple(n for n in NAMES_SELF if n not in OUT_DEC)
KEEP_REG = KEEP_DEC + tuple(n for n in NAMES_CROSS if n not in OUT_REG)


def ship(m, scratch, outs, sems):
    return pltpu.make_async_copy(scratch[m], outs[m], sems.at[m])


def decoder_weights_kernel(stacks, *refs):
    pairs, outs = dict(zip(OUT_DEC, refs[:8])), refs[8:12]
    scratch, (place, sems) = refs[12:16], refs[16:]

    @pl.when(lax.axis_index("section") == 1)
    def _():
        for m in (3, 2, 1, 0):
            left, right = PAIRS[m]
            rows = pairs[left].shape[1]
            weight_grad(
                scratch[m], pairs[left], pairs[right], place.at[0:rows, :], stacks[m]
            )
            ship(m, scratch, outs, sems).start()
        for m in range(4):
            ship(m, scratch, outs, sems).wait()


def finish_kernel(crops, *refs):
    refs = list(refs)
    returned, orders = refs[:2]
    lead_w, lead_vec, lead_bias = refs[2:6], refs[6], refs[7]
    del refs[:8]

    def grab(names):
        taken = dict(zip(names, refs))
        del refs[: len(names)]
        return taken

    enc, reg = grab(NAMES_SELF), grab(OUT_REG)
    outs, (rows_out, enc_vec, enc_bias) = refs[:4], refs[4:7]
    del refs[:7]
    enc.update(grab(NAMES_GRAD))
    places = refs[:4]
    scratch = refs[4:8]
    sems, out_sems, place, place_c, grad, temp, low_temp = refs[8:]
    section = lax.axis_index("section")

    def weights_of(pairs, joined):
        for m in (3, 2, 1, 0):
            left, right = PAIRS[m]
            rows = pairs[left].shape[1]
            extra = (pairs["normed_c"], pairs["dkv_c"], place_c) if joined and m == 0 else None
            weight_grad(
                scratch[m], pairs[left], pairs[right], place.at[0:rows, :], 0, extra, D
            )
            ship(m, scratch, outs, out_sems).start()
        for m in range(4):
            ship(m, scratch, outs, out_sems).wait()

    @pl.when(section == 0)
    def _():
        slots = Slots(places, sems)
        for m in (3, 2, 1, 0):
            slots.plan(m, lead_w[m])
        grad[...] = returned[...].astype(HIGH)
        block_backward(enc, grad, temp, low_temp, slots, lead_vec, enc_vec, enc_bias, False, None)
        for c in range(crops):
            rest = grad[crop_rows(c), :]
            pick = one_hot(orders, 0, c)
            total = jnp.zeros((PATCHES, D), HIGH)
            for _ in range(3):
                part = rest.astype(LOW)
                rest = rest - part.astype(HIGH)
                total = total + dot_tn(pick, part)
            rows_out[c] = total
        weights_of(enc, False)

    @pl.when(section == 1)
    def _():
        weights_of(reg, True)


ANYWHERE = pl.BlockSpec(memory_space=pl.ANY)
INSIDE = pl.BlockSpec(memory_space=pltpu.VMEM)


def specs(shapes):
    return [jax.ShapeDtypeStruct(s, d) for s, d in shapes]


def places_for(shapes):
    return [pltpu.VMEM(s, d) for s, d in shapes]


def params():
    return pltpu.CompilerParams(vmem_limit_bytes=60 << 20)


WEIGHT_SHAPES = [((D, 3 * D), LOW), ((D, D), LOW), ((D, FF), LOW), ((FF, D), LOW)]
SMALL_SHAPES = [((16, D), HIGH), ((1, FF), HIGH)]


def encode(crops, patches, orders, pos, lead_w, side_w, smalls):
    tokens = crops * ROWS
    shapes = [((2, tokens, D), LOW), ((tokens, D), HIGH), ((tokens, D), HIGH)]
    shapes += [save_shape(n, tokens) for n in NAMES_SELF]
    scratch = places_for(WEIGHT_SHAPES) + [pltpu.SemaphoreType.DMA((4,))]
    scratch += places_for([((tokens, D), HIGH)] * 3)
    scratch += places_for(
        [save_shape(n, tokens) for n in ("normed", "qkv", "mixed", "second", "hidden")]
    )
    return pl.pallas_call(
        functools.partial(encode_kernel, crops),
        out_shape=specs(shapes),
        in_specs=[INSIDE] * 3 + [ANYWHERE] * 8 + [INSIDE] * 4,
        out_specs=[INSIDE] * len(shapes),
        scratch_shapes=scratch,
        compiler_params=params(),
        name="encode",
    )(patches, orders, pos, *lead_w, *side_w, *smalls)


def regress(crops, pack, pos_visible, pos_masked, cotangent, lead_w, side_w, smalls):
    tokens = crops * ROWS
    shapes = [((tokens, D), LOW), ((crops, PATCHES, D), HIGH)] + SMALL_SHAPES * 2
    shapes += [save_shape(n, tokens) for n in OUT_REG + OUT_DEC]
    scratch = places_for([save_shape(n, tokens) for n in KEEP_REG + KEEP_DEC])
    scratch += places_for(WEIGHT_SHAPES) + [pltpu.SemaphoreType.DMA((4,))]
    scratch += places_for([((tokens, D), HIGH)] * 6 + [((tokens, D), LOW)])
    return pl.pallas_call(
        functools.partial(regress_kernel, crops),
        out_shape=specs(shapes),
        in_specs=[INSIDE] * 4 + [ANYWHERE] * 8 + [INSIDE] * 4,
        out_specs=[INSIDE] * len(shapes),
        scratch_shapes=scratch,
        compiler_params=params(),
        name="regress",
    )(pack, pos_visible, pos_masked, cotangent, *lead_w, *side_w, *smalls)


def dec_grad_shapes(devices, own_path):
    shapes, stacks = [], []
    for (rows, columns), kind in WEIGHT_SHAPES:
        r = rows // (2 * devices)
        stack = r if own_path and r % 16 else 0
        stacks.append(stack)
        shapes.append(
            ((2 * devices, 2 * r, columns // 2), kind) if stack else ((rows, columns), kind)
        )
    return shapes, tuple(stacks)


def decoder_weights(crops, pairs, devices, own_path):
    shapes, stacks = dec_grad_shapes(devices, own_path)
    return pl.pallas_call(
        functools.partial(decoder_weights_kernel, stacks),
        out_shape=specs(shapes),
        in_specs=[INSIDE] * 8,
        out_specs=[ANYWHERE] * 4,
        scratch_shapes=places_for(shapes)
        + places_for([((FF, crops * ROWS), LOW)])
        + [pltpu.SemaphoreType.DMA((4,))],
        compiler_params=params(),
        name="decoder_weights",
    )(*pairs)


def finish(crops, returned, orders, lead_w, lead_small, enc_saved, reg_pairs):
    tokens = crops * ROWS
    shapes = WEIGHT_SHAPES + [((crops, PATCHES, D), HIGH)] + SMALL_SHAPES
    scratch = places_for([save_shape(n, tokens) for n in NAMES_GRAD])
    scratch += places_for(WEIGHT_SHAPES * 2) + [pltpu.SemaphoreType.DMA((4,))] * 2
    scratch += places_for([((FF, tokens), LOW), ((D, tokens), LOW)])
    scratch += places_for([((tokens, D), HIGH)] * 2 + [((tokens, D), LOW)])
    count = len(enc_saved) + len(reg_pairs)
    return pl.pallas_call(
        functools.partial(finish_kernel, crops),
        out_shape=specs(shapes),
        in_specs=[INSIDE] * 2 + [ANYWHERE] * 4 + [INSIDE] * (2 + count),
        out_specs=[ANYWHERE] * 4 + [INSIDE] * 3,
        scratch_shapes=scratch,
        compiler_params=params(),
        name="finish",
    )(returned, orders, *lead_w, *lead_small, *enc_saved, *reg_pairs)


SMALL_ROWS = 48


class Feed:
    WINDOW = 3

    def __init__(self, groups, shards_in, wholes, sems):
        self.groups, self.shards, self.wholes = groups, shards_in, wholes
        self.own, self.us, self.ur, self.ds, self.dr, self.ys, self.yr, self.cs, self.cr = sems
        self.count = len(shards_in)
        self.section, self.index, self.outer, self.mid, self.core = place()
        self.begun = self.at = 0
        self.done = set()
        self.steps = [("z", 0), ("y", 0), ("z", 1)]
        for m in range(2, self.count):
            self.steps += [("z", m), ("y", m - 1)]
        self.steps.append(("y", self.count - 1))

    def branch(self):
        other = copy.copy(self)
        other.done = set(self.done)
        return other

    def devices(self):
        mid = (self.section, slot(self.outer, 1 - self.mid, self.core))
        core = (self.section, slot(self.outer, self.mid, 1 - self.core))
        return mid, core

    def outer_device(self, k):
        return (self.section, slot((self.outer + k) % self.groups, self.mid, self.core))

    def origin(self, k, far=0, other_core=False):
        outer = (self.outer - k + self.groups) % self.groups
        mid = 1 - self.mid if far else self.mid
        return slot(outer, mid, 1 - self.core if other_core else self.core)

    def own_copy(self, m):
        return pltpu.make_async_copy(
            self.shards[m], self.wholes[m].at[self.index], self.own.at[m]
        )

    def up_copy(self, m, k):
        piece = self.wholes[m].at[self.origin(k)]
        src = self.shards[m] if isinstance(k, int) and k == 0 else piece
        return remote(src, piece, self.us.at[m, k], self.ur.at[m, k], self.outer_device(1))

    def down_copy(self, m, k):
        piece = self.wholes[m].at[self.origin(k)]
        src = self.shards[m] if isinstance(k, int) and k == 0 else piece
        below = self.outer_device(self.groups - 1)
        return remote(src, piece, self.ds.at[m, k], self.dr.at[m, k], below)

    def up_arrival(self, m, k):
        piece = self.wholes[m].at[self.origin(k)]
        return remote(
            piece, piece, self.us.at[m, k - 1], self.ur.at[m, k - 1], self.outer_device(1)
        )

    def down_arrival(self, m, distance):
        k = (self.groups - distance) % self.groups
        piece = self.wholes[m].at[self.origin(k)]
        at = (self.groups - distance + 1) % self.groups
        return remote(piece, piece, self.ds.at[m, at], self.dr.at[m, at], self.outer_device(1))

    def y_copy(self, m, k, own=False, arrival=False):
        piece = self.wholes[m].at[self.origin(k, far=1 if arrival else 0)]
        src = self.shards[m] if own else piece
        return remote(src, piece, self.ys.at[m, k], self.yr.at[m, k], self.devices()[0])

    def c_copy(self, m, k, far, own=False, arrival=False):
        piece = self.wholes[m].at[self.origin(k, far, arrival)]
        src = self.shards[m] if own else piece
        at = k * 2 + far
        return remote(src, piece, self.cs.at[m, at], self.cr.at[m, at], self.devices()[1])

    def begin(self, upto):
        while self.begun < min(upto, self.count):
            m = self.begun

            @pl.when(self.outer < self.groups - 1)
            def _():
                self.up_copy(m, 0).start()

            @pl.when(self.outer > 0)
            def _():
                self.down_copy(m, 0).start()

            self.y_copy(m, 0, own=True).start()
            self.c_copy(m, 0, 0, own=True).start()
            self.own_copy(m).start()
            self.begun += 1

    def step(self):
        kind, m = self.steps[self.at]
        self.at += 1
        if kind == "z":

            top = self.groups - 1

            def spread(k):
                self.y_copy(m, k).start()
                self.c_copy(m, k, 0).start()

            def pass_on(before):
                distance = before + 1

                @pl.when(self.outer >= distance)
                def _():
                    self.up_arrival(m, distance).wait_recv()

                    @pl.when(self.outer < top)
                    def _():
                        self.up_copy(m, distance).start()

                    spread(distance)

                @pl.when(self.outer + distance <= top)
                def _():
                    self.down_arrival(m, distance).wait_recv()

                    @pl.when(self.outer > 0)
                    def _():
                        self.down_copy(m, self.groups - distance).start()

                    spread(self.groups - distance)

            each(top, pass_on)
            self.begin(m + 1 + self.WINDOW)
        else:

            def hand_over(k):
                self.y_copy(m, k, arrival=True).wait_recv()
                self.c_copy(m, k, 1).start()

            each(self.groups, hand_over)

    def pump(self, kind, m):
        while (kind, m) in self.steps[self.at :]:
            self.step()

    def need(self, m):
        self.pump("y", m)
        if m in self.done:
            return
        self.done.add(m)

        def last(k):
            for far in range(2):
                self.c_copy(m, k, far, arrival=True).wait_recv()

        each(self.groups, last)
        self.own_copy(m).wait()

    def drain(self):
        for m in range(self.count):
            self.need(m)
            top = self.groups - 1

            def line_sends(k):
                @pl.when((self.outer < top) & (self.outer >= k))
                def _():
                    self.up_copy(m, k).wait_send()

                @pl.when((self.outer > 0) & (self.outer + k <= top))
                def _():
                    self.down_copy(m, (self.groups - k) % self.groups).wait_send()

            each(self.groups, line_sends)

            def finish_sends(k):
                self.y_copy(m, k).wait_send()
                for far in range(2):
                    self.c_copy(m, k, far).wait_send()

            each(self.groups, finish_sends)


class FedSlots(Slots):
    def __init__(self, places, sems, feed):
        super().__init__(places, sems)
        self.feed = feed
        self.started = [False] * len(places)

    def plan(self, m, piece):
        self.queue[m].append(piece)

    def fetch(self, m):
        if not self.started[m] and self.queue[m]:
            piece = self.queue[m][0]
            self.feed.need(piece)
            self.copy(m, self.feed.flat[piece]).start()
            self.started[m] = True

    def open(self, m):
        self.fetch(m)
        if not self.ready[m]:
            self.copy(m, self.feed.flat[self.queue[m][0]]).wait()
            self.ready[m] = True
        return self.places[m]

    def close(self, m):
        self.queue[m].pop(0)
        self.ready[m] = self.started[m] = False
        if self.queue[m] and self.queue[m][0] in self.feed.done:
            self.fetch(m)


def unpack_small(small, devices, lead_vec, lead_bias, side_vec, side_bias):
    width = D // devices
    per = FF // devices // width
    for d in range(devices):
        lanes = slice(d * width, d * width + width)
        block = small[d].astype(HIGH)
        lead_vec[0:16, lanes] = block[0:16, 0:width]
        side_vec[0:16, lanes] = block[16:32, 0:width]
        for i in range(per):
            first = (d * per + i) * width
            lead_bias[0:1, first : first + width] = block[32 + i : 33 + i, 0:width]
            side_bias[0:1, first : first + width] = block[40 + i : 41 + i, 0:width]


def pack_small(lead_vectors, lead_bias, side_vectors, side_bias):
    width = lead_vectors.shape[1]

    def block(rows, height):
        rows = rows.reshape(-1, width)
        return jnp.pad(rows, ((0, height - rows.shape[0]), (0, 128 - width)))

    return jnp.concatenate(
        [block(lead_vectors, 16), block(side_vectors, 16), block(lead_bias, 8), block(side_bias, 8)]
    )


def layer_kernel(crops, devices, *refs):
    refs = list(refs)

    def grab(n):
        taken = refs[:n]
        del refs[:n]
        return taken

    def named(names):
        return dict(zip(names, grab(len(names))))

    shards_in = grab(9)
    patches, orders, pos, cotangent = grab(4)
    wholes = grab(9)
    rows_out, lead_small_out, dec_small_out = grab(3)
    own, reg = named(OUT_DEC), named(OUT_REG)
    own.update(named(KEEP_DEC))
    reg.update(named(KEEP_REG))
    places = grab(4)
    lead_vec_grad, lead_bias_grad, dec_vec_grad, dec_bias_grad = grab(4)
    lead_vec, lead_bias, side_vec, side_bias, small = grab(5)
    stream, context, resid, regressed, grad, temp, pos_visible, pos_masked = grab(8)
    low_temp, first_pack, second_pack = grab(3)
    sems, small_sem, x_send, x_recv = grab(4)
    groups = devices // 4
    feed = Feed(groups, shards_in, wholes, refs)
    feed.flat = [None] + [
        w.reshape(devices * w.shape[1], w.shape[2]) for w in wholes[1:]
    ]
    section = feed.section
    tokens = crops * ROWS
    x_device = (1 - section, feed.index)
    greet([*feed.devices(), x_device])
    barrier = pltpu.get_barrier_semaphore()
    each(
        groups - 1,
        lambda k: pl.semaphore_signal(
            barrier, inc=1, device_id=feed.outer_device(k + 1), device_id_type=MESH_ID
        ),
    )
    pl.semaphore_wait(barrier, groups + 2)
    feed.begin(Feed.WINDOW)

    def x_copy(n):
        piece = (first_pack.at[0], first_pack.at[1], second_pack)[n]
        return remote(piece, piece, x_send.at[n], x_recv.at[n], x_device)

    def vectors_in(feed):
        feed.need(0)
        fetched = pltpu.make_async_copy(wholes[0], small, small_sem)
        fetched.start()
        fetched.wait()
        unpack_small(small, devices, lead_vec, lead_bias, side_vec, side_bias)

    def slots_of(feed):
        slots = FedSlots(places, sems, feed)
        for base in (1, 5, 1):
            for m in range(4):
                slots.plan(m, base + m)
        return slots

    start = feed

    @pl.when(section == 0)
    def _():
        feed = start.branch()
        slots = slots_of(feed)
        for kind, vec, bias, keep in ((0, lead_vec, lead_bias, own), (1, side_vec, side_bias, reg)):
            for c in range(crops):
                stream[crop_rows(c), :] = dot(one_hot(orders, kind, c), patches[c])
            if kind == 0:
                vectors_in(feed)
            else:
                names = ("normed", "qkv", "mixed", "second", "hidden")
                keep = {n: reg[n] for n in names}
            block_forward(keep, stream, None, resid, slots, vec, bias, regressed)
            first_pack[kind] = regressed[...].astype(LOW)
            x_copy(kind).start()
        x_copy(2).wait_recv()
        grad[...] = second_pack[...].astype(HIGH)
        block_backward(
            own, grad, temp, low_temp, slots, lead_vec, lead_vec_grad, lead_bias_grad, False, None
        )
        for c in range(crops):
            rest = grad[crop_rows(c), :]
            pick = one_hot(orders, 0, c)
            total = jnp.zeros((PATCHES, D), HIGH)
            for _ in range(3):
                part = rest.astype(LOW)
                rest = rest - part.astype(HIGH)
                total = total + dot_tn(pick, part)
            rows_out[c] = total
        pack_small_grads(lead_small_out, lead_vec_grad, lead_bias_grad, 12, devices)
        for n in range(2):
            x_copy(n).wait_send()
        feed.drain()

    @pl.when(section == 1)
    def _():
        feed = start.branch()
        slots = slots_of(feed)
        for kind, place_of in enumerate((pos_visible, pos_masked)):
            for c in range(crops):
                pick = one_hot(orders, kind, c)
                place_of[crop_rows(c), :] = sum(dot(pick, pos[t]) for t in (2, 1, 0))
        vectors_in(feed)
        stream[...] = side_vec[12:13, :] + pos_masked[...]
        for m in range(4):
            slots.fetch(m)
        feed.pump("z", 5)
        x_copy(0).wait_recv()
        context[...] = first_pack[0].astype(HIGH) + pos_visible[...]
        block_forward(reg, stream, context, resid, slots, lead_vec, lead_bias, regressed)
        stream[...] = regressed[...] + pos_masked[...]
        block_forward(own, stream, None, resid, Held(slots), side_vec, side_bias, temp)
        for c in range(crops):
            first = c * ROWS
            rows_out[c, 0:MASKED, :] = regressed[first : first + MASKED, :]
            rows_out[c, MASKED : 2 * MASKED, :] = temp[first : first + MASKED, :]
            grad[first : first + ROWS, :] = jnp.zeros((ROWS, D), HIGH)
            grad[first : first + MASKED, :] = cotangent[c].astype(HIGH)
        block_backward(
            own, grad, temp, low_temp, slots, side_vec, dec_vec_grad, dec_bias_grad, False, None
        )
        x_copy(1).wait_recv()
        inside = lax.broadcasted_iota(jnp.int32, (ROWS, D), 0) < MASKED
        for c in range(crops):
            here = crop_rows(c)
            apart = regressed[here, :] - first_pack[1, here, :].astype(HIGH)
            grad[here, :] = grad[here, :] + jnp.where(inside, apart, 0.0)
        block_backward(
            reg, grad, temp, low_temp, slots, lead_vec, lead_vec_grad, lead_bias_grad, True, context
        )
        second_pack[...] = context[...].astype(LOW)
        x_copy(2).start()
        dec_vec_grad[12:13, :] = jnp.sum(grad[...], axis=0, keepdims=True)
        pack_small_grads(lead_small_out, lead_vec_grad, lead_bias_grad, 12, devices)
        for t in range(2):
            pack_small_grads(
                dec_small_out.at[t],
                dec_vec_grad.at[:, t * (D // 2) : (t + 1) * (D // 2)],
                dec_bias_grad.at[:, t * (FF // 2) : (t + 1) * (FF // 2)],
                13,
                devices,
                2,
            )
        feed.drain()
        x_copy(2).wait_send()


def layer(crops, devices, pieces, patches, orders, pos, cotangent):
    tokens = crops * ROWS
    groups = devices // 4
    inside = [((crops, PATCHES, D), HIGH), ((devices, LEAD_SMALL, 128), HIGH)]
    inside.append(((2, devices, DEC_SMALL, 128), HIGH))
    inside += [save_shape(n, tokens) for n in OUT_DEC + OUT_REG]
    scratch = places_for([save_shape(n, tokens) for n in KEEP_DEC + KEEP_REG])
    scratch += places_for(WEIGHT_SHAPES + SMALL_SHAPES * 4)
    scratch += places_for([((devices, SMALL_ROWS, 128), LOW)])
    scratch += places_for([((tokens, D), HIGH)] * 8)
    scratch += places_for([((tokens, D), LOW), ((2, tokens, D), LOW), ((tokens, D), LOW)])
    scratch += [pltpu.SemaphoreType.DMA(s) for s in ((4,), (), (3,), (3,))]
    scratch += [pltpu.SemaphoreType.DMA((9,))]
    for width in (groups,) * 6 + (2 * groups,) * 2:
        scratch.append(pltpu.SemaphoreType.DMA((9, width)))
    wholes = [((devices,) + p.shape, p.dtype) for p in pieces]
    return pl.pallas_call(
        functools.partial(layer_kernel, crops, devices),
        out_shape=specs(wholes + inside),
        in_specs=[ANYWHERE] * 9 + [INSIDE] * 4,
        out_specs=[ANYWHERE] * 9 + [INSIDE] * len(inside),
        scratch_shapes=scratch,
        compiler_params=pltpu.CompilerParams(
            collective_id=1, has_side_effects=True, vmem_limit_bytes=60 << 20
        ),
        name="layer",
    )(*pieces, patches, orders, pos, cotangent)


LEAD_SMALL = 16
DEC_SMALL = 24
LATE = (2, 0)
AHEAD = 2
SENDS = 2


def pack_small_grads(out, vectors, bias, rows, chunks, parts=1):
    width = D // (chunks * parts)
    for d in range(chunks):
        lanes = slice(d * width, d * width + width)
        out[d, 0:rows, 0:width] = vectors[0:rows, lanes]
        for i in range(FF // D):
            first = (d * (FF // D) + i) * width
            out[d, rows + i : rows + i + 1, 0:width] = bias[0:1, first : first + width]


def sums_kernel(devices, *refs):
    refs = list(refs)
    groups, half = devices // 4, devices // 2

    def grab(n):
        taken = refs[:n]
        del refs[:n]
        return taken

    own, reg = dict(zip(OUT_DEC, grab(8))), dict(zip(OUT_REG, grab(10)))
    (lead_small_in, dec_small_in) = grab(2)
    lead_out, dec_out = grab(4), grab(4)
    vec_out, bias_out, dec_vec_out, dec_bias_out = grab(4)
    dec_far = grab(5)
    lead_own, lead_c, lead_y, lead_z = (grab(5) for _ in range(4))
    dec_own, dec_near = grab(5), grab(5)
    dec_y, dec_z = grab(5 + len(LATE)), grab(5 + len(LATE))
    late_out, late_in = grab(len(LATE)), grab(len(LATE))
    pair_buf, far_left, far_right, place_of, place_far, lead_total, dec_total = grab(7)
    pair_sem, far_sem, near_sem, load, ready, l_send, l_recv = grab(7)
    c_send, c_recv, x_send, x_recv, y_send, y_recv, u_send, u_recv, d_send, d_recv = refs
    section, index, outer, mid, core = place()
    x_device = (1 - section, index)
    mid_device = (section, slot(outer, 1 - mid, core))
    core_device = (section, slot(outer, mid, 1 - core))

    def outer_device(k):
        return (section, slot((outer + k) % groups, mid, core))

    barrier = pltpu.get_barrier_semaphore()
    greet([mid_device, core_device])

    @pl.when(section == 1)
    def _():
        greet([x_device])

    each(
        groups - 1,
        lambda k: pl.semaphore_signal(
            barrier, inc=1, device_id=outer_device(k + 1), device_id_type=MESH_ID
        ),
    )

    own_of = lead_own + [r.at[1] for r in dec_own] + [dec_own[m].at[0] for m in LATE]
    y_of, z_of = lead_y + dec_y, lead_z + dec_z

    def mine(j):
        return j * 2 + core

    def lead_core(m, j):
        return remote(
            lead_own[m].at[j * 2 + 1 - core],
            lead_c[m].at[j],
            c_send.at[m, j],
            c_recv.at[m, j],
            core_device,
        )

    def dec_core(m, t, j):
        at = 5 + 2 * m + t
        return remote(
            dec_own[m].at[t, j * 2 + 1 - core],
            dec_far[m].at[t, j],
            c_send.at[at, j],
            c_recv.at[at, j],
            core_device,
        )

    def dec_load(m, t, j):
        return pltpu.make_async_copy(
            dec_far[m].at[t, j], dec_near[m].at[j % 2], near_sem.at[m, j % 2]
        )

    def x_copy(m, j):
        return remote(
            dec_own[m].at[0, mine(j)],
            dec_own[m].at[1, mine(j)],
            x_send.at[m, j],
            x_recv.at[m, j],
            x_device,
        )

    def y_copy(n, g):
        return remote(
            own_of[n].at[mine(g * 2 + 1 - mid)],
            y_of[n].at[g],
            y_send.at[n, g],
            y_recv.at[n, g],
            mid_device,
        )

    top = groups - 1

    def up_copy(n, d):
        return remote(
            own_of[n].at[mine(d * 2 + mid)],
            z_of[n].at[d + 1],
            u_send.at[n, d],
            u_recv.at[n, d],
            outer_device(1),
        )

    def down_copy(n, d):
        return remote(
            own_of[n].at[mine(d * 2 + mid)],
            z_of[n].at[d],
            d_send.at[n, d],
            d_recv.at[n, d],
            outer_device(groups - 1),
        )

    small_loads = (
        pltpu.make_async_copy(lead_small_in, lead_own[4], load.at[0]),
        pltpu.make_async_copy(dec_small_in, dec_own[4], load.at[1]),
    )

    def lead_begin(m):
        each(half, lambda j: lead_core(m, j).start())

    def y_begin(n):
        each(groups, lambda g: y_copy(n, g).start())

    def lead_sum(m, send=False):
        def far_pair(g):
            j = g * 2 + 1 - mid
            lead_core(m, j).wait_recv()
            add_rows(lead_own[m], mine(j), lead_c[m], j)
            if send:
                y_copy(m, g).start()

        def near_pair(g):
            j = g * 2 + mid
            lead_core(m, j).wait_recv()
            add_rows(lead_own[m], mine(j), lead_c[m], j)

        each(groups, far_pair)
        each(groups, near_pair)

    def dec_begin(m):
        for t in range(2):
            each(half, lambda j: dec_core(m, t, j).start())

    def dec_sum(m):
        for t in range(2):
            dec_core(m, t, 0).wait_recv()
            dec_load(m, t, 0).start()
            for j in range(half):
                if j + 1 < half:
                    dec_core(m, t, j + 1).wait_recv()
                    dec_load(m, t, j + 1).start()
                dec_load(m, t, j).wait()
                add_rows(dec_own[m].at[t], mine(j), dec_near[m], j % 2)

    def from_mid(n):
        def add_one(d):
            y_copy(n, d).wait_recv()
            add_rows(own_of[n], mine(d * 2 + mid), y_of[n], d)

        def up_first(before):
            d = top - before

            @pl.when(d > outer)
            def _():
                add_one(d)

                @pl.when(outer == 0)
                def _():
                    up_copy(n, d).start()

        def down_first(d):
            @pl.when(d < outer)
            def _():
                add_one(d)

                @pl.when(outer == top)
                def _():
                    down_copy(n, d).start()

        each(top, up_first)
        each(top, down_first)
        y_copy(n, outer).wait_recv()

        @pl.when(outer == 0)
        def _():
            blank(z_of[n], 1)

        @pl.when(outer == top)
        def _():
            blank(z_of[n], top)

    def going_up(n):
        def hop(before):
            d = top - before

            @pl.when(d > outer)
            def _():
                up_copy(n, d).wait_recv()
                add_rows(own_of[n], mine(d * 2 + mid), z_of[n], d + 1)
                up_copy(n, d).start()

        each(top, hop)

    def going_down(n):
        def hop(d):
            @pl.when(d < outer)
            def _():
                down_copy(n, d).wait_recv()
                add_rows(own_of[n], mine(d * 2 + mid), z_of[n], d)
                down_copy(n, d).start()

        each(top, hop)

    def near_half(n):
        @pl.when((outer > 0) & (outer < groups // 2))
        def _():
            going_up(n)

        @pl.when((outer < top) & (outer >= groups // 2))
        def _():
            going_down(n)

    def far_half(n):
        @pl.when((outer > 0) & (outer < groups // 2))
        def _():
            going_down(n)

        @pl.when((outer < top) & (outer >= groups // 2))
        def _():
            going_up(n)

    def across(queue, hooks=()):
        hooks = dict(hooks)
        for i in range(len(queue) + 2):
            if i < len(queue):
                if i >= SENDS:
                    line_sent(queue[i - SENDS], True)
                from_mid(queue[i])
            if i + AHEAD < len(queue):
                y_begin(queue[i + AHEAD])
            if 1 <= i <= len(queue):
                near_half(queue[i - 1])
            if i >= 2:
                far_half(queue[i - 2])
            if i in hooks:
                hooks[i]()

    def blank(buffer, at):
        buffer[at] = jnp.zeros(buffer.shape[1:], buffer.dtype)

    class Pairs:
        def __init__(self, tasks):
            self.tasks, self.at = tasks, 0
            self.begin(0)

        def parts(self, i):
            pairs, m, _ = self.tasks[i]
            first, second = (pairs[name].shape[1] for name in PAIRS[m])
            buf = pair_buf.at[i % 2]
            return buf.at[:, 0:first], buf.at[:, first : first + second]

        def copies(self, i):
            pairs, m, joined = self.tasks[i]
            moved = []
            for side, (name, part) in enumerate(zip(PAIRS[m], self.parts(i))):
                moved.append((pairs[name], part, pair_sem.at[i % 2, side]))
            if joined:
                moved.append((pairs["normed_c"], far_left, far_sem.at[0]))
                moved.append((pairs["dkv_c"], far_right, far_sem.at[1]))
            return [pltpu.make_async_copy(*a) for a in moved]

        def begin(self, i):
            if i < len(self.tasks):
                for moved in self.copies(i):
                    moved.start()

        def take(self, out, stacked):
            i = self.at
            self.begin(i + 1)
            for moved in self.copies(i):
                moved.wait()
            pairs, m, joined = self.tasks[i]
            left, right = self.parts(i)
            extra = (far_left, far_right, place_far) if joined else None
            weight_grad(
                out,
                left,
                right,
                place_of.at[0 : left.shape[1], :],
                stacked,
                extra,
                D,
            )
            self.at += 1

    def lead_view(m):
        rows = lead_own[m].shape[1]
        return lead_own[m].reshape(devices * rows, lead_own[m].shape[2])

    def dec_view(m):
        (rows, columns), _ = WEIGHT_SHAPES[m]
        piece = dec_own[m].shape[2:]
        if piece[1] == columns:
            return dec_own[m].reshape(rows, columns), 0
        return dec_own[m].reshape(2 * devices, *piece), piece[0] // 2

    small_loads[0].start()

    def late_copy(i):
        return remote(late_out[i], late_in[i], l_send.at[i], l_recv.at[i], x_device)

    def total_of(n, where, lanes):
        total = own_of[n][mine(outer * 2 + mid), where, lanes].astype(HIGH)
        total = total + y_of[n][outer, where, lanes].astype(HIGH)
        for k in (outer + 1, outer):
            total = total + z_of[n][k, where, lanes].astype(HIGH)
        return total

    def arrive(n):
        @pl.when(outer > 0)
        def _():
            up_copy(n, outer).wait_recv()

        @pl.when(outer < top)
        def _():
            down_copy(n, outer).wait_recv()

    def emit(out, rows, columns, value):
        stacked = out.shape[-1] != columns
        step = rows // 2 if stacked else 16
        for r in range(rows // step):
            where = pl.ds(r * step, step)
            if stacked:
                for q in range(columns // 128):
                    lanes = slice(q * 128, q * 128 + 128)
                    out[:, (2 * q + r) * 128 : (2 * q + r + 1) * 128] = value(where, lanes)
            else:
                out[where, :] = value(where, slice(None))

    def finish_sum(n):
        arrive(n)
        is_dec, m = divmod(n, 5)
        if m == 4:
            total = dec_total if is_dec else lead_total
            total[...] = total_of(n, slice(None), slice(None))
            vec, bias = (dec_vec_out, dec_bias_out) if is_dec else (vec_out, bias_out)
            count, width = vec.shape
            vec[...] = total[0:count, 0:width]
            for i in range(FF // D):
                bias[0:1, i * width : i * width + width] = total[count + i : count + i + 1, 0:width]
            return
        rows, columns = own_of[n].shape[-2:]
        out = dec_out[m] if is_dec else lead_out[m]
        emit(out, rows, columns, functools.partial(total_of, n))

    def line_sent(n, ends):
        def one(d):
            @pl.when((d > outer) & ((outer == 0) if ends else (outer > 0)))
            def _():
                up_copy(n, d).wait_send()

            @pl.when((d < outer) & ((outer == top) if ends else (outer < top)))
            def _():
                down_copy(n, d).wait_send()

        each(groups, one)

    def sent(queue):
        for n in queue:
            each(groups, lambda g: y_copy(n, g).wait_send())
            line_sent(n, False)
        for n in queue[-SENDS:]:
            line_sent(n, True)

    order = (1, 3, 2, 0, 4)
    early = tuple(m for m in (3, 2, 0, 1, 4) if m not in LATE)

    @pl.when(section == 0)
    def _():
        pairs = Pairs([(own, m, False) for m in order[:4]])
        pairs.take(lead_view(order[0]), 0)
        pl.semaphore_wait(barrier, groups + 2)
        pl.semaphore_signal(ready, inc=1, device_id=x_device, device_id_type=MESH_ID)
        small_loads[0].wait()
        lead_begin(order[0])
        lead_begin(4)
        for i in range(1, 4):
            pairs.take(lead_view(order[i]), 0)
            lead_begin(order[i])
            lead_sum(order[i - 1], i <= AHEAD)
        lead_sum(order[3], 3 < AHEAD)
        lead_sum(4)

        def early_in():
            for e in early:
                each(half, lambda j: x_copy(e, j).wait_recv())

        across(order + tuple(5 + m for m in early), {4 - AHEAD: early_in})
        for m in order:
            finish_sum(m)
        for m in early:
            finish_sum(5 + m)
        for i, m in enumerate(LATE):
            late_copy(i).wait_recv()
            rows, columns = late_in[i].shape
            emit(dec_out[m], rows, columns, lambda *at: late_in[i][at].astype(HIGH))
        for m in range(5):
            each(half, lambda j: lead_core(m, j).wait_send())
        sent(order + tuple(5 + m for m in early))

    @pl.when(section == 1)
    def _():
        dec_order = (3, 2, 0, 1)
        small_loads[1].start()
        tasks = []
        for i in range(4):
            tasks.append((reg, order[i], order[i] == 0))
            tasks.append((own, dec_order[i], False))
        pairs = Pairs(tasks)
        for i in range(4):
            pairs.take(lead_view(order[i]), 0)
            if i == 0:
                pl.semaphore_wait(barrier, groups + 1)
                for moved in small_loads:
                    moved.wait()
                lead_begin(4)
                dec_begin(4)
            lead_begin(order[i])
            pairs.take(*dec_view(dec_order[i]))
            dec_begin(dec_order[i])
            lead_sum(order[i], i < AHEAD)
        lead_sum(4)
        late = tuple(10 + i for i in range(len(LATE)))
        rest = late + tuple(5 + m for m in dec_order) + (9,)

        def early_out():
            for m in early[1:]:
                dec_sum(m)
            pl.semaphore_wait(ready, 1)
            for m in early:
                each(half, lambda j: x_copy(m, j).start())

        def late_out_of(i):
            n = late[i]
            arrive(n)
            rows, columns = late_out[i].shape
            for r in range(rows // 16):
                where = pl.ds(r * 16, 16)
                late_out[i][where, :] = total_of(n, where, slice(None)).astype(LOW)
            late_copy(i).start()

        hooks = {0: functools.partial(dec_sum, early[0]), 1: early_out}
        for i, m in enumerate(LATE):
            hooks[2 + i] = functools.partial(dec_sum, m)
            hooks[8 + 2 * i] = functools.partial(late_out_of, i)
        across(order + rest, hooks)
        for m in order:
            finish_sum(m)
        for n in rest[len(LATE) :]:
            finish_sum(n)
        for m in range(5):
            each(half, lambda j: lead_core(m, j).wait_send())
            for t in range(2):
                each(half, lambda j: dec_core(m, t, j).wait_send())
        for m in early:
            each(half, lambda j: x_copy(m, j).wait_send())
        for i in range(len(LATE)):
            late_copy(i).wait_send()
        sent(order + rest)


def hand_out_kernel(*refs):
    count = (len(refs) - 1) // 2
    moved = [
        pltpu.make_async_copy(refs[i], refs[count + i], refs[-1].at[i]) for i in range(count)
    ]
    for one in moved:
        one.start()
    for one in moved:
        one.wait()


def hand_out(arrays):
    return pl.pallas_call(
        hand_out_kernel,
        out_shape=specs([(a.shape, a.dtype) for a in arrays]),
        in_specs=[INSIDE] * len(arrays),
        out_specs=[ANYWHERE] * len(arrays),
        scratch_shapes=[pltpu.SemaphoreType.DMA((len(arrays),))],
        name="hand_out",
    )(*arrays)


def sums(crops, devices, rows, own_pairs, reg_pairs, lead_small, dec_small):
    tokens = crops * ROWS
    groups, half = devices // 4, devices // 2
    dec_kinds, _ = dec_grad_shapes(devices, True)
    lead_pieces, dec_pieces, lead_outs, dec_outs = [], [], [], []
    for (shape, kind), (dec_shape, _) in zip(WEIGHT_SHAPES, dec_kinds):
        height, columns = shape
        lead_pieces.append(((height // devices, columns), kind))
        lead_outs.append(((height // devices, columns), HIGH))
        dec_outs.append(((height // (2 * devices), columns), HIGH))
        piece = dec_shape[1:] if len(dec_shape) == 3 else (height // (2 * devices), columns)
        dec_pieces.append((piece, kind))
    lead_pieces.append(((LEAD_SMALL, 128), HIGH))
    dec_pieces.append(((DEC_SMALL, 128), HIGH))
    small_outs = []
    for height, chunks in ((12, devices), (13, 2 * devices)):
        small_outs += [((height, D // chunks), HIGH), ((1, FF // chunks), HIGH)]
    far = [((2, half) + s, k) for s, k in dec_pieces]
    scratch = []
    for lead in ((devices,), (half,), (groups,), (groups + 1,)):
        scratch += places_for([(lead + s, k) for s, k in lead_pieces])
    for lead in ((2, devices), (2,)):
        scratch += places_for([(lead + s, k) for s, k in dec_pieces])
    late_pieces = [dec_pieces[m] for m in LATE]
    for lead in (groups, groups + 1):
        scratch += places_for([((lead,) + s, k) for s, k in dec_pieces + late_pieces])
    scratch += places_for(late_pieces * 2)
    scratch += places_for(
        [((2, tokens, FF + D), LOW)]
        + [((tokens, D), LOW), ((tokens, 2 * D), LOW), ((FF, tokens), LOW), ((D, tokens), LOW)]
        + [((LEAD_SMALL, 128), HIGH), ((DEC_SMALL, 128), HIGH)]
    )
    scratch += [pltpu.SemaphoreType.DMA(s) for s in ((2, 2), (2,), (5, 2), (2,))]
    scratch.append(pltpu.SemaphoreType.REGULAR)
    sems = [(len(LATE),)] * 2 + [(15, half)] * 2 + [(5, half)] * 2
    sems += [(10 + len(LATE), groups)] * 6
    scratch += [pltpu.SemaphoreType.DMA(s) for s in sems]
    outs = pl.pallas_call(
        functools.partial(sums_kernel, devices),
        out_shape=specs(lead_outs + dec_outs + small_outs + far),
        in_specs=[ANYWHERE] * 20,
        out_specs=[INSIDE] * 12 + [ANYWHERE] * 5,
        scratch_shapes=scratch,
        compiler_params=pltpu.CompilerParams(
            collective_id=2, has_side_effects=True, vmem_limit_bytes=61 << 20
        ),
        name="sums",
    )(*own_pairs, *reg_pairs, lead_small, dec_small)
    outs = hand_out(outs[:12])
    lead, dec = list(outs[:4]), list(outs[4:8])
    lead += [outs[8], outs[9].reshape(-1)]
    dec += [outs[10], outs[11].reshape(-1)]
    return rows, lead, dec


def exchange(pieces):
    return [lax.all_gather(p, "dp", axis=0) for p in pieces]


def as_small(parts, rows_of):
    flat = jnp.concatenate([p.reshape(-1) for p in parts])
    block = rows_of * 128
    padded = -(-flat.shape[0] // block) * block
    return jnp.pad(flat, (0, padded - flat.shape[0])).reshape(-1, 128)


def take_flat(flat, shapes):
    taken, offset = [], 0
    for shape in shapes:
        size = 1
        for extent in shape:
            size *= extent
        taken.append(flat[:, offset : offset + size].reshape((-1,) + shape))
        offset += size
    return taken


def spread_columns(gathered):
    return gathered.transpose(1, 0, 2).reshape(gathered.shape[1], -1)


def small_chunks(vectors, bias, chunks):
    rows, columns = vectors.shape
    cut = vectors.reshape(rows, chunks, columns // chunks).transpose(1, 0, 2).reshape(chunks, -1)
    flat = jnp.concatenate([cut, bias.reshape(chunks, -1)], axis=1)
    padded = -(-flat.shape[1] // 1024) * 1024
    return jnp.pad(flat, ((0, 0), (0, padded - flat.shape[1]))).reshape(chunks, -1, 128)


def small_pieces(chunk, rows, chunks):
    flat = chunk.reshape(-1)
    vectors = rows * (D // chunks)
    bias = FF // chunks
    return flat[:vectors].reshape(rows, D // chunks), flat[vectors : vectors + bias]


def total_grads(lead_big, lead_small, dec_big, dec_small):
    devices = lax.axis_size("dp")
    on_encoder = lax.axis_index("section") == 0
    lead_chunks = [g.reshape(devices, -1, g.shape[1]) for g in lead_big]
    lead_chunks.append(small_chunks(*lead_small, devices))
    dec_chunks = [g.reshape(2, devices, -1, g.shape[1]) for g in dec_big]
    dec_chunk_small = small_chunks(*dec_small, 2 * devices)
    dec_chunks.append(dec_chunk_small.reshape((2, devices) + dec_chunk_small.shape[1:]))
    lead_out = [
        lax.psum_scatter(g.astype(jnp.float32), "dp", scatter_dimension=0) for g in lead_chunks
    ]
    dec_out = []
    for g in dec_chunks:
        mine = jnp.where(on_encoder, jnp.zeros_like(g), g).astype(jnp.float32)
        mine = lax.psum_scatter(mine, "dp", scatter_dimension=1)
        dec_out.append(lax.psum_scatter(mine, "section", scatter_dimension=0))
    lead_vectors, lead_bias = small_pieces(lead_out[4], 12, devices)
    dec_vectors, dec_bias = small_pieces(dec_out[4], 13, 2 * devices)
    return lead_out[:4] + [lead_vectors, lead_bias], dec_out[:4] + [dec_vectors, dec_bias]


def run_fused(crops, devices, patches, cotangent, orders, lead, side, smalls):
    pieces = [pack_small(*smalls)] + lead + side
    outs = layer(crops, devices, pieces, patches, orders, position_parts(), cotangent)
    rows, lead_small, dec_small, *pairs = outs[9:]
    own_pairs, reg_pairs = pairs[: len(OUT_DEC)], pairs[len(OUT_DEC) :]
    return sums(crops, devices, rows, own_pairs, reg_pairs, lead_small, dec_small)


def run_apart(crops, devices, patches, cotangent, orders, lead, side, smalls):
    on_encoder = lax.axis_index("section") == 0
    wholes = exchange(lead + side + [as_small(smalls, 16)])
    big = [w.reshape(-1, w.shape[2]) for w in wholes[:8]]
    flat = wholes[8].reshape(devices, -1).astype(jnp.float32)
    lv, lb, sv, sb = take_flat(flat, [p.shape for p in smalls])

    def sixteen(vectors):
        rows = spread_columns(vectors)
        return jnp.pad(rows, ((0, 16 - rows.shape[0]), (0, 0)))

    lead_w, side_w = big[:4], big[4:]
    lead_small = [sixteen(lv), lb.reshape(1, -1)]
    all_small = lead_small + [sixteen(sv), sb.reshape(1, -1)]
    pack, pos_visible, pos_masked, *enc_saved = encode(
        crops, patches, orders, position_parts(), lead_w, side_w, all_small
    )
    arrived = passed_along(pack, "section", 1)
    grad_latents, latent_rows, reg_vec, reg_bias, dec_vec, dec_bias, *pairs = regress(
        crops, arrived, pos_visible, pos_masked, cotangent, lead_w, side_w, all_small
    )
    reg_pairs, dec_pairs = pairs[: len(OUT_REG)], pairs[len(OUT_REG) :]
    returned = passed_along(grad_latents, "section", -1)
    dec_big = decoder_weights(crops, dec_pairs, devices, False)
    *lead_big, grad_rows, enc_vec, enc_bias = finish(
        crops, returned, orders, lead_w, lead_small, enc_saved, reg_pairs
    )
    vec = jnp.where(on_encoder, enc_vec, reg_vec)[:12]
    bias = jnp.where(on_encoder, enc_bias, reg_bias)
    rows = jnp.where(on_encoder, grad_rows, latent_rows)
    lead_small, dec_small = (vec, bias[0]), (dec_vec[:13], dec_bias[0])
    return (rows, *total_grads(lead_big, lead_small, dec_big, dec_small))


def padded_orders(ordering, part):
    cut = ordering[:, MASKED:] if part == 0 else ordering[:, :MASKED]
    cut = jnp.pad(cut, ((0, 0), (0, ROWS - MASKED)), constant_values=-1)
    return cut.reshape(-1, 1)


def shards(
    patches,
    cotangent,
    ordering,
    lead_qkv,
    lead_proj,
    lead_up,
    lead_down,
    lead_vectors,
    lead_bias,
    side_qkv,
    side_proj,
    side_up,
    side_down,
    side_vectors,
    side_bias,
):
    devices = lax.axis_size("dp")
    crops = patches.shape[0]
    orders = jnp.stack([padded_orders(ordering, 0), padded_orders(ordering, 1)])
    lead = [lead_qkv[0], lead_proj[0], lead_up[0], lead_down[0]]
    side = [side_qkv[0], side_proj[0], side_up[0], side_down[0]]
    smalls = [lead_vectors[0], lead_bias[0], side_vectors[0], side_bias[0]]
    own_path = devices % 4 == 0 and lead[0].shape[0] % 16 == 0
    run = run_fused if own_path else run_apart
    rows, lead_out, dec_out = run(
        crops, devices, patches, cotangent, orders, lead, side, smalls
    )
    return (rows[None],) + tuple(o[None] for o in lead_out) + tuple(dec_out)


def solution(mesh):
    return jax.shard_map(
        shards,
        mesh=mesh,
        in_specs=(
            P("dp", None, None),
            P("dp", None, None),
            P("dp", None),
            P("section", "dp", None),
            P("section", "dp", None),
            P("section", "dp", None),
            P("section", "dp", None),
            P("section", None, "dp"),
            P("section", "dp"),
            P("section", "dp", None),
            P("section", "dp", None),
            P("section", "dp", None),
            P("section", "dp", None),
            P("section", None, "dp"),
            P("section", "dp"),
        ),
        out_specs=(
            P("section", "dp", None, None),
            P("section", "dp", None),
            P("section", "dp", None),
            P("section", "dp", None),
            P("section", "dp", None),
            P("section", None, "dp"),
            P("section", "dp"),
            P(("section", "dp"), None),
            P(("section", "dp"), None),
            P(("section", "dp"), None),
            P(("section", "dp"), None),
            P(None, ("section", "dp")),
            P(("section", "dp")),
        ),
        check_vma=False,
    )
```

```python
import copy
import functools

import jax
import jax.experimental.pallas as pl
import jax.experimental.pallas.tpu as pltpu
import jax.numpy as jnp
import numpy as np
from jax import lax
from jax.sharding import PartitionSpec as P

D = 768
HEADS = 12
HEAD_DIM = 64
FF = 3072
GRID = 14
PATCHES = 196
MASKED = 98


def passed_along(array, axis, by):
    count = lax.axis_size(axis)
    pairs = [(i, i + by) for i in range(count) if 0 <= i + by < count]
    return lax.ppermute(array, axis, pairs)


def positions():
    ids = np.arange(PATCHES)
    quarter = D // 4
    frequency = 10000.0 ** (-np.arange(quarter) / quarter)
    rows = (ids // GRID)[:, None] * frequency
    cols = (ids % GRID)[:, None] * frequency
    return np.concatenate([np.sin(cols), np.cos(cols), np.sin(rows), np.cos(rows)], axis=1)


def position_parts():
    rest = positions().astype(np.float32)
    parts = []
    for _ in range(3):
        part = rest.astype(jnp.bfloat16)
        rest = rest - part.astype(np.float32)
        parts.append(part)
    return jnp.asarray(np.stack(parts))


MESH_ID = pl.DeviceIdType.MESH


def each(count, body):
    if count <= 4:
        for k in range(count):
            body(k)
    else:
        lax.fori_loop(0, count, lambda k, carry: (body(k), carry)[1], 0)


def place():
    section = lax.axis_index("section")
    index = lax.axis_index("dp")
    return section, index, index // 4, (index // 2) % 2, index % 2


def slot(outer, mid, core):
    return outer * 4 + mid * 2 + core


def remote(src, dst, send_sem, recv_sem, device):
    return pltpu.make_async_remote_copy(
        src_ref=src,
        dst_ref=dst,
        send_sem=send_sem,
        recv_sem=recv_sem,
        device_id=device,
        device_id_type=MESH_ID,
    )


def greet(devices):
    barrier = pltpu.get_barrier_semaphore()
    for device in devices:
        pl.semaphore_signal(barrier, inc=1, device_id=device, device_id_type=MESH_ID)


def add_rows(target, at, other, other_at):
    rows = target.shape[-2]
    step = 16 if target.dtype == jnp.bfloat16 else 8

    def body(r, carry):
        where = pl.ds(r * step, step)
        total = target[at, where, :].astype(jnp.float32) + other[other_at, where, :].astype(
            jnp.float32
        )
        target[at, where, :] = total.astype(target.dtype)
        return carry

    lax.fori_loop(0, rows // step, body, 0, unroll=True)


ROWS = 112
LOW = jnp.bfloat16
HIGH = jnp.float32
VISIBLE = PATCHES - MASKED
CHUNK = 32
NAMES_SELF = ("normed", "qkv", "probs", "mixed", "attn", "x1", "r1", "x2", "r2", "second")
NAMES_SELF += ("slope", "hidden", "branch", "x3", "r3")
NAMES_CROSS = ("normed_c", "kv_c", "probs_c", "x1_c", "r1_c")
NAMES_GRAD = ("dqkv", "dattn", "dpre", "dbranch")


def save_shape(name, tokens):
    pairs = tokens // ROWS * (HEADS // 2)
    kinds = {
        "qkv": ((tokens, 3 * D), LOW),
        "kv_c": ((tokens, 2 * D), LOW),
        "dqkv": ((tokens, 3 * D), LOW),
        "dkv_c": ((tokens, 2 * D), LOW),
        "probs": ((pairs, 2 * ROWS, ROWS), HIGH),
        "probs_c": ((pairs, 2 * ROWS, ROWS), HIGH),
        "hidden": ((tokens, FF), LOW),
        "dpre": ((tokens, FF), LOW),
        "slope": ((tokens, FF), HIGH),
    }
    if name in kinds:
        return kinds[name]
    if name in ("r1", "r2", "r3", "r1_c"):
        return ((tokens, 1), HIGH)
    if name in ("attn", "x1", "x1_c", "x2", "x3", "branch"):
        return ((tokens, D), HIGH)
    return ((tokens, D), LOW)


def dot(left, right):
    return jnp.dot(left, right, preferred_element_type=HIGH)


def dot_nt(left, right):
    return lax.dot_general(left, right, (((1,), (1,)), ((), ())), preferred_element_type=HIGH)


def dot_tn(left, right):
    return lax.dot_general(left, right, (((0,), (0,)), ((), ())), preferred_element_type=HIGH)


def by_rows(tokens, body, init=()):
    def step(i, carry):
        return body(pl.ds(pl.multiple_of(i * CHUNK, CHUNK), CHUNK), carry)

    return lax.fori_loop(0, tokens // CHUNK, step, init, unroll=True)


def tiles(width, body, size=256, unroll=True):
    def step(i, carry):
        body(pl.ds(pl.multiple_of(i * size, size), size))
        return carry

    lax.fori_loop(0, width // size, step, 0, unroll=unroll)


def fold(values):
    return jnp.sum(values.reshape(-1, 8, values.shape[-1]), axis=0)


def norm_forward(source, gain, shift, kept, spread, low, out=None):
    def body(where, carry):
        values = source[where, :]
        center = values - jnp.mean(values, axis=-1, keepdims=True)
        scale = lax.rsqrt(jnp.mean(center * center, axis=-1, keepdims=True) + 1e-06)
        center = center * scale
        if kept is not None:
            kept[where, :] = center
            spread[where, :] = scale
        result = center * gain + shift
        if low is not None:
            low[where, :] = result.astype(LOW)
        if out is not None:
            out[where, :] = result
        return carry

    by_rows(source.shape[0], body)


def norm_grad(grad, gain, center, scale):
    weighted = grad * gain
    first = jnp.mean(weighted, axis=-1, keepdims=True)
    second = jnp.mean(weighted * center, axis=-1, keepdims=True)
    return scale * (weighted - first - center * second)


def pair_masks(rows):
    lane = lax.broadcasted_iota(jnp.int32, (rows, 2 * HEAD_DIM), 1)
    return lane < HEAD_DIM


def two_heads(values):
    low_lanes = pair_masks(values.shape[0])
    zero = jnp.zeros_like(values)
    return jnp.concatenate(
        [jnp.where(low_lanes, values, zero), jnp.where(low_lanes, zero, values)], axis=0
    )


def one_pair(stacked):
    half = stacked.shape[0] // 2
    return jnp.where(pair_masks(half), stacked[:half], stacked[half:])


def head_loop(tokens, body):
    def step(p, carry):
        for crop in range(tokens // ROWS):
            rows = pl.ds(crop * ROWS, ROWS)
            body(crop * (HEADS // 2) + p, rows, p)
        return carry

    lax.fori_loop(0, HEADS // 2, step, 0, unroll=True)


def lanes_of(p, base):
    return pl.ds(pl.multiple_of(base + p * 128, 128), 128)


def attention(s, cross):
    tokens = s["normed"].shape[0]
    valid = lax.broadcasted_iota(jnp.int32, (2 * ROWS, ROWS), 1) < MASKED

    def body(at, rows, p):
        q2 = two_heads(s["qkv"][rows, lanes_of(p, 0)])
        sources = [(s["qkv"][rows, lanes_of(p, D)], s["qkv"][rows, lanes_of(p, 2 * D)], "probs")]
        if cross:
            sources.append(
                (s["kv_c"][rows, lanes_of(p, 0)], s["kv_c"][rows, lanes_of(p, D)], "probs_c")
            )
        scores = [
            jnp.where(valid, dot_nt(q2, k) * HEAD_DIM ** (-0.5), -1e30) for k, _, _ in sources
        ]
        top = jnp.max(scores[0], axis=-1, keepdims=True)
        if cross:
            top = jnp.maximum(top, jnp.max(scores[1], axis=-1, keepdims=True))
        powers = [jnp.exp(x - top) for x in scores]
        mass = jnp.sum(powers[0], axis=-1, keepdims=True)
        if cross:
            mass = mass + jnp.sum(powers[1], axis=-1, keepdims=True)
        mixed = None
        inverse = 1.0 / mass
        for power, (_, v, name) in zip(powers, sources):
            probs = power * inverse
            if name in s:
                s[name][at] = probs
            part = dot(probs.astype(LOW), v)
            mixed = part if mixed is None else mixed + part
        s["mixed"][rows, lanes_of(p, 0)] = one_pair(mixed).astype(LOW)

    head_loop(tokens, body)


def block_forward(s, stream, context, resid, weights, vectors, bias, out):
    def row(r, where=slice(None)):
        return vectors[r : r + 1, where]

    norm_forward(stream, row(0), row(1), s.get("x1"), s.get("r1"), s["normed"])
    if context is not None:
        norm_forward(context, row(0), row(1), s["x1_c"], s["r1_c"], s["normed_c"])
    w = weights.open(0)

    def qkv_tile(j):
        where = slice(j * 256, j * 256 + 256)
        kind, local = divmod(j, 3)
        extra = None if kind == 1 else row(6 if kind == 0 else 7, slice(local * 256, local * 256 + 256))
        values = dot(s["normed"][...], w[:, where])
        s["qkv"][:, where] = (values if extra is None else values + extra).astype(LOW)
        if context is not None and kind > 0:
            values = dot(s["normed_c"][...], w[:, where])
            here = slice(j * 256 - D, j * 256 - D + 256)
            s["kv_c"][:, here] = (values if extra is None else values + extra).astype(LOW)

    for j in range(9):
        qkv_tile(j)
    weights.close(0)
    attention(s, context is not None)
    w = weights.open(1)
    for j in range(3):
        where = slice(j * 256, j * 256 + 256)
        attn = dot(s["mixed"][...], w[:, where]) + row(8, where)
        if "attn" in s:
            s["attn"][:, where] = attn
        resid[:, where] = stream[:, where] + row(10, where) * attn
    weights.close(1)
    norm_forward(resid, row(2), row(3), s.get("x2"), s.get("r2"), s["second"])
    w = weights.open(2)

    def up_tile(where):
        pre = dot(s["second"][...], w[:, where]) + bias[0:1, where]
        phi = 0.5 + 0.5 * lax.erf(pre * 0.5**0.5)
        s["hidden"][:, where] = (pre * phi).astype(LOW)
        if "slope" in s:
            s["slope"][:, where] = phi + pre * jnp.exp(-0.5 * pre * pre) * 0.3989422804014327

    tiles(FF, up_tile)
    weights.close(2)
    w = weights.open(3)
    for j in range(3):
        where = slice(j * 256, j * 256 + 256)
        branch = dot(s["hidden"][...], w[:, where]) + row(9, where)
        if "branch" in s:
            s["branch"][:, where] = branch
        resid[:, where] = resid[:, where] + row(11, where) * branch
    weights.close(3)
    norm_forward(resid, row(4), row(5), s.get("x3"), s.get("r3"), None, out)


def attention_backward(s, grad_mixed, cross):
    tokens = s["normed"].shape[0]
    scale = HEAD_DIM ** (-0.5)

    def body(at, rows, p):
        q2 = two_heads(s["qkv"][rows, lanes_of(p, 0)])
        g2 = two_heads(grad_mixed[rows, lanes_of(p, 0)])
        sources = [("qkv", D, "dqkv", "probs")]
        if cross:
            sources.append(("kv_c", 0, "dkv_c", "probs_c"))
        parts = []
        inner = None
        for name, base, grad_name, probs_name in sources:
            v = s[name][rows, lanes_of(p, base + D)]
            probs = s[probs_name][at]
            s[grad_name][rows, lanes_of(p, base + D)] = dot_tn(probs.astype(LOW), g2).astype(LOW)
            dprobs = dot_nt(g2, v)
            parts.append((probs, dprobs))
            total = jnp.sum(dprobs * probs, axis=-1, keepdims=True)
            inner = total if inner is None else inner + total
        dq = None
        for (probs, dprobs), (name, base, grad_name, _) in zip(parts, sources):
            dscores = (probs * (dprobs - inner)).astype(LOW)
            part = dot(dscores, s[name][rows, lanes_of(p, base)])
            dq = part if dq is None else dq + part
            s[grad_name][rows, lanes_of(p, base)] = (dot_tn(dscores, q2) * scale).astype(LOW)
        s["dqkv"][rows, lanes_of(p, 0)] = (one_pair(dq) * scale).astype(LOW)

    head_loop(tokens, body)


def block_backward(s, grad, temp, low_temp, weights, vectors, vec_grad, bias_grad, cross, context_grad):
    tokens = grad.shape[0]
    zero = jnp.zeros((8, D), HIGH)

    def row(r):
        return vectors[r : r + 1, :]

    def put(r, total):
        vec_grad[r : r + 1, :] = jnp.sum(total, axis=0, keepdims=True)

    def final_rows(where, sums):
        gain, shift, scale, offset = sums
        g = grad[where, :]
        center = s["x3"][where, :]
        gf = norm_grad(g, row(4), center, s["r3"][where, :])
        grad[where, :] = gf
        low = (row(11) * gf).astype(LOW)
        s["dbranch"][where, :] = low
        return (
            gain + fold(g * center),
            shift + fold(g),
            scale + fold(gf * s["branch"][where, :]),
            offset + fold(low.astype(HIGH)),
        )

    sums = by_rows(tokens, final_rows, (zero,) * 4)
    for r, total in zip((4, 5, 11, 9), sums):
        put(r, total)
    w = weights.open(3)

    def down_tile(where):
        low = (dot_nt(s["dbranch"][...], w[where, :]) * s["slope"][:, where]).astype(LOW)
        s["dpre"][:, where] = low
        bias_grad[0:1, where] = jnp.sum(low.astype(HIGH), axis=0, keepdims=True)

    tiles(FF, down_tile)
    weights.close(3)
    w = weights.open(2)
    for j in range(3):
        where = slice(j * 256, j * 256 + 256)
        temp[:, where] = dot_nt(s["dpre"][...], w[where, :])
    weights.close(2)

    def second_rows(where, sums):
        gain, shift, scale, offset = sums
        g = temp[where, :]
        center = s["x2"][where, :]
        gr = norm_grad(g, row(2), center, s["r2"][where, :]) + grad[where, :]
        grad[where, :] = gr
        low = (row(10) * gr).astype(LOW)
        s["dattn"][where, :] = low
        return (
            gain + fold(g * center),
            shift + fold(g),
            scale + fold(gr * s["attn"][where, :]),
            offset + fold(low.astype(HIGH)),
        )

    sums = by_rows(tokens, second_rows, (zero,) * 4)
    for r, total in zip((2, 3, 10, 8), sums):
        put(r, total)
    w = weights.open(1)
    for j in range(3):
        where = slice(j * 256, j * 256 + 256)
        low_temp[:, where] = dot_nt(s["dattn"][...], w[where, :]).astype(LOW)
    weights.close(1)
    attention_backward(s, low_temp, cross)
    w = weights.open(0)
    for j in range(3):
        where = slice(j * 256, j * 256 + 256)
        temp[:, where] = dot_nt(s["dqkv"][...], w[where, :])
        if cross:
            context_grad[:, where] = dot_nt(s["dkv_c"][...], w[where, D:])
    weights.close(0)

    def first_rows(where, sums):
        gain, shift, dq, dv = sums
        g = temp[where, :]
        center = s["x1"][where, :]
        grad[where, :] = grad[where, :] + norm_grad(g, row(0), center, s["r1"][where, :])
        gain, shift = gain + fold(g * center), shift + fold(g)
        dq = dq + fold(s["dqkv"][where, 0:D].astype(HIGH))
        dv = dv + fold(s["dqkv"][where, 2 * D :].astype(HIGH))
        if cross:
            g = context_grad[where, :]
            center = s["x1_c"][where, :]
            context_grad[where, :] = norm_grad(g, row(0), center, s["r1_c"][where, :])
            gain, shift = gain + fold(g * center), shift + fold(g)
            dv = dv + fold(s["dkv_c"][where, D:].astype(HIGH))
        return gain, shift, dq, dv

    sums = by_rows(tokens, first_rows, (zero,) * 4)
    for r, total in zip((0, 1, 6, 7), sums):
        put(r, total)


class Slots:
    def __init__(self, places, sems):
        self.places, self.sems = places, sems
        self.queue = [[] for _ in places]
        self.ready = [False] * len(places)

    def copy(self, m, source):
        return pltpu.make_async_copy(source, self.places[m], self.sems.at[m])

    def plan(self, m, source):
        self.queue[m].append(source)
        if len(self.queue[m]) == 1:
            self.copy(m, source).start()

    def open(self, m):
        if not self.ready[m]:
            self.copy(m, self.queue[m][0]).wait()
            self.ready[m] = True
        return self.places[m]

    def close(self, m):
        self.queue[m].pop(0)
        self.ready[m] = False
        if self.queue[m]:
            self.copy(m, self.queue[m][0]).start()


class Held:
    def __init__(self, slots):
        self.slots = slots

    def open(self, m):
        return self.slots.open(m)

    def close(self, m):
        pass


def transposed(place, source):
    width = source.shape[1]
    for j in range(width // 256):
        where = slice(j * 256, j * 256 + 256)
        place[where, :] = source[:, where].T


def weight_grad(out, left, right, place, stacked=0, extra=None, base=0):
    rows, columns = left.shape[1], right.shape[1]
    transposed(place, left)
    if extra is not None:
        transposed(extra[2], extra[0])

    def column_tile(j, with_extra):
        where = pl.ds(pl.multiple_of(j * 256, 256), 256)
        for i in range(rows // 384):
            down = slice(i * 384, i * 384 + 384)
            total = dot(place[down, :], right[:, where])
            if with_extra:
                there = pl.ds(pl.multiple_of(j * 256 - base, 256), 256)
                total = total + dot(extra[2][down, :], extra[1][:, there])
            if stacked:
                count = 384 // stacked
                cut = total.reshape(count, stacked, 256)
                both = jnp.concatenate([cut[:, :, :128], cut[:, :, 128:]], axis=1)
                here = pl.ds(pl.multiple_of(j * 128, 128), 128)
                out[i * count : (i + 1) * count, :, here] = both.astype(LOW)
            else:
                out[down, where] = total.astype(LOW)

    def plain(j, carry):
        column_tile(j, False)
        return carry

    def joined(j, carry):
        column_tile(j, True)
        return carry

    first = base // 256 if extra is not None else columns // 256
    lax.fori_loop(0, first, plain, 0, unroll=True)
    if extra is not None:
        lax.fori_loop(first, columns // 256, joined, 0, unroll=True)


def crop_rows(c):
    return slice(c * ROWS, c * ROWS + ROWS)


def one_hot(orders, kind, crop):
    ids = orders[kind, crop_rows(crop), :]
    return (ids == lax.broadcasted_iota(jnp.int32, (ROWS, PATCHES), 1)).astype(LOW)


def encode_kernel(crops, *refs):
    refs = list(refs)
    patches, orders, pos = refs[:3]
    lead_w, side_w = refs[3:7], refs[7:11]
    lead_vec, lead_bias, side_vec, side_bias = refs[11:15]
    pack, pos_visible, pos_masked = refs[15:18]
    refs = refs[18:]
    saved = dict(zip(NAMES_SELF, refs))
    refs = refs[len(NAMES_SELF) :]
    places, (sems, stream, resid, latent) = refs[:4], refs[4:8]
    brief = dict(zip(("normed", "qkv", "mixed", "second", "hidden"), refs[8:13]))
    section = lax.axis_index("section")

    @pl.when(section == 0)
    def _():
        slots = Slots(places, sems)
        for source in (lead_w, side_w):
            for m in range(4):
                slots.plan(m, source[m])
        for kind in range(2):
            for c in range(crops):
                rows = dot(one_hot(orders, kind, c), patches[c])
                stream[crop_rows(c), :] = rows
            if kind == 0:
                block_forward(saved, stream, None, resid, slots, lead_vec, lead_bias, latent)
            else:
                block_forward(brief, stream, None, resid, slots, side_vec, side_bias, latent)
            pack[kind] = latent[...].astype(LOW)

    @pl.when(section == 1)
    def _():
        for kind, place_of in enumerate((pos_visible, pos_masked)):
            for c in range(crops):
                pick = one_hot(orders, kind, c)
                place_of[crop_rows(c), :] = sum(dot(pick, pos[t]) for t in (2, 1, 0))


def regress_kernel(crops, *refs):
    refs = list(refs)
    pack, pos_visible, pos_masked, cotangent = refs[:4]
    lead_w, side_w = refs[4:8], refs[8:12]
    lead_vec, lead_bias, side_vec, side_bias = refs[12:16]
    refs = refs[16:]

    def grab(names):
        taken = dict(zip(names, refs))
        del refs[: len(names)]
        return taken

    grad_latents, rows_out, reg_vec, reg_bias, dec_vec, dec_bias = refs[:6]
    del refs[:6]
    reg, dec = grab(OUT_REG), grab(OUT_DEC)
    reg.update(grab(KEEP_REG))
    dec.update(grab(KEEP_DEC))
    places = refs[:4]
    sems, stream, context, resid, regressed, grad, temp, low_temp = refs[4:]
    tokens = crops * ROWS

    @pl.when(lax.axis_index("section") == 1)
    def _():
        slots = Slots(places, sems)
        for source in (lead_w, side_w, lead_w):
            for m in range(4):
                slots.plan(m, source[m])
        stream[...] = side_vec[12:13, :] + pos_masked[...]
        context[...] = pack[0].astype(HIGH) + pos_visible[...]
        block_forward(reg, stream, context, resid, slots, lead_vec, lead_bias, regressed)
        stream[...] = regressed[...] + pos_masked[...]
        block_forward(dec, stream, None, resid, Held(slots), side_vec, side_bias, temp)
        for c in range(crops):
            first = c * ROWS
            rows_out[c, 0:MASKED, :] = regressed[first : first + MASKED, :]
            rows_out[c, MASKED : 2 * MASKED, :] = temp[first : first + MASKED, :]
            grad[first : first + ROWS, :] = jnp.zeros((ROWS, D), HIGH)
            grad[first : first + MASKED, :] = cotangent[c].astype(HIGH)
        block_backward(
            dec, grad, temp, low_temp, slots, side_vec, dec_vec, dec_bias, False, None
        )
        inside = lax.broadcasted_iota(jnp.int32, (ROWS, D), 0) < MASKED
        for c in range(crops):
            here = crop_rows(c)
            apart = regressed[here, :] - pack[1, here, :].astype(HIGH)
            grad[here, :] = grad[here, :] + jnp.where(inside, apart, 0.0)
        block_backward(
            reg, grad, temp, low_temp, slots, lead_vec, reg_vec, reg_bias, True, context
        )
        dec_vec[12:13, :] = jnp.sum(grad[...], axis=0, keepdims=True)
        grad_latents[...] = context[...].astype(LOW)


PAIRS = (("normed", "dqkv"), ("mixed", "dattn"), ("second", "dpre"), ("hidden", "dbranch"))
OUT_DEC = tuple(n for pair in PAIRS for n in pair)
OUT_REG = OUT_DEC + ("normed_c", "dkv_c")
KEEP_DEC = tuple(n for n in NAMES_SELF if n not in OUT_DEC)
KEEP_REG = KEEP_DEC + tuple(n for n in NAMES_CROSS if n not in OUT_REG)


def ship(m, scratch, outs, sems):
    return pltpu.make_async_copy(scratch[m], outs[m], sems.at[m])


def decoder_weights_kernel(stacks, *refs):
    pairs, outs = dict(zip(OUT_DEC, refs[:8])), refs[8:12]
    scratch, (place, sems) = refs[12:16], refs[16:]

    @pl.when(lax.axis_index("section") == 1)
    def _():
        for m in (3, 2, 1, 0):
            left, right = PAIRS[m]
            rows = pairs[left].shape[1]
            weight_grad(
                scratch[m], pairs[left], pairs[right], place.at[0:rows, :], stacks[m]
            )
            ship(m, scratch, outs, sems).start()
        for m in range(4):
            ship(m, scratch, outs, sems).wait()


def finish_kernel(crops, *refs):
    refs = list(refs)
    returned, orders = refs[:2]
    lead_w, lead_vec, lead_bias = refs[2:6], refs[6], refs[7]
    del refs[:8]

    def grab(names):
        taken = dict(zip(names, refs))
        del refs[: len(names)]
        return taken

    enc, reg = grab(NAMES_SELF), grab(OUT_REG)
    outs, (rows_out, enc_vec, enc_bias) = refs[:4], refs[4:7]
    del refs[:7]
    enc.update(grab(NAMES_GRAD))
    places = refs[:4]
    scratch = refs[4:8]
    sems, out_sems, place, place_c, grad, temp, low_temp = refs[8:]
    section = lax.axis_index("section")

    def weights_of(pairs, joined):
        for m in (3, 2, 1, 0):
            left, right = PAIRS[m]
            rows = pairs[left].shape[1]
            extra = (pairs["normed_c"], pairs["dkv_c"], place_c) if joined and m == 0 else None
            weight_grad(
                scratch[m], pairs[left], pairs[right], place.at[0:rows, :], 0, extra, D
            )
            ship(m, scratch, outs, out_sems).start()
        for m in range(4):
            ship(m, scratch, outs, out_sems).wait()

    @pl.when(section == 0)
    def _():
        slots = Slots(places, sems)
        for m in (3, 2, 1, 0):
            slots.plan(m, lead_w[m])
        grad[...] = returned[...].astype(HIGH)
        block_backward(enc, grad, temp, low_temp, slots, lead_vec, enc_vec, enc_bias, False, None)
        for c in range(crops):
            rest = grad[crop_rows(c), :]
            pick = one_hot(orders, 0, c)
            total = jnp.zeros((PATCHES, D), HIGH)
            for _ in range(3):
                part = rest.astype(LOW)
                rest = rest - part.astype(HIGH)
                total = total + dot_tn(pick, part)
            rows_out[c] = total
        weights_of(enc, False)

    @pl.when(section == 1)
    def _():
        weights_of(reg, True)


ANYWHERE = pl.BlockSpec(memory_space=pl.ANY)
INSIDE = pl.BlockSpec(memory_space=pltpu.VMEM)


def specs(shapes):
    return [jax.ShapeDtypeStruct(s, d) for s, d in shapes]


def places_for(shapes):
    return [pltpu.VMEM(s, d) for s, d in shapes]


def params():
    return pltpu.CompilerParams(vmem_limit_bytes=60 << 20)


WEIGHT_SHAPES = [((D, 3 * D), LOW), ((D, D), LOW), ((D, FF), LOW), ((FF, D), LOW)]
SMALL_SHAPES = [((16, D), HIGH), ((1, FF), HIGH)]


def encode(crops, patches, orders, pos, lead_w, side_w, smalls):
    tokens = crops * ROWS
    shapes = [((2, tokens, D), LOW), ((tokens, D), HIGH), ((tokens, D), HIGH)]
    shapes += [save_shape(n, tokens) for n in NAMES_SELF]
    scratch = places_for(WEIGHT_SHAPES) + [pltpu.SemaphoreType.DMA((4,))]
    scratch += places_for([((tokens, D), HIGH)] * 3)
    scratch += places_for(
        [save_shape(n, tokens) for n in ("normed", "qkv", "mixed", "second", "hidden")]
    )
    return pl.pallas_call(
        functools.partial(encode_kernel, crops),
        out_shape=specs(shapes),
        in_specs=[INSIDE] * 3 + [ANYWHERE] * 8 + [INSIDE] * 4,
        out_specs=[INSIDE] * len(shapes),
        scratch_shapes=scratch,
        compiler_params=params(),
        name="encode",
    )(patches, orders, pos, *lead_w, *side_w, *smalls)


def regress(crops, pack, pos_visible, pos_masked, cotangent, lead_w, side_w, smalls):
    tokens = crops * ROWS
    shapes = [((tokens, D), LOW), ((crops, PATCHES, D), HIGH)] + SMALL_SHAPES * 2
    shapes += [save_shape(n, tokens) for n in OUT_REG + OUT_DEC]
    scratch = places_for([save_shape(n, tokens) for n in KEEP_REG + KEEP_DEC])
    scratch += places_for(WEIGHT_SHAPES) + [pltpu.SemaphoreType.DMA((4,))]
    scratch += places_for([((tokens, D), HIGH)] * 6 + [((tokens, D), LOW)])
    return pl.pallas_call(
        functools.partial(regress_kernel, crops),
        out_shape=specs(shapes),
        in_specs=[INSIDE] * 4 + [ANYWHERE] * 8 + [INSIDE] * 4,
        out_specs=[INSIDE] * len(shapes),
        scratch_shapes=scratch,
        compiler_params=params(),
        name="regress",
    )(pack, pos_visible, pos_masked, cotangent, *lead_w, *side_w, *smalls)


def dec_grad_shapes(devices, own_path):
    shapes, stacks = [], []
    for (rows, columns), kind in WEIGHT_SHAPES:
        r = rows // (2 * devices)
        stack = r if own_path and r % 16 else 0
        stacks.append(stack)
        shapes.append(
            ((2 * devices, 2 * r, columns // 2), kind) if stack else ((rows, columns), kind)
        )
    return shapes, tuple(stacks)


def decoder_weights(crops, pairs, devices, own_path):
    shapes, stacks = dec_grad_shapes(devices, own_path)
    return pl.pallas_call(
        functools.partial(decoder_weights_kernel, stacks),
        out_shape=specs(shapes),
        in_specs=[INSIDE] * 8,
        out_specs=[ANYWHERE] * 4,
        scratch_shapes=places_for(shapes)
        + places_for([((FF, crops * ROWS), LOW)])
        + [pltpu.SemaphoreType.DMA((4,))],
        compiler_params=params(),
        name="decoder_weights",
    )(*pairs)


def finish(crops, returned, orders, lead_w, lead_small, enc_saved, reg_pairs):
    tokens = crops * ROWS
    shapes = WEIGHT_SHAPES + [((crops, PATCHES, D), HIGH)] + SMALL_SHAPES
    scratch = places_for([save_shape(n, tokens) for n in NAMES_GRAD])
    scratch += places_for(WEIGHT_SHAPES * 2) + [pltpu.SemaphoreType.DMA((4,))] * 2
    scratch += places_for([((FF, tokens), LOW), ((D, tokens), LOW)])
    scratch += places_for([((tokens, D), HIGH)] * 2 + [((tokens, D), LOW)])
    count = len(enc_saved) + len(reg_pairs)
    return pl.pallas_call(
        functools.partial(finish_kernel, crops),
        out_shape=specs(shapes),
        in_specs=[INSIDE] * 2 + [ANYWHERE] * 4 + [INSIDE] * (2 + count),
        out_specs=[ANYWHERE] * 4 + [INSIDE] * 3,
        scratch_shapes=scratch,
        compiler_params=params(),
        name="finish",
    )(returned, orders, *lead_w, *lead_small, *enc_saved, *reg_pairs)


SMALL_ROWS = 48


class Feed:
    WINDOW = 3

    def __init__(self, groups, shards_in, wholes, sems):
        self.groups, self.shards, self.wholes = groups, shards_in, wholes
        self.own, self.us, self.ur, self.ds, self.dr, self.ys, self.yr, self.cs, self.cr = sems
        self.count = len(shards_in)
        self.section, self.index, self.outer, self.mid, self.core = place()
        self.begun = self.at = 0
        self.done = set()
        self.steps = [("z", 0), ("y", 0), ("z", 1)]
        for m in range(2, self.count):
            self.steps += [("z", m), ("y", m - 1)]
        self.steps.append(("y", self.count - 1))

    def branch(self):
        other = copy.copy(self)
        other.done = set(self.done)
        return other

    def devices(self):
        mid = (self.section, slot(self.outer, 1 - self.mid, self.core))
        core = (self.section, slot(self.outer, self.mid, 1 - self.core))
        return mid, core

    def outer_device(self, k):
        return (self.section, slot((self.outer + k) % self.groups, self.mid, self.core))

    def origin(self, k, far=0, other_core=False):
        outer = (self.outer - k + self.groups) % self.groups
        mid = 1 - self.mid if far else self.mid
        return slot(outer, mid, 1 - self.core if other_core else self.core)

    def own_copy(self, m):
        return pltpu.make_async_copy(
            self.shards[m], self.wholes[m].at[self.index], self.own.at[m]
        )

    def up_copy(self, m, k):
        piece = self.wholes[m].at[self.origin(k)]
        src = self.shards[m] if isinstance(k, int) and k == 0 else piece
        return remote(src, piece, self.us.at[m, k], self.ur.at[m, k], self.outer_device(1))

    def down_copy(self, m, k):
        piece = self.wholes[m].at[self.origin(k)]
        src = self.shards[m] if isinstance(k, int) and k == 0 else piece
        below = self.outer_device(self.groups - 1)
        return remote(src, piece, self.ds.at[m, k], self.dr.at[m, k], below)

    def up_arrival(self, m, k):
        piece = self.wholes[m].at[self.origin(k)]
        return remote(
            piece, piece, self.us.at[m, k - 1], self.ur.at[m, k - 1], self.outer_device(1)
        )

    def down_arrival(self, m, distance):
        k = (self.groups - distance) % self.groups
        piece = self.wholes[m].at[self.origin(k)]
        at = (self.groups - distance + 1) % self.groups
        return remote(piece, piece, self.ds.at[m, at], self.dr.at[m, at], self.outer_device(1))

    def y_copy(self, m, k, own=False, arrival=False):
        piece = self.wholes[m].at[self.origin(k, far=1 if arrival else 0)]
        src = self.shards[m] if own else piece
        return remote(src, piece, self.ys.at[m, k], self.yr.at[m, k], self.devices()[0])

    def c_copy(self, m, k, far, own=False, arrival=False):
        piece = self.wholes[m].at[self.origin(k, far, arrival)]
        src = self.shards[m] if own else piece
        at = k * 2 + far
        return remote(src, piece, self.cs.at[m, at], self.cr.at[m, at], self.devices()[1])

    def begin(self, upto):
        while self.begun < min(upto, self.count):
            m = self.begun

            @pl.when(self.outer < self.groups - 1)
            def _():
                self.up_copy(m, 0).start()

            @pl.when(self.outer > 0)
            def _():
                self.down_copy(m, 0).start()

            self.y_copy(m, 0, own=True).start()
            self.c_copy(m, 0, 0, own=True).start()
            self.own_copy(m).start()
            self.begun += 1

    def step(self):
        kind, m = self.steps[self.at]
        self.at += 1
        if kind == "z":

            top = self.groups - 1

            def spread(k):
                self.y_copy(m, k).start()
                self.c_copy(m, k, 0).start()

            def pass_on(before):
                distance = before + 1

                @pl.when(self.outer >= distance)
                def _():
                    self.up_arrival(m, distance).wait_recv()

                    @pl.when(self.outer < top)
                    def _():
                        self.up_copy(m, distance).start()

                    spread(distance)

                @pl.when(self.outer + distance <= top)
                def _():
                    self.down_arrival(m, distance).wait_recv()

                    @pl.when(self.outer > 0)
                    def _():
                        self.down_copy(m, self.groups - distance).start()

                    spread(self.groups - distance)

            each(top, pass_on)
            self.begin(m + 1 + self.WINDOW)
        else:

            def hand_over(k):
                self.y_copy(m, k, arrival=True).wait_recv()
                self.c_copy(m, k, 1).start()

            each(self.groups, hand_over)

    def pump(self, kind, m):
        while (kind, m) in self.steps[self.at :]:
            self.step()

    def need(self, m):
        self.pump("y", m)
        if m in self.done:
            return
        self.done.add(m)

        def last(k):
            for far in range(2):
                self.c_copy(m, k, far, arrival=True).wait_recv()

        each(self.groups, last)
        self.own_copy(m).wait()

    def drain(self):
        for m in range(self.count):
            self.need(m)
            top = self.groups - 1

            def line_sends(k):
                @pl.when((self.outer < top) & (self.outer >= k))
                def _():
                    self.up_copy(m, k).wait_send()

                @pl.when((self.outer > 0) & (self.outer + k <= top))
                def _():
                    self.down_copy(m, (self.groups - k) % self.groups).wait_send()

            each(self.groups, line_sends)

            def finish_sends(k):
                self.y_copy(m, k).wait_send()
                for far in range(2):
                    self.c_copy(m, k, far).wait_send()

            each(self.groups, finish_sends)


class FedSlots(Slots):
    def __init__(self, places, sems, feed):
        super().__init__(places, sems)
        self.feed = feed
        self.started = [False] * len(places)

    def plan(self, m, piece):
        self.queue[m].append(piece)

    def fetch(self, m):
        if not self.started[m] and self.queue[m]:
            piece = self.queue[m][0]
            self.feed.need(piece)
            self.copy(m, self.feed.flat[piece]).start()
            self.started[m] = True

    def open(self, m):
        self.fetch(m)
        if not self.ready[m]:
            self.copy(m, self.feed.flat[self.queue[m][0]]).wait()
            self.ready[m] = True
        return self.places[m]

    def close(self, m):
        self.queue[m].pop(0)
        self.ready[m] = self.started[m] = False
        if self.queue[m] and self.queue[m][0] in self.feed.done:
            self.fetch(m)


def unpack_small(small, devices, lead_vec, lead_bias, side_vec, side_bias):
    width = D // devices
    per = FF // devices // width
    for d in range(devices):
        lanes = slice(d * width, d * width + width)
        block = small[d].astype(HIGH)
        lead_vec[0:16, lanes] = block[0:16, 0:width]
        side_vec[0:16, lanes] = block[16:32, 0:width]
        for i in range(per):
            first = (d * per + i) * width
            lead_bias[0:1, first : first + width] = block[32 + i : 33 + i, 0:width]
            side_bias[0:1, first : first + width] = block[40 + i : 41 + i, 0:width]


def pack_small(lead_vectors, lead_bias, side_vectors, side_bias):
    width = lead_vectors.shape[1]

    def block(rows, height):
        rows = rows.reshape(-1, width)
        return jnp.pad(rows, ((0, height - rows.shape[0]), (0, 128 - width)))

    return jnp.concatenate(
        [block(lead_vectors, 16), block(side_vectors, 16), block(lead_bias, 8), block(side_bias, 8)]
    )


def layer_kernel(crops, devices, *refs):
    refs = list(refs)

    def grab(n):
        taken = refs[:n]
        del refs[:n]
        return taken

    def named(names):
        return dict(zip(names, grab(len(names))))

    shards_in = grab(9)
    patches, orders, pos, cotangent = grab(4)
    wholes = grab(9)
    rows_out, lead_small_out, dec_small_out = grab(3)
    pairs_out = grab(len(OUT_DEC) + len(OUT_REG))
    own, reg = named(OUT_DEC), named(OUT_REG)
    own.update(named(KEEP_DEC))
    reg.update(named(KEEP_REG))
    places = grab(4)
    lead_vec_grad, lead_bias_grad, dec_vec_grad, dec_bias_grad = grab(4)
    lead_vec, lead_bias, side_vec, side_bias, small = grab(5)
    stream, context, resid, regressed, grad, temp, pos_visible, pos_masked = grab(8)
    low_temp, first_pack, second_pack = grab(3)
    sems, small_sem, x_send, x_recv, pair_sem = grab(5)
    groups = devices // 4
    feed = Feed(groups, shards_in, wholes, refs)
    feed.flat = [None] + [
        w.reshape(devices * w.shape[1], w.shape[2]) for w in wholes[1:]
    ]
    section = feed.section
    tokens = crops * ROWS
    x_device = (1 - section, feed.index)
    greet([*feed.devices(), x_device])
    barrier = pltpu.get_barrier_semaphore()
    each(
        groups - 1,
        lambda k: pl.semaphore_signal(
            barrier, inc=1, device_id=feed.outer_device(k + 1), device_id_type=MESH_ID
        ),
    )
    pl.semaphore_wait(barrier, groups + 2)
    feed.begin(Feed.WINDOW)

    def x_copy(n):
        piece = (first_pack.at[0], first_pack.at[1], second_pack)[n]
        return remote(piece, piece, x_send.at[n], x_recv.at[n], x_device)

    held = [own[n] for n in OUT_DEC] + [reg[n] for n in OUT_REG]

    def pair_copies(first, last):
        return [
            pltpu.make_async_copy(held[i], pairs_out[i], pair_sem.at[i])
            for i in range(first, last)
        ]

    def vectors_in(feed):
        feed.need(0)
        fetched = pltpu.make_async_copy(wholes[0], small, small_sem)
        fetched.start()
        fetched.wait()
        unpack_small(small, devices, lead_vec, lead_bias, side_vec, side_bias)

    def slots_of(feed):
        slots = FedSlots(places, sems, feed)
        for base in (1, 5, 1):
            for m in range(4):
                slots.plan(m, base + m)
        return slots

    start = feed

    @pl.when(section == 0)
    def _():
        feed = start.branch()
        slots = slots_of(feed)
        for kind, vec, bias, keep in ((0, lead_vec, lead_bias, own), (1, side_vec, side_bias, reg)):
            for c in range(crops):
                stream[crop_rows(c), :] = dot(one_hot(orders, kind, c), patches[c])
            if kind == 0:
                vectors_in(feed)
            else:
                names = ("normed", "qkv", "mixed", "second", "hidden")
                keep = {n: reg[n] for n in names}
            block_forward(keep, stream, None, resid, slots, vec, bias, regressed)
            first_pack[kind] = regressed[...].astype(LOW)
            x_copy(kind).start()
        x_copy(2).wait_recv()
        grad[...] = second_pack[...].astype(HIGH)
        block_backward(
            own, grad, temp, low_temp, slots, lead_vec, lead_vec_grad, lead_bias_grad, False, None
        )
        shipped = pair_copies(0, len(OUT_DEC))
        for moved in shipped:
            moved.start()
        for c in range(crops):
            rest = grad[crop_rows(c), :]
            pick = one_hot(orders, 0, c)
            total = jnp.zeros((PATCHES, D), HIGH)
            for _ in range(3):
                part = rest.astype(LOW)
                rest = rest - part.astype(HIGH)
                total = total + dot_tn(pick, part)
            rows_out[c] = total
        pack_small_grads(lead_small_out, lead_vec_grad, lead_bias_grad, 12, devices)
        for n in range(2):
            x_copy(n).wait_send()
        feed.drain()
        for moved in shipped:
            moved.wait()

    @pl.when(section == 1)
    def _():
        feed = start.branch()
        slots = slots_of(feed)
        for kind, place_of in enumerate((pos_visible, pos_masked)):
            for c in range(crops):
                pick = one_hot(orders, kind, c)
                place_of[crop_rows(c), :] = sum(dot(pick, pos[t]) for t in (2, 1, 0))
        vectors_in(feed)
        stream[...] = side_vec[12:13, :] + pos_masked[...]
        for m in range(4):
            slots.fetch(m)
        feed.pump("z", 5)
        x_copy(0).wait_recv()
        context[...] = first_pack[0].astype(HIGH) + pos_visible[...]
        block_forward(reg, stream, context, resid, slots, lead_vec, lead_bias, regressed)
        stream[...] = regressed[...] + pos_masked[...]
        block_forward(own, stream, None, resid, Held(slots), side_vec, side_bias, temp)
        for c in range(crops):
            first = c * ROWS
            rows_out[c, 0:MASKED, :] = regressed[first : first + MASKED, :]
            rows_out[c, MASKED : 2 * MASKED, :] = temp[first : first + MASKED, :]
            grad[first : first + ROWS, :] = jnp.zeros((ROWS, D), HIGH)
            grad[first : first + MASKED, :] = cotangent[c].astype(HIGH)
        block_backward(
            own, grad, temp, low_temp, slots, side_vec, dec_vec_grad, dec_bias_grad, False, None
        )
        shipped = pair_copies(0, len(OUT_DEC))
        for moved in shipped:
            moved.start()
        x_copy(1).wait_recv()
        inside = lax.broadcasted_iota(jnp.int32, (ROWS, D), 0) < MASKED
        for c in range(crops):
            here = crop_rows(c)
            apart = regressed[here, :] - first_pack[1, here, :].astype(HIGH)
            grad[here, :] = grad[here, :] + jnp.where(inside, apart, 0.0)
        block_backward(
            reg, grad, temp, low_temp, slots, lead_vec, lead_vec_grad, lead_bias_grad, True, context
        )
        second_pack[...] = context[...].astype(LOW)
        x_copy(2).start()
        rest = pair_copies(len(OUT_DEC), len(held))
        for moved in rest:
            moved.start()
        dec_vec_grad[12:13, :] = jnp.sum(grad[...], axis=0, keepdims=True)
        pack_small_grads(lead_small_out, lead_vec_grad, lead_bias_grad, 12, devices)
        for t in range(2):
            pack_small_grads(
                dec_small_out.at[t],
                dec_vec_grad.at[:, t * (D // 2) : (t + 1) * (D // 2)],
                dec_bias_grad.at[:, t * (FF // 2) : (t + 1) * (FF // 2)],
                13,
                devices,
                2,
            )
        feed.drain()
        x_copy(2).wait_send()
        for moved in shipped + rest:
            moved.wait()


def layer(crops, devices, pieces, patches, orders, pos, cotangent):
    tokens = crops * ROWS
    groups = devices // 4
    inside = [((crops, PATCHES, D), HIGH), ((devices, LEAD_SMALL, 128), HIGH)]
    inside.append(((2, devices, DEC_SMALL, 128), HIGH))
    pairs = [save_shape(n, tokens) for n in OUT_DEC + OUT_REG]
    scratch = places_for(pairs + [save_shape(n, tokens) for n in KEEP_DEC + KEEP_REG])
    scratch += places_for(WEIGHT_SHAPES + SMALL_SHAPES * 4)
    scratch += places_for([((devices, SMALL_ROWS, 128), LOW)])
    scratch += places_for([((tokens, D), HIGH)] * 8)
    scratch += places_for([((tokens, D), LOW), ((2, tokens, D), LOW), ((tokens, D), LOW)])
    scratch += [pltpu.SemaphoreType.DMA(s) for s in ((4,), (), (3,), (3,), (len(pairs),))]
    scratch += [pltpu.SemaphoreType.DMA((9,))]
    for width in (groups,) * 6 + (2 * groups,) * 2:
        scratch.append(pltpu.SemaphoreType.DMA((9, width)))
    wholes = [((devices,) + p.shape, p.dtype) for p in pieces]
    return pl.pallas_call(
        functools.partial(layer_kernel, crops, devices),
        out_shape=specs(wholes + inside + pairs),
        in_specs=[ANYWHERE] * 9 + [INSIDE] * 4,
        out_specs=[ANYWHERE] * 9 + [INSIDE] * len(inside) + [ANYWHERE] * len(pairs),
        scratch_shapes=scratch,
        compiler_params=pltpu.CompilerParams(
            collective_id=1, has_side_effects=True, vmem_limit_bytes=60 << 20
        ),
        name="layer",
    )(*pieces, patches, orders, pos, cotangent)


LEAD_SMALL = 16
DEC_SMALL = 24
LATE = (2,)
AHEAD = 2
SENDS = 2


def pack_small_grads(out, vectors, bias, rows, chunks, parts=1):
    width = D // (chunks * parts)
    for d in range(chunks):
        lanes = slice(d * width, d * width + width)
        out[d, 0:rows, 0:width] = vectors[0:rows, lanes]
        for i in range(FF // D):
            first = (d * (FF // D) + i) * width
            out[d, rows + i : rows + i + 1, 0:width] = bias[0:1, first : first + width]


def sums_kernel(devices, *refs):
    refs = list(refs)
    groups, half = devices // 4, devices // 2

    def grab(n):
        taken = refs[:n]
        del refs[:n]
        return taken

    own, reg = dict(zip(OUT_DEC, grab(8))), dict(zip(OUT_REG, grab(10)))
    (lead_small_in, dec_small_in) = grab(2)
    lead_out, dec_out = grab(4), grab(4)
    vec_out, bias_out, dec_vec_out, dec_bias_out = grab(4)
    dec_far = grab(5)
    lead_own, lead_c, lead_y, lead_z = (grab(5) for _ in range(4))
    dec_own, dec_near = grab(5), grab(5)
    dec_y, dec_z = grab(5 + len(LATE)), grab(5 + len(LATE))
    late_out, late_in = grab(len(LATE)), grab(len(LATE))
    pair_buf, far_left, far_right, place_of, place_far, lead_total, dec_total = grab(7)
    pair_sem, far_sem, near_sem, load, ready, l_send, l_recv = grab(7)
    c_send, c_recv, x_send, x_recv, y_send, y_recv, u_send, u_recv, d_send, d_recv = refs
    section, index, outer, mid, core = place()
    x_device = (1 - section, index)
    mid_device = (section, slot(outer, 1 - mid, core))
    core_device = (section, slot(outer, mid, 1 - core))

    def outer_device(k):
        return (section, slot((outer + k) % groups, mid, core))

    barrier = pltpu.get_barrier_semaphore()
    greet([mid_device, core_device])

    @pl.when(section == 1)
    def _():
        greet([x_device])

    each(
        groups - 1,
        lambda k: pl.semaphore_signal(
            barrier, inc=1, device_id=outer_device(k + 1), device_id_type=MESH_ID
        ),
    )

    own_of = lead_own + [r.at[1] for r in dec_own] + [dec_own[m].at[0] for m in LATE]
    y_of, z_of = lead_y + dec_y, lead_z + dec_z

    def mine(j):
        return j * 2 + core

    def lead_core(m, j):
        return remote(
            lead_own[m].at[j * 2 + 1 - core],
            lead_c[m].at[j],
            c_send.at[m, j],
            c_recv.at[m, j],
            core_device,
        )

    def dec_core(m, t, j):
        at = 5 + 2 * m + t
        return remote(
            dec_own[m].at[t, j * 2 + 1 - core],
            dec_far[m].at[t, j],
            c_send.at[at, j],
            c_recv.at[at, j],
            core_device,
        )

    def dec_load(m, t, j):
        return pltpu.make_async_copy(
            dec_far[m].at[t, j], dec_near[m].at[j % 2], near_sem.at[m, j % 2]
        )

    def x_copy(m, j):
        return remote(
            dec_own[m].at[0, mine(j)],
            dec_own[m].at[1, mine(j)],
            x_send.at[m, j],
            x_recv.at[m, j],
            x_device,
        )

    def y_copy(n, g):
        return remote(
            own_of[n].at[mine(g * 2 + 1 - mid)],
            y_of[n].at[g],
            y_send.at[n, g],
            y_recv.at[n, g],
            mid_device,
        )

    top = groups - 1

    def up_copy(n, d):
        return remote(
            own_of[n].at[mine(d * 2 + mid)],
            z_of[n].at[d + 1],
            u_send.at[n, d],
            u_recv.at[n, d],
            outer_device(1),
        )

    def down_copy(n, d):
        return remote(
            own_of[n].at[mine(d * 2 + mid)],
            z_of[n].at[d],
            d_send.at[n, d],
            d_recv.at[n, d],
            outer_device(groups - 1),
        )

    small_loads = (
        pltpu.make_async_copy(lead_small_in, lead_own[4], load.at[0]),
        pltpu.make_async_copy(dec_small_in, dec_own[4], load.at[1]),
    )

    def lead_begin(m):
        each(half, lambda j: lead_core(m, j).start())

    def y_begin(n):
        each(groups, lambda g: y_copy(n, g).start())

    def lead_sum(m, send=False):
        def far_pair(g):
            j = g * 2 + 1 - mid
            lead_core(m, j).wait_recv()
            add_rows(lead_own[m], mine(j), lead_c[m], j)
            if send:
                y_copy(m, g).start()

        def near_pair(g):
            j = g * 2 + mid
            lead_core(m, j).wait_recv()
            add_rows(lead_own[m], mine(j), lead_c[m], j)

        each(groups, far_pair)
        each(groups, near_pair)

    def dec_begin(m):
        for t in range(2):
            each(half, lambda j: dec_core(m, t, j).start())

    def dec_sum(m):
        for t in range(2):
            dec_core(m, t, 0).wait_recv()
            dec_load(m, t, 0).start()
            for j in range(half):
                if j + 1 < half:
                    dec_core(m, t, j + 1).wait_recv()
                    dec_load(m, t, j + 1).start()
                dec_load(m, t, j).wait()
                add_rows(dec_own[m].at[t], mine(j), dec_near[m], j % 2)

    def from_mid(n):
        def add_one(d):
            y_copy(n, d).wait_recv()
            add_rows(own_of[n], mine(d * 2 + mid), y_of[n], d)

        def up_first(before):
            d = top - before

            @pl.when(d > outer)
            def _():
                add_one(d)

                @pl.when(outer == 0)
                def _():
                    up_copy(n, d).start()

        def down_first(d):
            @pl.when(d < outer)
            def _():
                add_one(d)

                @pl.when(outer == top)
                def _():
                    down_copy(n, d).start()

        each(top, up_first)
        each(top, down_first)
        y_copy(n, outer).wait_recv()

        @pl.when(outer == 0)
        def _():
            blank(z_of[n], 1)

        @pl.when(outer == top)
        def _():
            blank(z_of[n], top)

    def going_up(n):
        def hop(before):
            d = top - before

            @pl.when(d > outer)
            def _():
                up_copy(n, d).wait_recv()
                add_rows(own_of[n], mine(d * 2 + mid), z_of[n], d + 1)
                up_copy(n, d).start()

        each(top, hop)

    def going_down(n):
        def hop(d):
            @pl.when(d < outer)
            def _():
                down_copy(n, d).wait_recv()
                add_rows(own_of[n], mine(d * 2 + mid), z_of[n], d)
                down_copy(n, d).start()

        each(top, hop)

    def near_half(n):
        @pl.when((outer > 0) & (outer < groups // 2))
        def _():
            going_up(n)

        @pl.when((outer < top) & (outer >= groups // 2))
        def _():
            going_down(n)

    def far_half(n):
        @pl.when((outer > 0) & (outer < groups // 2))
        def _():
            going_down(n)

        @pl.when((outer < top) & (outer >= groups // 2))
        def _():
            going_up(n)

    def across(queue, hooks=()):
        hooks = dict(hooks)
        for i in range(len(queue) + 2):
            if i < len(queue):
                if i >= SENDS:
                    line_sent(queue[i - SENDS], True)
                from_mid(queue[i])
            if i + AHEAD < len(queue):
                y_begin(queue[i + AHEAD])
            if 1 <= i <= len(queue):
                near_half(queue[i - 1])
            if i >= 2:
                far_half(queue[i - 2])
            if i in hooks:
                hooks[i]()

    def blank(buffer, at):
        buffer[at] = jnp.zeros(buffer.shape[1:], buffer.dtype)

    class Pairs:
        def __init__(self, tasks):
            self.tasks, self.at = tasks, 0
            self.begin(0)

        def parts(self, i):
            pairs, m, _ = self.tasks[i]
            first, second = (pairs[name].shape[1] for name in PAIRS[m])
            buf = pair_buf.at[i % 2]
            return buf.at[:, 0:first], buf.at[:, first : first + second]

        def copies(self, i):
            pairs, m, joined = self.tasks[i]
            moved = []
            for side, (name, part) in enumerate(zip(PAIRS[m], self.parts(i))):
                moved.append((pairs[name], part, pair_sem.at[i % 2, side]))
            if joined:
                moved.append((pairs["normed_c"], far_left, far_sem.at[0]))
                moved.append((pairs["dkv_c"], far_right, far_sem.at[1]))
            return [pltpu.make_async_copy(*a) for a in moved]

        def begin(self, i):
            if i < len(self.tasks):
                for moved in self.copies(i):
                    moved.start()

        def take(self, out, stacked):
            i = self.at
            self.begin(i + 1)
            for moved in self.copies(i):
                moved.wait()
            pairs, m, joined = self.tasks[i]
            left, right = self.parts(i)
            extra = (far_left, far_right, place_far) if joined else None
            weight_grad(
                out,
                left,
                right,
                place_of.at[0 : left.shape[1], :],
                stacked,
                extra,
                D,
            )
            self.at += 1

    def lead_view(m):
        rows = lead_own[m].shape[1]
        return lead_own[m].reshape(devices * rows, lead_own[m].shape[2])

    def dec_view(m):
        (rows, columns), _ = WEIGHT_SHAPES[m]
        piece = dec_own[m].shape[2:]
        if piece[1] == columns:
            return dec_own[m].reshape(rows, columns), 0
        return dec_own[m].reshape(2 * devices, *piece), piece[0] // 2

    small_loads[0].start()

    def late_copy(i):
        return remote(late_out[i], late_in[i], l_send.at[i], l_recv.at[i], x_device)

    def total_of(n, where, lanes):
        total = own_of[n][mine(outer * 2 + mid), where, lanes].astype(HIGH)
        total = total + y_of[n][outer, where, lanes].astype(HIGH)
        for k in (outer + 1, outer):
            total = total + z_of[n][k, where, lanes].astype(HIGH)
        return total

    def arrive(n):
        @pl.when(outer > 0)
        def _():
            up_copy(n, outer).wait_recv()

        @pl.when(outer < top)
        def _():
            down_copy(n, outer).wait_recv()

    def emit(out, rows, columns, value):
        stacked = out.shape[-1] != columns
        step = rows // 2 if stacked else 16
        for r in range(rows // step):
            where = pl.ds(r * step, step)
            if stacked:
                for q in range(columns // 128):
                    lanes = slice(q * 128, q * 128 + 128)
                    out[:, (2 * q + r) * 128 : (2 * q + r + 1) * 128] = value(where, lanes)
            else:
                out[where, :] = value(where, slice(None))

    def finish_sum(n):
        arrive(n)
        is_dec, m = divmod(n, 5)
        if m == 4:
            total = dec_total if is_dec else lead_total
            total[...] = total_of(n, slice(None), slice(None))
            vec, bias = (dec_vec_out, dec_bias_out) if is_dec else (vec_out, bias_out)
            count, width = vec.shape
            vec[...] = total[0:count, 0:width]
            for i in range(FF // D):
                bias[0:1, i * width : i * width + width] = total[count + i : count + i + 1, 0:width]
            return
        rows, columns = own_of[n].shape[-2:]
        out = dec_out[m] if is_dec else lead_out[m]
        emit(out, rows, columns, functools.partial(total_of, n))

    def line_sent(n, ends):
        def one(d):
            @pl.when((d > outer) & ((outer == 0) if ends else (outer > 0)))
            def _():
                up_copy(n, d).wait_send()

            @pl.when((d < outer) & ((outer == top) if ends else (outer < top)))
            def _():
                down_copy(n, d).wait_send()

        each(groups, one)

    def sent(queue):
        for n in queue:
            each(groups, lambda g: y_copy(n, g).wait_send())
            line_sent(n, False)
        for n in queue[-SENDS:]:
            line_sent(n, True)

    order = (1, 3, 2, 0, 4)
    early = tuple(m for m in (3, 2, 0, 1, 4) if m not in LATE)

    @pl.when(section == 0)
    def _():
        pairs = Pairs([(own, m, False) for m in order[:4]])
        pairs.take(lead_view(order[0]), 0)
        pl.semaphore_wait(barrier, groups + 2)
        pl.semaphore_signal(ready, inc=1, device_id=x_device, device_id_type=MESH_ID)
        small_loads[0].wait()
        lead_begin(order[0])
        lead_begin(4)
        for i in range(1, 4):
            pairs.take(lead_view(order[i]), 0)
            lead_begin(order[i])
            lead_sum(order[i - 1], i <= AHEAD)
        lead_sum(order[3], 3 < AHEAD)
        lead_sum(4)

        def early_in():
            for e in early:
                each(half, lambda j: x_copy(e, j).wait_recv())

        across(order + tuple(5 + m for m in early), {4 - AHEAD: early_in})
        for m in order:
            finish_sum(m)
        for m in early:
            finish_sum(5 + m)
        for i, m in enumerate(LATE):
            late_copy(i).wait_recv()
            rows, columns = late_in[i].shape
            emit(dec_out[m], rows, columns, lambda *at: late_in[i][at].astype(HIGH))
        for m in range(5):
            each(half, lambda j: lead_core(m, j).wait_send())
        sent(order + tuple(5 + m for m in early))

    @pl.when(section == 1)
    def _():
        dec_order = (3, 2, 0, 1)
        small_loads[1].start()
        tasks = []
        for i in range(4):
            tasks.append((reg, order[i], order[i] == 0))
            tasks.append((own, dec_order[i], False))
        pairs = Pairs(tasks)
        for i in range(4):
            pairs.take(lead_view(order[i]), 0)
            if i == 0:
                pl.semaphore_wait(barrier, groups + 1)
                for moved in small_loads:
                    moved.wait()
                lead_begin(4)
                dec_begin(4)
            lead_begin(order[i])
            pairs.take(*dec_view(dec_order[i]))
            dec_begin(dec_order[i])
            lead_sum(order[i], i < AHEAD)
        lead_sum(4)
        late = tuple(10 + i for i in range(len(LATE)))
        rest = late + tuple(5 + m for m in dec_order) + (9,)

        def early_sums(places):
            for m in places:
                dec_sum(m)

        def early_out(places):
            for m in places:
                each(half, lambda j: x_copy(m, j).start())

        def second_step():
            early_sums(early[1:2])
            pl.semaphore_wait(ready, 1)
            early_out(early[:2])

        def third_step():
            early_sums(early[2:])
            early_out(early[2:])
            dec_sum(LATE[0])

        def late_out_of(i):
            n = late[i]
            arrive(n)
            rows, columns = late_out[i].shape
            for r in range(rows // 16):
                where = pl.ds(r * 16, 16)
                late_out[i][where, :] = total_of(n, where, slice(None)).astype(LOW)
            late_copy(i).start()

        hooks = {0: functools.partial(dec_sum, early[0]), 1: second_step, 2: third_step}
        for i, m in enumerate(LATE):
            if i:
                hooks[2 + i] = functools.partial(dec_sum, m)
            hooks[7 + i] = functools.partial(late_out_of, i)
        across(order + rest, hooks)
        for m in order:
            finish_sum(m)
        for n in rest[len(LATE) :]:
            finish_sum(n)
        for m in range(5):
            each(half, lambda j: lead_core(m, j).wait_send())
            for t in range(2):
                each(half, lambda j: dec_core(m, t, j).wait_send())
        for m in early:
            each(half, lambda j: x_copy(m, j).wait_send())
        for i in range(len(LATE)):
            late_copy(i).wait_send()
        sent(order + rest)


def hand_out_kernel(*refs):
    count = (len(refs) - 1) // 2
    moved = [
        pltpu.make_async_copy(refs[i], refs[count + i], refs[-1].at[i]) for i in range(count)
    ]
    for one in moved:
        one.start()
    for one in moved:
        one.wait()


def hand_out(arrays):
    return pl.pallas_call(
        hand_out_kernel,
        out_shape=specs([(a.shape, a.dtype) for a in arrays]),
        in_specs=[INSIDE] * len(arrays),
        out_specs=[ANYWHERE] * len(arrays),
        scratch_shapes=[pltpu.SemaphoreType.DMA((len(arrays),))],
        name="hand_out",
    )(*arrays)


def sums(crops, devices, rows, own_pairs, reg_pairs, lead_small, dec_small):
    tokens = crops * ROWS
    groups, half = devices // 4, devices // 2
    dec_kinds, _ = dec_grad_shapes(devices, True)
    lead_pieces, dec_pieces, lead_outs, dec_outs = [], [], [], []
    for (shape, kind), (dec_shape, _) in zip(WEIGHT_SHAPES, dec_kinds):
        height, columns = shape
        lead_pieces.append(((height // devices, columns), kind))
        lead_outs.append(((height // devices, columns), HIGH))
        dec_outs.append(((height // (2 * devices), columns), HIGH))
        piece = dec_shape[1:] if len(dec_shape) == 3 else (height // (2 * devices), columns)
        dec_pieces.append((piece, kind))
    lead_pieces.append(((LEAD_SMALL, 128), HIGH))
    dec_pieces.append(((DEC_SMALL, 128), HIGH))
    small_outs = []
    for height, chunks in ((12, devices), (13, 2 * devices)):
        small_outs += [((height, D // chunks), HIGH), ((1, FF // chunks), HIGH)]
    far = [((2, half) + s, k) for s, k in dec_pieces]
    scratch = []
    for lead in ((devices,), (half,), (groups,), (groups + 1,)):
        scratch += places_for([(lead + s, k) for s, k in lead_pieces])
    for lead in ((2, devices), (2,)):
        scratch += places_for([(lead + s, k) for s, k in dec_pieces])
    late_pieces = [dec_pieces[m] for m in LATE]
    for lead in (groups, groups + 1):
        scratch += places_for([((lead,) + s, k) for s, k in dec_pieces + late_pieces])
    scratch += places_for(late_pieces * 2)
    scratch += places_for(
        [((2, tokens, FF + D), LOW)]
        + [((tokens, D), LOW), ((tokens, 2 * D), LOW), ((FF, tokens), LOW), ((D, tokens), LOW)]
        + [((LEAD_SMALL, 128), HIGH), ((DEC_SMALL, 128), HIGH)]
    )
    scratch += [pltpu.SemaphoreType.DMA(s) for s in ((2, 2), (2,), (5, 2), (2,))]
    scratch.append(pltpu.SemaphoreType.REGULAR)
    sems = [(len(LATE),)] * 2 + [(15, half)] * 2 + [(5, half)] * 2
    sems += [(10 + len(LATE), groups)] * 6
    scratch += [pltpu.SemaphoreType.DMA(s) for s in sems]
    outs = pl.pallas_call(
        functools.partial(sums_kernel, devices),
        out_shape=specs(lead_outs + dec_outs + small_outs + far),
        in_specs=[ANYWHERE] * 20,
        out_specs=[INSIDE] * 12 + [ANYWHERE] * 5,
        scratch_shapes=scratch,
        compiler_params=pltpu.CompilerParams(
            collective_id=2, has_side_effects=True, vmem_limit_bytes=61 << 20
        ),
        name="sums",
    )(*own_pairs, *reg_pairs, lead_small, dec_small)
    outs = hand_out(outs[:12])
    lead, dec = list(outs[:4]), list(outs[4:8])
    lead += [outs[8], outs[9].reshape(-1)]
    dec += [outs[10], outs[11].reshape(-1)]
    return rows, lead, dec


def exchange(pieces):
    return [lax.all_gather(p, "dp", axis=0) for p in pieces]


def as_small(parts, rows_of):
    flat = jnp.concatenate([p.reshape(-1) for p in parts])
    block = rows_of * 128
    padded = -(-flat.shape[0] // block) * block
    return jnp.pad(flat, (0, padded - flat.shape[0])).reshape(-1, 128)


def take_flat(flat, shapes):
    taken, offset = [], 0
    for shape in shapes:
        size = 1
        for extent in shape:
            size *= extent
        taken.append(flat[:, offset : offset + size].reshape((-1,) + shape))
        offset += size
    return taken


def spread_columns(gathered):
    return gathered.transpose(1, 0, 2).reshape(gathered.shape[1], -1)


def small_chunks(vectors, bias, chunks):
    rows, columns = vectors.shape
    cut = vectors.reshape(rows, chunks, columns // chunks).transpose(1, 0, 2).reshape(chunks, -1)
    flat = jnp.concatenate([cut, bias.reshape(chunks, -1)], axis=1)
    padded = -(-flat.shape[1] // 1024) * 1024
    return jnp.pad(flat, ((0, 0), (0, padded - flat.shape[1]))).reshape(chunks, -1, 128)


def small_pieces(chunk, rows, chunks):
    flat = chunk.reshape(-1)
    vectors = rows * (D // chunks)
    bias = FF // chunks
    return flat[:vectors].reshape(rows, D // chunks), flat[vectors : vectors + bias]


def total_grads(lead_big, lead_small, dec_big, dec_small):
    devices = lax.axis_size("dp")
    on_encoder = lax.axis_index("section") == 0
    lead_chunks = [g.reshape(devices, -1, g.shape[1]) for g in lead_big]
    lead_chunks.append(small_chunks(*lead_small, devices))
    dec_chunks = [g.reshape(2, devices, -1, g.shape[1]) for g in dec_big]
    dec_chunk_small = small_chunks(*dec_small, 2 * devices)
    dec_chunks.append(dec_chunk_small.reshape((2, devices) + dec_chunk_small.shape[1:]))
    lead_out = [
        lax.psum_scatter(g.astype(jnp.float32), "dp", scatter_dimension=0) for g in lead_chunks
    ]
    dec_out = []
    for g in dec_chunks:
        mine = jnp.where(on_encoder, jnp.zeros_like(g), g).astype(jnp.float32)
        mine = lax.psum_scatter(mine, "dp", scatter_dimension=1)
        dec_out.append(lax.psum_scatter(mine, "section", scatter_dimension=0))
    lead_vectors, lead_bias = small_pieces(lead_out[4], 12, devices)
    dec_vectors, dec_bias = small_pieces(dec_out[4], 13, 2 * devices)
    return lead_out[:4] + [lead_vectors, lead_bias], dec_out[:4] + [dec_vectors, dec_bias]


def run_fused(crops, devices, patches, cotangent, orders, lead, side, smalls):
    pieces = [pack_small(*smalls)] + lead + side
    outs = layer(crops, devices, pieces, patches, orders, position_parts(), cotangent)
    rows, lead_small, dec_small, *pairs = outs[9:]
    own_pairs, reg_pairs = pairs[: len(OUT_DEC)], pairs[len(OUT_DEC) :]
    return sums(crops, devices, rows, own_pairs, reg_pairs, lead_small, dec_small)


def run_apart(crops, devices, patches, cotangent, orders, lead, side, smalls):
    on_encoder = lax.axis_index("section") == 0
    wholes = exchange(lead + side + [as_small(smalls, 16)])
    big = [w.reshape(-1, w.shape[2]) for w in wholes[:8]]
    flat = wholes[8].reshape(devices, -1).astype(jnp.float32)
    lv, lb, sv, sb = take_flat(flat, [p.shape for p in smalls])

    def sixteen(vectors):
        rows = spread_columns(vectors)
        return jnp.pad(rows, ((0, 16 - rows.shape[0]), (0, 0)))

    lead_w, side_w = big[:4], big[4:]
    lead_small = [sixteen(lv), lb.reshape(1, -1)]
    all_small = lead_small + [sixteen(sv), sb.reshape(1, -1)]
    pack, pos_visible, pos_masked, *enc_saved = encode(
        crops, patches, orders, position_parts(), lead_w, side_w, all_small
    )
    arrived = passed_along(pack, "section", 1)
    grad_latents, latent_rows, reg_vec, reg_bias, dec_vec, dec_bias, *pairs = regress(
        crops, arrived, pos_visible, pos_masked, cotangent, lead_w, side_w, all_small
    )
    reg_pairs, dec_pairs = pairs[: len(OUT_REG)], pairs[len(OUT_REG) :]
    returned = passed_along(grad_latents, "section", -1)
    dec_big = decoder_weights(crops, dec_pairs, devices, False)
    *lead_big, grad_rows, enc_vec, enc_bias = finish(
        crops, returned, orders, lead_w, lead_small, enc_saved, reg_pairs
    )
    vec = jnp.where(on_encoder, enc_vec, reg_vec)[:12]
    bias = jnp.where(on_encoder, enc_bias, reg_bias)
    rows = jnp.where(on_encoder, grad_rows, latent_rows)
    lead_small, dec_small = (vec, bias[0]), (dec_vec[:13], dec_bias[0])
    return (rows, *total_grads(lead_big, lead_small, dec_big, dec_small))


def padded_orders(ordering, part):
    cut = ordering[:, MASKED:] if part == 0 else ordering[:, :MASKED]
    cut = jnp.pad(cut, ((0, 0), (0, ROWS - MASKED)), constant_values=-1)
    return cut.reshape(-1, 1)


def shards(
    patches,
    cotangent,
    ordering,
    lead_qkv,
    lead_proj,
    lead_up,
    lead_down,
    lead_vectors,
    lead_bias,
    side_qkv,
    side_proj,
    side_up,
    side_down,
    side_vectors,
    side_bias,
):
    devices = lax.axis_size("dp")
    crops = patches.shape[0]
    orders = jnp.stack([padded_orders(ordering, 0), padded_orders(ordering, 1)])
    lead = [lead_qkv[0], lead_proj[0], lead_up[0], lead_down[0]]
    side = [side_qkv[0], side_proj[0], side_up[0], side_down[0]]
    smalls = [lead_vectors[0], lead_bias[0], side_vectors[0], side_bias[0]]
    own_path = devices % 4 == 0 and lead[0].shape[0] % 16 == 0
    run = run_fused if own_path else run_apart
    rows, lead_out, dec_out = run(
        crops, devices, patches, cotangent, orders, lead, side, smalls
    )
    return (rows[None],) + tuple(o[None] for o in lead_out) + tuple(dec_out)


def solution(mesh):
    return jax.shard_map(
        shards,
        mesh=mesh,
        in_specs=(
            P("dp", None, None),
            P("dp", None, None),
            P("dp", None),
            P("section", "dp", None),
            P("section", "dp", None),
            P("section", "dp", None),
            P("section", "dp", None),
            P("section", None, "dp"),
            P("section", "dp"),
            P("section", "dp", None),
            P("section", "dp", None),
            P("section", "dp", None),
            P("section", "dp", None),
            P("section", None, "dp"),
            P("section", "dp"),
        ),
        out_specs=(
            P("section", "dp", None, None),
            P("section", "dp", None),
            P("section", "dp", None),
            P("section", "dp", None),
            P("section", "dp", None),
            P("section", None, "dp"),
            P("section", "dp"),
            P(("section", "dp"), None),
            P(("section", "dp"), None),
            P(("section", "dp"), None),
            P(("section", "dp"), None),
            P(None, ("section", "dp")),
            P(("section", "dp")),
        ),
        check_vma=False,
    )
```
